32 devices in a mesh: tile: 16 (over z, y, core), ch: 2 (over x).
Axes of the slice: x: 2, y: 2, z: 4, core: 2. Of those that a mesh axis runs over, the one named last changes fastest.
Arguments:
- features: bfloat16 [16, 32, 32, 384], P('tile', None, None, 'ch'), may hold values from -6 to 6
- weight: bfloat16 [3, 3, 384, 384], replicated, may hold values from -0.109375 to 0.109375
- cotangent: bfloat16 [16, 32, 32, 384], P('tile', None, None, 'ch'), may hold values from -6 to 6
- edge_tiles: int32 [16, 4], replicated, may hold values from 0 to 15, as said below
- edge_turns: int32 [16, 4], replicated, may hold values from 0 to 3
- corner_tiles: int32 [16, 4], replicated, may hold values from 0 to 15, as said below
- corner_turns: int32 [16, 4], replicated, may hold values from 0 to 3
Outputs:
- output: bfloat16 [16, 32, 32, 384], P('tile', None, None, 'ch')
- grad_features: bfloat16 [16, 32, 32, 384], P('tile', None, None, 'ch')
- grad_weight: float32 [3, 3, 384, 384], P(None, None, 'ch')
The draws below stay inside these ranges and needn't reach their ends.
Inputs may be any that keep to these rules, and one draw needn't show every extreme that they name: (edge_tiles[t, e] - t) mod 16 lies in 1 .. 4 or in 12 .. 15; both distances 4 and -4 occur. (corner_tiles[t, c] - t) mod 16 lies in 1 .. 4 or in 12 .. 15; both distances 4 and -4 occur.
All inputs are finite; a program needn't handle non-finite values.
Results may differ from the reference program's by a relative error of at most 0.0029.
Values may be sent and summed in bfloat16 or wider, within the bound.
No kernel may reach another device: no remote copies, remote signals or barrier semaphores. Data moves between devices by JAX's collectives and lax.ppermute only.
A program may use at most 64 MiB of HBM per device.

```python
import math
import jax
import jax.numpy as jnp
import numpy as np
from jax import lax

C = 384
S = 32
SPAN = 4
TILES = 16


def draw_near(key, salt):
    base_key = jax.random.fold_in(key, salt)
    distance = jax.random.randint(base_key, (TILES, 4), 1, SPAN + 1)
    direction = jax.random.randint(jax.random.fold_in(base_key, 7), (TILES, 4), 0, 2) * 2 - 1
    offset = distance * direction
    offset = offset.at[0, 0].set(SPAN).at[0, 1].set(-SPAN)
    return jnp.mod(jnp.arange(TILES, dtype=jnp.int32)[:, None] + offset, TILES).astype(jnp.int32)


def draw_edge_tiles(key, part):
    return draw_near(key, 11)


def draw_corner_tiles(key, part):
    return draw_near(key, 23)


def touch_ends(values, key, least, largest):
    longest = values.shape.index(max(values.shape))
    spots = []
    for shift in (0, 1):
        where = [jax.random.randint(jax.random.fold_in(key, axis), (), 0, length) for axis, length in enumerate(values.shape)]
        where[longest] = (where[longest] + shift) % values.shape[longest]
        spots.append(tuple(where))
    return values.at[spots[0]].set(least).at[spots[1]].set(largest)


def shard_levels(rng, extent, cuts, least, top_value):
    loudness = 1.0
    for position, blocks in cuts:
        steps = jax.random.uniform(jax.random.fold_in(jax.random.fold_in(rng, 6), position), (blocks,), jnp.float32, least / len(cuts), top_value / len(cuts))
        loudness = loudness * jnp.repeat(jnp.exp(steps), extent[position] // blocks).reshape((-1,) + (1,) * (len(extent) - 1 - position))
    return loudness


def noise(stream_key, dims, scale, limit, cuts=(), kind=jnp.bfloat16):
    entries = jax.random.normal(stream_key, dims, jnp.float32) * scale
    if len(cuts) > 0:
        entries = shard_levels(stream_key, dims, cuts, -0.22, 0.18) * entries
    return jnp.clip(entries, min=-limit, max=limit).astype(kind)


def setup_inputs(seed: int = 0) -> dict:
    key_list = jax.random.split(jax.random.key(seed), 8)
    return {
        "features": noise(key_list[0], (TILES, S, S, C), 1.0, 6.0, ((0, 16), (3, 2))),
        "weight": noise(key_list[1], (3, 3, C, C), (9 * C) ** -0.5, 0.109375),
        "cotangent": noise(key_list[2], (TILES, S, S, C), 1.0, 6.0, ((0, 16), (3, 2))),
        "edge_tiles": draw_edge_tiles(jax.random.fold_in(key_list[7], 71), 0),
        "edge_turns": touch_ends(jax.random.randint(key_list[4], (TILES, 4), 0, 4), jax.random.fold_in(key_list[4], 1), 0, 3).astype(jnp.int32),
        "corner_tiles": draw_corner_tiles(jax.random.fold_in(key_list[7], 71), 0),
        "corner_turns": touch_ends(jax.random.randint(key_list[6], (TILES, 4), 0, 4), jax.random.fold_in(key_list[6], 1), 0, 3).astype(jnp.int32),
    }


def turn_tables():
    labels = [[3 * row + col for col in range(3)] for row in range(3)]

    def turn_once(block):
        return [[block[col][2 - row] for col in range(3)] for row in range(3)]

    def sides_of(block):
        return [list(block[0]), [block[row][2] for row in range(3)], list(block[2]), [block[row][0] for row in range(3)]]

    def corners_of(block):
        return [block[0][0], block[0][2], block[2][2], block[2][0]]
    base_sides = sides_of(labels)
    base_corners = corners_of(labels)
    edge_table = np.zeros((4, 4), np.int32)
    corner_table = np.zeros((4, 4), np.int32)
    for border in range(4):
        turned = labels
        for quarter in range(4):
            wanted = sides_of(turned)[(border + 2) % 4]
            for side_index in range(4):
                if base_sides[side_index] == wanted:
                    edge_table[border, quarter] = side_index
                if base_sides[side_index][::-1] == wanted:
                    edge_table[border, quarter] = side_index + 4
            corner_cell = corners_of(turned)[(border + 2) % 4]
            for corner_index in range(4):
                if base_corners[corner_index] == corner_cell:
                    corner_table[border, quarter] = corner_index
            turned = turn_once(turned)
    return (edge_table, corner_table)

def rounded(values):
    return lax.optimization_barrier(values.astype(jnp.bfloat16)).astype(jnp.float32)

def reference(features, weight, cotangent, edge_tiles, edge_turns, corner_tiles, corner_turns):
    edge_table, corner_table = turn_tables()
    tile_count, side_len, _, chan_count = features.shape
    sides = jnp.stack([features[:, 0], features[:, :, -1], features[:, -1], features[:, :, 0]], axis=1)
    sides_both = jnp.concatenate([sides, sides[:, :, ::-1]], axis=1)
    corners = jnp.stack([features[:, 0, 0], features[:, 0, -1], features[:, -1, -1], features[:, -1, 0]], axis=1)
    edge_slots = [jnp.asarray(edge_table[border])[edge_turns[:, border]] for border in range(4)]
    corner_slots = [jnp.asarray(corner_table[border])[corner_turns[:, border]] for border in range(4)]
    halos = [sides_both[edge_tiles[:, border], edge_slots[border]] for border in range(4)]
    corner_halos = [corners[corner_tiles[:, border], corner_slots[border]] for border in range(4)]
    padded = jnp.pad(features, ((0, 0), (1, 1), (1, 1), (0, 0)))
    padded = padded.at[:, 0, 1:-1].set(halos[0]).at[:, 1:-1, -1].set(halos[1])
    padded = padded.at[:, -1, 1:-1].set(halos[2]).at[:, 1:-1, 0].set(halos[3])
    padded = padded.at[:, 0, 0].set(corner_halos[0]).at[:, 0, -1].set(corner_halos[1])
    padded = padded.at[:, -1, -1].set(corner_halos[2]).at[:, -1, 0].set(corner_halos[3])
    rows = tile_count * side_len * side_len
    cot_rows = cotangent.reshape(rows, chan_count)
    output = jnp.zeros((rows, chan_count), jnp.float32)
    grad_padded = jnp.zeros(padded.shape, jnp.float32)
    grads = []
    for row_off in range(3):
        for col_off in range(3):
            window = padded[:, row_off:row_off + side_len, col_off:col_off + side_len].reshape(rows, chan_count)
            output = output + jnp.dot(window, weight[row_off, col_off], preferred_element_type=jnp.float32)
            back = jnp.dot(cot_rows, weight[row_off, col_off].T, preferred_element_type=jnp.float32)
            grad_padded = grad_padded.at[:, row_off:row_off + side_len, col_off:col_off + side_len].add(back.reshape(tile_count, side_len, side_len, chan_count))
            grads.append(jnp.dot(window.T, cot_rows, preferred_element_type=jnp.float32))
    grad_weight = jnp.stack(grads).reshape(3, 3, chan_count, chan_count) * (1.0 / math.sqrt(rows))
    pieces = [grad_padded[:, 0, 1:-1], grad_padded[:, 1:-1, -1], grad_padded[:, -1, 1:-1], grad_padded[:, 1:-1, 0]]
    corner_pieces = [grad_padded[:, 0, 0], grad_padded[:, 0, -1], grad_padded[:, -1, -1], grad_padded[:, -1, 0]]
    collected = jnp.zeros((tile_count, 8, side_len, chan_count), jnp.float32)
    corner_sums = jnp.zeros((tile_count, 4, chan_count), jnp.float32)
    for border in range(4):
        collected = collected.at[edge_tiles[:, border], edge_slots[border]].add(rounded(pieces[border]))
        corner_sums = corner_sums.at[corner_tiles[:, border], corner_slots[border]].add(rounded(corner_pieces[border]))
    side_sums = collected[:, :4] + collected[:, 4:, ::-1]
    interior = grad_padded[:, 1:-1, 1:-1]
    interior = interior.at[:, 0].add(side_sums[:, 0]).at[:, :, -1].add(side_sums[:, 1])
    interior = interior.at[:, -1].add(side_sums[:, 2]).at[:, :, 0].add(side_sums[:, 3])
    interior = interior.at[:, 0, 0].add(corner_sums[:, 0]).at[:, 0, -1].add(corner_sums[:, 1])
    interior = interior.at[:, -1, -1].add(corner_sums[:, 2]).at[:, -1, 0].add(corner_sums[:, 3])
    output = output.reshape(features.shape).astype(jnp.bfloat16)
    return (output, interior.astype(jnp.bfloat16), grad_weight)
```

```python
import math

import jax
import jax.numpy as jnp
import numpy as np
from jax import lax
from jax.sharding import PartitionSpec as P

SPAN = 4


def turn_tables():
    labels = [[3 * row + col for col in range(3)] for row in range(3)]

    def turn_once(block):
        return [[block[col][2 - row] for col in range(3)] for row in range(3)]

    def sides_of(block):
        return [
            list(block[0]),
            [block[row][2] for row in range(3)],
            list(block[2]),
            [block[row][0] for row in range(3)],
        ]

    def corners_of(block):
        return [block[0][0], block[0][2], block[2][2], block[2][0]]

    base_sides = sides_of(labels)
    base_corners = corners_of(labels)
    edge_table = np.zeros((4, 4), np.int32)
    corner_table = np.zeros((4, 4), np.int32)
    for border in range(4):
        turned = labels
        for quarter in range(4):
            wanted = sides_of(turned)[(border + 2) % 4]
            for side_index in range(4):
                if base_sides[side_index] == wanted:
                    edge_table[border, quarter] = side_index
                if base_sides[side_index][::-1] == wanted:
                    edge_table[border, quarter] = side_index + 4
            corner_cell = corners_of(turned)[(border + 2) % 4]
            for corner_index in range(4):
                if base_corners[corner_index] == corner_cell:
                    corner_table[border, quarter] = corner_index
            turned = turn_once(turned)
    return (edge_table, corner_table)


def moved(value, axis, pairs):
    return lax.ppermute(value, axis, pairs)


def by_offset(value, offset, count):
    return moved(value, "tile", [(i, (i + offset) % count) for i in range(count)])


def by_mask(value, mask, count):
    return moved(value, "tile", [(i, i ^ mask) for i in range(count)])


def mask_stages(count):
    bits = [1 << b for b in range(count.bit_length() - 1)]
    stages = [bits[:1]]
    rest = bits[1:]
    while rest:
        stages.append(rest[:2])
        rest = rest[2:]
    return stages


def group_masks(bits):
    masks = [0]
    for bit in bits:
        masks = masks + [m + bit for m in masks]
    return masks


def sum_over_tiles(partial, own_tile, count):
    stages = mask_stages(count)
    held = partial
    for index, bits in enumerate(stages):
        masks = group_masks(bits)
        part = held.shape[0] // len(masks)
        base = (own_tile // bits[0]) % len(masks)
        kind = jnp.float32 if index == 0 else jnp.bfloat16

        def piece(mask):
            return lax.dynamic_slice_in_dim(held, (base ^ (mask // bits[0])) * part, part, 0)

        got = [by_mask(piece(mask).astype(kind), mask, count) for mask in masks[1:]]
        total = piece(0)
        for value in got:
            total = total + value.astype(jnp.float32)
        held = total
    held = held.astype(jnp.bfloat16)
    for bits in stages[::-1]:
        masks = group_masks(bits)
        part = held.shape[0]
        base = (own_tile // bits[0]) % len(masks)
        got = [held] + [by_mask(held, mask, count) for mask in masks[1:]]
        whole = jnp.zeros((part * len(masks), held.shape[1]), held.dtype)
        for mask, value in zip(masks, got):
            whole = lax.dynamic_update_slice_in_dim(
                whole, value, (base ^ (mask // bits[0])) * part, 0
            )
        held = whole
    return held


def body(features, weight, cotangent, edge_tiles, edge_turns, corner_tiles, corner_turns):
    edge_table, corner_table = turn_tables()
    count = lax.axis_size("tile")
    own_tile = lax.axis_index("tile")
    own_ch = lax.axis_index("ch")
    field = features[0]
    side = field.shape[0]
    part = field.shape[2]
    chans = weight.shape[3]
    rows = side * side
    start = own_ch * part
    offsets = list(range(-SPAN, 0)) + list(range(1, SPAN + 1))
    others = [(0, 1), (1, 0)]
    cells = jnp.arange(side)

    cot_own = cotangent[0].reshape(rows, part)
    cot_other = moved(cot_own, "ch", others)

    sides = jnp.concatenate([field[0], field[:, -1], field[-1], field[:, 0]], axis=0)
    near = jnp.concatenate([by_offset(sides, -offset, count) for offset in offsets], axis=0)

    def position(target):
        wrapped = jnp.mod(target - own_tile, count)
        signed = jnp.where(wrapped > count // 2, wrapped - count, wrapped)
        return jnp.where(signed < 0, signed + SPAN, signed + SPAN - 1)

    edge_slot_all = jnp.asarray(edge_table)[jnp.arange(4)[None, :], edge_turns]
    corner_slot_all = jnp.asarray(corner_table)[jnp.arange(4)[None, :], corner_turns]
    corner_cell = jnp.asarray([0, side - 1, 3 * side - 1, 2 * side])

    def side_cell(slots):
        along = jnp.where((slots >= 4)[..., None], side - 1 - cells, cells)
        return (slots % 4)[..., None] * side + along

    edge_from = position(edge_tiles[own_tile])[:, None] * (4 * side) + side_cell(edge_slot_all[own_tile])
    corner_from = position(corner_tiles[own_tile]) * (4 * side) + corner_cell[corner_slot_all[own_tile]]
    wanted = jnp.concatenate([edge_from.reshape(-1), corner_from])
    pick = (wanted[:, None] == jnp.arange(8 * 4 * side)[None, :]).astype(jnp.bfloat16)
    halos = jnp.dot(pick, near, preferred_element_type=jnp.float32).astype(jnp.bfloat16)
    top, right, bottom, left = [halos[e * side : (e + 1) * side] for e in range(4)]
    corners = [halos[4 * side + c : 4 * side + c + 1] for c in range(4)]
    tall = jnp.concatenate([top[None], field, bottom[None]], axis=0)
    west = jnp.concatenate([corners[0], left, corners[3]], axis=0)[:, None]
    east = jnp.concatenate([corners[1], right, corners[2]], axis=0)[:, None]
    shifted = [
        jnp.concatenate([west, tall[:, :-1]], axis=1),
        tall,
        jnp.concatenate([tall[:, 1:], east], axis=1),
    ]
    flat = (side + 2) * side
    columns = jnp.concatenate([s.reshape(flat, part) for s in shifted], axis=1)

    def both(own, other):
        return jnp.where(
            own_ch == 0,
            jnp.concatenate([own, other], axis=-1),
            jnp.concatenate([other, own], axis=-1),
        )

    cot_full = both(cot_own, cot_other)

    grads = [
        lax.dot_general(
            columns[a * side : a * side + rows],
            cot_full,
            (((0,), (0,)), ((), ())),
            preferred_element_type=jnp.float32,
        )
        for a in range(3)
    ]
    chunk = -(-9 * part // (16 * count)) * 16
    padding = jnp.zeros((chunk * count - 9 * part, chans), jnp.float32)
    local_grad = jnp.concatenate(grads + [padding], axis=0) * (1.0 / math.sqrt(count * rows))
    grad_weight = sum_over_tiles(local_grad, own_tile, count)[: 9 * part]
    grad_weight = grad_weight.astype(jnp.float32).reshape(3, 3, part, chans)

    weight_back = lax.dynamic_slice_in_dim(weight, start, part, 2)
    zeros = jnp.zeros((2 * side, chans), jnp.bfloat16)
    cot_tall = jnp.concatenate([zeros, cot_full, zeros], axis=0)
    cot_rows = jnp.concatenate([cot_tall[(2 - a) * side : (2 - a) * side + flat] for a in range(3)], axis=1)
    backs = []
    for b in range(3):
        taps = jnp.concatenate([weight_back[a, b] for a in range(3)], axis=1)
        back = lax.dot_general(
            cot_rows, taps, (((1,), (1,)), ((), ())), preferred_element_type=jnp.float32
        )
        backs.append(back.reshape(side + 2, side, part))
    blank = jnp.zeros((side + 2, 1, part), jnp.float32)
    inner = (
        jnp.concatenate([backs[0][:, 1:], blank], axis=1)
        + backs[1]
        + jnp.concatenate([blank, backs[2][:, :-1]], axis=1)
    )
    west_back, east_back = backs[0][:, 0], backs[2][:, -1]
    pieces = jnp.concatenate(
        [
            inner[0],
            east_back[1:-1],
            inner[-1],
            west_back[1:-1],
            west_back[:1],
            east_back[:1],
            east_back[-1:],
            west_back[-1:],
            jnp.zeros((4, part), jnp.float32),
        ],
        axis=0,
    ).astype(jnp.bfloat16)
    inner = inner[1:-1]
    got = jnp.concatenate([by_offset(pieces, offset, count) for offset in offsets], axis=0)
    sources = jnp.mod(own_tile - jnp.asarray(offsets), count)
    edge_to = jnp.where(
        (edge_tiles[sources] == own_tile)[..., None], side_cell(edge_slot_all[sources]), -1
    ).reshape(8, 4 * side)
    corner_to = jnp.where(
        corner_tiles[sources] == own_tile, corner_cell[corner_slot_all[sources]], -1
    )
    target = jnp.concatenate([edge_to, corner_to, jnp.full((8, 4), -1)], axis=1).reshape(-1)
    place = (jnp.arange(4 * side)[:, None] == target[None, :]).astype(jnp.bfloat16)
    sums = jnp.dot(place, got, preferred_element_type=jnp.float32)
    inner = inner.at[0].add(sums[:side]).at[:, -1].add(sums[side : 2 * side])
    inner = inner.at[-1].add(sums[2 * side : 3 * side]).at[:, 0].add(sums[3 * side :])
    grad_features = inner.astype(jnp.bfloat16)[None]

    field_other = moved(jnp.concatenate([field.reshape(rows, part), halos], axis=0), "ch", others)
    other_field = field_other[:rows].reshape(side, side, part)
    other_halos = field_other[rows:]

    def columns_of(field, halos):
        top, right, bottom, left = [halos[e * side : (e + 1) * side] for e in range(4)]
        corners = [halos[4 * side + c : 4 * side + c + 1] for c in range(4)]
        tall = jnp.concatenate([top[None], field, bottom[None]], axis=0)
        west = jnp.concatenate([corners[0], left, corners[3]], axis=0)[:, None]
        east = jnp.concatenate([corners[1], right, corners[2]], axis=0)[:, None]
        return [
            jnp.concatenate([west, tall[:, :-1]], axis=1).reshape(flat, part),
            tall.reshape(flat, part),
            jnp.concatenate([tall[:, 1:], east], axis=1).reshape(flat, part),
        ]

    others_columns = columns_of(other_field, other_halos)
    weight_out = lax.dynamic_slice_in_dim(weight, start, part, 3)
    weight_own = lax.dynamic_slice_in_dim(weight_out, start, part, 2)
    weight_other = lax.dynamic_slice_in_dim(weight_out, part - start, part, 2)
    output = jnp.zeros((rows, part), jnp.float32)
    for a in range(3):
        for b in range(3):
            output = output + jnp.dot(
                columns[a * side : a * side + rows, b * part : (b + 1) * part],
                weight_own[a, b],
                preferred_element_type=jnp.float32,
            )
            output = output + jnp.dot(
                others_columns[b][a * side : a * side + rows],
                weight_other[a, b],
                preferred_element_type=jnp.float32,
            )
    output = output.astype(jnp.bfloat16).reshape(1, side, side, part)
    return (output, grad_features, grad_weight)


def solution(mesh):
    return jax.shard_map(
        body,
        mesh=mesh,
        in_specs=(
            P("tile", None, None, "ch"),
            P(),
            P("tile", None, None, "ch"),
            P(),
            P(),
            P(),
            P(),
        ),
        out_specs=(
            P("tile", None, None, "ch"),
            P("tile", None, None, "ch"),
            P(None, None, "ch", None),
        ),
        check_vma=False,
    )
```

```python
import functools
import math

import jax
import jax.numpy as jnp
import numpy as np
from jax import lax
from jax.experimental import pallas as pl
from jax.experimental.pallas import tpu as pltpu
from jax.sharding import PartitionSpec as P

SPAN = 4
OFFSETS = list(range(-SPAN, 0)) + list(range(1, SPAN + 1))
EXTRA = 16


def turn_tables():
    labels = [[3 * row + col for col in range(3)] for row in range(3)]

    def turn_once(block):
        return [[block[col][2 - row] for col in range(3)] for row in range(3)]

    def sides_of(block):
        return [
            list(block[0]),
            [block[row][2] for row in range(3)],
            list(block[2]),
            [block[row][0] for row in range(3)],
        ]

    def corners_of(block):
        return [block[0][0], block[0][2], block[2][2], block[2][0]]

    base_sides = sides_of(labels)
    base_corners = corners_of(labels)
    edge_table = np.zeros((4, 4), np.int32)
    corner_table = np.zeros((4, 4), np.int32)
    for border in range(4):
        turned = labels
        for quarter in range(4):
            wanted = sides_of(turned)[(border + 2) % 4]
            for side_index in range(4):
                if base_sides[side_index] == wanted:
                    edge_table[border, quarter] = side_index
                if base_sides[side_index][::-1] == wanted:
                    edge_table[border, quarter] = side_index + 4
            corner_cell = corners_of(turned)[(border + 2) % 4]
            for corner_index in range(4):
                if base_corners[corner_index] == corner_cell:
                    corner_table[border, quarter] = corner_index
            turned = turn_once(turned)
    return np.concatenate([edge_table, corner_table], axis=0)


def by_offset(value, offset, count):
    return lax.ppermute(value, "tile", [(i, (i + offset) % count) for i in range(count)])


def by_mask(value, mask, count):
    return lax.ppermute(value, "tile", [(i, i ^ mask) for i in range(count)])


def mask_stages(count):
    bits = [1 << b for b in range(count.bit_length() - 1)]
    stages = [bits[:1]]
    rest = bits[1:]
    while rest:
        stages.append(rest[:2])
        rest = rest[2:]
    return stages


def group_masks(bits):
    masks = [0]
    for bit in bits:
        masks = masks + [m + bit for m in masks]
    return masks


def slot_of_mask(mask, count):
    place = 0
    for bits in mask_stages(count):
        size = 1 << len(bits)
        place = place * size + (mask // bits[0]) % size
    return place


def corner_spot(slot, side):
    return jnp.where(
        slot == 0, 0, jnp.where(slot == 1, side - 1, jnp.where(slot == 2, 3 * side - 1, 2 * side))
    )


def vmem(shape, dtype):
    return jax.ShapeDtypeStruct(shape, dtype)


def call(kernel, outs, args, smem=(), scratch=(), flops=0):
    in_specs = [
        pl.BlockSpec(memory_space=pltpu.SMEM if i in smem else pltpu.VMEM) for i in range(len(args))
    ]
    size = sum(math.prod(x.shape) * x.dtype.itemsize for x in list(args) + list(outs))
    return pl.pallas_call(
        kernel,
        out_shape=tuple(outs),
        in_specs=in_specs,
        out_specs=tuple(pl.BlockSpec(memory_space=pltpu.VMEM) for _ in outs),
        scratch_shapes=list(scratch),
        compiler_params=pltpu.CompilerParams(vmem_limit_bytes=40 * 1024 * 1024),
        cost_estimate=pl.CostEstimate(flops=flops, bytes_accessed=size, transcendentals=0),
    )(*args)


def sides_kernel(side, field_ref, sides_ref):
    sides_ref[0:side, :] = field_ref[0]
    sides_ref[side : 2 * side, :] = field_ref[:, side - 1, :]
    sides_ref[2 * side : 3 * side, :] = field_ref[side - 1]
    sides_ref[3 * side : 4 * side, :] = field_ref[:, 0, :]


def shifted_columns(side, part, field_ref, halos, out_ref):
    rows = side * side
    flat = rows + 2 * side
    tall = jnp.concatenate(
        [
            halos[0:side].astype(jnp.float32),
            field_ref[...].reshape(rows, part).astype(jnp.float32),
            halos[2 * side : 3 * side].astype(jnp.float32),
        ],
        axis=0,
    )
    edge = halos.astype(jnp.float32)
    corner = [edge[4 * side + c : 4 * side + c + 1] for c in range(4)]
    east = jnp.concatenate([corner[1], edge[side : 2 * side], corner[2]], axis=0)
    west = jnp.concatenate([corner[0], edge[3 * side : 4 * side], corner[3]], axis=0)
    spread = lambda col: jnp.broadcast_to(col[:, None, :], (side + 2, side, part)).reshape(flat, part)
    column = lax.broadcasted_iota(jnp.int32, (flat, part), 0) % side
    out_ref[0] = jnp.where(column == 0, spread(west), pltpu.roll(tall, 1, 0)).astype(jnp.bfloat16)
    out_ref[1] = tall.astype(jnp.bfloat16)
    out_ref[2] = jnp.where(column == side - 1, spread(east), pltpu.roll(tall, flat - 1, 0)).astype(
        jnp.bfloat16
    )


def halo_kernel(side, part, tables_ref, et_ref, eu_ref, ct_ref, cu_ref, *refs):
    near_refs, halos_ref = refs[: len(OFFSETS)], refs[len(OFFSETS)]
    count = lax.axis_size("tile")
    own = lax.axis_index("tile")

    def base(target):
        wrapped = lax.rem(target - own + count, count)
        signed = jnp.where(wrapped > count // 2, wrapped - count, wrapped)
        return jnp.where(signed < 0, signed + SPAN, signed + SPAN - 1) * (4 * side)

    row = lax.broadcasted_iota(jnp.int32, (4 * side + EXTRA, 1), 0)
    wanted = jnp.full((4 * side + EXTRA, 1), -1, jnp.int32)
    for e in range(4):
        slot = tables_ref[e, eu_ref[own, e]]
        start = base(et_ref[own, e]) + lax.rem(slot, 4) * side
        along = row - e * side
        along = jnp.where(slot >= 4, side - 1 - along, along)
        wanted = jnp.where((row >= e * side) & (row < (e + 1) * side), start + along, wanted)
        corner = tables_ref[4 + e, cu_ref[own, e]]
        spot = base(ct_ref[own, e]) + corner_spot(corner, side)
        wanted = jnp.where(row == 4 * side + e, spot, wanted)
    near = jnp.concatenate([ref[...] for ref in near_refs], axis=0)
    lane = lax.broadcasted_iota(jnp.int32, (4 * side + EXTRA, near.shape[0]), 1)
    pick = jnp.where(lane == wanted, 1.0, 0.0).astype(jnp.bfloat16)
    halos_ref[...] = jnp.dot(pick, near, preferred_element_type=jnp.float32).astype(jnp.bfloat16)


def grad_weight_kernel(side, part, chunk, scale, field_ref, halos_ref, cot_ref, out_ref, cols, total):
    rows = side * side
    chans = cot_ref.shape[1]
    count = lax.axis_size("tile")
    own = lax.axis_index("tile")
    shifted_columns(side, part, field_ref, halos_ref[...], cols)
    cot = cot_ref[...]
    for a in range(3):
        for b in range(3):
            tap = 3 * a + b
            total[tap * part : (tap + 1) * part, :] = (
                lax.dot_general(
                    cols[b, a * side : a * side + rows, :],
                    cot,
                    (((0,), (0,)), ((), ())),
                    preferred_element_type=jnp.float32,
                )
                * scale
            )
    total[9 * part :, :] = jnp.zeros((chunk * count - 9 * part, chans), jnp.float32)
    for mask in range(count):
        to = slot_of_mask(mask, count) * chunk
        start = pl.multiple_of((own ^ mask) * chunk, 16)
        out_ref[to : to + chunk, :] = total[pl.ds(start, chunk), :]


def unfold_kernel(part, chunk, mine_ref, other_ref, out_ref):
    count = lax.axis_size("tile")
    own = lax.axis_index("tile")
    half = mine_ref.shape[0] // chunk
    whole = 9 * part
    core = lax.rem(own, 2)
    for block in range(count):
        size = min(chunk, whole - block * chunk)
        if size <= 0:
            continue
        mask = own ^ block
        place = 0
        for bits in mask_stages(count)[1:]:
            span = 1 << len(bits)
            place = place * span + lax.rem(mask // bits[0], span)
        start = pl.multiple_of(place * chunk, 16)
        mine = mine_ref[pl.ds(start, size), :]
        other = other_ref[pl.ds(start, size), :]
        value = jnp.where(core == block % 2, mine.astype(jnp.float32), other.astype(jnp.float32))
        out_ref[block * chunk : block * chunk + size, :] = value


def both_kernel(own_ref, other_ref, out_ref):
    part = own_ref.shape[1]

    @pl.when(lax.axis_index("ch") == 0)
    def _():
        out_ref[:, 0:part] = own_ref[...]
        out_ref[:, part:] = other_ref[...]

    @pl.when(lax.axis_index("ch") != 0)
    def _():
        out_ref[:, 0:part] = other_ref[...]
        out_ref[:, part:] = own_ref[...]


def back_kernel(side, part, cot_ref, weight_ref, inner_ref, pieces_ref, tall):
    rows = side * side
    flat = rows + 2 * side
    start = pl.multiple_of(lax.axis_index("ch") * part, 16)
    chans = cot_ref.shape[1]
    blank = jnp.zeros((2 * side, chans), jnp.bfloat16)
    tall[0 : 2 * side, :] = blank
    tall[2 * side : 2 * side + rows, :] = cot_ref[...]
    tall[2 * side + rows :, :] = blank
    backs = []
    for b in range(3):
        back = jnp.zeros((flat, part), jnp.float32)
        for a in range(3):
            back = back + lax.dot_general(
                tall[(2 - a) * side : (2 - a) * side + flat, :],
                weight_ref[3 * a + b, pl.ds(start, part), :],
                (((1,), (1,)), ((), ())),
                preferred_element_type=jnp.float32,
            )
        backs.append(back)
    column = lax.broadcasted_iota(jnp.int32, (flat, part), 0) % side
    inner = (
        jnp.where(column == side - 1, 0.0, pltpu.roll(backs[0], flat - 1, 0))
        + backs[1]
        + jnp.where(column == 0, 0.0, pltpu.roll(backs[2], 1, 0))
    )
    inner_ref[...] = inner[side : side + rows]
    west = backs[0].reshape(side + 2, side, part)[:, 0, :]
    east = backs[2].reshape(side + 2, side, part)[:, side - 1, :]
    pieces_ref[...] = jnp.concatenate(
        [
            inner[0:side],
            east[1 : side + 1],
            inner[side + rows :],
            west[1 : side + 1],
            west[0:1],
            east[0:1],
            east[side + 1 :],
            west[side + 1 :],
            jnp.zeros((EXTRA - 4, part), jnp.float32),
        ],
        axis=0,
    ).astype(jnp.bfloat16)


def add_halo_kernel(side, part, tables_ref, et_ref, eu_ref, ct_ref, cu_ref, inner_ref, *refs):
    got_refs, out_ref = refs[: len(OFFSETS)], refs[len(OFFSETS)]
    count = lax.axis_size("tile")
    own = lax.axis_index("tile")
    block = 4 * side + EXTRA
    total = len(OFFSETS) * block
    lane = lax.broadcasted_iota(jnp.int32, (1, total), 1)
    target = jnp.full((1, total), -1, jnp.int32)
    for index, offset in enumerate(OFFSETS):
        source = lax.rem(own - offset + count, count)
        for e in range(4):
            first = index * block + e * side
            slot = tables_ref[e, eu_ref[source, e]]
            along = lane - first
            along = jnp.where(slot >= 4, side - 1 - along, along)
            hit = (lane >= first) & (lane < first + side) & (et_ref[source, e] == own)
            target = jnp.where(hit, lax.rem(slot, 4) * side + along, target)
            spot = corner_spot(tables_ref[4 + e, cu_ref[source, e]], side)
            hit = (lane == index * block + 4 * side + e) & (ct_ref[source, e] == own)
            target = jnp.where(hit, spot, target)
    row = lax.broadcasted_iota(jnp.int32, (4 * side, total), 0)
    place = jnp.where(row == target, 1.0, 0.0).astype(jnp.bfloat16)
    got = jnp.concatenate([ref[...] for ref in got_refs], axis=0)
    sums = jnp.dot(place, got, preferred_element_type=jnp.float32)
    rows = side * side
    spread = lambda col: jnp.broadcast_to(col[:, None, :], (side, side, part)).reshape(rows, part)
    column = lax.broadcasted_iota(jnp.int32, (rows, part), 0) % side
    inner = inner_ref[...]
    inner = inner + jnp.where(column == side - 1, spread(sums[side : 2 * side]), 0.0)
    inner = inner + jnp.where(column == 0, spread(sums[3 * side :]), 0.0)
    ends = jnp.concatenate(
        [
            inner[0:side] + sums[0:side],
            inner[side : rows - side],
            inner[rows - side :] + sums[2 * side : 3 * side],
        ],
        axis=0,
    )
    out_ref[...] = ends.astype(jnp.bfloat16)


def output_kernel(side, part, field_ref, halos_ref, other_ref, weight_ref, out_ref, cols, other_cols):
    rows = side * side
    ch = lax.axis_index("ch")
    start = pl.multiple_of(ch * part, 16)
    other = pl.multiple_of((1 - ch) * part, 16)
    chans = weight_ref.shape[2]
    wide = -(-part // 128) * 128
    lanes = pl.multiple_of(ch * (chans - wide), 128)
    shifted_columns(side, part, field_ref, halos_ref[...], cols)
    shifted_columns(side, part, other_ref.at[0:rows], other_ref[rows:, :], other_cols)
    total = jnp.zeros((rows, wide), jnp.float32)
    for a in range(3):
        for b in range(3):
            for ref, first in ((cols, start), (other_cols, other)):
                total = total + jnp.dot(
                    ref[b, a * side : a * side + rows, :],
                    weight_ref[3 * a + b, pl.ds(first, part), pl.ds(lanes, wide)],
                    preferred_element_type=jnp.float32,
                )
    result = jnp.where(ch == 0, total[:, :part], total[:, wide - part :])
    out_ref[...] = result.astype(jnp.bfloat16)


def sum_over_tiles(partial, own_tile, count):
    stages = mask_stages(count)
    held = partial
    for index, bits in enumerate(stages):
        masks = group_masks(bits)
        part = held.shape[0] // len(masks)
        kind = jnp.float32 if index == 0 else jnp.bfloat16
        pieces = [held[i * part : (i + 1) * part] for i in range(len(masks))]
        got = [by_mask(p.astype(kind), m, count) for p, m in zip(pieces[1:], masks[1:])]
        held = pieces[0]
        for value in got:
            held = held + value.astype(jnp.float32)
    held = held.astype(jnp.bfloat16)
    for bits in stages[:0:-1]:
        masks = group_masks(bits)
        held = jnp.concatenate([held] + [by_mask(held, m, count) for m in masks[1:]], axis=0)
    return held, by_mask(held, 1, count)


def body(features, weight, cotangent, edge_tiles, edge_turns, corner_tiles, corner_turns):
    tables = jnp.asarray(turn_tables())
    count = lax.axis_size("tile")
    own_tile = lax.axis_index("tile")
    field = features[0]
    side, part = field.shape[0], field.shape[2]
    chans = weight.shape[3]
    rows = side * side
    flat = rows + 2 * side
    taps = weight.reshape(9, chans, chans)
    others = [(0, 1), (1, 0)]
    smalls = (tables, edge_tiles, edge_turns, corner_tiles, corner_turns)

    cot_own = cotangent[0].reshape(rows, part)
    cot_other = lax.ppermute(cot_own, "ch", others)
    (sides,) = call(functools.partial(sides_kernel, side), [vmem((4 * side, part), jnp.bfloat16)], [field])
    near = [by_offset(sides, -offset, count) for offset in OFFSETS]
    (cot_full,) = call(both_kernel, [vmem((rows, chans), jnp.bfloat16)], [cot_own, cot_other])

    (halos,) = call(
        functools.partial(halo_kernel, side, part),
        [vmem((4 * side + EXTRA, part), jnp.bfloat16)],
        [*smalls, *near],
        smem=range(5),
    )
    chunk = -(-9 * part // (16 * count)) * 16
    (local,) = call(
        functools.partial(grad_weight_kernel, side, part, chunk, 1.0 / math.sqrt(count * rows)),
        [vmem((chunk * count, chans), jnp.float32)],
        [field, halos, cot_full],
        scratch=[
            pltpu.VMEM((3, flat, part), jnp.bfloat16),
            pltpu.VMEM((chunk * count, chans), jnp.float32),
        ],
        flops=2 * rows * 9 * part * chans,
    )
    mine, other = sum_over_tiles(local, own_tile, count)
    (grad_weight,) = call(
        functools.partial(unfold_kernel, part, chunk),
        [vmem((9 * part, chans), jnp.float32)],
        [mine, other],
    )

    inner, pieces = call(
        functools.partial(back_kernel, side, part),
        [vmem((rows, part), jnp.float32), vmem((4 * side + EXTRA, part), jnp.bfloat16)],
        [cot_full, taps],
        scratch=[pltpu.VMEM((rows + 4 * side, chans), jnp.bfloat16)],
        flops=2 * rows * 9 * part * chans,
    )
    got = [by_offset(pieces, offset, count) for offset in OFFSETS]
    (grad_features,) = call(
        functools.partial(add_halo_kernel, side, part),
        [vmem((rows, part), jnp.bfloat16)],
        [*smalls, inner, *got],
        smem=range(5),
    )

    packet = jnp.concatenate([field.reshape(rows, part), halos], axis=0)
    (output,) = call(
        functools.partial(output_kernel, side, part),
        [vmem((rows, part), jnp.bfloat16)],
        [field, halos, lax.ppermute(packet, "ch", others), taps],
        scratch=[pltpu.VMEM((3, flat, part), jnp.bfloat16)] * 2,
        flops=2 * rows * 9 * part * chans,
    )
    shape = (1, side, side, part)
    return (
        output.reshape(shape),
        grad_features.reshape(shape),
        grad_weight.reshape(3, 3, part, chans),
    )


def solution(mesh):
    return jax.shard_map(
        body,
        mesh=mesh,
        in_specs=(
            P("tile", None, None, "ch"),
            P(),
            P("tile", None, None, "ch"),
            P(),
            P(),
            P(),
            P(),
        ),
        out_specs=(
            P("tile", None, None, "ch"),
            P("tile", None, None, "ch"),
            P(None, None, "ch", None),
        ),
        check_vma=False,
    )
```

```python
import functools
import math

import jax
import jax.numpy as jnp
import numpy as np
from jax import lax
from jax.experimental import pallas as pl
from jax.experimental.pallas import tpu as pltpu
from jax.sharding import PartitionSpec as P

SPAN = 4
OFFSETS = list(range(-SPAN, 0)) + list(range(1, SPAN + 1))
EXTRA = 16
PER_STAGE = (1, 3, 2, 0)


def turn_tables():
    labels = [[3 * row + col for col in range(3)] for row in range(3)]

    def turn_once(block):
        return [[block[col][2 - row] for col in range(3)] for row in range(3)]

    def sides_of(block):
        return [
            list(block[0]),
            [block[row][2] for row in range(3)],
            list(block[2]),
            [block[row][0] for row in range(3)],
        ]

    def corners_of(block):
        return [block[0][0], block[0][2], block[2][2], block[2][0]]

    base_sides = sides_of(labels)
    base_corners = corners_of(labels)
    edge_table = np.zeros((4, 4), np.int32)
    corner_table = np.zeros((4, 4), np.int32)
    for border in range(4):
        turned = labels
        for quarter in range(4):
            wanted = sides_of(turned)[(border + 2) % 4]
            for side_index in range(4):
                if base_sides[side_index] == wanted:
                    edge_table[border, quarter] = side_index
                if base_sides[side_index][::-1] == wanted:
                    edge_table[border, quarter] = side_index + 4
            corner_cell = corners_of(turned)[(border + 2) % 4]
            for corner_index in range(4):
                if base_corners[corner_index] == corner_cell:
                    corner_table[border, quarter] = corner_index
            turned = turn_once(turned)
    return np.concatenate([edge_table, corner_table], axis=0)


def by_offset(value, offset, count):
    return lax.ppermute(value, "tile", [(i, (i + offset) % count) for i in range(count)])


def by_mask(value, mask, count):
    return lax.ppermute(value, "tile", [(i, i ^ mask) for i in range(count)])


def mask_stages(count):
    bits = [1 << b for b in range(count.bit_length() - 1)]
    stages = [bits[:1]]
    rest = bits[1:]
    while rest:
        stages.append(rest[:2])
        rest = rest[2:]
    return stages


def group_masks(bits):
    masks = [0]
    for bit in bits:
        masks = masks + [m + bit for m in masks]
    return masks


def slot_of_mask(mask, count):
    place = 0
    for bits in mask_stages(count):
        size = 1 << len(bits)
        place = place * size + (mask // bits[0]) % size
    return place


def corner_spot(slot, side):
    return jnp.where(
        slot == 0, 0, jnp.where(slot == 1, side - 1, jnp.where(slot == 2, 3 * side - 1, 2 * side))
    )


def vmem(shape, dtype):
    return jax.ShapeDtypeStruct(shape, dtype)


def call(kernel, outs, args, smem=(), scratch=(), flops=0):
    in_specs = [
        pl.BlockSpec(memory_space=pltpu.SMEM if i in smem else pltpu.VMEM) for i in range(len(args))
    ]
    size = sum(math.prod(x.shape) * x.dtype.itemsize for x in list(args) + list(outs))
    return pl.pallas_call(
        kernel,
        out_shape=tuple(outs),
        in_specs=in_specs,
        out_specs=tuple(pl.BlockSpec(memory_space=pltpu.VMEM) for _ in outs),
        scratch_shapes=list(scratch),
        compiler_params=pltpu.CompilerParams(vmem_limit_bytes=40 * 1024 * 1024),
        cost_estimate=pl.CostEstimate(flops=flops, bytes_accessed=size, transcendentals=0),
    )(*args)


def sides_kernel(side, field_ref, sides_ref):
    sides_ref[0:side, :] = field_ref[0]
    sides_ref[side : 2 * side, :] = field_ref[:, side - 1, :]
    sides_ref[2 * side : 3 * side, :] = field_ref[side - 1]
    sides_ref[3 * side : 4 * side, :] = field_ref[:, 0, :]


def shifted_columns(side, part, field_ref, halos, out_ref):
    rows = side * side
    flat = rows + 2 * side
    tall = jnp.concatenate(
        [
            halos[0:side].astype(jnp.float32),
            field_ref[...].reshape(rows, part).astype(jnp.float32),
            halos[2 * side : 3 * side].astype(jnp.float32),
        ],
        axis=0,
    )
    edge = halos.astype(jnp.float32)
    corner = [edge[4 * side + c : 4 * side + c + 1] for c in range(4)]
    east = jnp.concatenate([corner[1], edge[side : 2 * side], corner[2]], axis=0)
    west = jnp.concatenate([corner[0], edge[3 * side : 4 * side], corner[3]], axis=0)
    spread = lambda col: jnp.broadcast_to(col[:, None, :], (side + 2, side, part)).reshape(flat, part)
    column = lax.broadcasted_iota(jnp.int32, (flat, part), 0) % side
    out_ref[0] = jnp.where(column == 0, spread(west), pltpu.roll(tall, 1, 0)).astype(jnp.bfloat16)
    out_ref[1] = tall.astype(jnp.bfloat16)
    out_ref[2] = jnp.where(column == side - 1, spread(east), pltpu.roll(tall, flat - 1, 0)).astype(
        jnp.bfloat16
    )


def halo_kernel(side, part, tables_ref, et_ref, eu_ref, ct_ref, cu_ref, *refs):
    near_refs, halos_ref = refs[: len(OFFSETS)], refs[len(OFFSETS)]
    count = lax.axis_size("tile")
    own = lax.axis_index("tile")

    def base(target):
        wrapped = lax.rem(target - own + count, count)
        signed = jnp.where(wrapped > count // 2, wrapped - count, wrapped)
        return jnp.where(signed < 0, signed + SPAN, signed + SPAN - 1) * (4 * side)

    row = lax.broadcasted_iota(jnp.int32, (4 * side + EXTRA, 1), 0)
    wanted = jnp.full((4 * side + EXTRA, 1), -1, jnp.int32)
    for e in range(4):
        slot = tables_ref[e, eu_ref[e, own]]
        start = base(et_ref[e, own]) + lax.rem(slot, 4) * side
        along = row - e * side
        along = jnp.where(slot >= 4, side - 1 - along, along)
        wanted = jnp.where((row >= e * side) & (row < (e + 1) * side), start + along, wanted)
        corner = tables_ref[4 + e, cu_ref[e, own]]
        spot = base(ct_ref[e, own]) + corner_spot(corner, side)
        wanted = jnp.where(row == 4 * side + e, spot, wanted)
    near = jnp.concatenate([ref[...] for ref in near_refs], axis=0)
    lane = lax.broadcasted_iota(jnp.int32, (4 * side + EXTRA, near.shape[0]), 1)
    pick = jnp.where(lane == wanted, 1.0, 0.0).astype(jnp.bfloat16)
    halos_ref[...] = jnp.dot(pick, near, preferred_element_type=jnp.float32).astype(jnp.bfloat16)


def grad_weight_kernel(side, part, chunk, scale, field_ref, halos_ref, cot_ref, out_ref, cols, total):
    rows = side * side
    chans = cot_ref.shape[1]
    count = lax.axis_size("tile")
    own = lax.axis_index("tile")
    shifted_columns(side, part, field_ref, halos_ref[...], cols)
    cot = cot_ref[...]
    for a in range(3):
        for b in range(3):
            tap = 3 * a + b
            total[tap * part : (tap + 1) * part, :] = (
                lax.dot_general(
                    cols[b, a * side : a * side + rows, :],
                    cot,
                    (((0,), (0,)), ((), ())),
                    preferred_element_type=jnp.float32,
                )
                * scale
            )
    total[9 * part :, :] = jnp.zeros((chunk * count - 9 * part, chans), jnp.float32)
    for mask in range(count):
        to = slot_of_mask(mask, count) * chunk
        start = pl.multiple_of((own ^ mask) * chunk, 16)
        out_ref[to : to + chunk, :] = total[pl.ds(start, chunk), :]


def unfold_kernel(part, chunk, mine_ref, other_ref, out_ref):
    count = lax.axis_size("tile")
    own = lax.axis_index("tile")
    half = mine_ref.shape[0] // chunk
    whole = 9 * part
    core = lax.rem(own, 2)
    for block in range(count):
        size = min(chunk, whole - block * chunk)
        if size <= 0:
            continue
        mask = own ^ block
        place = 0
        for bits in mask_stages(count)[1:]:
            span = 1 << len(bits)
            place = place * span + lax.rem(mask // bits[0], span)
        start = pl.multiple_of(place * chunk, 16)
        mine = mine_ref[pl.ds(start, size), :]
        other = other_ref[pl.ds(start, size), :]
        value = jnp.where(core == block % 2, mine.astype(jnp.float32), other.astype(jnp.float32))
        out_ref[block * chunk : block * chunk + size, :] = value


def both_kernel(own_ref, other_ref, out_ref):
    part = own_ref.shape[1]

    @pl.when(lax.axis_index("ch") == 0)
    def _():
        out_ref[:, 0:part] = own_ref[...]
        out_ref[:, part:] = other_ref[...]

    @pl.when(lax.axis_index("ch") != 0)
    def _():
        out_ref[:, 0:part] = other_ref[...]
        out_ref[:, part:] = own_ref[...]


def back_kernel(side, part, cot_ref, weight_ref, inner_ref, pieces_ref, tall):
    rows = side * side
    flat = rows + 2 * side
    start = pl.multiple_of(lax.axis_index("ch") * part, 16)
    chans = cot_ref.shape[1]
    blank = jnp.zeros((2 * side, chans), jnp.bfloat16)
    tall[0 : 2 * side, :] = blank
    tall[2 * side : 2 * side + rows, :] = cot_ref[...]
    tall[2 * side + rows :, :] = blank
    backs = []
    for b in range(3):
        back = jnp.zeros((flat, part), jnp.float32)
        for a in range(3):
            back = back + lax.dot_general(
                tall[(2 - a) * side : (2 - a) * side + flat, :],
                weight_ref[3 * a + b, pl.ds(start, part), :],
                (((1,), (1,)), ((), ())),
                preferred_element_type=jnp.float32,
            )
        backs.append(back)
    column = lax.broadcasted_iota(jnp.int32, (flat, part), 0) % side
    inner = (
        jnp.where(column == side - 1, 0.0, pltpu.roll(backs[0], flat - 1, 0))
        + backs[1]
        + jnp.where(column == 0, 0.0, pltpu.roll(backs[2], 1, 0))
    )
    inner_ref[...] = inner[side : side + rows]
    west = backs[0].reshape(side + 2, side, part)[:, 0, :]
    east = backs[2].reshape(side + 2, side, part)[:, side - 1, :]
    pieces_ref[...] = jnp.concatenate(
        [
            inner[0:side],
            east[1 : side + 1],
            inner[side + rows :],
            west[1 : side + 1],
            west[0:1],
            east[0:1],
            east[side + 1 :],
            west[side + 1 :],
            jnp.zeros((EXTRA - 4, part), jnp.float32),
        ],
        axis=0,
    ).astype(jnp.bfloat16)


def add_halo_kernel(side, part, tables_ref, et_ref, eu_ref, ct_ref, cu_ref, inner_ref, *refs):
    got_refs, out_ref = refs[: len(OFFSETS)], refs[len(OFFSETS)]
    count = lax.axis_size("tile")
    own = lax.axis_index("tile")
    block = 4 * side + EXTRA
    total = len(OFFSETS) * block
    lane = lax.broadcasted_iota(jnp.int32, (1, total), 1)
    target = jnp.full((1, total), -1, jnp.int32)
    for index, offset in enumerate(OFFSETS):
        source = lax.rem(own - offset + count, count)
        for e in range(4):
            first = index * block + e * side
            slot = tables_ref[e, eu_ref[e, source]]
            along = lane - first
            along = jnp.where(slot >= 4, side - 1 - along, along)
            hit = (lane >= first) & (lane < first + side) & (et_ref[e, source] == own)
            target = jnp.where(hit, lax.rem(slot, 4) * side + along, target)
            spot = corner_spot(tables_ref[4 + e, cu_ref[e, source]], side)
            hit = (lane == index * block + 4 * side + e) & (ct_ref[e, source] == own)
            target = jnp.where(hit, spot, target)
    row = lax.broadcasted_iota(jnp.int32, (4 * side, total), 0)
    place = jnp.where(row == target, 1.0, 0.0).astype(jnp.bfloat16)
    got = jnp.concatenate([ref[...] for ref in got_refs], axis=0)
    sums = jnp.dot(place, got, preferred_element_type=jnp.float32)
    rows = side * side
    spread = lambda col: jnp.broadcast_to(col[:, None, :], (side, side, part)).reshape(rows, part)
    column = lax.broadcasted_iota(jnp.int32, (rows, part), 0) % side
    inner = inner_ref[...]
    inner = inner + jnp.where(column == side - 1, spread(sums[side : 2 * side]), 0.0)
    inner = inner + jnp.where(column == 0, spread(sums[3 * side :]), 0.0)
    ends = jnp.concatenate(
        [
            inner[0:side] + sums[0:side],
            inner[side : rows - side],
            inner[rows - side :] + sums[2 * side : 3 * side],
        ],
        axis=0,
    )
    out_ref[...] = ends.astype(jnp.bfloat16)


def output_kernel(side, part, field_ref, halos_ref, other_ref, weight_ref, out_ref, cols, other_cols):
    rows = side * side
    ch = lax.axis_index("ch")
    start = pl.multiple_of(ch * part, 16)
    other = pl.multiple_of((1 - ch) * part, 16)
    chans = weight_ref.shape[2]
    wide = -(-part // 128) * 128
    lanes = pl.multiple_of(ch * (chans - wide), 128)
    shifted_columns(side, part, field_ref, halos_ref[...], cols)
    shifted_columns(side, part, other_ref.at[0:rows], other_ref[rows:, :], other_cols)
    total = jnp.zeros((rows, wide), jnp.float32)
    for a in range(3):
        for b in range(3):
            for ref, first in ((cols, start), (other_cols, other)):
                total = total + jnp.dot(
                    ref[b, a * side : a * side + rows, :],
                    weight_ref[3 * a + b, pl.ds(first, part), pl.ds(lanes, wide)],
                    preferred_element_type=jnp.float32,
                )
    result = jnp.where(ch == 0, total[:, :part], total[:, wide - part :])
    out_ref[...] = result.astype(jnp.bfloat16)


def body(features, weight, cotangent, edge_tiles, edge_turns, corner_tiles, corner_turns):
    tables = jnp.asarray(turn_tables())
    count = lax.axis_size("tile")
    own_tile = lax.axis_index("tile")
    field = features[0]
    side, part = field.shape[0], field.shape[2]
    chans = weight.shape[3]
    rows = side * side
    flat = rows + 2 * side
    taps = weight.reshape(9, chans, chans)
    others = [(0, 1), (1, 0)]
    smalls = (tables, edge_tiles.T, edge_turns.T, corner_tiles.T, corner_turns.T)

    cot_own = cotangent[0].reshape(rows, part)
    cot_other = lax.ppermute(cot_own, "ch", others)
    (sides,) = call(functools.partial(sides_kernel, side), [vmem((4 * side, part), jnp.bfloat16)], [field])
    near = [by_offset(sides, -offset, count) for offset in OFFSETS]
    (cot_full,) = call(both_kernel, [vmem((rows, chans), jnp.bfloat16)], [cot_own, cot_other])

    inner, pieces = call(
        functools.partial(back_kernel, side, part),
        [vmem((rows, part), jnp.float32), vmem((4 * side + EXTRA, part), jnp.bfloat16)],
        [cot_full, taps],
        scratch=[pltpu.VMEM((rows + 4 * side, chans), jnp.bfloat16)],
        flops=2 * rows * 9 * part * chans,
    )
    near, inner, pieces = lax.optimization_barrier((near, inner, pieces))

    (halos,) = call(
        functools.partial(halo_kernel, side, part),
        [vmem((4 * side + EXTRA, part), jnp.bfloat16)],
        [*smalls, *near],
        smem=range(5),
    )
    chunk = -(-9 * part // (16 * count)) * 16
    (local,) = call(
        functools.partial(grad_weight_kernel, side, part, chunk, 1.0 / math.sqrt(count * rows)),
        [vmem((chunk * count, chans), jnp.float32)],
        [field, halos, cot_full],
        scratch=[
            pltpu.VMEM((3, flat, part), jnp.bfloat16),
            pltpu.VMEM((chunk * count, chans), jnp.float32),
        ],
        flops=2 * rows * 9 * part * chans,
    )
    packet = jnp.concatenate([field.reshape(rows, part), halos], axis=0)

    stages = mask_stages(count)
    waiting = list(OFFSETS)
    got_pieces = []
    other_field = lax.ppermute(packet, "ch", others)
    held = local
    for index, bits in enumerate(stages):
        masks = group_masks(bits)
        size = held.shape[0] // len(masks)
        kind = jnp.float32 if index == 0 else jnp.bfloat16
        cut = [held[i * size : (i + 1) * size] for i in range(len(masks))]
        got = [by_mask(p.astype(kind), m, count) for p, m in zip(cut[1:], masks[1:])]
        beside = [by_offset(pieces, offset, count) for offset in waiting[:PER_STAGE[min(index, 3)]]]
        waiting = waiting[PER_STAGE[min(index, 3)]:]
        keep, got, beside, pieces = lax.optimization_barrier((cut[0], got, beside, pieces))
        got_pieces += beside
        held = keep
        for value in got:
            held = held + value.astype(jnp.float32)
    held = held.astype(jnp.bfloat16)
    for index, bits in enumerate(stages[:0:-1]):
        masks = group_masks(bits)
        got = [by_mask(held, m, count) for m in masks[1:]]
        if index == 0:
            beside = [by_offset(pieces, offset, count) for offset in waiting]
            held, got, beside, other_field = lax.optimization_barrier((held, got, beside, other_field))
            got_pieces += beside
        if index == len(stages) - 2:
            (grad_features,) = call(
                functools.partial(add_halo_kernel, side, part),
                [vmem((rows, part), jnp.bfloat16)],
                [*smalls, inner, *got_pieces],
                smem=range(5),
            )
            (output,) = call(
                functools.partial(output_kernel, side, part),
                [vmem((rows, part), jnp.bfloat16)],
                [field, halos, other_field, taps],
                scratch=[pltpu.VMEM((3, flat, part), jnp.bfloat16)] * 2,
                flops=2 * rows * 9 * part * chans,
            )
            held, got, output, grad_features = lax.optimization_barrier((held, got, output, grad_features))
        held = jnp.concatenate([held] + got, axis=0)
    (grad_weight,) = call(
        functools.partial(unfold_kernel, part, chunk),
        [vmem((9 * part, chans), jnp.float32)],
        [held, by_mask(held, 1, count)],
    )
    shape = (1, side, side, part)
    return (
        output.reshape(shape),
        grad_features.reshape(shape),
        grad_weight.reshape(3, 3, part, chans),
    )


def solution(mesh):
    return jax.shard_map(
        body,
        mesh=mesh,
        in_specs=(
            P("tile", None, None, "ch"),
            P(),
            P("tile", None, None, "ch"),
            P(),
            P(),
            P(),
            P(),
        ),
        out_specs=(
            P("tile", None, None, "ch"),
            P("tile", None, None, "ch"),
            P(None, None, "ch", None),
        ),
        check_vma=False,
    )
```

```python
import functools
import math

import jax
import jax.numpy as jnp
import numpy as np
from jax import lax
from jax.experimental import pallas as pl
from jax.experimental.pallas import tpu as pltpu
from jax.sharding import PartitionSpec as P

SPAN = 4
OFFSETS = list(range(-SPAN, 0)) + list(range(1, SPAN + 1))
EXTRA = 16


def turn_tables():
    labels = [[3 * row + col for col in range(3)] for row in range(3)]

    def turn_once(block):
        return [[block[col][2 - row] for col in range(3)] for row in range(3)]

    def sides_of(block):
        return [
            list(block[0]),
            [block[row][2] for row in range(3)],
            list(block[2]),
            [block[row][0] for row in range(3)],
        ]

    def corners_of(block):
        return [block[0][0], block[0][2], block[2][2], block[2][0]]

    base_sides = sides_of(labels)
    base_corners = corners_of(labels)
    edge_table = np.zeros((4, 4), np.int32)
    corner_table = np.zeros((4, 4), np.int32)
    for border in range(4):
        turned = labels
        for quarter in range(4):
            wanted = sides_of(turned)[(border + 2) % 4]
            for side_index in range(4):
                if base_sides[side_index] == wanted:
                    edge_table[border, quarter] = side_index
                if base_sides[side_index][::-1] == wanted:
                    edge_table[border, quarter] = side_index + 4
            corner_cell = corners_of(turned)[(border + 2) % 4]
            for corner_index in range(4):
                if base_corners[corner_index] == corner_cell:
                    corner_table[border, quarter] = corner_index
            turned = turn_once(turned)
    return np.concatenate([edge_table, corner_table], axis=0)


def by_offset(value, offset, count):
    return lax.ppermute(value, "tile", [(i, (i + offset) % count) for i in range(count)])


def by_mask(value, mask, count):
    return lax.ppermute(value, "tile", [(i, i ^ mask) for i in range(count)])


def mask_stages(count):
    bits = [1 << b for b in range(count.bit_length() - 1)]
    stages = [bits[:1]]
    rest = bits[1:]
    while rest:
        stages.append(rest[:2])
        rest = rest[2:]
    return stages


def group_masks(bits):
    masks = [0]
    for bit in bits:
        masks = masks + [m + bit for m in masks]
    return masks


def slot_of_mask(mask, count):
    place = 0
    for bits in mask_stages(count):
        size = 1 << len(bits)
        place = place * size + (mask // bits[0]) % size
    return place


def corner_spot(slot, side):
    return jnp.where(
        slot == 0, 0, jnp.where(slot == 1, side - 1, jnp.where(slot == 2, 3 * side - 1, 2 * side))
    )


def vmem(shape, dtype):
    return jax.ShapeDtypeStruct(shape, dtype)


def call(kernel, outs, args, smem=(), scratch=(), flops=0):
    in_specs = [
        pl.BlockSpec(memory_space=pltpu.SMEM if i in smem else pltpu.VMEM) for i in range(len(args))
    ]
    size = sum(math.prod(x.shape) * x.dtype.itemsize for x in list(args) + list(outs))
    return pl.pallas_call(
        kernel,
        out_shape=tuple(outs),
        in_specs=in_specs,
        out_specs=tuple(pl.BlockSpec(memory_space=pltpu.VMEM) for _ in outs),
        scratch_shapes=list(scratch),
        compiler_params=pltpu.CompilerParams(vmem_limit_bytes=40 * 1024 * 1024),
        cost_estimate=pl.CostEstimate(flops=flops, bytes_accessed=size, transcendentals=0),
    )(*args)


def sides_kernel(side, field_ref, sides_ref):
    sides_ref[0:side, :] = field_ref[0]
    sides_ref[side : 2 * side, :] = field_ref[:, side - 1, :]
    sides_ref[2 * side : 3 * side, :] = field_ref[side - 1]
    sides_ref[3 * side : 4 * side, :] = field_ref[:, 0, :]


def shifted_columns(side, part, field_ref, halos, out_ref):
    rows = side * side
    flat = rows + 2 * side
    tall = jnp.concatenate(
        [
            halos[0:side].astype(jnp.float32),
            field_ref[...].reshape(rows, part).astype(jnp.float32),
            halos[2 * side : 3 * side].astype(jnp.float32),
        ],
        axis=0,
    )
    edge = halos.astype(jnp.float32)
    corner = [edge[4 * side + c : 4 * side + c + 1] for c in range(4)]
    east = jnp.concatenate([corner[1], edge[side : 2 * side], corner[2]], axis=0)
    west = jnp.concatenate([corner[0], edge[3 * side : 4 * side], corner[3]], axis=0)
    spread = lambda col: jnp.broadcast_to(col[:, None, :], (side + 2, side, part)).reshape(flat, part)
    column = lax.broadcasted_iota(jnp.int32, (flat, part), 0) % side
    out_ref[0] = jnp.where(column == 0, spread(west), pltpu.roll(tall, 1, 0)).astype(jnp.bfloat16)
    out_ref[1] = tall.astype(jnp.bfloat16)
    out_ref[2] = jnp.where(column == side - 1, spread(east), pltpu.roll(tall, flat - 1, 0)).astype(
        jnp.bfloat16
    )


def halo_kernel(side, part, tables_ref, et_ref, eu_ref, ct_ref, cu_ref, *refs):
    near_refs, halos_ref = refs[: len(OFFSETS)], refs[len(OFFSETS)]
    count = lax.axis_size("tile")
    own = lax.axis_index("tile")

    def base(target):
        wrapped = lax.rem(target - own + count, count)
        signed = jnp.where(wrapped > count // 2, wrapped - count, wrapped)
        return jnp.where(signed < 0, signed + SPAN, signed + SPAN - 1) * (4 * side)

    row = lax.broadcasted_iota(jnp.int32, (4 * side + EXTRA, 1), 0)
    wanted = jnp.full((4 * side + EXTRA, 1), -1, jnp.int32)
    for e in range(4):
        slot = tables_ref[e, eu_ref[e, own]]
        start = base(et_ref[e, own]) + lax.rem(slot, 4) * side
        along = row - e * side
        along = jnp.where(slot >= 4, side - 1 - along, along)
        wanted = jnp.where((row >= e * side) & (row < (e + 1) * side), start + along, wanted)
        corner = tables_ref[4 + e, cu_ref[e, own]]
        spot = base(ct_ref[e, own]) + corner_spot(corner, side)
        wanted = jnp.where(row == 4 * side + e, spot, wanted)
    near = jnp.concatenate([ref[...] for ref in near_refs], axis=0)
    lane = lax.broadcasted_iota(jnp.int32, (4 * side + EXTRA, near.shape[0]), 1)
    pick = jnp.where(lane == wanted, 1.0, 0.0).astype(jnp.bfloat16)
    halos_ref[...] = jnp.dot(pick, near, preferred_element_type=jnp.float32).astype(jnp.bfloat16)


def join_halves(own, other, out_ref):
    part = own.shape[1]

    @pl.when(lax.axis_index("ch") == 0)
    def _():
        out_ref[:, 0:part] = own
        out_ref[:, part:] = other

    @pl.when(lax.axis_index("ch") != 0)
    def _():
        out_ref[:, 0:part] = other
        out_ref[:, part:] = own


def grad_weight_kernel(
    side, part, chunk, scale, field_ref, halos_ref, own_ref, other_ref, mine_ref, send_ref, cols, total, cot_ref
):
    rows = side * side
    chans = cot_ref.shape[1]
    count = lax.axis_size("tile")
    own = lax.axis_index("tile")
    join_halves(own_ref[...], other_ref[...], cot_ref)
    shifted_columns(side, part, field_ref, halos_ref[...], cols)
    cot = cot_ref[...]
    for a in range(3):
        for b in range(3):
            tap = 3 * a + b
            total[tap * part : (tap + 1) * part, :] = (
                lax.dot_general(
                    cols[b, a * side : a * side + rows, :],
                    cot,
                    (((0,), (0,)), ((), ())),
                    preferred_element_type=jnp.float32,
                )
                * scale
            )
    total[9 * part :, :] = jnp.zeros((chunk * count - 9 * part, chans), jnp.float32)
    half = count * chunk // 2
    for mask in range(count):
        to = slot_of_mask(mask, count) * chunk
        start = pl.multiple_of((own ^ mask) * chunk, 16)
        value = total[pl.ds(start, chunk), :]
        if to < half:
            mine_ref[to : to + chunk, :] = value
        else:
            send_ref[to - half : to - half + chunk, :] = value


def sum_kernel(n_got, n_out, n_join, *refs):
    held_ref, got_refs = refs[0], refs[1 : 1 + n_got]
    join_refs, outs = refs[1 + n_got : 1 + n_got + n_join], refs[1 + n_got + n_join :]
    size = held_ref.shape[0] // n_out
    for index in range(n_out):
        here = slice(index * size, (index + 1) * size)
        value = held_ref[here, :]
        for ref in got_refs:
            value = value + ref[here, :].astype(jnp.float32)
        outs[index][...] = value.astype(outs[index].dtype)
    if n_join:
        join_kernel(*join_refs, outs[n_out])


def join_kernel(*refs):
    row = 0
    for ref in refs[:-1]:
        refs[-1][row : row + ref.shape[0], :] = ref[...]
        row += ref.shape[0]


def unfold_kernel(whole, chunk, bit, masks, n_dep, *refs):
    refs = refs[n_dep:]
    n = len(masks)
    in_refs, out_ref, wide, sems = refs[:n], refs[n], refs[n + 1], refs[n + 2]
    own = lax.axis_index("tile")
    full, rest = whole // chunk, whole % chunk
    copies = []
    for i, (ref, inner) in enumerate(zip(in_refs, masks)):
        for k, mask in enumerate(inner):
            at = i * len(inner) + k
            wide[at] = ref[k * chunk : (k + 1) * chunk, :].astype(jnp.float32)
            block = own ^ mask ^ bit
            start = pl.multiple_of(block * chunk, 16)
            copy = pltpu.make_async_copy(wide.at[at], out_ref.at[pl.ds(start, chunk), :], sems.at[at])
            copies.append((block, copy))
            pl.when(block < full)(copy.start)
            if rest:
                copy = pltpu.make_async_copy(
                    wide.at[at, 0:rest], out_ref.at[full * chunk : whole, :], sems.at[at]
                )
                copies.append((None, copy))
                pl.when(block == full)(copy.start)
                copies[-1] = (block == full, copy)
            copies[-1 - bool(rest)] = (block < full, copies[-1 - bool(rest)][1])
    for going, copy in copies:
        pl.when(going)(copy.wait)


def back_kernel(side, part, own_ref, other_ref, weight_ref, inner_ref, pieces_ref, tall):
    rows = side * side
    flat = rows + 2 * side
    start = pl.multiple_of(lax.axis_index("ch") * part, 16)
    blank = jnp.zeros((2 * side, tall.shape[1]), jnp.bfloat16)
    tall[0 : 2 * side, :] = blank
    join_halves(own_ref[...], other_ref[...], tall.at[2 * side : 2 * side + rows, :])
    tall[2 * side + rows :, :] = blank
    backs = []
    for b in range(3):
        back = jnp.zeros((flat, part), jnp.float32)
        for a in range(3):
            back = back + lax.dot_general(
                tall[(2 - a) * side : (2 - a) * side + flat, :],
                weight_ref[3 * a + b, pl.ds(start, part), :],
                (((1,), (1,)), ((), ())),
                preferred_element_type=jnp.float32,
            )
        backs.append(back)
    column = lax.broadcasted_iota(jnp.int32, (flat, part), 0) % side
    inner = (
        jnp.where(column == side - 1, 0.0, pltpu.roll(backs[0], flat - 1, 0))
        + backs[1]
        + jnp.where(column == 0, 0.0, pltpu.roll(backs[2], 1, 0))
    )
    inner_ref[...] = inner[side : side + rows]
    west = backs[0].reshape(side + 2, side, part)[:, 0, :]
    east = backs[2].reshape(side + 2, side, part)[:, side - 1, :]
    pieces_ref[...] = jnp.concatenate(
        [
            inner[0:side],
            east[1 : side + 1],
            inner[side + rows :],
            west[1 : side + 1],
            west[0:1],
            east[0:1],
            east[side + 1 :],
            west[side + 1 :],
            jnp.zeros((EXTRA - 4, part), jnp.float32),
        ],
        axis=0,
    ).astype(jnp.bfloat16)


def add_halo_kernel(side, part, tables_ref, et_ref, eu_ref, ct_ref, cu_ref, inner_ref, *refs):
    out_ref = refs[-1]
    count = lax.axis_size("tile")
    own = lax.axis_index("tile")
    block = 4 * side + EXTRA
    lane = lax.broadcasted_iota(jnp.int32, (1, block), 1)
    row = lax.broadcasted_iota(jnp.int32, (4 * side, block), 0)
    sums = jnp.zeros((4 * side, part), jnp.float32)
    for ref, mask in zip(refs[:-1], (0, 2, 1, 3)):
        for index, offset in enumerate((0, SPAN, -SPAN)):
            if mask == 0 and offset == 0:
                continue
            source = lax.rem((own ^ mask) + offset + count, count)
            target = jnp.full((1, block), -1, jnp.int32)
            for e in range(4):
                slot = tables_ref[e, eu_ref[e, source]]
                along = lane - e * side
                along = jnp.where(slot >= 4, side - 1 - along, along)
                hit = (lane >= e * side) & (lane < (e + 1) * side) & (et_ref[e, source] == own)
                target = jnp.where(hit, lax.rem(slot, 4) * side + along, target)
                spot = corner_spot(tables_ref[4 + e, cu_ref[e, source]], side)
                hit = (lane == 4 * side + e) & (ct_ref[e, source] == own)
                target = jnp.where(hit, spot, target)
            place = jnp.where(row == target, 1.0, 0.0).astype(jnp.bfloat16)
            sums = sums + jnp.dot(
                place, ref[index * block : (index + 1) * block, :], preferred_element_type=jnp.float32
            )
    rows = side * side
    spread = lambda col: jnp.broadcast_to(col[:, None, :], (side, side, part)).reshape(rows, part)
    column = lax.broadcasted_iota(jnp.int32, (rows, part), 0) % side
    inner = inner_ref[...]
    inner = inner + jnp.where(column == side - 1, spread(sums[side : 2 * side]), 0.0)
    inner = inner + jnp.where(column == 0, spread(sums[3 * side :]), 0.0)
    ends = jnp.concatenate(
        [
            inner[0:side] + sums[0:side],
            inner[side : rows - side],
            inner[rows - side :] + sums[2 * side : 3 * side],
        ],
        axis=0,
    )
    out_ref[...] = ends.astype(jnp.bfloat16)


def output_kernel(side, part, field_ref, halos_ref, other_ref, weight_ref, out_ref, cols, other_cols):
    rows = side * side
    ch = lax.axis_index("ch")
    start = pl.multiple_of(ch * part, 16)
    other = pl.multiple_of((1 - ch) * part, 16)
    chans = weight_ref.shape[2]
    wide = -(-part // 128) * 128
    lanes = pl.multiple_of(ch * (chans - wide), 128)
    shifted_columns(side, part, field_ref, halos_ref[...], cols)
    shifted_columns(side, part, other_ref.at[0:rows], other_ref[rows:, :], other_cols)
    total = jnp.zeros((rows, wide), jnp.float32)
    for a in range(3):
        for b in range(3):
            for ref, first in ((cols, start), (other_cols, other)):
                total = total + jnp.dot(
                    ref[b, a * side : a * side + rows, :],
                    weight_ref[3 * a + b, pl.ds(first, part), pl.ds(lanes, wide)],
                    preferred_element_type=jnp.float32,
                )
    result = jnp.where(ch == 0, total[:, :part], total[:, wide - part :])
    out_ref[...] = result.astype(jnp.bfloat16)


def unfold(whole, chunk, bit, masks, blocks, before):
    n_dep = 0 if before is None else 1
    anywhere = pl.BlockSpec(memory_space=pl.ANY)
    n_copies = len(masks) * len(masks[0])
    return pl.pallas_call(
        functools.partial(unfold_kernel, whole.shape[0], chunk, bit, masks, n_dep),
        out_shape=whole,
        in_specs=[anywhere] * n_dep + [pl.BlockSpec(memory_space=pltpu.VMEM)] * len(blocks),
        out_specs=anywhere,
        scratch_shapes=[
            pltpu.VMEM((n_copies, chunk, whole.shape[1]), jnp.float32),
            pltpu.SemaphoreType.DMA((n_copies,)),
        ],
        input_output_aliases={0: 0} if n_dep else {},
        compiler_params=pltpu.CompilerParams(vmem_limit_bytes=40 * 1024 * 1024),
    )(*([before] if n_dep else []), *blocks)


def body(features, weight, cotangent, edge_tiles, edge_turns, corner_tiles, corner_turns):
    tables = jnp.asarray(turn_tables())
    count = lax.axis_size("tile")
    own_tile = lax.axis_index("tile")
    field = features[0]
    side, part = field.shape[0], field.shape[2]
    chans = weight.shape[3]
    rows = side * side
    flat = rows + 2 * side
    taps = weight.reshape(9, chans, chans)
    others = [(0, 1), (1, 0)]
    smalls = (tables, edge_tiles.T, edge_turns.T, corner_tiles.T, corner_turns.T)

    cot_own = cotangent[0].reshape(rows, part)
    cot_other = lax.ppermute(cot_own, "ch", others)
    (sides,) = call(functools.partial(sides_kernel, side), [vmem((4 * side, part), jnp.bfloat16)], [field])
    near = [by_offset(sides, -offset, count) for offset in OFFSETS]
    (halos,) = call(
        functools.partial(halo_kernel, side, part),
        [vmem((4 * side + EXTRA, part), jnp.bfloat16)],
        [*smalls, *near],
        smem=range(5),
    )
    chunk = -(-9 * part // (16 * count)) * 16
    half = count * chunk // 2
    flops = 2 * rows * 9 * part * chans
    held, send = call(
        functools.partial(grad_weight_kernel, side, part, chunk, 1.0 / math.sqrt(count * rows)),
        [vmem((half, chans), jnp.float32)] * 2,
        [field, halos, cot_own, cot_other],
        scratch=[
            pltpu.VMEM((3, flat, part), jnp.bfloat16),
            pltpu.VMEM((chunk * count, chans), jnp.float32),
            pltpu.VMEM((rows, chans), jnp.bfloat16),
        ],
        flops=flops,
    )
    packet = jnp.concatenate([field.reshape(rows, part), halos], axis=0)

    stages = mask_stages(count)
    send, cot_other = lax.optimization_barrier((send, cot_other))
    got = [by_mask(send, 1, count)]
    inner, pieces = call(
        functools.partial(back_kernel, side, part),
        [vmem((rows, part), jnp.float32), vmem((4 * side + EXTRA, part), jnp.bfloat16)],
        [cot_own, cot_other, taps],
        scratch=[pltpu.VMEM((rows + 4 * side, chans), jnp.bfloat16)],
        flops=flops,
    )
    got, pieces, inner = lax.optimization_barrier((got, pieces, inner))
    joined = []
    for index, bits in enumerate(stages[1:]):
        masks = group_masks(bits)
        n_out = len(masks)
        size = held.shape[0] // n_out
        outs = [vmem((size, chans), jnp.float32)] + [vmem((size, chans), jnp.bfloat16)] * (n_out - 1)
        to_join = joined if index == 1 else []
        if to_join:
            outs = outs + [vmem((3 * (4 * side + EXTRA), part), jnp.bfloat16)]
        held, *send = call(
            functools.partial(sum_kernel, len(got), n_out, len(to_join)), outs, [held, *got, *to_join]
        )
        if index == 0:
            send, pieces, packet = lax.optimization_barrier((send, pieces, packet))
            got = [by_mask(v, m, count) for v, m in zip(send, masks[1:])]
            other_field = lax.ppermute(packet, "ch", others)
            joined = [pieces, by_offset(pieces, -SPAN, count), by_offset(pieces, SPAN, count)]
            got, joined = lax.optimization_barrier((got, joined))
        elif index == 1:
            here = send[-1]
            got = [by_mask(v, m, count) for v, m in zip(send[:-1], masks[1:])]
            beside = by_mask(here, 2, count)
            got, here, beside = lax.optimization_barrier((got, here, beside))
        else:
            got = [by_mask(v, m, count) for v, m in zip(send, masks[1:])]
    (held,) = call(
        functools.partial(sum_kernel, len(got), 1, 0), [vmem(held.shape, jnp.bfloat16)], [held, *got]
    )
    order = [0]
    for index, bits in enumerate(stages[:0:-1]):
        masks = group_masks(bits)
        got = [by_mask(held, m, count) for m in masks[1:]]
        if index == 0:
            got_pieces = [here, beside, by_mask(here, 1, count), by_mask(beside, 1, count)]
            (output,) = call(
                functools.partial(output_kernel, side, part),
                [vmem((rows, part), jnp.bfloat16)],
                [field, halos, other_field, taps],
                scratch=[pltpu.VMEM((3, flat, part), jnp.bfloat16)] * 2,
                flops=2 * flops,
            )
            held, got, output, got_pieces = lax.optimization_barrier((held, got, output, got_pieces))
        if index < len(stages) - 2:
            order = [m + v for m in masks for v in order]
            (held,) = call(
                join_kernel, [vmem((held.shape[0] * len(masks), chans), jnp.bfloat16)], [held, *got]
            )
            continue
        (grad_features,) = call(
            functools.partial(add_halo_kernel, side, part),
            [vmem((rows, part), jnp.bfloat16)],
            [*smalls, inner, *got_pieces],
            smem=range(5),
        )
        got = [held, *got]
        order = [[m + v for v in order] for m in masks]
    mates = [by_mask(v, 1, count) for v in got]
    mates, grad_features = lax.optimization_barrier((mates, grad_features))
    whole = vmem((9 * part, chans), jnp.float32)
    first = unfold(whole, chunk, 0, order, got, None)
    grad_weight = unfold(whole, chunk, 1, order, mates, first)
    shape = (1, side, side, part)
    return (
        output.reshape(shape),
        grad_features.reshape(shape),
        grad_weight.reshape(3, 3, part, chans),
    )


def solution(mesh):
    return jax.shard_map(
        body,
        mesh=mesh,
        in_specs=(
            P("tile", None, None, "ch"),
            P(),
            P("tile", None, None, "ch"),
            P(),
            P(),
            P(),
            P(),
        ),
        out_specs=(
            P("tile", None, None, "ch"),
            P("tile", None, None, "ch"),
            P(None, None, "ch", None),
        ),
        check_vma=False,
    )
```

```python
import functools
import math

import jax
import jax.numpy as jnp
import numpy as np
from jax import lax
from jax.experimental import pallas as pl
from jax.experimental.pallas import tpu as pltpu
from jax.sharding import PartitionSpec as P

SPAN = 4
EXTRA = 16


def turn_tables():
    labels = [[3 * row + col for col in range(3)] for row in range(3)]

    def turn_once(block):
        return [[block[col][2 - row] for col in range(3)] for row in range(3)]

    def sides_of(block):
        return [
            list(block[0]),
            [block[row][2] for row in range(3)],
            list(block[2]),
            [block[row][0] for row in range(3)],
        ]

    def corners_of(block):
        return [block[0][0], block[0][2], block[2][2], block[2][0]]

    base_sides = sides_of(labels)
    base_corners = corners_of(labels)
    edge_table = np.zeros((4, 4), np.int32)
    corner_table = np.zeros((4, 4), np.int32)
    for border in range(4):
        turned = labels
        for quarter in range(4):
            wanted = sides_of(turned)[(border + 2) % 4]
            for side_index in range(4):
                if base_sides[side_index] == wanted:
                    edge_table[border, quarter] = side_index
                if base_sides[side_index][::-1] == wanted:
                    edge_table[border, quarter] = side_index + 4
            corner_cell = corners_of(turned)[(border + 2) % 4]
            for corner_index in range(4):
                if base_corners[corner_index] == corner_cell:
                    corner_table[border, quarter] = corner_index
            turned = turn_once(turned)
    return np.concatenate([edge_table, corner_table], axis=0)


def by_offset(value, offset, count):
    return lax.ppermute(value, "tile", [(i, (i + offset) % count) for i in range(count)])


def by_mask(value, mask, count):
    return lax.ppermute(value, "tile", [(i, i ^ mask) for i in range(count)])


def mask_stages(count):
    bits = [1 << b for b in range(count.bit_length() - 1)]
    stages = [bits[:1]]
    rest = bits[1:]
    while rest:
        stages.append(rest[:2])
        rest = rest[2:]
    return stages


def group_masks(bits):
    masks = [0]
    for bit in bits:
        masks = masks + [m + bit for m in masks]
    return masks


def slot_of_mask(mask, count):
    place = 0
    for bits in mask_stages(count)[1:]:
        size = 1 << len(bits)
        place = place * size + (mask // bits[0]) % size
    return place


def corner_spot(slot, side):
    return jnp.where(
        slot == 0, 0, jnp.where(slot == 1, side - 1, jnp.where(slot == 2, 3 * side - 1, 2 * side))
    )


def vmem(shape, dtype):
    return jax.ShapeDtypeStruct(shape, dtype)


def call(kernel, outs, args, anywhere=(), scratch=(), flops=0):
    in_specs = [
        pl.BlockSpec(memory_space=pltpu.HBM if i in anywhere else pltpu.VMEM) for i in range(len(args))
    ]
    size = sum(math.prod(x.shape) * x.dtype.itemsize for x in list(args) + list(outs))
    return pl.pallas_call(
        kernel,
        out_shape=tuple(outs),
        in_specs=in_specs,
        out_specs=tuple(pl.BlockSpec(memory_space=pltpu.VMEM) for _ in outs),
        scratch_shapes=list(scratch),
        compiler_params=pltpu.CompilerParams(vmem_limit_bytes=40 * 1024 * 1024),
        cost_estimate=pl.CostEstimate(flops=flops, bytes_accessed=size, transcendentals=0),
    )(*args)


def packed_shape(rows, part):
    if part % 128 != 64:
        return (rows, part)
    return (rows * (part // 128) + rows // 2, 128)


def pack(value, out_ref, first=0):
    rows, part = value.shape
    if part % 128 != 64:
        out_ref[first : first + rows, :] = value
        return
    for i in range(part // 128):
        out_ref[first + i * rows : first + (i + 1) * rows, :] = value[:, i * 128 : (i + 1) * 128]
    rest = value[:, part - 64 :]
    at = first + rows * (part // 128)
    out_ref[at : at + rows // 2, :] = jnp.concatenate([rest[: rows // 2], rest[rows // 2 :]], axis=1)


def unpack(ref, out_ref, first, row, rows, part):
    if part % 128 != 64:
        out_ref[row : row + rows, :] = ref[first : first + rows, :]
        return
    for i in range(part // 128):
        out_ref[row : row + rows, i * 128 : (i + 1) * 128] = ref[first + i * rows : first + (i + 1) * rows, :]
    at = first + rows * (part // 128)
    rest = ref[at : at + rows // 2, :]
    out_ref[row : row + rows // 2, part - 64 :] = rest[:, :64]
    out_ref[row + rows // 2 : row + rows, part - 64 :] = rest[:, 64:]


def prepare_kernel(side, part, field_in, cot_in, sides_ref, cot_packed_ref, field_ref, cot_ref, sems):
    field_copy = pltpu.make_async_copy(field_in, field_ref, sems.at[0])
    cot_copy = pltpu.make_async_copy(cot_in, cot_ref, sems.at[1])
    field_copy.start()
    cot_copy.start()
    field_copy.wait()
    sides = jnp.concatenate(
        [field_ref[0], field_ref[:, side - 1, :], field_ref[side - 1], field_ref[:, 0, :]], axis=0
    )
    pack(sides, sides_ref)
    cot_copy.wait()
    pack(cot_ref[...], cot_packed_ref)


def shifted_columns(side, part, field, halos, out_ref):
    rows = side * side
    flat = rows + 2 * side
    column = lax.broadcasted_iota(jnp.int32, (flat, part), 0) % side
    if halos is None:
        none = jnp.zeros((side, part), jnp.float32)
        tall = jnp.concatenate([none, field.astype(jnp.float32), none], axis=0)
        west = east = 0.0
    else:
        edge = halos.astype(jnp.float32)
        tall = jnp.concatenate([edge[0:side], field.astype(jnp.float32), edge[2 * side : 3 * side]], axis=0)
        corner = [edge[4 * side + c : 4 * side + c + 1] for c in range(4)]
        spread = lambda col: jnp.broadcast_to(col[:, None, :], (side + 2, side, part)).reshape(flat, part)
        east = spread(jnp.concatenate([corner[1], edge[side : 2 * side], corner[2]], axis=0))
        west = spread(jnp.concatenate([corner[0], edge[3 * side : 4 * side], corner[3]], axis=0))
    out_ref[0] = jnp.where(column == 0, west, pltpu.roll(tall, 1, 0)).astype(jnp.bfloat16)
    out_ref[1] = tall.astype(jnp.bfloat16)
    out_ref[2] = jnp.where(column == side - 1, east, pltpu.roll(tall, flat - 1, 0)).astype(jnp.bfloat16)


def onehot_kernel(
    side, tables_in, et_in, eu_in, ct_in, cu_in, border_ref, halo_ref, place_ref, tables, et, eu, ct, cu, sems
):
    copies = [
        pltpu.make_async_copy(a, b, sems.at[i])
        for i, (a, b) in enumerate(
            [(tables_in, tables), (et_in, et), (eu_in, eu), (ct_in, ct), (cu_in, cu)]
        )
    ]
    for copy in copies:
        copy.start()
    for copy in copies:
        copy.wait()
    count = lax.axis_size("tile")
    own = lax.axis_index("tile")
    core = lax.rem(own, 2)
    groups = count // SPAN

    def base(source):
        slab = lax.rem(source // SPAN - own // SPAN + groups, groups)
        cross = source ^ own
        turn = lax.rem(cross // 2, 2)
        at = jnp.where(slab == 0, turn, jnp.where(slab == 1, 2, 3) + 2 * turn)
        return (6 * lax.rem(cross, 2) + at) * (4 * side)

    step = lax.broadcasted_iota(jnp.int32, (side, 1), 0)
    nothing = jnp.full((side, 1), -1, jnp.int32)

    def halo(tile, e):
        slot = tables[e, eu[e, tile]]
        start = base(et[e, tile]) + lax.rem(slot, 4) * side
        return lambda at: jnp.where(slot >= 4, start + side - 1 - at, start + at)

    def corner(tile, c):
        return base(ct[c, tile]) + corner_spot(tables[4 + c, cu[c, tile]], side)

    def onehot(wanted, width):
        lane = lax.broadcasted_iota(jnp.int32, (wanted.shape[0], width), 1)
        return jnp.where(lane == wanted, 1.0, 0.0).astype(jnp.bfloat16)

    width = 12 * 4 * side
    pieces = [[] for _ in range(4)]
    for tile in (own, own ^ 1):
        top, right, bottom, left = [halo(tile, e) for e in range(4)]
        corners = [corner(tile, c) for c in range(4)]
        low = core == 0
        row = lambda at: jnp.where(low, top(at), bottom(at))
        first = jnp.where(low, corners[0], corners[3])
        last = jnp.where(low, corners[1], corners[2])
        along = jnp.where(low, step - 1, step + 1)
        fits = (along >= 0) & (along < side)
        pieces[0] += [jnp.where(step == 0, first, row(step - 1)), jnp.where(fits, left(along), nothing)]
        pieces[1] += [row(step), nothing]
        pieces[2] += [jnp.where(step == side - 1, last, row(step + 1)), jnp.where(fits, right(along), nothing)]
        pieces[3] += [nothing, jnp.where(low, left(step), right(step))]
    border_ref[...] = onehot(jnp.concatenate(sum(pieces, []), axis=0), width)
    spots = lax.broadcasted_iota(jnp.int32, (EXTRA, 1), 0)
    ends = jnp.full((EXTRA, 1), -1, jnp.int32)
    for c in range(4):
        ends = jnp.where(spots == c, corner(own, c), ends)
    halo_ref[...] = onehot(jnp.concatenate([halo(own, e)(step) for e in range(4)] + [ends], axis=0), width)

    block = 4 * side + EXTRA
    lane = lax.broadcasted_iota(jnp.int32, (1, block), 1)
    row = lax.broadcasted_iota(jnp.int32, (4 * side, block), 0)
    places = []
    for mask in (0, 2, 1, 3):
        for offset in (0, SPAN, -SPAN):
            source = lax.rem((own ^ mask) + offset + count, count)
            target = jnp.full((1, block), -1, jnp.int32)
            for e in range(4):
                slot = tables[e, eu[e, source]]
                along = lane - e * side
                along = jnp.where(slot >= 4, side - 1 - along, along)
                hit = (lane >= e * side) & (lane < (e + 1) * side) & (et[e, source] == own)
                target = jnp.where(hit, lax.rem(slot, 4) * side + along, target)
                spot = corner_spot(tables[4 + e, cu[e, source]], side)
                hit = (lane == 4 * side + e) & (ct[e, source] == own)
                target = jnp.where(hit, spot, target)
            places.append(jnp.where(row == target, 1.0, 0.0))
    place_ref[...] = jnp.concatenate(places, axis=1).astype(jnp.bfloat16)


def inner_kernel(
    side, part, half, scale, field_ref, own_ref, other_ref, mine_ref, send_ref, cot_ref, rim_ref, cols, total
):
    rows = side * side
    chans = cot_ref.shape[1]
    first = lax.axis_index("ch") == 0
    unpack(other_ref, cols.at[0], 0, 0, rows, part)

    @pl.when(first)
    def _():
        cot_ref[:, 0:part] = own_ref[...]
        cot_ref[:, part:] = cols[0, 0:rows, :]

    @pl.when(jnp.logical_not(first))
    def _():
        cot_ref[:, 0:part] = cols[0, 0:rows, :]
        cot_ref[:, part:] = own_ref[...]

    shifted_columns(side, part, field_ref[...].reshape(rows, part), None, cols)
    cot = cot_ref[...]
    used = 9 * part // 2
    for a in range(3):
        for b in range(3):
            tap = 3 * a + b
            value = (
                lax.dot_general(
                    cols[b, a * side : a * side + rows, :],
                    cot,
                    (((0,), (0,)), ((), ())),
                    preferred_element_type=jnp.float32,
                )
                * scale
            )
            if tap < 4:
                total[tap * part : (tap + 1) * part, :] = value
            elif tap > 4:
                start = half + part // 2 + (tap - 5) * part
                total[start : start + part, :] = value
            else:
                total[4 * part : used, :] = value[: part // 2]
                total[half : half + part // 2, :] = value[part // 2 :]
    blank = jnp.zeros((half - used, chans), jnp.float32)
    total[used:half, :] = blank
    total[half + used : 2 * half, :] = blank
    core = lax.rem(lax.axis_index("tile"), 2)
    mine_ref[...] = total[pl.ds(pl.multiple_of(core * half, 16), half), :]
    send_ref[...] = total[pl.ds(pl.multiple_of((1 - core) * half, 16), half), :]
    rim_ref[...] = jnp.concatenate(
        [
            cot[0:side],
            cot[rows - side :],
            cot.reshape(side, side, chans)[:, 0, :],
            cot.reshape(side, side, chans)[:, side - 1, :],
        ],
        axis=0,
    )


def border_kernel(side, part, chunk, scale, n_near, *refs):
    near_refs = refs[:n_near]
    onehot_ref, mine_ref, got_ref, rim_ref, mate_ref = refs[n_near : n_near + 5]
    outs, near, total = refs[n_near + 5 : -2], refs[-2], refs[-1]
    count = lax.axis_size("tile")
    own = lax.axis_index("tile")
    core = lax.rem(own, 2)
    for i, ref in enumerate(near_refs):
        unpack(ref, near, 0, i * 4 * side, 4 * side, part)
    total[...] = mine_ref[...] + got_ref[...]
    left = jnp.dot(onehot_ref[...], near[...], preferred_element_type=jnp.float32).astype(jnp.bfloat16)

    def rim(ref, at):
        return ref[pl.ds(pl.multiple_of(at, 16), side), :]

    for q in range(4):
        column = (2 + q // 2) * side if q < 3 else (2 + core) * side
        right = jnp.concatenate(
            [value for ref in (rim_ref, mate_ref) for value in (rim(ref, core * side), rim(ref, column))],
            axis=0,
        )
        value = lax.dot_general(
            left[q * 4 * side : (q + 1) * 4 * side],
            right,
            (((0,), (0,)), ((), ())),
            preferred_element_type=jnp.float32,
        )
        if q < 3:
            start = q * part + core * (part // 2 + part)
        else:
            start = 3 * part - core * (3 * part - part // 2)
        here = pl.ds(pl.multiple_of(start, 16), part)
        total[here, :] = total[here, :] + value * scale
    size = outs[0].shape[0]
    for index in range(count // 2):
        to = slot_of_mask(2 * index, count) * chunk
        block = pl.multiple_of(((own // 2) ^ index) * chunk, 16)
        out = outs[to // size]
        out[to % size : to % size + chunk, :] = total[pl.ds(block, chunk), :].astype(out.dtype)


def sum_kernel(n_got, n_out, *refs):
    held_ref, got_refs, outs = refs[0], refs[1 : 1 + n_got], refs[1 + n_got :]
    size = held_ref.shape[0] // n_out
    for index in range(n_out):
        here = slice(index * size, (index + 1) * size)
        value = held_ref[here, :]
        for ref in got_refs:
            value = value + ref[here, :].astype(jnp.float32)
        outs[index][...] = value.astype(outs[index].dtype)


def join_kernel(*refs):
    row = 0
    for ref in refs[:-1]:
        refs[-1][row : row + ref.shape[0], :] = ref[...]
        row += ref.shape[0]


def unfold_kernel(used, chunk, bit, masks, n_dep, *refs):
    refs = refs[n_dep:]
    n = len(masks)
    in_refs, out_ref, wide, sems = refs[:n], refs[n], refs[n + 1], refs[n + 2]
    own = lax.axis_index("tile")
    origin = (lax.rem(own, 2) ^ bit) * used
    full, rest = used // chunk, used % chunk
    copies = []
    for i, (ref, inner) in enumerate(zip(in_refs, masks)):
        for k, mask in enumerate(inner):
            at = i * len(inner) + k
            wide[at] = ref[k * chunk : (k + 1) * chunk, :].astype(jnp.float32)
            block = (own ^ mask) // 2
            start = pl.multiple_of(origin + block * chunk, 16)
            copies.append(
                (
                    block < full,
                    pltpu.make_async_copy(wide.at[at], out_ref.at[pl.ds(start, chunk), :], sems.at[at]),
                )
            )
            if rest:
                start = pl.multiple_of(origin + full * chunk, 16)
                copies.append(
                    (
                        block == full,
                        pltpu.make_async_copy(
                            wide.at[at, 0:rest], out_ref.at[pl.ds(start, rest), :], sems.at[at]
                        ),
                    )
                )
    for going, copy in copies:
        pl.when(going)(copy.start)
    for going, copy in copies:
        pl.when(going)(copy.wait)


def unfold(whole, chunk, bit, masks, blocks, before):
    n_dep = 0 if before is None else 1
    anywhere = pl.BlockSpec(memory_space=pl.ANY)
    n_copies = len(masks) * len(masks[0])
    return pl.pallas_call(
        functools.partial(unfold_kernel, whole.shape[0] // 2, chunk, bit, masks, n_dep),
        out_shape=whole,
        in_specs=[anywhere] * n_dep + [pl.BlockSpec(memory_space=pltpu.VMEM)] * len(blocks),
        out_specs=anywhere,
        scratch_shapes=[
            pltpu.VMEM((n_copies, chunk, whole.shape[1]), jnp.float32),
            pltpu.SemaphoreType.DMA((n_copies,)),
        ],
        input_output_aliases={0: 0} if n_dep else {},
        compiler_params=pltpu.CompilerParams(vmem_limit_bytes=40 * 1024 * 1024),
    )(*([before] if n_dep else []), *blocks)


def back_kernel(side, part, cot_ref, weight_in, inner_ref, pieces_ref, tall, weight, sems):
    rows = side * side
    flat = rows + 2 * side
    start = pl.multiple_of(lax.axis_index("ch") * part, 16)
    copies = [
        pltpu.make_async_copy(weight_in.at[tap, pl.ds(start, part), :], weight.at[tap], sems.at[tap])
        for tap in range(9)
    ]
    for copy in copies:
        copy.start()
    blank = jnp.zeros((2 * side, tall.shape[1]), jnp.bfloat16)
    tall[0 : 2 * side, :] = blank
    tall[2 * side : 2 * side + rows, :] = cot_ref[...]
    tall[2 * side + rows :, :] = blank
    for copy in copies:
        copy.wait()
    backs = []
    for b in range(3):
        back = jnp.zeros((flat, part), jnp.float32)
        for a in range(3):
            back = back + lax.dot_general(
                tall[(2 - a) * side : (2 - a) * side + flat, :],
                weight[3 * a + b],
                (((1,), (1,)), ((), ())),
                preferred_element_type=jnp.float32,
            )
        backs.append(back)
    column = lax.broadcasted_iota(jnp.int32, (flat, part), 0) % side
    inner = (
        jnp.where(column == side - 1, 0.0, pltpu.roll(backs[0], flat - 1, 0))
        + backs[1]
        + jnp.where(column == 0, 0.0, pltpu.roll(backs[2], 1, 0))
    )
    inner_ref[...] = inner[side : side + rows]
    west = backs[0].reshape(side + 2, side, part)[:, 0, :]
    east = backs[2].reshape(side + 2, side, part)[:, side - 1, :]
    pieces = jnp.concatenate(
        [
            inner[0:side],
            east[1 : side + 1],
            inner[side + rows :],
            west[1 : side + 1],
            west[0:1],
            east[0:1],
            east[side + 1 :],
            west[side + 1 :],
            jnp.zeros((EXTRA - 4, part), jnp.float32),
        ],
        axis=0,
    )
    pack(pieces.astype(jnp.bfloat16), pieces_ref)


def add_halo_kernel(side, part, place_ref, inner_ref, *refs):
    got_refs, out_ref, got = refs[:-2], refs[-2], refs[-1]
    block = 4 * side + EXTRA
    size = packed_shape(block, part)[0]
    for i, ref in enumerate(got_refs):
        for k in range(3):
            unpack(ref, got, k * size, (3 * i + k) * block, block, part)
    sums = jnp.dot(place_ref[...], got[...], preferred_element_type=jnp.float32)
    rows = side * side
    spread = lambda col: jnp.broadcast_to(col[:, None, :], (side, side, part)).reshape(rows, part)
    column = lax.broadcasted_iota(jnp.int32, (rows, part), 0) % side
    inner = inner_ref[...]
    inner = inner + jnp.where(column == side - 1, spread(sums[side : 2 * side]), 0.0)
    inner = inner + jnp.where(column == 0, spread(sums[3 * side :]), 0.0)
    ends = jnp.concatenate(
        [
            inner[0:side] + sums[0:side],
            inner[side : rows - side],
            inner[rows - side :] + sums[2 * side : 3 * side],
        ],
        axis=0,
    )
    out_ref[...] = ends.astype(jnp.bfloat16)


def halo_kernel(side, part, n_near, *refs):
    near_refs, onehot_ref, field_ref = refs[:n_near], refs[n_near], refs[n_near + 1]
    halos_ref, packet_ref, near = refs[n_near + 2 :]
    rows = side * side
    for i, ref in enumerate(near_refs):
        unpack(ref, near, 0, i * 4 * side, 4 * side, part)
    halos = jnp.dot(onehot_ref[...], near[...], preferred_element_type=jnp.float32).astype(jnp.bfloat16)
    halos_ref[...] = halos
    pack(field_ref[...].reshape(rows, part), packet_ref)
    pack(halos, packet_ref, packed_shape(rows, part)[0])


def output_kernel(side, part, field_ref, halos_ref, other_ref, weight_in, out_ref, cols, other_cols, other, weight, sems):
    rows = side * side
    ch = lax.axis_index("ch")
    wide = weight.shape[2]
    lanes = pl.multiple_of(ch * (weight_in.shape[2] - wide), 128)
    copies = [
        pltpu.make_async_copy(weight_in.at[tap, :, pl.ds(lanes, wide)], weight.at[tap], sems.at[tap])
        for tap in range(9)
    ]
    for copy in copies:
        copy.start()
    unpack(other_ref, other, 0, 0, rows, part)
    unpack(other_ref, other, packed_shape(rows, part)[0], rows, 4 * side + EXTRA, part)
    shifted_columns(side, part, field_ref[...].reshape(rows, part), halos_ref[...], cols)
    shifted_columns(side, part, other[0:rows, :], other[rows:, :], other_cols)
    for copy in copies:
        copy.wait()
    starts = (pl.multiple_of(ch * part, 16), pl.multiple_of((1 - ch) * part, 16))
    total = jnp.zeros((rows, wide), jnp.float32)
    for a in range(3):
        for b in range(3):
            for ref, first in zip((cols, other_cols), starts):
                total = total + jnp.dot(
                    ref[b, a * side : a * side + rows, :],
                    weight[3 * a + b, pl.ds(first, part), :],
                    preferred_element_type=jnp.float32,
                )
    result = jnp.where(ch == 0, total[:, :part], total[:, wide - part :])
    out_ref[...] = result.astype(jnp.bfloat16)


def body(features, weight, cotangent, edge_tiles, edge_turns, corner_tiles, corner_turns):
    count = lax.axis_size("tile")
    field = features[0]
    side, part = field.shape[0], field.shape[2]
    chans = weight.shape[3]
    rows = side * side
    flat = rows + 2 * side
    block = 4 * side + EXTRA
    taps = weight.reshape(9, chans, chans)
    others = [(0, 1), (1, 0)]
    flops = 2 * rows * 9 * part * chans
    half_bytes = jnp.bfloat16
    chunk = -(-9 * part // (16 * count)) * 16
    half = count * chunk // 2
    scale = 1.0 / math.sqrt(count * rows)

    sides, cot_packed, field, cot_own = call(
        functools.partial(prepare_kernel, side, part),
        [
            vmem(packed_shape(4 * side, part), half_bytes),
            vmem(packed_shape(rows, part), half_bytes),
            vmem((side, side, part), half_bytes),
            vmem((rows, part), half_bytes),
        ],
        [field, cotangent[0].reshape(rows, part)],
        anywhere=(0, 1),
        scratch=[pltpu.SemaphoreType.DMA((2,))],
    )
    cot_other = lax.ppermute(cot_packed, "ch", others)
    near = [sides, by_mask(sides, 2, count)]
    for flip in (0, 2):
        for offset in (SPAN, -SPAN):
            pairs = [(i, ((i - offset) % count) ^ flip) for i in range(count)]
            near.append(lax.ppermute(sides, "tile", pairs))
    near, cot_other = lax.optimization_barrier((near, cot_other))
    near = near + [by_mask(v, 1, count) for v in near]

    border_pick, halo_pick, place = call(
        functools.partial(onehot_kernel, side),
        [
            vmem((16 * side, 48 * side), half_bytes),
            vmem((block, 48 * side), half_bytes),
            vmem((4 * side, 12 * block), half_bytes),
        ],
        [jnp.asarray(turn_tables()), edge_tiles.T, edge_turns.T, corner_tiles.T, corner_turns.T],
        anywhere=range(5),
        scratch=[pltpu.SMEM((8, 4), jnp.int32)]
        + [pltpu.SMEM((4, count), jnp.int32)] * 4
        + [pltpu.SemaphoreType.DMA((5,))],
    )
    mine, send, cot_full, rim = call(
        functools.partial(inner_kernel, side, part, half, scale),
        [
            vmem((half, chans), jnp.float32),
            vmem((half, chans), jnp.float32),
            vmem((rows, chans), half_bytes),
            vmem((4 * side, chans), half_bytes),
        ],
        [field, cot_own, cot_other],
        scratch=[pltpu.VMEM((3, flat, part), half_bytes), pltpu.VMEM((2 * half, chans), jnp.float32)],
        flops=flops,
    )

    stages = mask_stages(count)
    masks = group_masks(stages[1])
    size = half // len(masks)
    held, *send = call(
        functools.partial(border_kernel, side, part, chunk, scale, len(near)),
        [vmem((size, chans), jnp.float32)] + [vmem((size, chans), half_bytes)] * (len(masks) - 1),
        [*near, border_pick, mine, by_mask(send, 1, count), rim, by_mask(rim, 1, count)],
        scratch=[pltpu.VMEM((48 * side, part), half_bytes), pltpu.VMEM((half, chans), jnp.float32)],
    )
    send, near, cot_full = lax.optimization_barrier((send, near, cot_full))
    got = [by_mask(v, m, count) for v, m in zip(send, masks[1:])]
    halos, packet = call(
        functools.partial(halo_kernel, side, part, len(near)),
        [vmem((block, part), half_bytes), vmem(packed_shape(rows + block, part), half_bytes)],
        [*near, halo_pick, field],
        scratch=[pltpu.VMEM((48 * side, part), half_bytes)],
    )
    other_field = lax.ppermute(packet, "ch", others)
    inner, pieces = call(
        functools.partial(back_kernel, side, part),
        [vmem((rows, part), jnp.float32), vmem(packed_shape(block, part), half_bytes)],
        [cot_full, taps],
        anywhere=(1,),
        scratch=[
            pltpu.VMEM((rows + 4 * side, chans), half_bytes),
            pltpu.VMEM((9, part, chans), half_bytes),
            pltpu.SemaphoreType.DMA((9,)),
        ],
        flops=flops,
    )
    got, pieces, inner, halos = lax.optimization_barrier((got, pieces, inner, halos))
    for index, bits in enumerate(stages[2:]):
        masks = group_masks(bits)
        size = held.shape[0] // len(masks)
        held, *send = call(
            functools.partial(sum_kernel, len(got), len(masks)),
            [vmem((size, chans), jnp.float32)] + [vmem((size, chans), half_bytes)] * (len(masks) - 1),
            [held, *got],
        )
        send, pieces = lax.optimization_barrier((send, pieces))
        got = [by_mask(v, m, count) for v, m in zip(send, masks[1:])]
        if index == 0:
            here = [pieces, by_offset(pieces, -SPAN, count), by_offset(pieces, SPAN, count)]
            (here,) = call(join_kernel, [vmem((3 * pieces.shape[0], pieces.shape[1]), half_bytes)], here)
            got, here = lax.optimization_barrier((got, here))
    (held,) = call(functools.partial(sum_kernel, len(got), 1), [vmem(held.shape, half_bytes)], [held, *got])
    order = [0]
    for index, bits in enumerate(stages[:0:-1]):
        masks = group_masks(bits)
        if index == 0:
            held, here, other_field = lax.optimization_barrier((held, here, other_field))
            beside = by_mask(here, 2, count)
            wide = -(-part // 128) * 128
            (output,) = call(
                functools.partial(output_kernel, side, part),
                [vmem((rows, part), half_bytes)],
                [field, halos, other_field, taps],
                anywhere=(3,),
                scratch=[
                    pltpu.VMEM((3, flat, part), half_bytes),
                    pltpu.VMEM((3, flat, part), half_bytes),
                    pltpu.VMEM((rows + block, part), half_bytes),
                    pltpu.VMEM((9, chans, wide), half_bytes),
                    pltpu.SemaphoreType.DMA((9,)),
                ],
                flops=2 * flops,
            )
        got = [by_mask(held, m, count) for m in masks[1:]]
        if index == 0:
            held, got, output, beside = lax.optimization_barrier((held, got, output, beside))
        if index < len(stages) - 2:
            order = [m + v for m in masks for v in order]
            (held,) = call(
                join_kernel, [vmem((held.shape[0] * len(masks), chans), half_bytes)], [held, *got]
            )
            continue
        got_pieces = [here, beside, by_mask(here, 1, count), by_mask(beside, 1, count)]
        (grad_features,) = call(
            functools.partial(add_halo_kernel, side, part),
            [vmem((rows, part), half_bytes)],
            [place, inner, *got_pieces],
            scratch=[pltpu.VMEM((12 * block, part), half_bytes)],
        )
        got, grad_features = lax.optimization_barrier((got, grad_features))
        got = [held, *got]
        order = [[m + v for v in order] for m in masks]
    mates = [by_mask(v, 1, count) for v in got]
    whole = vmem((9 * part, chans), jnp.float32)
    first = unfold(whole, chunk, 0, order, got, None)
    grad_weight = unfold(whole, chunk, 1, order, mates, first)
    shape = (1, side, side, part)
    return (
        output.reshape(shape),
        grad_features.reshape(shape),
        grad_weight.reshape(3, 3, part, chans),
    )


def solution(mesh):
    return jax.shard_map(
        body,
        mesh=mesh,
        in_specs=(
            P("tile", None, None, "ch"),
            P(),
            P("tile", None, None, "ch"),
            P(),
            P(),
            P(),
            P(),
        ),
        out_specs=(
            P("tile", None, None, "ch"),
            P("tile", None, None, "ch"),
            P(None, None, "ch", None),
        ),
        check_vma=False,
    )
```

```python
import functools
import math

import jax
import jax.numpy as jnp
import numpy as np
from jax import lax
from jax.experimental import pallas as pl
from jax.experimental.pallas import tpu as pltpu
from jax.sharding import PartitionSpec as P

SPAN = 4
EXTRA = 16


def turn_tables():
    labels = [[3 * row + col for col in range(3)] for row in range(3)]

    def turn_once(block):
        return [[block[col][2 - row] for col in range(3)] for row in range(3)]

    def sides_of(block):
        return [
            list(block[0]),
            [block[row][2] for row in range(3)],
            list(block[2]),
            [block[row][0] for row in range(3)],
        ]

    def corners_of(block):
        return [block[0][0], block[0][2], block[2][2], block[2][0]]

    base_sides = sides_of(labels)
    base_corners = corners_of(labels)
    edge_table = np.zeros((4, 4), np.int32)
    corner_table = np.zeros((4, 4), np.int32)
    for border in range(4):
        turned = labels
        for quarter in range(4):
            wanted = sides_of(turned)[(border + 2) % 4]
            for side_index in range(4):
                if base_sides[side_index] == wanted:
                    edge_table[border, quarter] = side_index
                if base_sides[side_index][::-1] == wanted:
                    edge_table[border, quarter] = side_index + 4
            corner_cell = corners_of(turned)[(border + 2) % 4]
            for corner_index in range(4):
                if base_corners[corner_index] == corner_cell:
                    corner_table[border, quarter] = corner_index
            turned = turn_once(turned)
    return np.concatenate([edge_table, corner_table], axis=0)


def by_offset(value, offset, count):
    return lax.ppermute(value, "tile", [(i, (i + offset) % count) for i in range(count)])


def by_mask(value, mask, count):
    return lax.ppermute(value, "tile", [(i, i ^ mask) for i in range(count)])


def mask_stages(count):
    bits = [1 << b for b in range(count.bit_length() - 1)]
    stages = [bits[:1]]
    rest = bits[1:]
    while rest:
        stages.append(rest[:2])
        rest = rest[2:]
    return stages


def group_masks(bits):
    masks = [0]
    for bit in bits:
        masks = masks + [m + bit for m in masks]
    return masks


def slot_of_mask(mask, count):
    place = 0
    for bits in mask_stages(count)[1:]:
        size = 1 << len(bits)
        place = place * size + (mask // bits[0]) % size
    return place


def corner_spot(slot, side):
    return jnp.where(
        slot == 0, 0, jnp.where(slot == 1, side - 1, jnp.where(slot == 2, 3 * side - 1, 2 * side))
    )


def vmem(shape, dtype):
    return jax.ShapeDtypeStruct(shape, dtype)


def call(kernel, outs, args, anywhere=(), scratch=(), flops=0):
    in_specs = [
        pl.BlockSpec(memory_space=pltpu.HBM if i in anywhere else pltpu.VMEM) for i in range(len(args))
    ]
    size = sum(math.prod(x.shape) * x.dtype.itemsize for x in list(args) + list(outs))
    return pl.pallas_call(
        kernel,
        out_shape=tuple(outs),
        in_specs=in_specs,
        out_specs=tuple(pl.BlockSpec(memory_space=pltpu.VMEM) for _ in outs),
        scratch_shapes=list(scratch),
        compiler_params=pltpu.CompilerParams(vmem_limit_bytes=40 * 1024 * 1024),
        cost_estimate=pl.CostEstimate(flops=flops, bytes_accessed=size, transcendentals=0),
    )(*args)


def packed_shape(rows, part):
    if part % 128 != 64:
        return (rows, part)
    return (rows * (part // 128) + rows // 2, 128)


def pack(value, out_ref, first=0):
    rows, part = value.shape
    if part % 128 != 64:
        out_ref[first : first + rows, :] = value
        return
    for i in range(part // 128):
        out_ref[first + i * rows : first + (i + 1) * rows, :] = value[:, i * 128 : (i + 1) * 128]
    rest = value[:, part - 64 :]
    at = first + rows * (part // 128)
    out_ref[at : at + rows // 2, :] = jnp.concatenate([rest[: rows // 2], rest[rows // 2 :]], axis=1)


def unpack(ref, out_ref, first, row, rows, part):
    if part % 128 != 64:
        out_ref[row : row + rows, :] = ref[first : first + rows, :]
        return
    for i in range(part // 128):
        out_ref[row : row + rows, i * 128 : (i + 1) * 128] = ref[first + i * rows : first + (i + 1) * rows, :]
    at = first + rows * (part // 128)
    rest = ref[at : at + rows // 2, :]
    out_ref[row : row + rows // 2, part - 64 :] = rest[:, :64]
    out_ref[row + rows // 2 : row + rows, part - 64 :] = rest[:, 64:]


def sides_kernel(side, field_ref, sides_ref, copy_ref):
    sides = jnp.concatenate(
        [field_ref[0], field_ref[:, side - 1, :], field_ref[side - 1], field_ref[:, 0, :]], axis=0
    )
    pack(sides, sides_ref)
    copy_ref[...] = field_ref[...]


def shifted_columns(side, part, field, halos, out_ref):
    rows = side * side
    flat = rows + 2 * side
    column = lax.broadcasted_iota(jnp.int32, (flat, part), 0) % side
    if halos is None:
        none = jnp.zeros((side, part), jnp.float32)
        tall = jnp.concatenate([none, field.astype(jnp.float32), none], axis=0)
        west = east = 0.0
    else:
        edge = halos.astype(jnp.float32)
        tall = jnp.concatenate([edge[0:side], field.astype(jnp.float32), edge[2 * side : 3 * side]], axis=0)
        corner = [edge[4 * side + c : 4 * side + c + 1] for c in range(4)]
        spread = lambda col: jnp.broadcast_to(col[:, None, :], (side + 2, side, part)).reshape(flat, part)
        east = spread(jnp.concatenate([corner[1], edge[side : 2 * side], corner[2]], axis=0))
        west = spread(jnp.concatenate([corner[0], edge[3 * side : 4 * side], corner[3]], axis=0))
    out_ref[0] = jnp.where(column == 0, west, pltpu.roll(tall, 1, 0)).astype(jnp.bfloat16)
    out_ref[1] = tall.astype(jnp.bfloat16)
    out_ref[2] = jnp.where(column == side - 1, east, pltpu.roll(tall, flat - 1, 0)).astype(jnp.bfloat16)


def onehot_kernel(side, tables_in, cot_in, border_ref, halo_ref, place_ref, cot_ref, tables, sem):
    copy = pltpu.make_async_copy(tables_in, tables, sem)
    copy.start()
    cot_ref[...] = cot_in[...]
    copy.wait()
    et, eu, ct, cu = [tables.at[8 + 4 * i : 12 + 4 * i] for i in range(4)]
    count = lax.axis_size("tile")
    own = lax.axis_index("tile")
    core = lax.rem(own, 2)
    groups = count // SPAN

    def base(source):
        slab = lax.rem(source // SPAN - own // SPAN + groups, groups)
        cross = source ^ own
        turn = lax.rem(cross // 2, 2)
        at = jnp.where(slab == 0, 0, jnp.where(slab == 1, 2, 4)) + turn
        return (6 * lax.rem(cross, 2) + at) * (4 * side)

    step = lax.broadcasted_iota(jnp.int32, (side, 1), 0)
    nothing = jnp.full((side, 1), -1, jnp.int32)

    def halo(tile, e):
        slot = tables[e, eu[e, tile]]
        start = base(et[e, tile]) + lax.rem(slot, 4) * side
        return lambda at: jnp.where(slot >= 4, start + side - 1 - at, start + at)

    def corner(tile, c):
        return base(ct[c, tile]) + corner_spot(tables[4 + c, cu[c, tile]], side)

    def onehot(wanted, width):
        lane = lax.broadcasted_iota(jnp.int32, (wanted.shape[0], width), 1)
        return jnp.where(lane == wanted, 1.0, 0.0).astype(jnp.bfloat16)

    width = 12 * 4 * side
    pieces = [[] for _ in range(4)]
    for tile in (own, own ^ 1):
        top, right, bottom, left = [halo(tile, e) for e in range(4)]
        corners = [corner(tile, c) for c in range(4)]
        low = core == 0
        row = lambda at: jnp.where(low, top(at), bottom(at))
        first = jnp.where(low, corners[0], corners[3])
        last = jnp.where(low, corners[1], corners[2])
        along = jnp.where(low, step - 1, step + 1)
        fits = (along >= 0) & (along < side)
        pieces[0] += [jnp.where(step == 0, first, row(step - 1)), jnp.where(fits, left(along), nothing)]
        pieces[1] += [row(step), nothing]
        pieces[2] += [jnp.where(step == side - 1, last, row(step + 1)), jnp.where(fits, right(along), nothing)]
        pieces[3] += [nothing, jnp.where(low, left(step), right(step))]
    border_ref[...] = onehot(jnp.concatenate(sum(pieces, []), axis=0), width)
    spots = lax.broadcasted_iota(jnp.int32, (EXTRA, 1), 0)
    ends = jnp.full((EXTRA, 1), -1, jnp.int32)
    for c in range(4):
        ends = jnp.where(spots == c, corner(own, c), ends)
    halo_ref[...] = onehot(jnp.concatenate([halo(own, e)(step) for e in range(4)] + [ends], axis=0), width)

    block = 4 * side + EXTRA
    lane = lax.broadcasted_iota(jnp.int32, (1, block), 1)
    row = lax.broadcasted_iota(jnp.int32, (4 * side, block), 0)
    places = []
    for mask in (0, 2, 1, 3):
        for offset in (0, SPAN, -SPAN):
            source = lax.rem((own ^ mask) + offset + count, count)
            target = jnp.full((1, block), -1, jnp.int32)
            for e in range(4):
                slot = tables[e, eu[e, source]]
                along = lane - e * side
                along = jnp.where(slot >= 4, side - 1 - along, along)
                hit = (lane >= e * side) & (lane < (e + 1) * side) & (et[e, source] == own)
                target = jnp.where(hit, lax.rem(slot, 4) * side + along, target)
                spot = corner_spot(tables[4 + e, cu[e, source]], side)
                hit = (lane == 4 * side + e) & (ct[e, source] == own)
                target = jnp.where(hit, spot, target)
            places.append(jnp.where(row == target, 1.0, 0.0))
    place_ref[...] = jnp.concatenate(places, axis=1).astype(jnp.bfloat16)


def half_taps(side, part, half, scale, which, cols, cot, out_ref, middle):
    rows = side * side
    used = 9 * part // 2

    def product(a, b):
        value = lax.dot_general(
            cols[b, pl.ds(pl.multiple_of(a * side, 16), rows), :],
            cot,
            (((0,), (0,)), ((), ())),
            preferred_element_type=jnp.float32,
        )
        return value * scale

    for j in range(4):
        tap = j + 5 * which
        start = pl.multiple_of(which * (part // 2) + j * part, 16)
        out_ref[pl.ds(start, part), :] = product(tap // 3, lax.rem(tap, 3))
    middle[...] = product(1, 1)
    start = pl.multiple_of((1 - which) * 4 * part, 16)
    out_ref[pl.ds(start, part // 2), :] = middle[pl.ds(pl.multiple_of(which * (part // 2), 16), part // 2), :]
    out_ref[used:, :] = jnp.zeros((half - used, cot.shape[1]), jnp.float32)


def send_kernel(
    side, part, half, scale, field_ref, own_ref, other_ref, send_ref, cot_ref, rim_ref, cols, middle
):
    rows = side * side
    chans = cot_ref.shape[1]
    first = lax.axis_index("ch") == 0

    @pl.when(first)
    def _():
        cot_ref[:, 0:part] = own_ref[...]
        cot_ref[:, part:] = other_ref[...]

    @pl.when(jnp.logical_not(first))
    def _():
        cot_ref[:, 0:part] = other_ref[...]
        cot_ref[:, part:] = own_ref[...]

    shifted_columns(side, part, field_ref[...].reshape(rows, part), None, cols)
    cot = cot_ref[...]
    rim_ref[...] = jnp.concatenate(
        [
            cot[0:side],
            cot[rows - side :],
            cot.reshape(side, side, chans)[:, 0, :],
            cot.reshape(side, side, chans)[:, side - 1, :],
        ],
        axis=0,
    )
    which = 1 - lax.rem(lax.axis_index("tile"), 2)
    half_taps(side, part, half, scale, which, cols, cot, send_ref, middle)


def mine_kernel(side, part, half, scale, cols, cot_ref, mine_ref, middle):
    which = lax.rem(lax.axis_index("tile"), 2)
    half_taps(side, part, half, scale, which, cols, cot_ref[...], mine_ref, middle)


def unpack_near(near_refs, near, side, part):
    size = packed_shape(4 * side, part)[0]
    for i, ref in enumerate(near_refs):
        for k in range(2):
            unpack(ref, near, k * size, (2 * i + k) * 4 * side, 4 * side, part)


def border_kernel(side, part, chunk, scale, n_near, *refs):
    near_refs = refs[:n_near]
    onehot_ref, mine_ref, got_ref, rim_ref, mate_ref = refs[n_near : n_near + 5]
    outs, near, total = refs[n_near + 5 : -2], refs[-2], refs[-1]
    count = lax.axis_size("tile")
    own = lax.axis_index("tile")
    core = lax.rem(own, 2)
    unpack_near(near_refs, near, side, part)
    total[...] = mine_ref[...] + got_ref[...]
    left = jnp.dot(onehot_ref[...], near[...], preferred_element_type=jnp.float32).astype(jnp.bfloat16)

    def rim(ref, at):
        return ref[pl.ds(pl.multiple_of(at, 16), side), :]

    for q in range(4):
        column = (2 + q // 2) * side if q < 3 else (2 + core) * side
        right = jnp.concatenate(
            [value for ref in (rim_ref, mate_ref) for value in (rim(ref, core * side), rim(ref, column))],
            axis=0,
        )
        value = lax.dot_general(
            left[q * 4 * side : (q + 1) * 4 * side],
            right,
            (((0,), (0,)), ((), ())),
            preferred_element_type=jnp.float32,
        )
        if q < 3:
            start = q * part + core * (part // 2 + part)
        else:
            start = 3 * part - core * (3 * part - part // 2)
        here = pl.ds(pl.multiple_of(start, 16), part)
        total[here, :] = total[here, :] + value * scale
    size = outs[0].shape[0]
    for index in range(count // 2):
        to = slot_of_mask(2 * index, count) * chunk
        block = pl.multiple_of(((own // 2) ^ index) * chunk, 16)
        out = outs[to // size]
        out[to % size : to % size + chunk, :] = total[pl.ds(block, chunk), :].astype(out.dtype)


def sum_kernel(n_got, n_out, *refs):
    held_ref, got_refs, outs = refs[0], refs[1 : 1 + n_got], refs[1 + n_got :]
    size = held_ref.shape[0] // n_out
    for index in range(n_out):
        here = slice(index * size, (index + 1) * size)
        value = held_ref[here, :]
        for ref in got_refs:
            value = value + ref[here, :].astype(jnp.float32)
        outs[index][...] = value.astype(outs[index].dtype)


def join_kernel(*refs):
    row = 0
    for ref in refs[:-1]:
        refs[-1][row : row + ref.shape[0], :] = ref[...]
        row += ref.shape[0]


def unfold_kernel(used, chunk, bits, masks, n_dep, *refs):
    refs = refs[n_dep:]
    n = len(masks)
    in_refs, out_ref, wide, sems = refs[:n], refs[n], refs[n + 1], refs[n + 2]
    own = lax.axis_index("tile")
    full, rest = used // chunk, used % chunk
    copies = []
    for i, (ref, inner, bit) in enumerate(zip(in_refs, masks, bits)):
        origin = (lax.rem(own, 2) ^ bit) * used
        for k, mask in enumerate(inner):
            at = i * len(inner) + k
            wide[at] = ref[k * chunk : (k + 1) * chunk, :].astype(jnp.float32)
            block = (own ^ mask) // 2
            start = pl.multiple_of(origin + block * chunk, 16)
            copies.append(
                (
                    block < full,
                    pltpu.make_async_copy(wide.at[at], out_ref.at[pl.ds(start, chunk), :], sems.at[at]),
                )
            )
            if rest:
                start = pl.multiple_of(origin + full * chunk, 16)
                copies.append(
                    (
                        block == full,
                        pltpu.make_async_copy(
                            wide.at[at, 0:rest], out_ref.at[pl.ds(start, rest), :], sems.at[at]
                        ),
                    )
                )
    for going, copy in copies:
        pl.when(going)(copy.start)
    for going, copy in copies:
        pl.when(going)(copy.wait)


def unfold(whole, chunk, bits, masks, blocks, before):
    n_dep = 0 if before is None else 1
    anywhere = pl.BlockSpec(memory_space=pl.ANY)
    n_copies = len(masks) * len(masks[0])
    return pl.pallas_call(
        functools.partial(unfold_kernel, whole.shape[0] // 2, chunk, bits, masks, n_dep),
        out_shape=whole,
        in_specs=[anywhere] * n_dep + [pl.BlockSpec(memory_space=pltpu.VMEM)] * len(blocks),
        out_specs=anywhere,
        scratch_shapes=[
            pltpu.VMEM((n_copies, chunk, whole.shape[1]), jnp.float32),
            pltpu.SemaphoreType.DMA((n_copies,)),
        ],
        input_output_aliases={0: 0} if n_dep else {},
        compiler_params=pltpu.CompilerParams(vmem_limit_bytes=40 * 1024 * 1024),
    )(*([before] if n_dep else []), *blocks)


def back_kernel(side, part, cot_ref, weight_ref, inner_ref, pieces_ref, tall):
    rows = side * side
    flat = rows + 2 * side
    start = pl.multiple_of(lax.axis_index("ch") * part, 16)
    blank = jnp.zeros((2 * side, tall.shape[1]), jnp.bfloat16)
    tall[0 : 2 * side, :] = blank
    tall[2 * side : 2 * side + rows, :] = cot_ref[...]
    tall[2 * side + rows :, :] = blank
    backs = []
    for b in range(3):
        back = jnp.zeros((flat, part), jnp.float32)
        for a in range(3):
            back = back + lax.dot_general(
                tall[(2 - a) * side : (2 - a) * side + flat, :],
                weight_ref[3 * a + b, pl.ds(start, part), :],
                (((1,), (1,)), ((), ())),
                preferred_element_type=jnp.float32,
            )
        backs.append(back)
    column = lax.broadcasted_iota(jnp.int32, (flat, part), 0) % side
    inner = (
        jnp.where(column == side - 1, 0.0, pltpu.roll(backs[0], flat - 1, 0))
        + backs[1]
        + jnp.where(column == 0, 0.0, pltpu.roll(backs[2], 1, 0))
    )
    inner_ref[...] = inner[side : side + rows]
    west = backs[0].reshape(side + 2, side, part)[:, 0, :]
    east = backs[2].reshape(side + 2, side, part)[:, side - 1, :]
    pieces = jnp.concatenate(
        [
            inner[0:side],
            east[1 : side + 1],
            inner[side + rows :],
            west[1 : side + 1],
            west[0:1],
            east[0:1],
            east[side + 1 :],
            west[side + 1 :],
            jnp.zeros((EXTRA - 4, part), jnp.float32),
        ],
        axis=0,
    )
    pack(pieces.astype(jnp.bfloat16), pieces_ref)


def add_halo_kernel(side, part, place_ref, inner_ref, *refs):
    got_refs, out_ref, got = refs[:-2], refs[-2], refs[-1]
    block = 4 * side + EXTRA
    size = packed_shape(block, part)[0]
    for i, ref in enumerate(got_refs):
        for k in range(3):
            unpack(ref, got, k * size, (3 * i + k) * block, block, part)
    sums = jnp.dot(place_ref[...], got[...], preferred_element_type=jnp.float32)
    rows = side * side
    spread = lambda col: jnp.broadcast_to(col[:, None, :], (side, side, part)).reshape(rows, part)
    column = lax.broadcasted_iota(jnp.int32, (rows, part), 0) % side
    inner = inner_ref[...]
    inner = inner + jnp.where(column == side - 1, spread(sums[side : 2 * side]), 0.0)
    inner = inner + jnp.where(column == 0, spread(sums[3 * side :]), 0.0)
    ends = jnp.concatenate(
        [
            inner[0:side] + sums[0:side],
            inner[side : rows - side],
            inner[rows - side :] + sums[2 * side : 3 * side],
        ],
        axis=0,
    )
    out_ref[...] = ends.astype(jnp.bfloat16)


def halo_kernel(side, part, n_near, *refs):
    near_refs, onehot_ref, field_ref = refs[:n_near], refs[n_near], refs[n_near + 1]
    halos_ref, packet_ref, near = refs[n_near + 2 :]
    rows = side * side
    unpack_near(near_refs, near, side, part)
    halos = jnp.dot(onehot_ref[...], near[...], preferred_element_type=jnp.float32).astype(jnp.bfloat16)
    halos_ref[...] = halos
    pack(field_ref[...].reshape(rows, part), packet_ref)
    pack(halos, packet_ref, packed_shape(rows, part)[0])


def output_kernel(side, part, field_ref, halos_ref, other_ref, weight_ref, out_ref, cols, other_cols, other):
    rows = side * side
    ch = lax.axis_index("ch")
    wide = -(-part // 128) * 128
    lanes = pl.multiple_of(ch * (weight_ref.shape[2] - wide), 128)
    unpack(other_ref, other, 0, 0, rows, part)
    unpack(other_ref, other, packed_shape(rows, part)[0], rows, 4 * side + EXTRA, part)
    shifted_columns(side, part, field_ref[...].reshape(rows, part), halos_ref[...], cols)
    shifted_columns(side, part, other[0:rows, :], other[rows:, :], other_cols)
    starts = (pl.multiple_of(ch * part, 16), pl.multiple_of((1 - ch) * part, 16))
    total = jnp.zeros((rows, wide), jnp.float32)
    for a in range(3):
        for b in range(3):
            for ref, first in zip((cols, other_cols), starts):
                total = total + jnp.dot(
                    ref[b, a * side : a * side + rows, :],
                    weight_ref[3 * a + b, pl.ds(first, part), pl.ds(lanes, wide)],
                    preferred_element_type=jnp.float32,
                )
    result = jnp.where(ch == 0, total[:, :part], total[:, wide - part :])
    out_ref[...] = result.astype(jnp.bfloat16)


def body(features, weight, cotangent, edge_tiles, edge_turns, corner_tiles, corner_turns):
    count = lax.axis_size("tile")
    field = features[0]
    side, part = field.shape[0], field.shape[2]
    chans = weight.shape[3]
    rows = side * side
    flat = rows + 2 * side
    block = 4 * side + EXTRA
    taps = weight.reshape(9, chans, chans)
    others = [(0, 1), (1, 0)]
    flops = 2 * rows * 9 * part * chans
    half_bytes = jnp.bfloat16
    chunk = -(-9 * part // (16 * count)) * 16
    half = count * chunk // 2
    scale = 1.0 / math.sqrt(count * rows)

    cot_own = cotangent[0].reshape(rows, part)
    cot_other = lax.ppermute(cot_own, "ch", others)
    sides, field = call(
        functools.partial(sides_kernel, side),
        [vmem(packed_shape(4 * side, part), half_bytes), vmem(field.shape, half_bytes)],
        [field],
    )
    pair = packed_shape(8 * side, part)
    (near,) = call(join_kernel, [vmem(pair, half_bytes)], [sides, by_mask(sides, 2, count)])
    near = [near, by_offset(near, -SPAN, count), by_offset(near, SPAN, count)]
    tables = jnp.pad(jnp.asarray(turn_tables()), ((0, 0), (0, count - 4)))
    tables = jnp.concatenate([tables, edge_tiles.T, edge_turns.T, corner_tiles.T, corner_turns.T], axis=0)
    border_pick, halo_pick, place, cot_own = call(
        functools.partial(onehot_kernel, side),
        [
            vmem((16 * side, 48 * side), half_bytes),
            vmem((block, 48 * side), half_bytes),
            vmem((4 * side, 12 * block), half_bytes),
            vmem((rows, part), half_bytes),
        ],
        [tables, cot_own],
        scratch=[pltpu.SMEM(tables.shape, jnp.int32), pltpu.SemaphoreType.DMA],
    )
    near, cot_other, border_pick = lax.optimization_barrier((near, cot_other, border_pick))
    near = near + [by_mask(v, 1, count) for v in near]
    send, cot_full, rim, cols = call(
        functools.partial(send_kernel, side, part, half, scale),
        [
            vmem((half, chans), jnp.float32),
            vmem((rows, chans), half_bytes),
            vmem((4 * side, chans), half_bytes),
            vmem((3, flat, part), half_bytes),
        ],
        [field, cot_own, cot_other],
        scratch=[pltpu.VMEM((part, chans), jnp.float32)],
        flops=flops // 2,
    )
    (mine,) = call(
        functools.partial(mine_kernel, side, part, half, scale),
        [vmem((half, chans), jnp.float32)],
        [cols, cot_full],
        scratch=[pltpu.VMEM((part, chans), jnp.float32)],
        flops=flops // 2,
    )

    stages = mask_stages(count)
    masks = group_masks(stages[1])
    size = half // len(masks)
    held, *send = call(
        functools.partial(border_kernel, side, part, chunk, scale, len(near)),
        [vmem((size, chans), jnp.float32)] + [vmem((size, chans), half_bytes)] * (len(masks) - 1),
        [*near, border_pick, mine, by_mask(send, 1, count), rim, by_mask(rim, 1, count)],
        scratch=[pltpu.VMEM((48 * side, part), half_bytes), pltpu.VMEM((half, chans), jnp.float32)],
    )
    send, cot_full = lax.optimization_barrier((send, cot_full))
    got = [by_mask(v, m, count) for v, m in zip(send, masks[1:])]
    halos, packet = call(
        functools.partial(halo_kernel, side, part, len(near)),
        [vmem((block, part), half_bytes), vmem(packed_shape(rows + block, part), half_bytes)],
        [*near, halo_pick, field],
        scratch=[pltpu.VMEM((48 * side, part), half_bytes)],
    )
    other_field = lax.ppermute(packet, "ch", others)
    inner, pieces = call(
        functools.partial(back_kernel, side, part),
        [vmem((rows, part), jnp.float32), vmem(packed_shape(block, part), half_bytes)],
        [cot_full, taps],
        scratch=[pltpu.VMEM((rows + 4 * side, chans), half_bytes)],
        flops=flops,
    )
    got, pieces, inner, halos = lax.optimization_barrier((got, pieces, inner, halos))
    for index, bits in enumerate(stages[2:]):
        masks = group_masks(bits)
        size = held.shape[0] // len(masks)
        held, *send = call(
            functools.partial(sum_kernel, len(got), len(masks)),
            [vmem((size, chans), jnp.float32)] + [vmem((size, chans), half_bytes)] * (len(masks) - 1),
            [held, *got],
        )
        send, pieces = lax.optimization_barrier((send, pieces))
        got = [by_mask(v, m, count) for v, m in zip(send, masks[1:])]
        if index == 0:
            here = [pieces, by_offset(pieces, -SPAN, count), by_offset(pieces, SPAN, count)]
    (held,) = call(functools.partial(sum_kernel, len(got), 1), [vmem(held.shape, half_bytes)], [held, *got])
    order = [0]
    for index, bits in enumerate(stages[:0:-1]):
        masks = group_masks(bits)
        if index == 0:
            _, here, other_field = lax.optimization_barrier((held, here, other_field))
            (here,) = call(join_kernel, [vmem((3 * pieces.shape[0], pieces.shape[1]), half_bytes)], here)
            beside = by_mask(here, 2, count)
            (output,) = call(
                functools.partial(output_kernel, side, part),
                [vmem((rows, part), half_bytes)],
                [field, halos, other_field, taps],
                scratch=[
                    pltpu.VMEM((3, flat, part), half_bytes),
                    pltpu.VMEM((3, flat, part), half_bytes),
                    pltpu.VMEM((rows + block, part), half_bytes),
                ],
                flops=2 * flops,
            )
        got = [by_mask(held, m, count) for m in masks[1:]]
        if index == 0:
            held, got, output, beside = lax.optimization_barrier((held, got, output, beside))
        if index < len(stages) - 2:
            order = [m + v for m in masks for v in order]
            (held,) = call(
                join_kernel, [vmem((held.shape[0] * len(masks), chans), half_bytes)], [held, *got]
            )
            continue
        got_pieces = [here, beside, by_mask(here, 1, count), by_mask(beside, 1, count)]
        (grad_features,) = call(
            functools.partial(add_halo_kernel, side, part),
            [vmem((rows, part), half_bytes)],
            [place, inner, *got_pieces],
            scratch=[pltpu.VMEM((12 * block, part), half_bytes)],
        )
        got, grad_features = lax.optimization_barrier((got, grad_features))
        got = [held, *got]
        order = [[m + v for v in order] for m in masks]
    mates = [by_mask(v, 1, count) for v in got]
    whole = vmem((9 * part, chans), jnp.float32)
    early = len(got) - 1
    bits = [0] * early + [1] * early
    first = unfold(whole, chunk, bits, order[:-1] + order[:-1], got[:-1] + mates[:-1], None)
    grad_weight = unfold(whole, chunk, [0, 1], order[-1:] * 2, [got[-1], mates[-1]], first)
    shape = (1, side, side, part)
    return (
        output.reshape(shape),
        grad_features.reshape(shape),
        grad_weight.reshape(3, 3, part, chans),
    )


def solution(mesh):
    return jax.shard_map(
        body,
        mesh=mesh,
        in_specs=(
            P("tile", None, None, "ch"),
            P(),
            P("tile", None, None, "ch"),
            P(),
            P(),
            P(),
            P(),
        ),
        out_specs=(
            P("tile", None, None, "ch"),
            P("tile", None, None, "ch"),
            P(None, None, "ch", None),
        ),
        check_vma=False,
    )
```

```python
import functools
import math

import jax
import jax.numpy as jnp
import numpy as np
from jax import lax
from jax.experimental import pallas as pl
from jax.experimental.pallas import tpu as pltpu
from jax.sharding import PartitionSpec as P

SPAN = 4
EXTRA = 16
CUTS = 2


def turn_tables():
    labels = [[3 * row + col for col in range(3)] for row in range(3)]

    def turn_once(block):
        return [[block[col][2 - row] for col in range(3)] for row in range(3)]

    def sides_of(block):
        return [
            list(block[0]),
            [block[row][2] for row in range(3)],
            list(block[2]),
            [block[row][0] for row in range(3)],
        ]

    def corners_of(block):
        return [block[0][0], block[0][2], block[2][2], block[2][0]]

    base_sides = sides_of(labels)
    base_corners = corners_of(labels)
    edge_table = np.zeros((4, 4), np.int32)
    corner_table = np.zeros((4, 4), np.int32)
    for border in range(4):
        turned = labels
        for quarter in range(4):
            wanted = sides_of(turned)[(border + 2) % 4]
            for side_index in range(4):
                if base_sides[side_index] == wanted:
                    edge_table[border, quarter] = side_index
                if base_sides[side_index][::-1] == wanted:
                    edge_table[border, quarter] = side_index + 4
            corner_cell = corners_of(turned)[(border + 2) % 4]
            for corner_index in range(4):
                if base_corners[corner_index] == corner_cell:
                    corner_table[border, quarter] = corner_index
            turned = turn_once(turned)
    tables = np.concatenate([edge_table, corner_table], axis=0)
    return [sum(int(slot) << (3 * quarter) for quarter, slot in enumerate(row)) for row in tables]


def by_offset(value, offset, count):
    return lax.ppermute(value, "tile", [(i, (i + offset) % count) for i in range(count)])


def by_mask(value, mask, count):
    return lax.ppermute(value, "tile", [(i, i ^ mask) for i in range(count)])


def mask_stages(count):
    bits = [1 << b for b in range(count.bit_length() - 1)]
    stages = [bits[:1]]
    rest = bits[1:]
    while rest:
        stages.append(rest[:2])
        rest = rest[2:]
    return stages


def group_masks(bits):
    masks = [0]
    for bit in bits:
        masks = masks + [m + bit for m in masks]
    return masks


def slot_of_mask(mask, count):
    place = 0
    for bits in mask_stages(count)[1:]:
        size = 1 << len(bits)
        place = place * size + (mask // bits[0]) % size
    return place


def slot_in(row, quarter):
    return (row >> (3 * quarter)) & 7


def corner_spot(slot, side):
    return jnp.where(
        slot == 0, 0, jnp.where(slot == 1, side - 1, jnp.where(slot == 2, 3 * side - 1, 2 * side))
    )


def vmem(shape, dtype):
    return jax.ShapeDtypeStruct(shape, dtype)


def call(kernel, outs, args, anywhere=(), scratch=(), flops=0):
    in_specs = [
        pl.BlockSpec(memory_space=pltpu.HBM if i in anywhere else pltpu.VMEM) for i in range(len(args))
    ]
    size = sum(math.prod(x.shape) * x.dtype.itemsize for x in list(args) + list(outs))
    return pl.pallas_call(
        kernel,
        out_shape=tuple(outs),
        in_specs=in_specs,
        out_specs=tuple(pl.BlockSpec(memory_space=pltpu.VMEM) for _ in outs),
        scratch_shapes=list(scratch),
        compiler_params=pltpu.CompilerParams(vmem_limit_bytes=40 * 1024 * 1024),
        cost_estimate=pl.CostEstimate(flops=flops, bytes_accessed=size, transcendentals=0),
    )(*args)


def packed_shape(rows, part):
    if part % 128 != 64:
        return (rows, part)
    return (rows * (part // 128) + rows // 2, 128)


def pack(value, out_ref, first=0):
    rows, part = value.shape
    if part % 128 != 64:
        out_ref[first : first + rows, :] = value
        return
    for i in range(part // 128):
        out_ref[first + i * rows : first + (i + 1) * rows, :] = value[:, i * 128 : (i + 1) * 128]
    rest = value[:, part - 64 :]
    at = first + rows * (part // 128)
    out_ref[at : at + rows // 2, :] = jnp.concatenate([rest[: rows // 2], rest[rows // 2 :]], axis=1)


def unpack(ref, out_ref, first, row, rows, part):
    if part % 128 != 64:
        out_ref[row : row + rows, :] = ref[first : first + rows, :]
        return
    for i in range(part // 128):
        out_ref[row : row + rows, i * 128 : (i + 1) * 128] = ref[first + i * rows : first + (i + 1) * rows, :]
    at = first + rows * (part // 128)
    rest = ref[at : at + rows // 2, :]
    out_ref[row : row + rows // 2, part - 64 :] = rest[:, :64]
    out_ref[row + rows // 2 : row + rows, part - 64 :] = rest[:, 64:]


def sides_kernel(side, field_ref, sides_ref, copy_ref):
    sides = jnp.concatenate(
        [field_ref[0], field_ref[:, side - 1, :], field_ref[side - 1], field_ref[:, 0, :]], axis=0
    )
    pack(sides, sides_ref)
    copy_ref[...] = field_ref[...]


def shifted_columns(side, part, field, halos, out_ref):
    rows = side * side
    flat = rows + 2 * side
    column = lax.broadcasted_iota(jnp.int32, (flat, part), 0) % side
    if halos is None:
        none = jnp.zeros((side, part), jnp.float32)
        tall = jnp.concatenate([none, field.astype(jnp.float32), none], axis=0)
        west = east = 0.0
    else:
        edge = halos.astype(jnp.float32)
        tall = jnp.concatenate([edge[0:side], field.astype(jnp.float32), edge[2 * side : 3 * side]], axis=0)
        corner = [edge[4 * side + c : 4 * side + c + 1] for c in range(4)]
        spread = lambda col: jnp.broadcast_to(col[:, None, :], (side + 2, side, part)).reshape(flat, part)
        east = spread(jnp.concatenate([corner[1], edge[side : 2 * side], corner[2]], axis=0))
        west = spread(jnp.concatenate([corner[0], edge[3 * side : 4 * side], corner[3]], axis=0))
    out_ref[0] = jnp.where(column == 0, west, pltpu.roll(tall, 1, 0)).astype(jnp.bfloat16)
    out_ref[1] = tall.astype(jnp.bfloat16)
    out_ref[2] = jnp.where(column == side - 1, east, pltpu.roll(tall, flat - 1, 0)).astype(jnp.bfloat16)


def onehot_kernel(side, tables_in, cot_in, border_ref, halo_ref, place_ref, cot_ref, tables, sem):
    copy = pltpu.make_async_copy(tables_in, tables, sem)
    copy.start()
    cot_ref[...] = cot_in[...]
    copy.wait()
    et, eu, ct, cu = [tables.at[4 * i : 4 * i + 4] for i in range(4)]
    digits = turn_tables()
    count = lax.axis_size("tile")
    own = lax.axis_index("tile")
    core = lax.rem(own, 2)
    groups = count // SPAN

    def base(source):
        slab = lax.rem(source // SPAN - own // SPAN + groups, groups)
        cross = source ^ own
        turn = lax.rem(cross // 2, 2)
        at = jnp.where(slab == 0, turn, jnp.where(slab == 1, 2, 3) + 2 * turn)
        return (6 * lax.rem(cross, 2) + at) * (4 * side)

    step = lax.broadcasted_iota(jnp.int32, (side, 1), 0)
    nothing = jnp.full((side, 1), -1, jnp.int32)

    def halo(tile, e):
        slot = slot_in(digits[e], eu[e, tile])
        start = base(et[e, tile]) + lax.rem(slot, 4) * side
        return lambda at: jnp.where(slot >= 4, start + side - 1 - at, start + at)

    def corner(tile, c):
        return base(ct[c, tile]) + corner_spot(slot_in(digits[4 + c], cu[c, tile]), side)

    def onehot(wanted, width):
        lane = lax.broadcasted_iota(jnp.int32, (wanted.shape[0], width), 1)
        return jnp.where(lane == wanted, 1.0, 0.0).astype(jnp.bfloat16)

    width = 12 * 4 * side
    pieces = [[] for _ in range(4)]
    for tile in (own, own ^ 1):
        top, right, bottom, left = [halo(tile, e) for e in range(4)]
        corners = [corner(tile, c) for c in range(4)]
        low = core == 0
        row = lambda at: jnp.where(low, top(at), bottom(at))
        first = jnp.where(low, corners[0], corners[3])
        last = jnp.where(low, corners[1], corners[2])
        along = jnp.where(low, step - 1, step + 1)
        fits = (along >= 0) & (along < side)
        pieces[0] += [jnp.where(step == 0, first, row(step - 1)), jnp.where(fits, left(along), nothing)]
        pieces[1] += [row(step), nothing]
        pieces[2] += [jnp.where(step == side - 1, last, row(step + 1)), jnp.where(fits, right(along), nothing)]
        pieces[3] += [nothing, jnp.where(low, left(step), right(step))]
    border_ref[...] = onehot(jnp.concatenate(sum(pieces, []), axis=0), width)
    spots = lax.broadcasted_iota(jnp.int32, (EXTRA, 1), 0)
    ends = jnp.full((EXTRA, 1), -1, jnp.int32)
    for c in range(4):
        ends = jnp.where(spots == c, corner(own, c), ends)
    halo_ref[...] = onehot(jnp.concatenate([halo(own, e)(step) for e in range(4)] + [ends], axis=0), width)

    block = 4 * side + EXTRA
    lane = lax.broadcasted_iota(jnp.int32, (1, block), 1)
    row = lax.broadcasted_iota(jnp.int32, (4 * side, block), 0)
    places = []
    for mask in (0, 2, 1, 3):
        for offset in (0, SPAN, -SPAN):
            source = lax.rem((own ^ mask) + offset + count, count)
            target = jnp.full((1, block), -1, jnp.int32)
            for e in range(4):
                slot = slot_in(digits[e], eu[e, source])
                along = lane - e * side
                along = jnp.where(slot >= 4, side - 1 - along, along)
                hit = (lane >= e * side) & (lane < (e + 1) * side) & (et[e, source] == own)
                target = jnp.where(hit, lax.rem(slot, 4) * side + along, target)
                spot = corner_spot(slot_in(digits[4 + e], cu[e, source]), side)
                hit = (lane == 4 * side + e) & (ct[e, source] == own)
                target = jnp.where(hit, spot, target)
            places.append(jnp.where(row == target, 1.0, 0.0))
    place_ref[...] = jnp.concatenate(places, axis=1).astype(jnp.bfloat16)


def half_taps(side, part, half, scale, which, cols, cot, out_ref, middle):
    rows = side * side
    used = 9 * part // 2

    def product(a, b):
        value = lax.dot_general(
            cols[b, pl.ds(pl.multiple_of(a * side, 16), rows), :],
            cot,
            (((0,), (0,)), ((), ())),
            preferred_element_type=jnp.float32,
        )
        return value * scale

    for j in range(4):
        tap = j + 5 * which
        start = pl.multiple_of(which * (part // 2) + j * part, 16)
        out_ref[pl.ds(start, part), :] = product(tap // 3, lax.rem(tap, 3))
    middle[...] = product(1, 1)
    start = pl.multiple_of((1 - which) * 4 * part, 16)
    out_ref[pl.ds(start, part // 2), :] = middle[pl.ds(pl.multiple_of(which * (part // 2), 16), part // 2), :]
    out_ref[used:, :] = jnp.zeros((half - used, cot.shape[1]), jnp.float32)


def send_kernel(side, part, half, scale, field_ref, own_ref, other_ref, *refs):
    send_refs, (cot_ref, rim_ref, cols, middle, send) = refs[:CUTS], refs[CUTS:]
    rows = side * side
    chans = cot_ref.shape[1]
    first = lax.axis_index("ch") == 0

    @pl.when(first)
    def _():
        cot_ref[:, 0:part] = own_ref[...]
        cot_ref[:, part:] = other_ref[...]

    @pl.when(jnp.logical_not(first))
    def _():
        cot_ref[:, 0:part] = other_ref[...]
        cot_ref[:, part:] = own_ref[...]

    shifted_columns(side, part, field_ref[...].reshape(rows, part), None, cols)
    cot = cot_ref[...]
    rim_ref[...] = jnp.concatenate(
        [
            cot[0:side],
            cot[rows - side :],
            cot.reshape(side, side, chans)[:, 0, :],
            cot.reshape(side, side, chans)[:, side - 1, :],
        ],
        axis=0,
    )
    which = 1 - lax.rem(lax.axis_index("tile"), 2)
    half_taps(side, part, half, scale, which, cols, cot, send, middle)
    for i, ref in enumerate(send_refs):
        ref[...] = send[i * (half // CUTS) : (i + 1) * (half // CUTS), :]


def mine_kernel(side, part, half, scale, cols, cot_ref, mine_ref, middle):
    which = lax.rem(lax.axis_index("tile"), 2)
    half_taps(side, part, half, scale, which, cols, cot_ref[...], mine_ref, middle)


def unpack_near(near_refs, near, side, part):
    size = packed_shape(4 * side, part)[0]
    row = 0
    for ref in near_refs:
        for k in range(ref.shape[0] // size):
            unpack(ref, near, k * size, row, 4 * side, part)
            row += 4 * side


def border_kernel(side, part, chunk, scale, n_near, *refs):
    near_refs = refs[:n_near]
    onehot_ref, mine_ref, rim_ref, mate_ref = refs[n_near : n_near + 4]
    got_refs = refs[n_near + 4 : n_near + 4 + CUTS]
    outs, near, total = refs[n_near + 4 + CUTS : -2], refs[-2], refs[-1]
    count = lax.axis_size("tile")
    own = lax.axis_index("tile")
    core = lax.rem(own, 2)
    unpack_near(near_refs, near, side, part)
    for i, ref in enumerate(got_refs):
        here = slice(i * ref.shape[0], (i + 1) * ref.shape[0])
        total[here, :] = mine_ref[here, :] + ref[...]
    left = jnp.dot(onehot_ref[...], near[...], preferred_element_type=jnp.float32).astype(jnp.bfloat16)

    def rim(ref, at):
        return ref[pl.ds(pl.multiple_of(at, 16), side), :]

    for q in range(4):
        column = (2 + q // 2) * side if q < 3 else (2 + core) * side
        right = jnp.concatenate(
            [value for ref in (rim_ref, mate_ref) for value in (rim(ref, core * side), rim(ref, column))],
            axis=0,
        )
        value = lax.dot_general(
            left[q * 4 * side : (q + 1) * 4 * side],
            right,
            (((0,), (0,)), ((), ())),
            preferred_element_type=jnp.float32,
        )
        if q < 3:
            start = q * part + core * (part // 2 + part)
        else:
            start = 3 * part - core * (3 * part - part // 2)
        here = pl.ds(pl.multiple_of(start, 16), part)
        total[here, :] = total[here, :] + value * scale
    size = outs[0].shape[0]
    for index in range(count // 2):
        to = slot_of_mask(2 * index, count) * chunk
        block = pl.multiple_of(((own // 2) ^ index) * chunk, 16)
        out = outs[to // size]
        out[to % size : to % size + chunk, :] = total[pl.ds(block, chunk), :].astype(out.dtype)


def sum_kernel(n_got, n_out, *refs):
    held_ref, got_refs, outs = refs[0], refs[1 : 1 + n_got], refs[1 + n_got :]
    size = held_ref.shape[0] // n_out
    for index in range(n_out):
        here = slice(index * size, (index + 1) * size)
        value = held_ref[here, :]
        for ref in got_refs:
            value = value + ref[here, :].astype(jnp.float32)
        outs[index][...] = value.astype(outs[index].dtype)


def join_kernel(*refs):
    row = 0
    for ref in refs[:-1]:
        refs[-1][row : row + ref.shape[0], :] = ref[...]
        row += ref.shape[0]


def unfold_kernel(used, chunk, bits, masks, n_dep, *refs):
    refs = refs[n_dep:]
    n = len(masks)
    in_refs, out_ref, wide, sems = refs[:n], refs[n], refs[n + 1], refs[n + 2]
    own = lax.axis_index("tile")
    full, rest = used // chunk, used % chunk
    copies = []
    for i, (ref, inner, bit) in enumerate(zip(in_refs, masks, bits)):
        origin = (lax.rem(own, 2) ^ bit) * used
        for k, mask in enumerate(inner):
            at = i * len(inner) + k
            wide[at] = ref[k * chunk : (k + 1) * chunk, :].astype(jnp.float32)
            block = (own ^ mask) // 2
            start = pl.multiple_of(origin + block * chunk, 16)
            copies.append(
                (
                    block < full,
                    pltpu.make_async_copy(wide.at[at], out_ref.at[pl.ds(start, chunk), :], sems.at[at]),
                )
            )
            if rest:
                start = pl.multiple_of(origin + full * chunk, 16)
                copies.append(
                    (
                        block == full,
                        pltpu.make_async_copy(
                            wide.at[at, 0:rest], out_ref.at[pl.ds(start, rest), :], sems.at[at]
                        ),
                    )
                )
    for going, copy in copies:
        pl.when(going)(copy.start)
    for going, copy in copies:
        pl.when(going)(copy.wait)


def unfold(whole, chunk, bits, masks, blocks, before):
    n_dep = 0 if before is None else 1
    anywhere = pl.BlockSpec(memory_space=pl.ANY)
    n_copies = len(masks) * len(masks[0])
    return pl.pallas_call(
        functools.partial(unfold_kernel, whole.shape[0] // 2, chunk, bits, masks, n_dep),
        out_shape=whole,
        in_specs=[anywhere] * n_dep + [pl.BlockSpec(memory_space=pltpu.VMEM)] * len(blocks),
        out_specs=anywhere,
        scratch_shapes=[
            pltpu.VMEM((n_copies, chunk, whole.shape[1]), jnp.float32),
            pltpu.SemaphoreType.DMA((n_copies,)),
        ],
        input_output_aliases={0: 0} if n_dep else {},
        compiler_params=pltpu.CompilerParams(vmem_limit_bytes=40 * 1024 * 1024),
    )(*([before] if n_dep else []), *blocks)


def back_kernel(side, part, cot_ref, weight_ref, inner_ref, pieces_ref, tall):
    rows = side * side
    flat = rows + 2 * side
    start = pl.multiple_of(lax.axis_index("ch") * part, 16)
    blank = jnp.zeros((2 * side, tall.shape[1]), jnp.bfloat16)
    tall[0 : 2 * side, :] = blank
    tall[2 * side : 2 * side + rows, :] = cot_ref[...]
    tall[2 * side + rows :, :] = blank
    backs = []
    for b in range(3):
        back = jnp.zeros((flat, part), jnp.float32)
        for a in range(3):
            back = back + lax.dot_general(
                tall[(2 - a) * side : (2 - a) * side + flat, :],
                weight_ref[3 * a + b, pl.ds(start, part), :],
                (((1,), (1,)), ((), ())),
                preferred_element_type=jnp.float32,
            )
        backs.append(back)
    column = lax.broadcasted_iota(jnp.int32, (flat, part), 0) % side
    inner = (
        jnp.where(column == side - 1, 0.0, pltpu.roll(backs[0], flat - 1, 0))
        + backs[1]
        + jnp.where(column == 0, 0.0, pltpu.roll(backs[2], 1, 0))
    )
    inner_ref[...] = inner[side : side + rows]
    west = backs[0].reshape(side + 2, side, part)[:, 0, :]
    east = backs[2].reshape(side + 2, side, part)[:, side - 1, :]
    pieces = jnp.concatenate(
        [
            inner[0:side],
            east[1 : side + 1],
            inner[side + rows :],
            west[1 : side + 1],
            west[0:1],
            east[0:1],
            east[side + 1 :],
            west[side + 1 :],
            jnp.zeros((EXTRA - 4, part), jnp.float32),
        ],
        axis=0,
    )
    pack(pieces.astype(jnp.bfloat16), pieces_ref)


def add_halo_kernel(side, part, place_ref, inner_ref, *refs):
    got_refs, out_ref, got = refs[:-2], refs[-2], refs[-1]
    block = 4 * side + EXTRA
    size = packed_shape(block, part)[0]
    for i, ref in enumerate(got_refs):
        for k in range(3):
            unpack(ref, got, k * size, (3 * i + k) * block, block, part)
    sums = jnp.dot(place_ref[...], got[...], preferred_element_type=jnp.float32)
    rows = side * side
    spread = lambda col: jnp.broadcast_to(col[:, None, :], (side, side, part)).reshape(rows, part)
    column = lax.broadcasted_iota(jnp.int32, (rows, part), 0) % side
    inner = inner_ref[...]
    inner = inner + jnp.where(column == side - 1, spread(sums[side : 2 * side]), 0.0)
    inner = inner + jnp.where(column == 0, spread(sums[3 * side :]), 0.0)
    ends = jnp.concatenate(
        [
            inner[0:side] + sums[0:side],
            inner[side : rows - side],
            inner[rows - side :] + sums[2 * side : 3 * side],
        ],
        axis=0,
    )
    out_ref[...] = ends.astype(jnp.bfloat16)


def halo_kernel(side, part, n_near, *refs):
    near_refs, onehot_ref, field_ref = refs[:n_near], refs[n_near], refs[n_near + 1]
    halos_ref, packet_ref, near = refs[n_near + 2 :]
    rows = side * side
    unpack_near(near_refs, near, side, part)
    halos = jnp.dot(onehot_ref[...], near[...], preferred_element_type=jnp.float32).astype(jnp.bfloat16)
    halos_ref[...] = halos
    pack(field_ref[...].reshape(rows, part), packet_ref)
    pack(halos, packet_ref, packed_shape(rows, part)[0])


def output_kernel(side, part, field_ref, halos_ref, other_ref, weight_ref, out_ref, cols, other_cols, other):
    rows = side * side
    ch = lax.axis_index("ch")
    wide = -(-part // 128) * 128
    lanes = pl.multiple_of(ch * (weight_ref.shape[2] - wide), 128)
    unpack(other_ref, other, 0, 0, rows, part)
    unpack(other_ref, other, packed_shape(rows, part)[0], rows, 4 * side + EXTRA, part)
    shifted_columns(side, part, field_ref[...].reshape(rows, part), halos_ref[...], cols)
    shifted_columns(side, part, other[0:rows, :], other[rows:, :], other_cols)
    starts = (pl.multiple_of(ch * part, 16), pl.multiple_of((1 - ch) * part, 16))
    total = jnp.zeros((rows, wide), jnp.float32)
    for a in range(3):
        for b in range(3):
            for ref, first in zip((cols, other_cols), starts):
                total = total + jnp.dot(
                    ref[b, a * side : a * side + rows, :],
                    weight_ref[3 * a + b, pl.ds(first, part), pl.ds(lanes, wide)],
                    preferred_element_type=jnp.float32,
                )
    result = jnp.where(ch == 0, total[:, :part], total[:, wide - part :])
    out_ref[...] = result.astype(jnp.bfloat16)


def body(features, weight, cotangent, edge_tiles, edge_turns, corner_tiles, corner_turns):
    count = lax.axis_size("tile")
    field = features[0]
    side, part = field.shape[0], field.shape[2]
    chans = weight.shape[3]
    rows = side * side
    flat = rows + 2 * side
    block = 4 * side + EXTRA
    taps = weight.reshape(9, chans, chans)
    others = [(0, 1), (1, 0)]
    flops = 2 * rows * 9 * part * chans
    half_bytes = jnp.bfloat16
    chunk = -(-9 * part // (16 * count)) * 16
    half = count * chunk // 2
    scale = 1.0 / math.sqrt(count * rows)

    cot_own = cotangent[0].reshape(rows, part)
    cot_other = lax.ppermute(cot_own, "ch", others)
    sides, field = call(
        functools.partial(sides_kernel, side),
        [vmem(packed_shape(4 * side, part), half_bytes), vmem(field.shape, half_bytes)],
        [field],
    )
    ahead, behind = by_offset(sides, -SPAN, count), by_offset(sides, SPAN, count)
    across = by_mask(sides, 2, count)
    tables = jnp.concatenate([edge_tiles.T, edge_turns.T, corner_tiles.T, corner_turns.T], axis=0)
    border_pick, halo_pick, place, cot_own = call(
        functools.partial(onehot_kernel, side),
        [
            vmem((16 * side, 48 * side), half_bytes),
            vmem((block, 48 * side), half_bytes),
            vmem((4 * side, 12 * block), half_bytes),
            vmem((rows, part), half_bytes),
        ],
        [tables, cot_own],
        scratch=[pltpu.SMEM(tables.shape, jnp.int32), pltpu.SemaphoreType.DMA],
    )
    pair = packed_shape(8 * side, part)
    (beyond,) = call(join_kernel, [vmem(pair, half_bytes)], [ahead, behind])
    near = [sides, across, ahead, behind, by_mask(beyond, 2, count)]
    near, cot_other, border_pick = lax.optimization_barrier((near, cot_other, border_pick))
    (near,) = call(join_kernel, [vmem(packed_shape(24 * side, part), half_bytes)], near)
    mates = by_mask(near, 1, count)
    *send, cot_full, rim, cols = call(
        functools.partial(send_kernel, side, part, half, scale),
        [
            *[vmem((half // CUTS, chans), jnp.float32)] * CUTS,
            vmem((rows, chans), half_bytes),
            vmem((4 * side, chans), half_bytes),
            vmem((3, flat, part), half_bytes),
        ],
        [field, cot_own, cot_other],
        scratch=[pltpu.VMEM((part, chans), jnp.float32), pltpu.VMEM((half, chans), jnp.float32)],
        flops=flops // 2,
    )
    (mine,) = call(
        functools.partial(mine_kernel, side, part, half, scale),
        [vmem((half, chans), jnp.float32)],
        [cols, cot_full],
        scratch=[pltpu.VMEM((part, chans), jnp.float32)],
        flops=flops // 2,
    )

    mates, mine, rim_mate = lax.optimization_barrier((mates, mine, by_mask(rim, 1, count)))
    near = [near, mates]

    stages = mask_stages(count)
    masks = group_masks(stages[1])
    size = half // len(masks)
    held, *send = call(
        functools.partial(border_kernel, side, part, chunk, scale, len(near)),
        [vmem((size, chans), jnp.float32)] + [vmem((size, chans), half_bytes)] * (len(masks) - 1),
        [*near, border_pick, mine, rim, rim_mate, *[by_mask(v, 1, count) for v in send]],
        scratch=[pltpu.VMEM((48 * side, part), half_bytes), pltpu.VMEM((half, chans), jnp.float32)],
    )
    send, cot_full = lax.optimization_barrier((send, cot_full))
    got = [by_mask(v, m, count) for v, m in zip(send, masks[1:])]
    halos, packet = call(
        functools.partial(halo_kernel, side, part, len(near)),
        [vmem((block, part), half_bytes), vmem(packed_shape(rows + block, part), half_bytes)],
        [*near, halo_pick, field],
        scratch=[pltpu.VMEM((48 * side, part), half_bytes)],
    )
    other_field = lax.ppermute(packet, "ch", others)
    inner, pieces = call(
        functools.partial(back_kernel, side, part),
        [vmem((rows, part), jnp.float32), vmem(packed_shape(block, part), half_bytes)],
        [cot_full, taps],
        scratch=[pltpu.VMEM((rows + 4 * side, chans), half_bytes)],
        flops=flops,
    )
    got, pieces, inner, halos = lax.optimization_barrier((got, pieces, inner, halos))
    for index, bits in enumerate(stages[2:]):
        masks = group_masks(bits)
        size = held.shape[0] // len(masks)
        held, *send = call(
            functools.partial(sum_kernel, len(got), len(masks)),
            [vmem((size, chans), jnp.float32)] + [vmem((size, chans), half_bytes)] * (len(masks) - 1),
            [held, *got],
        )
        send, pieces = lax.optimization_barrier((send, pieces))
        got = [by_mask(v, m, count) for v, m in zip(send, masks[1:])]
        if index == 0:
            here = [pieces, by_offset(pieces, -SPAN, count), by_offset(pieces, SPAN, count)]
    (held,) = call(functools.partial(sum_kernel, len(got), 1), [vmem(held.shape, half_bytes)], [held, *got])
    order = [0]
    for index, bits in enumerate(stages[:0:-1]):
        masks = group_masks(bits)
        if index == 0:
            _, here, other_field = lax.optimization_barrier((held, here, other_field))
            (here,) = call(join_kernel, [vmem((3 * pieces.shape[0], pieces.shape[1]), half_bytes)], here)
            beside = by_mask(here, 2, count)
            (output,) = call(
                functools.partial(output_kernel, side, part),
                [vmem((rows, part), half_bytes)],
                [field, halos, other_field, taps],
                scratch=[
                    pltpu.VMEM((3, flat, part), half_bytes),
                    pltpu.VMEM((3, flat, part), half_bytes),
                    pltpu.VMEM((rows + block, part), half_bytes),
                ],
                flops=2 * flops,
            )
        got = [by_mask(held, m, count) for m in masks[1:]]
        if index == 0:
            held, got, output, beside = lax.optimization_barrier((held, got, output, beside))
        if index < len(stages) - 2:
            order = [m + v for m in masks for v in order]
            (held,) = call(
                join_kernel, [vmem((held.shape[0] * len(masks), chans), half_bytes)], [held, *got]
            )
            continue
        got_pieces = [here, beside, by_mask(here, 1, count), by_mask(beside, 1, count)]
        (grad_features,) = call(
            functools.partial(add_halo_kernel, side, part),
            [vmem((rows, part), half_bytes)],
            [place, inner, *got_pieces],
            scratch=[pltpu.VMEM((12 * block, part), half_bytes)],
        )
        got, grad_features = lax.optimization_barrier((got, grad_features))
        got = [held, *got]
        order = [[m + v for v in order] for m in masks]
    mates = [by_mask(v, 1, count) for v in got]
    whole = vmem((9 * part, chans), jnp.float32)
    early = len(got) - 1
    bits = [0] * early + [1] * early
    first = unfold(whole, chunk, bits, order[:-1] + order[:-1], got[:-1] + mates[:-1], None)
    grad_weight = unfold(whole, chunk, [0, 1], order[-1:] * 2, [got[-1], mates[-1]], first)
    shape = (1, side, side, part)
    return (
        output.reshape(shape),
        grad_features.reshape(shape),
        grad_weight.reshape(3, 3, part, chans),
    )


def solution(mesh):
    return jax.shard_map(
        body,
        mesh=mesh,
        in_specs=(
            P("tile", None, None, "ch"),
            P(),
            P("tile", None, None, "ch"),
            P(),
            P(),
            P(),
            P(),
        ),
        out_specs=(
            P("tile", None, None, "ch"),
            P("tile", None, None, "ch"),
            P(None, None, "ch", None),
        ),
        check_vma=False,
    )
```

```python
import functools
import math

import jax
import jax.numpy as jnp
import numpy as np
from jax import lax
from jax.experimental import pallas as pl
from jax.experimental.pallas import tpu as pltpu
from jax.sharding import PartitionSpec as P

SPAN = 4
EXTRA = 16
CUTS = 2


def turn_tables():
    labels = [[3 * row + col for col in range(3)] for row in range(3)]

    def turn_once(block):
        return [[block[col][2 - row] for col in range(3)] for row in range(3)]

    def sides_of(block):
        return [
            list(block[0]),
            [block[row][2] for row in range(3)],
            list(block[2]),
            [block[row][0] for row in range(3)],
        ]

    def corners_of(block):
        return [block[0][0], block[0][2], block[2][2], block[2][0]]

    base_sides = sides_of(labels)
    base_corners = corners_of(labels)
    edge_table = np.zeros((4, 4), np.int32)
    corner_table = np.zeros((4, 4), np.int32)
    for border in range(4):
        turned = labels
        for quarter in range(4):
            wanted = sides_of(turned)[(border + 2) % 4]
            for side_index in range(4):
                if base_sides[side_index] == wanted:
                    edge_table[border, quarter] = side_index
                if base_sides[side_index][::-1] == wanted:
                    edge_table[border, quarter] = side_index + 4
            corner_cell = corners_of(turned)[(border + 2) % 4]
            for corner_index in range(4):
                if base_corners[corner_index] == corner_cell:
                    corner_table[border, quarter] = corner_index
            turned = turn_once(turned)
    tables = np.concatenate([edge_table, corner_table], axis=0)
    return [sum(int(slot) << (3 * quarter) for quarter, slot in enumerate(row)) for row in tables]


def by_offset(value, offset, count):
    return lax.ppermute(value, "tile", [(i, (i + offset) % count) for i in range(count)])


def by_mask(value, mask, count):
    return lax.ppermute(value, "tile", [(i, i ^ mask) for i in range(count)])


def mask_stages(count):
    bits = [1 << b for b in range(count.bit_length() - 1)]
    stages = [bits[:1]]
    rest = bits[1:]
    while rest:
        stages.append(rest[:2])
        rest = rest[2:]
    return stages


def group_masks(bits):
    masks = [0]
    for bit in bits:
        masks = masks + [m + bit for m in masks]
    return masks


def slot_of_mask(mask, count):
    place = 0
    for bits in mask_stages(count)[1:]:
        size = 1 << len(bits)
        place = place * size + (mask // bits[0]) % size
    return place


def slot_in(row, quarter):
    return (row >> (3 * quarter)) & 7


def corner_spot(slot, side):
    return jnp.where(
        slot == 0, 0, jnp.where(slot == 1, side - 1, jnp.where(slot == 2, 3 * side - 1, 2 * side))
    )


def vmem(shape, dtype):
    return jax.ShapeDtypeStruct(shape, dtype)


def call(kernel, outs, args, anywhere=(), scratch=(), flops=0):
    in_specs = [
        pl.BlockSpec(memory_space=pltpu.HBM if i in anywhere else pltpu.VMEM) for i in range(len(args))
    ]
    size = sum(math.prod(x.shape) * x.dtype.itemsize for x in list(args) + list(outs))
    return pl.pallas_call(
        kernel,
        out_shape=tuple(outs),
        in_specs=in_specs,
        out_specs=tuple(pl.BlockSpec(memory_space=pltpu.VMEM) for _ in outs),
        scratch_shapes=list(scratch),
        compiler_params=pltpu.CompilerParams(vmem_limit_bytes=40 * 1024 * 1024),
        cost_estimate=pl.CostEstimate(flops=flops, bytes_accessed=size, transcendentals=0),
    )(*args)


def packed_shape(rows, part):
    if part % 128 != 64:
        return (rows, part)
    return (rows * (part // 128) + rows // 2, 128)


def pack(value, out_ref, first=0):
    rows, part = value.shape
    if part % 128 != 64:
        out_ref[first : first + rows, :] = value
        return
    for i in range(part // 128):
        out_ref[first + i * rows : first + (i + 1) * rows, :] = value[:, i * 128 : (i + 1) * 128]
    rest = value[:, part - 64 :]
    at = first + rows * (part // 128)
    out_ref[at : at + rows // 2, :] = jnp.concatenate([rest[: rows // 2], rest[rows // 2 :]], axis=1)


def unpack(ref, out_ref, first, row, rows, part):
    if part % 128 != 64:
        out_ref[row : row + rows, :] = ref[first : first + rows, :]
        return
    for i in range(part // 128):
        out_ref[row : row + rows, i * 128 : (i + 1) * 128] = ref[first + i * rows : first + (i + 1) * rows, :]
    at = first + rows * (part // 128)
    rest = ref[at : at + rows // 2, :]
    out_ref[row : row + rows // 2, part - 64 :] = rest[:, :64]
    out_ref[row + rows // 2 : row + rows, part - 64 :] = rest[:, 64:]


def sides_kernel(side, field_ref, sides_ref, copy_ref):
    sides = jnp.concatenate(
        [field_ref[0], field_ref[:, side - 1, :], field_ref[side - 1], field_ref[:, 0, :]], axis=0
    )
    pack(sides, sides_ref)
    copy_ref[...] = field_ref[...]


def shifted_columns(side, part, field, halos, out_ref):
    rows = side * side
    flat = rows + 2 * side
    column = lax.broadcasted_iota(jnp.int32, (flat, part), 0) % side
    if halos is None:
        none = jnp.zeros((side, part), jnp.float32)
        tall = jnp.concatenate([none, field.astype(jnp.float32), none], axis=0)
        west = east = 0.0
    else:
        edge = halos.astype(jnp.float32)
        tall = jnp.concatenate([edge[0:side], field.astype(jnp.float32), edge[2 * side : 3 * side]], axis=0)
        corner = [edge[4 * side + c : 4 * side + c + 1] for c in range(4)]
        spread = lambda col: jnp.broadcast_to(col[:, None, :], (side + 2, side, part)).reshape(flat, part)
        east = spread(jnp.concatenate([corner[1], edge[side : 2 * side], corner[2]], axis=0))
        west = spread(jnp.concatenate([corner[0], edge[3 * side : 4 * side], corner[3]], axis=0))
    out_ref[0] = jnp.where(column == 0, west, pltpu.roll(tall, 1, 0)).astype(jnp.bfloat16)
    out_ref[1] = tall.astype(jnp.bfloat16)
    out_ref[2] = jnp.where(column == side - 1, east, pltpu.roll(tall, flat - 1, 0)).astype(jnp.bfloat16)


class Neighbours:
    def __init__(self, side, tables):
        self.side = side
        self.et, self.eu, self.ct, self.cu = [tables.at[4 * i : 4 * i + 4] for i in range(4)]
        self.digits = turn_tables()
        self.count = lax.axis_size("tile")
        self.own = lax.axis_index("tile")

    def block(self, source):
        groups = self.count // SPAN
        slab = lax.rem(source // SPAN - self.own // SPAN + groups, groups)
        cross = source ^ self.own
        turn = lax.rem(cross // 2, 2)
        at = jnp.where(slab == 0, turn, jnp.where(slab == 1, 2, 3) + 2 * turn)
        return 6 * lax.rem(cross, 2) + at

    def edge(self, tile, e):
        slot = slot_in(self.digits[e], self.eu[e, tile])
        start = lax.rem(slot, 4) * self.side
        end = start + self.side - 1
        return self.block(self.et[e, tile]), lambda at: jnp.where(slot >= 4, end - at, start + at)

    def corner(self, tile, c):
        slot = slot_in(self.digits[4 + c], self.cu[c, tile])
        return self.block(self.ct[c, tile]), corner_spot(slot, self.side)


def onehot(wanted, width):
    lane = lax.broadcasted_iota(jnp.int32, (wanted.shape[0], width), 1)
    return jnp.where(lane == wanted, 1.0, 0.0).astype(jnp.bfloat16)


def border_onehot_kernel(side, tables_in, cot_in, border_ref, cot_ref, tables, sem):
    copy = pltpu.make_async_copy(tables_in, tables, sem)
    copy.start()
    cot_ref[...] = cot_in[...]
    border_ref[...] = jnp.zeros_like(border_ref)
    copy.wait()
    near = Neighbours(side, tables)
    low = lax.rem(near.own, 2) == 0
    width = 4 * side
    step = lax.broadcasted_iota(jnp.int32, (side, 1), 0)

    def put(row, block, wanted, add=False):
        here = (slice(row, row + side), pl.ds(pl.multiple_of(block * width, 128), width))
        value = onehot(wanted, width)
        border_ref[here] = border_ref[here] + value if add else value

    for m, tile in enumerate((near.own, near.own ^ 1)):
        first = 2 * m * side
        flat = [near.edge(tile, e) for e in range(4)]
        corners = [near.corner(tile, c) for c in range(4)]
        pick = lambda a, b: (jnp.where(low, a[0], b[0]), lambda at: jnp.where(low, a[1](at), b[1](at)))
        block, at = pick(flat[0], flat[2])
        left, right = [
            (jnp.where(low, corners[a][0], corners[b][0]), jnp.where(low, corners[a][1], corners[b][1]))
            for a, b in ((0, 3), (1, 2))
        ]
        along = jnp.where(low, step - 1, step + 1)
        fits = (along >= 0) & (along < side)
        put(first, block, jnp.where(step == 0, -1, at(step - 1)))
        put(first, left[0], jnp.where(step == 0, left[1], -1), add=True)
        put(first + side, flat[3][0], jnp.where(fits, flat[3][1](along), -1))
        put(first + 4 * side, block, at(step))
        put(first + 8 * side, block, jnp.where(step == side - 1, -1, at(step + 1)))
        put(first + 8 * side, right[0], jnp.where(step == side - 1, right[1], -1), add=True)
        put(first + 9 * side, flat[1][0], jnp.where(fits, flat[1][1](along), -1))
        block, at = pick(flat[3], flat[1])
        put(first + 13 * side, block, at(step))


def place_kernel(side, tables_in, place_ref, tables, sem):
    copy = pltpu.make_async_copy(tables_in, tables, sem)
    copy.start()
    copy.wait()
    near = Neighbours(side, tables)
    block = 4 * side + EXTRA
    lane = lax.broadcasted_iota(jnp.int32, (1, block), 1)
    row = lax.broadcasted_iota(jnp.int32, (4 * side, block), 0)
    places = []
    for mask in (0, 2, 1, 3):
        for offset in (0, SPAN, -SPAN):
            source = lax.rem((near.own ^ mask) + offset + near.count, near.count)
            target = jnp.full((1, block), -1, jnp.int32)
            for e in range(4):
                slot = slot_in(near.digits[e], near.eu[e, source])
                along = lane - e * side
                along = jnp.where(slot >= 4, side - 1 - along, along)
                hit = (lane >= e * side) & (lane < (e + 1) * side) & (near.et[e, source] == near.own)
                target = jnp.where(hit, lax.rem(slot, 4) * side + along, target)
                spot = corner_spot(slot_in(near.digits[4 + e], near.cu[e, source]), side)
                hit = (lane == 4 * side + e) & (near.ct[e, source] == near.own)
                target = jnp.where(hit, spot, target)
            places.append(jnp.where(row == target, 1.0, 0.0))
    place_ref[...] = jnp.concatenate(places, axis=1).astype(jnp.bfloat16)


def half_taps(side, part, half, scale, which, cols, cot, out_ref, middle):
    rows = side * side
    used = 9 * part // 2

    def product(a, b):
        value = lax.dot_general(
            cols[b, pl.ds(pl.multiple_of(a * side, 16), rows), :],
            cot,
            (((0,), (0,)), ((), ())),
            preferred_element_type=jnp.float32,
        )
        return value * scale

    for j in range(4):
        tap = j + 5 * which
        start = pl.multiple_of(which * (part // 2) + j * part, 16)
        out_ref[pl.ds(start, part), :] = product(tap // 3, lax.rem(tap, 3))
    middle[...] = product(1, 1)
    start = pl.multiple_of((1 - which) * 4 * part, 16)
    out_ref[pl.ds(start, part // 2), :] = middle[pl.ds(pl.multiple_of(which * (part // 2), 16), part // 2), :]
    out_ref[used:, :] = jnp.zeros((half - used, cot.shape[1]), jnp.float32)


def send_kernel(side, part, half, scale, field_ref, own_ref, other_ref, *refs):
    send_refs, (cot_ref, rim_ref, cols, middle, send) = refs[:CUTS], refs[CUTS:]
    rows = side * side
    chans = cot_ref.shape[1]
    first = lax.axis_index("ch") == 0

    @pl.when(first)
    def _():
        cot_ref[:, 0:part] = own_ref[...]
        cot_ref[:, part:] = other_ref[...]

    @pl.when(jnp.logical_not(first))
    def _():
        cot_ref[:, 0:part] = other_ref[...]
        cot_ref[:, part:] = own_ref[...]

    shifted_columns(side, part, field_ref[...].reshape(rows, part), None, cols)
    cot = cot_ref[...]
    rim_ref[...] = jnp.concatenate(
        [
            cot[0:side],
            cot[rows - side :],
            cot.reshape(side, side, chans)[:, 0, :],
            cot.reshape(side, side, chans)[:, side - 1, :],
        ],
        axis=0,
    )
    which = 1 - lax.rem(lax.axis_index("tile"), 2)
    half_taps(side, part, half, scale, which, cols, cot, send, middle)
    for i, ref in enumerate(send_refs):
        ref[...] = send[i * (half // CUTS) : (i + 1) * (half // CUTS), :]


def mine_kernel(side, part, half, scale, cols, cot_ref, mine_ref, middle):
    which = lax.rem(lax.axis_index("tile"), 2)
    half_taps(side, part, half, scale, which, cols, cot_ref[...], mine_ref, middle)


def unpack_near(near_refs, near, side, part):
    size = packed_shape(4 * side, part)[0]
    row = 0
    for ref in near_refs:
        for k in range(ref.shape[0] // size):
            unpack(ref, near, k * size, row, 4 * side, part)
            row += 4 * side


def border_kernel(side, part, chunk, scale, n_near, *refs):
    near_refs = refs[:n_near]
    onehot_ref, mine_ref, rim_ref, mate_ref = refs[n_near : n_near + 4]
    got_refs = refs[n_near + 4 : n_near + 4 + CUTS]
    outs, near, total = refs[n_near + 4 + CUTS : -2], refs[-2], refs[-1]
    count = lax.axis_size("tile")
    own = lax.axis_index("tile")
    core = lax.rem(own, 2)
    unpack_near(near_refs, near, side, part)
    for i, ref in enumerate(got_refs):
        here = slice(i * ref.shape[0], (i + 1) * ref.shape[0])
        total[here, :] = mine_ref[here, :] + ref[...]
    left = jnp.dot(onehot_ref[...], near[...], preferred_element_type=jnp.float32).astype(jnp.bfloat16)

    def rim(ref, at):
        return ref[pl.ds(pl.multiple_of(at, 16), side), :]

    for q in range(4):
        column = (2 + q // 2) * side if q < 3 else (2 + core) * side
        right = jnp.concatenate(
            [value for ref in (rim_ref, mate_ref) for value in (rim(ref, core * side), rim(ref, column))],
            axis=0,
        )
        value = lax.dot_general(
            left[q * 4 * side : (q + 1) * 4 * side],
            right,
            (((0,), (0,)), ((), ())),
            preferred_element_type=jnp.float32,
        )
        if q < 3:
            start = q * part + core * (part // 2 + part)
        else:
            start = 3 * part - core * (3 * part - part // 2)
        here = pl.ds(pl.multiple_of(start, 16), part)
        total[here, :] = total[here, :] + value * scale
    size = outs[0].shape[0]
    for index in range(count // 2):
        to = slot_of_mask(2 * index, count) * chunk
        block = pl.multiple_of(((own // 2) ^ index) * chunk, 16)
        out = outs[to // size]
        out[to % size : to % size + chunk, :] = total[pl.ds(block, chunk), :].astype(out.dtype)


def sum_kernel(n_got, n_out, *refs):
    held_ref, got_refs, outs = refs[0], refs[1 : 1 + n_got], refs[1 + n_got :]
    size = held_ref.shape[0] // n_out
    for index in range(n_out):
        here = slice(index * size, (index + 1) * size)
        value = held_ref[here, :]
        for ref in got_refs:
            value = value + ref[here, :].astype(jnp.float32)
        outs[index][...] = value.astype(outs[index].dtype)


def join_kernel(*refs):
    row = 0
    for ref in refs[:-1]:
        refs[-1][row : row + ref.shape[0], :] = ref[...]
        row += ref.shape[0]


def unfold_kernel(used, chunk, bits, masks, n_dep, *refs):
    refs = refs[n_dep:]
    n = len(masks)
    in_refs, out_ref, wide, sems = refs[:n], refs[n], refs[n + 1], refs[n + 2]
    own = lax.axis_index("tile")
    full, rest = used // chunk, used % chunk
    copies = []
    for i, (ref, inner, bit) in enumerate(zip(in_refs, masks, bits)):
        origin = (lax.rem(own, 2) ^ bit) * used
        for k, mask in enumerate(inner):
            at = i * len(inner) + k
            wide[at] = ref[k * chunk : (k + 1) * chunk, :].astype(jnp.float32)
            block = (own ^ mask) // 2
            start = pl.multiple_of(origin + block * chunk, 16)
            copies.append(
                (
                    block < full,
                    pltpu.make_async_copy(wide.at[at], out_ref.at[pl.ds(start, chunk), :], sems.at[at]),
                )
            )
            if rest:
                start = pl.multiple_of(origin + full * chunk, 16)
                copies.append(
                    (
                        block == full,
                        pltpu.make_async_copy(
                            wide.at[at, 0:rest], out_ref.at[pl.ds(start, rest), :], sems.at[at]
                        ),
                    )
                )
    for going, copy in copies:
        pl.when(going)(copy.start)
    for going, copy in copies:
        pl.when(going)(copy.wait)


def unfold(whole, chunk, bits, masks, blocks, before):
    n_dep = 0 if before is None else 1
    anywhere = pl.BlockSpec(memory_space=pl.ANY)
    n_copies = len(masks) * len(masks[0])
    return pl.pallas_call(
        functools.partial(unfold_kernel, whole.shape[0] // 2, chunk, bits, masks, n_dep),
        out_shape=whole,
        in_specs=[anywhere] * n_dep + [pl.BlockSpec(memory_space=pltpu.VMEM)] * len(blocks),
        out_specs=anywhere,
        scratch_shapes=[
            pltpu.VMEM((n_copies, chunk, whole.shape[1]), jnp.float32),
            pltpu.SemaphoreType.DMA((n_copies,)),
        ],
        input_output_aliases={0: 0} if n_dep else {},
        compiler_params=pltpu.CompilerParams(vmem_limit_bytes=40 * 1024 * 1024),
    )(*([before] if n_dep else []), *blocks)


def back_kernel(side, part, cot_ref, weight_ref, inner_ref, pieces_ref, tall):
    rows = side * side
    flat = rows + 2 * side
    start = pl.multiple_of(lax.axis_index("ch") * part, 16)
    blank = jnp.zeros((2 * side, tall.shape[1]), jnp.bfloat16)
    tall[0 : 2 * side, :] = blank
    tall[2 * side : 2 * side + rows, :] = cot_ref[...]
    tall[2 * side + rows :, :] = blank
    backs = []
    for b in range(3):
        back = jnp.zeros((flat, part), jnp.float32)
        for a in range(3):
            back = back + lax.dot_general(
                tall[(2 - a) * side : (2 - a) * side + flat, :],
                weight_ref[3 * a + b, pl.ds(start, part), :],
                (((1,), (1,)), ((), ())),
                preferred_element_type=jnp.float32,
            )
        backs.append(back)
    column = lax.broadcasted_iota(jnp.int32, (flat, part), 0) % side
    inner = (
        jnp.where(column == side - 1, 0.0, pltpu.roll(backs[0], flat - 1, 0))
        + backs[1]
        + jnp.where(column == 0, 0.0, pltpu.roll(backs[2], 1, 0))
    )
    inner_ref[...] = inner[side : side + rows]
    west = backs[0].reshape(side + 2, side, part)[:, 0, :]
    east = backs[2].reshape(side + 2, side, part)[:, side - 1, :]
    pieces = jnp.concatenate(
        [
            inner[0:side],
            east[1 : side + 1],
            inner[side + rows :],
            west[1 : side + 1],
            west[0:1],
            east[0:1],
            east[side + 1 :],
            west[side + 1 :],
            jnp.zeros((EXTRA - 4, part), jnp.float32),
        ],
        axis=0,
    )
    pack(pieces.astype(jnp.bfloat16), pieces_ref)


def add_halo_kernel(side, part, place_ref, inner_ref, *refs):
    got_refs, out_ref, got = refs[:-2], refs[-2], refs[-1]
    block = 4 * side + EXTRA
    size = packed_shape(block, part)[0]
    for i, ref in enumerate(got_refs):
        for k in range(3):
            unpack(ref, got, k * size, (3 * i + k) * block, block, part)
    sums = jnp.dot(place_ref[...], got[...], preferred_element_type=jnp.float32)
    rows = side * side
    spread = lambda col: jnp.broadcast_to(col[:, None, :], (side, side, part)).reshape(rows, part)
    column = lax.broadcasted_iota(jnp.int32, (rows, part), 0) % side
    inner = inner_ref[...]
    inner = inner + jnp.where(column == side - 1, spread(sums[side : 2 * side]), 0.0)
    inner = inner + jnp.where(column == 0, spread(sums[3 * side :]), 0.0)
    ends = jnp.concatenate(
        [
            inner[0:side] + sums[0:side],
            inner[side : rows - side],
            inner[rows - side :] + sums[2 * side : 3 * side],
        ],
        axis=0,
    )
    out_ref[...] = ends.astype(jnp.bfloat16)


def halo_kernel(side, part, n_near, *refs):
    near_refs, tables_in, field_ref = refs[:n_near], refs[n_near], refs[n_near + 1]
    halos_ref, packet_ref, near, tables, sem = refs[n_near + 2 :]
    copy = pltpu.make_async_copy(tables_in, tables, sem)
    copy.start()
    rows = side * side
    unpack_near(near_refs, near, side, part)
    pack(field_ref[...].reshape(rows, part), packet_ref)
    copy.wait()
    index = Neighbours(side, tables)
    step = lax.broadcasted_iota(jnp.int32, (side, 1), 0)
    wanted = []
    for e in range(4):
        block, at = index.edge(index.own, e)
        wanted.append(block * (4 * side) + at(step))
    spots = lax.broadcasted_iota(jnp.int32, (EXTRA, 1), 0)
    ends = jnp.full((EXTRA, 1), -1, jnp.int32)
    for c in range(4):
        block, spot = index.corner(index.own, c)
        ends = jnp.where(spots == c, block * (4 * side) + spot, ends)
    pick = onehot(jnp.concatenate(wanted + [ends], axis=0), near.shape[0])
    halos = jnp.dot(pick, near[...], preferred_element_type=jnp.float32).astype(jnp.bfloat16)
    halos_ref[...] = halos
    pack(halos, packet_ref, packed_shape(rows, part)[0])


def output_kernel(side, part, field_ref, halos_ref, other_ref, weight_ref, out_ref, cols, other_cols, other):
    rows = side * side
    ch = lax.axis_index("ch")
    wide = -(-part // 128) * 128
    lanes = pl.multiple_of(ch * (weight_ref.shape[2] - wide), 128)
    unpack(other_ref, other, 0, 0, rows, part)
    unpack(other_ref, other, packed_shape(rows, part)[0], rows, 4 * side + EXTRA, part)
    shifted_columns(side, part, field_ref[...].reshape(rows, part), halos_ref[...], cols)
    shifted_columns(side, part, other[0:rows, :], other[rows:, :], other_cols)
    starts = (pl.multiple_of(ch * part, 16), pl.multiple_of((1 - ch) * part, 16))
    total = jnp.zeros((rows, wide), jnp.float32)
    for a in range(3):
        for b in range(3):
            for ref, first in zip((cols, other_cols), starts):
                total = total + jnp.dot(
                    ref[b, a * side : a * side + rows, :],
                    weight_ref[3 * a + b, pl.ds(first, part), pl.ds(lanes, wide)],
                    preferred_element_type=jnp.float32,
                )
    result = jnp.where(ch == 0, total[:, :part], total[:, wide - part :])
    out_ref[...] = result.astype(jnp.bfloat16)


def body(features, weight, cotangent, edge_tiles, edge_turns, corner_tiles, corner_turns):
    count = lax.axis_size("tile")
    field = features[0]
    side, part = field.shape[0], field.shape[2]
    chans = weight.shape[3]
    rows = side * side
    flat = rows + 2 * side
    block = 4 * side + EXTRA
    taps = weight.reshape(9, chans, chans)
    others = [(0, 1), (1, 0)]
    flops = 2 * rows * 9 * part * chans
    half_bytes = jnp.bfloat16
    chunk = -(-9 * part // (16 * count)) * 16
    half = count * chunk // 2
    scale = 1.0 / math.sqrt(count * rows)

    cot_own = cotangent[0].reshape(rows, part)
    cot_other = lax.ppermute(cot_own, "ch", others)
    sides, field = call(
        functools.partial(sides_kernel, side),
        [vmem(packed_shape(4 * side, part), half_bytes), vmem(field.shape, half_bytes)],
        [field],
    )
    ahead, behind = by_offset(sides, -SPAN, count), by_offset(sides, SPAN, count)
    across = by_mask(sides, 2, count)
    tables = jnp.concatenate([edge_tiles.T, edge_turns.T, corner_tiles.T, corner_turns.T], axis=0)
    table_scratch = [pltpu.SMEM(tables.shape, jnp.int32), pltpu.SemaphoreType.DMA]
    border_pick, cot_own = call(
        functools.partial(border_onehot_kernel, side),
        [vmem((16 * side, 48 * side), half_bytes), vmem((rows, part), half_bytes)],
        [tables, cot_own],
        scratch=table_scratch,
    )
    pair = packed_shape(8 * side, part)
    (beyond,) = call(join_kernel, [vmem(pair, half_bytes)], [ahead, behind])
    near = [sides, across, ahead, behind, by_mask(beyond, 2, count)]
    near, cot_other, border_pick = lax.optimization_barrier((near, cot_other, border_pick))
    (near,) = call(join_kernel, [vmem(packed_shape(24 * side, part), half_bytes)], near)
    mates = by_mask(near, 1, count)
    *send, cot_full, rim, cols = call(
        functools.partial(send_kernel, side, part, half, scale),
        [
            *[vmem((half // CUTS, chans), jnp.float32)] * CUTS,
            vmem((rows, chans), half_bytes),
            vmem((4 * side, chans), half_bytes),
            vmem((3, flat, part), half_bytes),
        ],
        [field, cot_own, cot_other],
        scratch=[pltpu.VMEM((part, chans), jnp.float32), pltpu.VMEM((half, chans), jnp.float32)],
        flops=flops // 2,
    )
    (mine,) = call(
        functools.partial(mine_kernel, side, part, half, scale),
        [vmem((half, chans), jnp.float32)],
        [cols, cot_full],
        scratch=[pltpu.VMEM((part, chans), jnp.float32)],
        flops=flops // 2,
    )

    mates, mine, rim_mate = lax.optimization_barrier((mates, mine, by_mask(rim, 1, count)))
    near = [near, mates]

    stages = mask_stages(count)
    masks = group_masks(stages[1])
    size = half // len(masks)
    held, *send = call(
        functools.partial(border_kernel, side, part, chunk, scale, len(near)),
        [vmem((size, chans), jnp.float32)] + [vmem((size, chans), half_bytes)] * (len(masks) - 1),
        [*near, border_pick, mine, rim, rim_mate, *[by_mask(v, 1, count) for v in send]],
        scratch=[pltpu.VMEM((48 * side, part), half_bytes), pltpu.VMEM((half, chans), jnp.float32)],
    )
    send, cot_full, near = lax.optimization_barrier((send, cot_full, near))
    got = [by_mask(v, m, count) for v, m in zip(send, masks[1:])]
    inner, pieces = call(
        functools.partial(back_kernel, side, part),
        [vmem((rows, part), jnp.float32), vmem(packed_shape(block, part), half_bytes)],
        [cot_full, taps],
        scratch=[pltpu.VMEM((rows + 4 * side, chans), half_bytes)],
        flops=flops,
    )
    here = [pieces, by_offset(pieces, -SPAN, count), by_offset(pieces, SPAN, count)]
    (place,) = call(
        functools.partial(place_kernel, side),
        [vmem((4 * side, 12 * block), half_bytes)],
        [tables],
        scratch=table_scratch,
    )
    halos, packet = call(
        functools.partial(halo_kernel, side, part, len(near)),
        [vmem((block, part), half_bytes), vmem(packed_shape(rows + block, part), half_bytes)],
        [*near, tables, field],
        scratch=[pltpu.VMEM((48 * side, part), half_bytes), *table_scratch],
    )
    got, here, inner, halos, packet = lax.optimization_barrier((got, here, inner, halos, packet))
    for index, bits in enumerate(stages[2:]):
        masks = group_masks(bits)
        size = held.shape[0] // len(masks)
        held, *send = call(
            functools.partial(sum_kernel, len(got), len(masks)),
            [vmem((size, chans), jnp.float32)] + [vmem((size, chans), half_bytes)] * (len(masks) - 1),
            [held, *got],
        )
        if index == 0:
            send, here, packet = lax.optimization_barrier((send, here, packet))
        got = [by_mask(v, m, count) for v, m in zip(send, masks[1:])]
        if index == 0:
            (here,) = call(join_kernel, [vmem((3 * pieces.shape[0], pieces.shape[1]), half_bytes)], here)
            beside = by_mask(here, 2, count)
            other_field = lax.ppermute(packet, "ch", others)
            got, here = lax.optimization_barrier((got, here))
    (held,) = call(functools.partial(sum_kernel, len(got), 1), [vmem(held.shape, half_bytes)], [held, *got])
    order = [0]
    for index, bits in enumerate(stages[:0:-1]):
        masks = group_masks(bits)
        got = [by_mask(held, m, count) for m in masks[1:]]
        if index == 0:
            held, got, beside = lax.optimization_barrier((held, got, beside))
        if index < len(stages) - 2:
            order = [m + v for m in masks for v in order]
            (held,) = call(
                join_kernel, [vmem((held.shape[0] * len(masks), chans), half_bytes)], [held, *got]
            )
            continue
        got_pieces = [here, beside, by_mask(here, 1, count), by_mask(beside, 1, count)]
        (grad_features,) = call(
            functools.partial(add_halo_kernel, side, part),
            [vmem((rows, part), half_bytes)],
            [place, inner, *got_pieces],
            scratch=[pltpu.VMEM((12 * block, part), half_bytes)],
        )
        (output,) = call(
            functools.partial(output_kernel, side, part),
            [vmem((rows, part), half_bytes)],
            [field, halos, other_field, taps],
            scratch=[
                pltpu.VMEM((3, flat, part), half_bytes),
                pltpu.VMEM((3, flat, part), half_bytes),
                pltpu.VMEM((rows + block, part), half_bytes),
            ],
            flops=2 * flops,
        )
        got, grad_features, output = lax.optimization_barrier((got, grad_features, output))
        got = [held, *got]
        order = [[m + v for v in order] for m in masks]
    mates = [by_mask(v, 1, count) for v in got]
    whole = vmem((9 * part, chans), jnp.float32)
    early = len(got) - 1
    bits = [0] * early + [1] * early
    first = unfold(whole, chunk, bits, order[:-1] + order[:-1], got[:-1] + mates[:-1], None)
    grad_weight = unfold(whole, chunk, [0, 1], order[-1:] * 2, [got[-1], mates[-1]], first)
    shape = (1, side, side, part)
    return (
        output.reshape(shape),
        grad_features.reshape(shape),
        grad_weight.reshape(3, 3, part, chans),
    )


def solution(mesh):
    return jax.shard_map(
        body,
        mesh=mesh,
        in_specs=(
            P("tile", None, None, "ch"),
            P(),
            P("tile", None, None, "ch"),
            P(),
            P(),
            P(),
            P(),
        ),
        out_specs=(
            P("tile", None, None, "ch"),
            P("tile", None, None, "ch"),
            P(None, None, "ch", None),
        ),
        check_vma=False,
    )
```

```python
import functools
import math

import jax
import jax.numpy as jnp
import numpy as np
from jax import lax
from jax.experimental import pallas as pl
from jax.experimental.pallas import tpu as pltpu
from jax.sharding import PartitionSpec as P

SPAN = 4
EXTRA = 16
CUTS = 2


def turn_tables():
    labels = [[3 * row + col for col in range(3)] for row in range(3)]

    def turn_once(block):
        return [[block[col][2 - row] for col in range(3)] for row in range(3)]

    def sides_of(block):
        return [
            list(block[0]),
            [block[row][2] for row in range(3)],
            list(block[2]),
            [block[row][0] for row in range(3)],
        ]

    def corners_of(block):
        return [block[0][0], block[0][2], block[2][2], block[2][0]]

    base_sides = sides_of(labels)
    base_corners = corners_of(labels)
    edge_table = np.zeros((4, 4), np.int32)
    corner_table = np.zeros((4, 4), np.int32)
    for border in range(4):
        turned = labels
        for quarter in range(4):
            wanted = sides_of(turned)[(border + 2) % 4]
            for side_index in range(4):
                if base_sides[side_index] == wanted:
                    edge_table[border, quarter] = side_index
                if base_sides[side_index][::-1] == wanted:
                    edge_table[border, quarter] = side_index + 4
            corner_cell = corners_of(turned)[(border + 2) % 4]
            for corner_index in range(4):
                if base_corners[corner_index] == corner_cell:
                    corner_table[border, quarter] = corner_index
            turned = turn_once(turned)
    tables = np.concatenate([edge_table, corner_table], axis=0)
    return [sum(int(slot) << (3 * quarter) for quarter, slot in enumerate(row)) for row in tables]


def by_swap(value, odd, count):
    pairs = [
        (i, (i + (SPAN if (i // SPAN) % 2 == odd else -SPAN)) % count) for i in range(count)
    ]
    return lax.ppermute(value, "tile", pairs)


def by_mask(value, mask, count):
    return lax.ppermute(value, "tile", [(i, i ^ mask) for i in range(count)])


def mask_stages(count):
    bits = [1 << b for b in range(count.bit_length() - 1)]
    stages = [bits[:1]]
    rest = bits[1:]
    while rest:
        stages.append(rest[:2])
        rest = rest[2:]
    return stages


def group_masks(bits):
    masks = [0]
    for bit in bits:
        masks = masks + [m + bit for m in masks]
    return masks


def slot_of_mask(mask, count):
    place = 0
    for bits in mask_stages(count)[1:]:
        size = 1 << len(bits)
        place = place * size + (mask // bits[0]) % size
    return place


def slot_in(row, quarter):
    return (row >> (3 * quarter)) & 7


def corner_spot(slot, side):
    return jnp.where(
        slot == 0, 0, jnp.where(slot == 1, side - 1, jnp.where(slot == 2, 3 * side - 1, 2 * side))
    )


def vmem(shape, dtype):
    return jax.ShapeDtypeStruct(shape, dtype)


def call(kernel, outs, args, anywhere=(), scratch=(), flops=0):
    in_specs = [
        pl.BlockSpec(memory_space=pltpu.HBM if i in anywhere else pltpu.VMEM) for i in range(len(args))
    ]
    size = sum(math.prod(x.shape) * x.dtype.itemsize for x in list(args) + list(outs))
    return pl.pallas_call(
        kernel,
        out_shape=tuple(outs),
        in_specs=in_specs,
        out_specs=tuple(pl.BlockSpec(memory_space=pltpu.VMEM) for _ in outs),
        scratch_shapes=list(scratch),
        compiler_params=pltpu.CompilerParams(vmem_limit_bytes=40 * 1024 * 1024),
        cost_estimate=pl.CostEstimate(flops=flops, bytes_accessed=size, transcendentals=0),
    )(*args)


def packed_shape(rows, part):
    if part % 128 != 64:
        return (rows, part)
    return (rows * (part // 128) + rows // 2, 128)


def pack(value, out_ref, first=0):
    rows, part = value.shape
    if part % 128 != 64:
        out_ref[first : first + rows, :] = value
        return
    for i in range(part // 128):
        out_ref[first + i * rows : first + (i + 1) * rows, :] = value[:, i * 128 : (i + 1) * 128]
    rest = value[:, part - 64 :]
    at = first + rows * (part // 128)
    out_ref[at : at + rows // 2, :] = jnp.concatenate([rest[: rows // 2], rest[rows // 2 :]], axis=1)


def unpack(ref, out_ref, first, row, rows, part):
    if part % 128 != 64:
        out_ref[row : row + rows, :] = ref[first : first + rows, :]
        return
    for i in range(part // 128):
        out_ref[row : row + rows, i * 128 : (i + 1) * 128] = ref[first + i * rows : first + (i + 1) * rows, :]
    at = first + rows * (part // 128)
    rest = ref[at : at + rows // 2, :]
    out_ref[row : row + rows // 2, part - 64 :] = rest[:, :64]
    out_ref[row + rows // 2 : row + rows, part - 64 :] = rest[:, 64:]


def sides_kernel(side, field_ref, sides_ref, copy_ref):
    sides = jnp.concatenate(
        [field_ref[0], field_ref[:, side - 1, :], field_ref[side - 1], field_ref[:, 0, :]], axis=0
    )
    pack(sides, sides_ref)
    copy_ref[...] = field_ref[...]


def shifted_columns(side, part, field, halos, out_ref):
    rows = side * side
    flat = rows + 2 * side
    column = lax.broadcasted_iota(jnp.int32, (flat, part), 0) % side
    if halos is None:
        none = jnp.zeros((side, part), jnp.float32)
        tall = jnp.concatenate([none, field.astype(jnp.float32), none], axis=0)
        west = east = 0.0
    else:
        edge = halos.astype(jnp.float32)
        tall = jnp.concatenate([edge[0:side], field.astype(jnp.float32), edge[2 * side : 3 * side]], axis=0)
        corner = [edge[4 * side + c : 4 * side + c + 1] for c in range(4)]
        spread = lambda col: jnp.broadcast_to(col[:, None, :], (side + 2, side, part)).reshape(flat, part)
        east = spread(jnp.concatenate([corner[1], edge[side : 2 * side], corner[2]], axis=0))
        west = spread(jnp.concatenate([corner[0], edge[3 * side : 4 * side], corner[3]], axis=0))
    out_ref[0] = jnp.where(column == 0, west, pltpu.roll(tall, 1, 0)).astype(jnp.bfloat16)
    out_ref[1] = tall.astype(jnp.bfloat16)
    out_ref[2] = jnp.where(column == side - 1, east, pltpu.roll(tall, flat - 1, 0)).astype(jnp.bfloat16)


class Neighbours:
    def __init__(self, side, tables):
        self.side = side
        self.et, self.eu, self.ct, self.cu = [tables.at[4 * i : 4 * i + 4] for i in range(4)]
        self.digits = turn_tables()
        self.count = lax.axis_size("tile")
        self.own = lax.axis_index("tile")

    def block(self, source):
        groups = self.count // SPAN
        slab = lax.rem(source // SPAN - self.own // SPAN + groups, groups)
        cross = source ^ self.own
        turn = lax.rem(cross // 2, 2)
        even = lax.rem(self.own // SPAN, 2) == 0
        at = jnp.where(slab == 0, turn, jnp.where((slab == 1) == even, 2, 3) + 2 * turn)
        return 6 * lax.rem(cross, 2) + at

    def edge(self, tile, e):
        slot = slot_in(self.digits[e], self.eu[e, tile])
        start = lax.rem(slot, 4) * self.side
        end = start + self.side - 1
        return self.block(self.et[e, tile]), lambda at: jnp.where(slot >= 4, end - at, start + at)

    def corner(self, tile, c):
        slot = slot_in(self.digits[4 + c], self.cu[c, tile])
        return self.block(self.ct[c, tile]), corner_spot(slot, self.side)


def onehot(wanted, width):
    lane = lax.broadcasted_iota(jnp.int32, (wanted.shape[0], width), 1)
    return jnp.where(lane == wanted, 1.0, 0.0).astype(jnp.bfloat16)


def border_onehot_kernel(side, tables_in, cot_in, border_ref, cot_ref, tables, sem):
    copy = pltpu.make_async_copy(tables_in, tables, sem)
    copy.start()
    cot_ref[...] = cot_in[...]
    border_ref[...] = jnp.zeros_like(border_ref)
    copy.wait()
    near = Neighbours(side, tables)
    low = lax.rem(near.own, 2) == 0
    width = 4 * side
    step = lax.broadcasted_iota(jnp.int32, (side, 1), 0)

    def put(row, block, wanted, add=False):
        here = (slice(row, row + side), pl.ds(pl.multiple_of(block * width, 128), width))
        value = onehot(wanted, width)
        border_ref[here] = border_ref[here] + value if add else value

    for m, tile in enumerate((near.own, near.own ^ 1)):
        first = 2 * m * side
        flat = [near.edge(tile, e) for e in range(4)]
        corners = [near.corner(tile, c) for c in range(4)]
        pick = lambda a, b: (jnp.where(low, a[0], b[0]), lambda at: jnp.where(low, a[1](at), b[1](at)))
        block, at = pick(flat[0], flat[2])
        left, right = [
            (jnp.where(low, corners[a][0], corners[b][0]), jnp.where(low, corners[a][1], corners[b][1]))
            for a, b in ((0, 3), (1, 2))
        ]
        along = jnp.where(low, step - 1, step + 1)
        fits = (along >= 0) & (along < side)
        put(first, block, jnp.where(step == 0, -1, at(step - 1)))
        put(first, left[0], jnp.where(step == 0, left[1], -1), add=True)
        put(first + side, flat[3][0], jnp.where(fits, flat[3][1](along), -1))
        put(first + 4 * side, block, at(step))
        put(first + 8 * side, block, jnp.where(step == side - 1, -1, at(step + 1)))
        put(first + 8 * side, right[0], jnp.where(step == side - 1, right[1], -1), add=True)
        put(first + 9 * side, flat[1][0], jnp.where(fits, flat[1][1](along), -1))
        block, at = pick(flat[3], flat[1])
        put(first + 13 * side, block, at(step))


def place_kernel(side, tables_in, place_ref, tables, sem):
    copy = pltpu.make_async_copy(tables_in, tables, sem)
    copy.start()
    copy.wait()
    near = Neighbours(side, tables)
    block = 4 * side + EXTRA
    lane = lax.broadcasted_iota(jnp.int32, (1, block), 1)
    row = lax.broadcasted_iota(jnp.int32, (4 * side, block), 0)
    places = []
    swap = jnp.where(lax.rem(near.own // SPAN, 2) == 0, SPAN, -SPAN)
    for mask in (0, 2, 1, 3):
        for offset in (0, swap, -swap):
            source = lax.rem((near.own ^ mask) + offset + near.count, near.count)
            target = jnp.full((1, block), -1, jnp.int32)
            for e in range(4):
                slot = slot_in(near.digits[e], near.eu[e, source])
                along = lane - e * side
                along = jnp.where(slot >= 4, side - 1 - along, along)
                hit = (lane >= e * side) & (lane < (e + 1) * side) & (near.et[e, source] == near.own)
                target = jnp.where(hit, lax.rem(slot, 4) * side + along, target)
                spot = corner_spot(slot_in(near.digits[4 + e], near.cu[e, source]), side)
                hit = (lane == 4 * side + e) & (near.ct[e, source] == near.own)
                target = jnp.where(hit, spot, target)
            places.append(jnp.where(row == target, 1.0, 0.0))
    place_ref[...] = jnp.concatenate(places, axis=1).astype(jnp.bfloat16)


def half_taps(side, part, half, scale, which, cols, cot, out_ref, middle):
    rows = side * side
    used = 9 * part // 2

    def product(a, b):
        value = lax.dot_general(
            cols[b, pl.ds(pl.multiple_of(a * side, 16), rows), :],
            cot,
            (((0,), (0,)), ((), ())),
            preferred_element_type=jnp.float32,
        )
        return value * scale

    for j in range(4):
        tap = j + 5 * which
        start = pl.multiple_of(which * (part // 2) + j * part, 16)
        out_ref[pl.ds(start, part), :] = product(tap // 3, lax.rem(tap, 3))
    middle[...] = product(1, 1)
    start = pl.multiple_of((1 - which) * 4 * part, 16)
    out_ref[pl.ds(start, part // 2), :] = middle[pl.ds(pl.multiple_of(which * (part // 2), 16), part // 2), :]
    out_ref[used:, :] = jnp.zeros((half - used, cot.shape[1]), jnp.float32)


def send_kernel(side, part, half, scale, field_ref, own_ref, other_ref, *refs):
    send_refs, (cot_ref, rim_ref, cols, middle, send) = refs[:CUTS], refs[CUTS:]
    rows = side * side
    chans = cot_ref.shape[1]
    first = lax.axis_index("ch") == 0

    @pl.when(first)
    def _():
        cot_ref[:, 0:part] = own_ref[...]
        cot_ref[:, part:] = other_ref[...]

    @pl.when(jnp.logical_not(first))
    def _():
        cot_ref[:, 0:part] = other_ref[...]
        cot_ref[:, part:] = own_ref[...]

    shifted_columns(side, part, field_ref[...].reshape(rows, part), None, cols)
    cot = cot_ref[...]
    rim_ref[...] = jnp.concatenate(
        [
            cot[0:side],
            cot[rows - side :],
            cot.reshape(side, side, chans)[:, 0, :],
            cot.reshape(side, side, chans)[:, side - 1, :],
        ],
        axis=0,
    )
    which = 1 - lax.rem(lax.axis_index("tile"), 2)
    half_taps(side, part, half, scale, which, cols, cot, send, middle)
    for i, ref in enumerate(send_refs):
        ref[...] = send[i * (half // CUTS) : (i + 1) * (half // CUTS), :]


def mine_kernel(side, part, half, scale, cols, cot_ref, mine_ref, middle):
    which = lax.rem(lax.axis_index("tile"), 2)
    half_taps(side, part, half, scale, which, cols, cot_ref[...], mine_ref, middle)


def unpack_near(near_refs, near, side, part):
    size = packed_shape(4 * side, part)[0]
    row = 0
    for ref in near_refs:
        for k in range(ref.shape[0] // size):
            unpack(ref, near, k * size, row, 4 * side, part)
            row += 4 * side


def border_kernel(side, part, chunk, scale, n_near, *refs):
    near_refs = refs[:n_near]
    onehot_ref, mine_ref, rim_ref, mate_ref = refs[n_near : n_near + 4]
    got_refs = refs[n_near + 4 : n_near + 4 + CUTS]
    outs, near, total = refs[n_near + 4 + CUTS : -2], refs[-2], refs[-1]
    count = lax.axis_size("tile")
    own = lax.axis_index("tile")
    core = lax.rem(own, 2)
    unpack_near(near_refs, near, side, part)
    for i, ref in enumerate(got_refs):
        here = slice(i * ref.shape[0], (i + 1) * ref.shape[0])
        total[here, :] = mine_ref[here, :] + ref[...]
    left = jnp.dot(onehot_ref[...], near[...], preferred_element_type=jnp.float32).astype(jnp.bfloat16)

    def rim(ref, at):
        return ref[pl.ds(pl.multiple_of(at, 16), side), :]

    for q in range(4):
        column = (2 + q // 2) * side if q < 3 else (2 + core) * side
        right = jnp.concatenate(
            [value for ref in (rim_ref, mate_ref) for value in (rim(ref, core * side), rim(ref, column))],
            axis=0,
        )
        value = lax.dot_general(
            left[q * 4 * side : (q + 1) * 4 * side],
            right,
            (((0,), (0,)), ((), ())),
            preferred_element_type=jnp.float32,
        )
        if q < 3:
            start = q * part + core * (part // 2 + part)
        else:
            start = 3 * part - core * (3 * part - part // 2)
        here = pl.ds(pl.multiple_of(start, 16), part)
        total[here, :] = total[here, :] + value * scale
    size = outs[0].shape[0]
    for index in range(count // 2):
        to = slot_of_mask(2 * index, count) * chunk
        block = pl.multiple_of(((own // 2) ^ index) * chunk, 16)
        out = outs[to // size]
        out[to % size : to % size + chunk, :] = total[pl.ds(block, chunk), :].astype(out.dtype)


def sum_kernel(n_got, n_out, *refs):
    held_ref, got_refs, outs = refs[0], refs[1 : 1 + n_got], refs[1 + n_got :]
    size = held_ref.shape[0] // n_out
    for index in range(n_out):
        here = slice(index * size, (index + 1) * size)
        value = held_ref[here, :]
        for ref in got_refs:
            value = value + ref[here, :].astype(jnp.float32)
        outs[index][...] = value.astype(outs[index].dtype)


def join_kernel(*refs):
    row = 0
    for ref in refs[:-1]:
        refs[-1][row : row + ref.shape[0], :] = ref[...]
        row += ref.shape[0]


def unfold_kernel(used, chunk, bits, masks, n_dep, *refs):
    refs = refs[n_dep:]
    n = len(masks)
    in_refs, out_ref, wide, sems = refs[:n], refs[n], refs[n + 1], refs[n + 2]
    own = lax.axis_index("tile")
    full, rest = used // chunk, used % chunk
    copies = []
    for i, (ref, inner, bit) in enumerate(zip(in_refs, masks, bits)):
        origin = (lax.rem(own, 2) ^ bit) * used
        for k, mask in enumerate(inner):
            at = i * len(inner) + k
            wide[at] = ref[k * chunk : (k + 1) * chunk, :].astype(jnp.float32)
            block = (own ^ mask) // 2
            start = pl.multiple_of(origin + block * chunk, 16)
            copies.append(
                (
                    block < full,
                    pltpu.make_async_copy(wide.at[at], out_ref.at[pl.ds(start, chunk), :], sems.at[at]),
                )
            )
            if rest:
                start = pl.multiple_of(origin + full * chunk, 16)
                copies.append(
                    (
                        block == full,
                        pltpu.make_async_copy(
                            wide.at[at, 0:rest], out_ref.at[pl.ds(start, rest), :], sems.at[at]
                        ),
                    )
                )
    for going, copy in copies:
        pl.when(going)(copy.start)
    for going, copy in copies:
        pl.when(going)(copy.wait)


def unfold(whole, chunk, bits, masks, blocks, before):
    n_dep = 0 if before is None else 1
    anywhere = pl.BlockSpec(memory_space=pl.ANY)
    n_copies = len(masks) * len(masks[0])
    return pl.pallas_call(
        functools.partial(unfold_kernel, whole.shape[0] // 2, chunk, bits, masks, n_dep),
        out_shape=whole,
        in_specs=[anywhere] * n_dep + [pl.BlockSpec(memory_space=pltpu.VMEM)] * len(blocks),
        out_specs=anywhere,
        scratch_shapes=[
            pltpu.VMEM((n_copies, chunk, whole.shape[1]), jnp.float32),
            pltpu.SemaphoreType.DMA((n_copies,)),
        ],
        input_output_aliases={0: 0} if n_dep else {},
        compiler_params=pltpu.CompilerParams(vmem_limit_bytes=40 * 1024 * 1024),
    )(*([before] if n_dep else []), *blocks)


def back_kernel(side, part, cot_ref, weight_ref, inner_ref, pieces_ref, tall):
    rows = side * side
    flat = rows + 2 * side
    start = pl.multiple_of(lax.axis_index("ch") * part, 16)
    blank = jnp.zeros((2 * side, tall.shape[1]), jnp.bfloat16)
    tall[0 : 2 * side, :] = blank
    tall[2 * side : 2 * side + rows, :] = cot_ref[...]
    tall[2 * side + rows :, :] = blank
    backs = []
    for b in range(3):
        back = jnp.zeros((flat, part), jnp.float32)
        for a in range(3):
            back = back + lax.dot_general(
                tall[(2 - a) * side : (2 - a) * side + flat, :],
                weight_ref[3 * a + b, pl.ds(start, part), :],
                (((1,), (1,)), ((), ())),
                preferred_element_type=jnp.float32,
            )
        backs.append(back)
    column = lax.broadcasted_iota(jnp.int32, (flat, part), 0) % side
    inner = (
        jnp.where(column == side - 1, 0.0, pltpu.roll(backs[0], flat - 1, 0))
        + backs[1]
        + jnp.where(column == 0, 0.0, pltpu.roll(backs[2], 1, 0))
    )
    inner_ref[...] = inner[side : side + rows]
    west = backs[0].reshape(side + 2, side, part)[:, 0, :]
    east = backs[2].reshape(side + 2, side, part)[:, side - 1, :]
    pieces = jnp.concatenate(
        [
            inner[0:side],
            east[1 : side + 1],
            inner[side + rows :],
            west[1 : side + 1],
            west[0:1],
            east[0:1],
            east[side + 1 :],
            west[side + 1 :],
            jnp.zeros((EXTRA - 4, part), jnp.float32),
        ],
        axis=0,
    )
    pack(pieces.astype(jnp.bfloat16), pieces_ref)


def add_halo_kernel(side, part, place_ref, inner_ref, *refs):
    got_refs, out_ref, got = refs[:-2], refs[-2], refs[-1]
    block = 4 * side + EXTRA
    size = packed_shape(block, part)[0]
    for i, ref in enumerate(got_refs):
        for k in range(3):
            unpack(ref, got, k * size, (3 * i + k) * block, block, part)
    sums = jnp.dot(place_ref[...], got[...], preferred_element_type=jnp.float32)
    rows = side * side
    spread = lambda col: jnp.broadcast_to(col[:, None, :], (side, side, part)).reshape(rows, part)
    column = lax.broadcasted_iota(jnp.int32, (rows, part), 0) % side
    inner = inner_ref[...]
    inner = inner + jnp.where(column == side - 1, spread(sums[side : 2 * side]), 0.0)
    inner = inner + jnp.where(column == 0, spread(sums[3 * side :]), 0.0)
    ends = jnp.concatenate(
        [
            inner[0:side] + sums[0:side],
            inner[side : rows - side],
            inner[rows - side :] + sums[2 * side : 3 * side],
        ],
        axis=0,
    )
    out_ref[...] = ends.astype(jnp.bfloat16)


def halo_kernel(side, part, n_near, *refs):
    near_refs, tables_in, field_ref = refs[:n_near], refs[n_near], refs[n_near + 1]
    halos_ref, packet_ref, near, tables, sem = refs[n_near + 2 :]
    copy = pltpu.make_async_copy(tables_in, tables, sem)
    copy.start()
    rows = side * side
    unpack_near(near_refs, near, side, part)
    pack(field_ref[...].reshape(rows, part), packet_ref)
    copy.wait()
    index = Neighbours(side, tables)
    step = lax.broadcasted_iota(jnp.int32, (side, 1), 0)
    wanted = []
    for e in range(4):
        block, at = index.edge(index.own, e)
        wanted.append(block * (4 * side) + at(step))
    spots = lax.broadcasted_iota(jnp.int32, (EXTRA, 1), 0)
    ends = jnp.full((EXTRA, 1), -1, jnp.int32)
    for c in range(4):
        block, spot = index.corner(index.own, c)
        ends = jnp.where(spots == c, block * (4 * side) + spot, ends)
    pick = onehot(jnp.concatenate(wanted + [ends], axis=0), near.shape[0])
    halos = jnp.dot(pick, near[...], preferred_element_type=jnp.float32).astype(jnp.bfloat16)
    halos_ref[...] = halos
    pack(halos, packet_ref, packed_shape(rows, part)[0])


def output_kernel(side, part, field_ref, halos_ref, other_ref, weight_ref, out_ref, cols, other_cols, other):
    rows = side * side
    ch = lax.axis_index("ch")
    wide = -(-part // 128) * 128
    lanes = pl.multiple_of(ch * (weight_ref.shape[2] - wide), 128)
    unpack(other_ref, other, 0, 0, rows, part)
    unpack(other_ref, other, packed_shape(rows, part)[0], rows, 4 * side + EXTRA, part)
    shifted_columns(side, part, field_ref[...].reshape(rows, part), halos_ref[...], cols)
    shifted_columns(side, part, other[0:rows, :], other[rows:, :], other_cols)
    starts = (pl.multiple_of(ch * part, 16), pl.multiple_of((1 - ch) * part, 16))
    total = jnp.zeros((rows, wide), jnp.float32)
    for a in range(3):
        for b in range(3):
            for ref, first in zip((cols, other_cols), starts):
                total = total + jnp.dot(
                    ref[b, a * side : a * side + rows, :],
                    weight_ref[3 * a + b, pl.ds(first, part), pl.ds(lanes, wide)],
                    preferred_element_type=jnp.float32,
                )
    result = jnp.where(ch == 0, total[:, :part], total[:, wide - part :])
    out_ref[...] = result.astype(jnp.bfloat16)


def body(features, weight, cotangent, edge_tiles, edge_turns, corner_tiles, corner_turns):
    count = lax.axis_size("tile")
    field = features[0]
    side, part = field.shape[0], field.shape[2]
    chans = weight.shape[3]
    rows = side * side
    flat = rows + 2 * side
    block = 4 * side + EXTRA
    taps = weight.reshape(9, chans, chans)
    others = [(0, 1), (1, 0)]
    flops = 2 * rows * 9 * part * chans
    half_bytes = jnp.bfloat16
    chunk = -(-9 * part // (16 * count)) * 16
    half = count * chunk // 2
    scale = 1.0 / math.sqrt(count * rows)

    cot_own = cotangent[0].reshape(rows, part)
    cot_other = lax.ppermute(cot_own, "ch", others)
    sides, field = call(
        functools.partial(sides_kernel, side),
        [vmem(packed_shape(4 * side, part), half_bytes), vmem(field.shape, half_bytes)],
        [field],
    )
    swaps = [by_swap(sides, odd, count) for odd in (0, 1)]
    across = by_mask(sides, 2, count)
    tables = jnp.concatenate([edge_tiles.T, edge_turns.T, corner_tiles.T, corner_turns.T], axis=0)
    table_scratch = [pltpu.SMEM(tables.shape, jnp.int32), pltpu.SemaphoreType.DMA]
    border_pick, cot_own = call(
        functools.partial(border_onehot_kernel, side),
        [vmem((16 * side, 48 * side), half_bytes), vmem((rows, part), half_bytes)],
        [tables, cot_own],
        scratch=table_scratch,
    )
    pair = packed_shape(8 * side, part)
    (beyond,) = call(join_kernel, [vmem(pair, half_bytes)], swaps)
    near = [sides, across, *swaps, by_mask(beyond, 2, count)]
    near, cot_other, border_pick = lax.optimization_barrier((near, cot_other, border_pick))
    (near,) = call(join_kernel, [vmem(packed_shape(24 * side, part), half_bytes)], near)
    mates = by_mask(near, 1, count)
    *send, cot_full, rim, cols = call(
        functools.partial(send_kernel, side, part, half, scale),
        [
            *[vmem((half // CUTS, chans), jnp.float32)] * CUTS,
            vmem((rows, chans), half_bytes),
            vmem((4 * side, chans), half_bytes),
            vmem((3, flat, part), half_bytes),
        ],
        [field, cot_own, cot_other],
        scratch=[pltpu.VMEM((part, chans), jnp.float32), pltpu.VMEM((half, chans), jnp.float32)],
        flops=flops // 2,
    )
    (mine,) = call(
        functools.partial(mine_kernel, side, part, half, scale),
        [vmem((half, chans), jnp.float32)],
        [cols, cot_full],
        scratch=[pltpu.VMEM((part, chans), jnp.float32)],
        flops=flops // 2,
    )

    mates, mine, rim_mate = lax.optimization_barrier((mates, mine, by_mask(rim, 1, count)))
    near = [near, mates]

    stages = mask_stages(count)
    masks = group_masks(stages[1])
    size = half // len(masks)
    held, *send = call(
        functools.partial(border_kernel, side, part, chunk, scale, len(near)),
        [vmem((size, chans), jnp.float32)] + [vmem((size, chans), half_bytes)] * (len(masks) - 1),
        [*near, border_pick, mine, rim, rim_mate, *[by_mask(v, 1, count) for v in send]],
        scratch=[pltpu.VMEM((48 * side, part), half_bytes), pltpu.VMEM((half, chans), jnp.float32)],
    )
    send, cot_full, near = lax.optimization_barrier((send, cot_full, near))
    got = [by_mask(v, m, count) for v, m in zip(send, masks[1:])]
    inner, pieces = call(
        functools.partial(back_kernel, side, part),
        [vmem((rows, part), jnp.float32), vmem(packed_shape(block, part), half_bytes)],
        [cot_full, taps],
        scratch=[pltpu.VMEM((rows + 4 * side, chans), half_bytes)],
        flops=flops,
    )
    pieces, near = lax.optimization_barrier((pieces, near))
    here = [pieces, *[by_swap(pieces, odd, count) for odd in (0, 1)]]
    (place,) = call(
        functools.partial(place_kernel, side),
        [vmem((4 * side, 12 * block), half_bytes)],
        [tables],
        scratch=table_scratch,
    )
    halos, packet = call(
        functools.partial(halo_kernel, side, part, len(near)),
        [vmem((block, part), half_bytes), vmem(packed_shape(rows + block, part), half_bytes)],
        [*near, tables, field],
        scratch=[pltpu.VMEM((48 * side, part), half_bytes), *table_scratch],
    )
    got, here, inner, halos, packet, place = lax.optimization_barrier(
        (got, here, inner, halos, packet, place)
    )
    for index, bits in enumerate(stages[2:]):
        masks = group_masks(bits)
        size = held.shape[0] // len(masks)
        held, *send = call(
            functools.partial(sum_kernel, len(got), len(masks)),
            [vmem((size, chans), jnp.float32)] + [vmem((size, chans), half_bytes)] * (len(masks) - 1),
            [held, *got],
        )
        if index == 0:
            send, here = lax.optimization_barrier((send, here))
        got = [by_mask(v, m, count) for v, m in zip(send, masks[1:])]
        if index == 0:
            (here,) = call(join_kernel, [vmem((3 * pieces.shape[0], pieces.shape[1]), half_bytes)], here)
            beside = by_mask(here, 2, count)
            other_field = lax.ppermute(packet, "ch", others)
            got, here = lax.optimization_barrier((got, here))
    (held,) = call(functools.partial(sum_kernel, len(got), 1), [vmem(held.shape, half_bytes)], [held, *got])
    order = [0]
    for index, bits in enumerate(stages[:0:-1]):
        masks = group_masks(bits)
        got = [by_mask(held, m, count) for m in masks[1:]]
        if index == 0:
            held, got, beside = lax.optimization_barrier((held, got, beside))
        if index < len(stages) - 2:
            order = [m + v for m in masks for v in order]
            (held,) = call(
                join_kernel, [vmem((held.shape[0] * len(masks), chans), half_bytes)], [held, *got]
            )
            continue
        got_pieces = [here, beside, by_mask(here, 1, count), by_mask(beside, 1, count)]
        (grad_features,) = call(
            functools.partial(add_halo_kernel, side, part),
            [vmem((rows, part), half_bytes)],
            [place, inner, *got_pieces],
            scratch=[pltpu.VMEM((12 * block, part), half_bytes)],
        )
        (output,) = call(
            functools.partial(output_kernel, side, part),
            [vmem((rows, part), half_bytes)],
            [field, halos, other_field, taps],
            scratch=[
                pltpu.VMEM((3, flat, part), half_bytes),
                pltpu.VMEM((3, flat, part), half_bytes),
                pltpu.VMEM((rows + block, part), half_bytes),
            ],
            flops=2 * flops,
        )
        got, grad_features, output = lax.optimization_barrier((got, grad_features, output))
        got = [held, *got]
        order = [[m + v for v in order] for m in masks]
    mates = [by_mask(v, 1, count) for v in got]
    whole = vmem((9 * part, chans), jnp.float32)
    own = len(got)
    first = unfold(whole, chunk, [0] * own + [1], order + order[:1], got + mates[:1], None)
    grad_weight = unfold(whole, chunk, [1] * (own - 1), order[1:], mates[1:], first)
    shape = (1, side, side, part)
    return (
        output.reshape(shape),
        grad_features.reshape(shape),
        grad_weight.reshape(3, 3, part, chans),
    )


def solution(mesh):
    return jax.shard_map(
        body,
        mesh=mesh,
        in_specs=(
            P("tile", None, None, "ch"),
            P(),
            P("tile", None, None, "ch"),
            P(),
            P(),
            P(),
            P(),
        ),
        out_specs=(
            P("tile", None, None, "ch"),
            P("tile", None, None, "ch"),
            P(None, None, "ch", None),
        ),
        check_vma=False,
    )
```

```python
import functools
import math

import jax
import jax.numpy as jnp
import numpy as np
from jax import lax
from jax.experimental import pallas as pl
from jax.experimental.pallas import tpu as pltpu
from jax.sharding import PartitionSpec as P

SPAN = 4
EXTRA = 16


def turn_tables():
    labels = [[3 * row + col for col in range(3)] for row in range(3)]

    def turn_once(block):
        return [[block[col][2 - row] for col in range(3)] for row in range(3)]

    def sides_of(block):
        return [
            list(block[0]),
            [block[row][2] for row in range(3)],
            list(block[2]),
            [block[row][0] for row in range(3)],
        ]

    def corners_of(block):
        return [block[0][0], block[0][2], block[2][2], block[2][0]]

    base_sides = sides_of(labels)
    base_corners = corners_of(labels)
    edge_table = np.zeros((4, 4), np.int32)
    corner_table = np.zeros((4, 4), np.int32)
    for border in range(4):
        turned = labels
        for quarter in range(4):
            wanted = sides_of(turned)[(border + 2) % 4]
            for side_index in range(4):
                if base_sides[side_index] == wanted:
                    edge_table[border, quarter] = side_index
                if base_sides[side_index][::-1] == wanted:
                    edge_table[border, quarter] = side_index + 4
            corner_cell = corners_of(turned)[(border + 2) % 4]
            for corner_index in range(4):
                if base_corners[corner_index] == corner_cell:
                    corner_table[border, quarter] = corner_index
            turned = turn_once(turned)
    tables = np.concatenate([edge_table, corner_table], axis=0)
    return [sum(int(slot) << (3 * quarter) for quarter, slot in enumerate(row)) for row in tables]


def by_swap(value, odd, count):
    pairs = [
        (i, (i + (SPAN if (i // SPAN) % 2 == odd else -SPAN)) % count) for i in range(count)
    ]
    return lax.ppermute(value, "tile", pairs)


def by_mask(value, mask, count):
    return lax.ppermute(value, "tile", [(i, i ^ mask) for i in range(count)])


def mask_stages(count):
    bits = [1 << b for b in range(count.bit_length() - 1)]
    stages = [bits[:1]]
    rest = bits[1:]
    while rest:
        stages.append(rest[:2])
        rest = rest[2:]
    return stages


def group_masks(bits):
    masks = [0]
    for bit in bits:
        masks = masks + [m + bit for m in masks]
    return masks


def slot_of_mask(mask, count):
    place = 0
    for bits in mask_stages(count)[1:]:
        size = 1 << len(bits)
        place = place * size + (mask // bits[0]) % size
    return place


def slot_in(row, quarter):
    return (row >> (3 * quarter)) & 7


def corner_spot(slot, side):
    return jnp.where(
        slot == 0, 0, jnp.where(slot == 1, side - 1, jnp.where(slot == 2, 3 * side - 1, 2 * side))
    )


def vmem(shape, dtype):
    return jax.ShapeDtypeStruct(shape, dtype)


def call(kernel, outs, args, anywhere=(), scratch=(), flops=0, costed=True):
    in_specs = [
        pl.BlockSpec(memory_space=pltpu.HBM if i in anywhere else pltpu.VMEM) for i in range(len(args))
    ]
    size = costed * sum(math.prod(x.shape) * x.dtype.itemsize for x in list(args) + list(outs))
    return pl.pallas_call(
        kernel,
        out_shape=tuple(outs),
        in_specs=in_specs,
        out_specs=tuple(pl.BlockSpec(memory_space=pltpu.VMEM) for _ in outs),
        scratch_shapes=list(scratch),
        compiler_params=pltpu.CompilerParams(vmem_limit_bytes=40 * 1024 * 1024),
        cost_estimate=pl.CostEstimate(flops=flops, bytes_accessed=size, transcendentals=0),
    )(*args)


def packed_shape(rows, part):
    if part % 128 != 64:
        return (rows, part)
    return (rows * (part // 128) + rows // 2, 128)


def pack(value, out_ref, first=0):
    rows, part = value.shape
    if part % 128 != 64:
        out_ref[first : first + rows, :] = value
        return
    for i in range(part // 128):
        out_ref[first + i * rows : first + (i + 1) * rows, :] = value[:, i * 128 : (i + 1) * 128]
    rest = value[:, part - 64 :]
    at = first + rows * (part // 128)
    out_ref[at : at + rows // 2, :] = jnp.concatenate([rest[: rows // 2], rest[rows // 2 :]], axis=1)


def unpack(ref, out_ref, first, row, rows, part):
    if part % 128 != 64:
        out_ref[row : row + rows, :] = ref[first : first + rows, :]
        return
    for i in range(part // 128):
        out_ref[row : row + rows, i * 128 : (i + 1) * 128] = ref[first + i * rows : first + (i + 1) * rows, :]
    at = first + rows * (part // 128)
    rest = ref[at : at + rows // 2, :]
    out_ref[row : row + rows // 2, part - 64 :] = rest[:, :64]
    out_ref[row + rows // 2 : row + rows, part - 64 :] = rest[:, 64:]


def sides_kernel(side, field_ref, sides_ref, copy_ref):
    sides = jnp.concatenate(
        [field_ref[0], field_ref[:, side - 1, :], field_ref[side - 1], field_ref[:, 0, :]], axis=0
    )
    pack(sides, sides_ref)
    copy_ref[...] = field_ref[...]


def shifted_columns(side, part, field, halos, out_ref):
    rows = side * side
    flat = rows + 2 * side
    column = lax.broadcasted_iota(jnp.int32, (flat, part), 0) % side
    if halos is None:
        none = jnp.zeros((side, part), jnp.float32)
        tall = jnp.concatenate([none, field.astype(jnp.float32), none], axis=0)
        west = east = 0.0
    else:
        edge = halos.astype(jnp.float32)
        tall = jnp.concatenate([edge[0:side], field.astype(jnp.float32), edge[2 * side : 3 * side]], axis=0)
        corner = [edge[4 * side + c : 4 * side + c + 1] for c in range(4)]
        spread = lambda col: jnp.broadcast_to(col[:, None, :], (side + 2, side, part)).reshape(flat, part)
        east = spread(jnp.concatenate([corner[1], edge[side : 2 * side], corner[2]], axis=0))
        west = spread(jnp.concatenate([corner[0], edge[3 * side : 4 * side], corner[3]], axis=0))
    out_ref[0] = jnp.where(column == 0, west, pltpu.roll(tall, 1, 0)).astype(jnp.bfloat16)
    out_ref[1] = tall.astype(jnp.bfloat16)
    out_ref[2] = jnp.where(column == side - 1, east, pltpu.roll(tall, flat - 1, 0)).astype(jnp.bfloat16)


class Neighbours:
    def __init__(self, side, tables):
        self.side = side
        self.et, self.eu, self.ct, self.cu = [tables.at[4 * i : 4 * i + 4] for i in range(4)]
        self.digits = turn_tables()
        self.count = lax.axis_size("tile")
        self.own = lax.axis_index("tile")

    def block(self, source):
        groups = self.count // SPAN
        slab = lax.rem(source // SPAN - self.own // SPAN + groups, groups)
        cross = source ^ self.own
        turn = lax.rem(cross // 2, 2)
        even = lax.rem(self.own // SPAN, 2) == 0
        at = jnp.where(slab == 0, turn, jnp.where((slab == 1) == even, 2, 3) + 2 * turn)
        return 6 * lax.rem(cross, 2) + at

    def edge(self, tile, e):
        slot = slot_in(self.digits[e], self.eu[e, tile])
        start = lax.rem(slot, 4) * self.side
        end = start + self.side - 1
        return self.block(self.et[e, tile]), lambda at: jnp.where(slot >= 4, end - at, start + at)

    def corner(self, tile, c):
        slot = slot_in(self.digits[4 + c], self.cu[c, tile])
        return self.block(self.ct[c, tile]), corner_spot(slot, self.side)


def onehot(wanted, width):
    lane = lax.broadcasted_iota(jnp.int32, (wanted.shape[0], width), 1)
    return jnp.where(lane == wanted, 1.0, 0.0).astype(jnp.bfloat16)


def border_onehot_kernel(side, tables_in, cot_in, border_ref, cot_ref, tables, sem):
    copy = pltpu.make_async_copy(tables_in, tables, sem)
    copy.start()
    cot_ref[...] = cot_in[...]
    border_ref[...] = jnp.zeros_like(border_ref)
    copy.wait()
    near = Neighbours(side, tables)
    low = lax.rem(near.own, 2) == 0
    width = 4 * side
    step = lax.broadcasted_iota(jnp.int32, (side, 1), 0)

    def put(row, block, wanted, add=False):
        here = (slice(row, row + side), pl.ds(pl.multiple_of(block * width, 128), width))
        value = onehot(wanted, width)
        border_ref[here] = border_ref[here] + value if add else value

    for m, tile in enumerate((near.own, near.own ^ 1)):
        first = 2 * m * side
        flat = [near.edge(tile, e) for e in range(4)]
        corners = [near.corner(tile, c) for c in range(4)]
        pick = lambda a, b: (jnp.where(low, a[0], b[0]), lambda at: jnp.where(low, a[1](at), b[1](at)))
        block, at = pick(flat[0], flat[2])
        left, right = [
            (jnp.where(low, corners[a][0], corners[b][0]), jnp.where(low, corners[a][1], corners[b][1]))
            for a, b in ((0, 3), (1, 2))
        ]
        along = jnp.where(low, step - 1, step + 1)
        fits = (along >= 0) & (along < side)
        put(first, block, jnp.where(step == 0, -1, at(step - 1)))
        put(first, left[0], jnp.where(step == 0, left[1], -1), add=True)
        put(first + side, flat[3][0], jnp.where(fits, flat[3][1](along), -1))
        put(first + 4 * side, block, at(step))
        put(first + 8 * side, block, jnp.where(step == side - 1, -1, at(step + 1)))
        put(first + 8 * side, right[0], jnp.where(step == side - 1, right[1], -1), add=True)
        put(first + 9 * side, flat[1][0], jnp.where(fits, flat[1][1](along), -1))
        block, at = pick(flat[3], flat[1])
        put(first + 13 * side, block, at(step))


def place_kernel(side, tables_in, place_ref, tables, sem):
    copy = pltpu.make_async_copy(tables_in, tables, sem)
    copy.start()
    copy.wait()
    near = Neighbours(side, tables)
    block = 4 * side + EXTRA
    lane = lax.broadcasted_iota(jnp.int32, (1, block), 1)
    row = lax.broadcasted_iota(jnp.int32, (4 * side, block), 0)
    places = []
    swap = jnp.where(lax.rem(near.own // SPAN, 2) == 0, SPAN, -SPAN)
    for mask in (0, 2, 1, 3):
        for offset in (0, swap, -swap):
            source = lax.rem((near.own ^ mask) + offset + near.count, near.count)
            target = jnp.full((1, block), -1, jnp.int32)
            for e in range(4):
                slot = slot_in(near.digits[e], near.eu[e, source])
                along = lane - e * side
                along = jnp.where(slot >= 4, side - 1 - along, along)
                hit = (lane >= e * side) & (lane < (e + 1) * side) & (near.et[e, source] == near.own)
                target = jnp.where(hit, lax.rem(slot, 4) * side + along, target)
                spot = corner_spot(slot_in(near.digits[4 + e], near.cu[e, source]), side)
                hit = (lane == 4 * side + e) & (near.ct[e, source] == near.own)
                target = jnp.where(hit, spot, target)
            places.append(jnp.where(row == target, 1.0, 0.0))
    place_ref[...] = jnp.concatenate(places, axis=1).astype(jnp.bfloat16)


def tap_product(side, scale, tap, cols, tall):
    rows = side * side
    start = pl.multiple_of((3 - tap // 3) * side, 16)
    value = jnp.dot(
        cols[lax.rem(tap, 3)], tall[pl.ds(start, rows), :], preferred_element_type=jnp.float32
    )
    return value * scale


def send_kernel(
    side, part, scale, field_ref, own_ref, other_ref, send_ref, tall_ref, rim_ref, cols_ref
):
    rows = side * side
    first = lax.axis_index("ch") == 0
    here = slice(2 * side, 2 * side + rows)
    blank = jnp.zeros((2 * side, tall_ref.shape[1]), jnp.bfloat16)
    tall_ref[0 : 2 * side, :] = blank
    tall_ref[2 * side + rows :, :] = blank

    @pl.when(first)
    def _():
        tall_ref[here, 0:part] = own_ref[...]
        tall_ref[here, part:] = other_ref[...]

    @pl.when(jnp.logical_not(first))
    def _():
        tall_ref[here, 0:part] = other_ref[...]
        tall_ref[here, part:] = own_ref[...]

    cot = tall_ref[here, :]
    column = lax.broadcasted_iota(jnp.int32, (rows, part), 0) % side
    field = field_ref[...].reshape(rows, part).astype(jnp.float32)
    cols_ref[0] = jnp.where(column == 0, 0.0, pltpu.roll(field, 1, 0)).astype(jnp.bfloat16).T
    cols_ref[1] = field.astype(jnp.bfloat16).T
    cols_ref[2] = jnp.where(column == side - 1, 0.0, pltpu.roll(field, rows - 1, 0)).astype(jnp.bfloat16).T
    which = 1 - lax.rem(lax.axis_index("tile"), 2)
    for j in range(2):
        send_ref[j * part : (j + 1) * part, :] = tap_product(side, scale, j + 5 * which, cols_ref, tall_ref)
    rim = cot.reshape(side, side, cot.shape[1])
    rim_ref[...] = jnp.concatenate([cot[0:side], cot[rows - side :], rim[:, 0, :], rim[:, side - 1, :]], axis=0)


def half_kernel(side, part, scale, mate, taps, cols, tall, out_ref, middle):
    which = lax.rem(lax.axis_index("tile") + mate, 2)
    for at, j in enumerate(taps):
        out_ref[at * part : (at + 1) * part, :] = tap_product(side, scale, j + 5 * which, cols, tall)
    middle[...] = tap_product(side, scale, 4, cols, tall)
    start = pl.multiple_of(which * (part // 2), 16)
    out_ref[len(taps) * part :, :] = middle[pl.ds(start, part // 2), :]


def unpack_near(near_refs, near, side, part):
    size = packed_shape(4 * side, part)[0]
    row = 0
    for ref in near_refs:
        for k in range(ref.shape[0] // size):
            unpack(ref, near, k * size, row, 4 * side, part)
            row += 4 * side


def border_kernel(side, part, chunk, scale, n_near, *refs):
    near_refs = refs[:n_near]
    onehot_ref, mine_ref, rim_ref, mate_ref, first_ref, second_ref = refs[n_near : n_near + 6]
    outs, near, total = refs[n_near + 6 : -2], refs[-2], refs[-1]
    count = lax.axis_size("tile")
    own = lax.axis_index("tile")
    core = lax.rem(own, 2)
    unpack_near(near_refs, near, side, part)
    half = part // 2
    used = 9 * half

    def place(start, value):
        total[pl.ds(pl.multiple_of(start, 16), value.shape[0]), :] = value

    place(core * half, mine_ref[0 : 2 * part, :] + first_ref[...])
    place(core * half + 2 * part, mine_ref[2 * part : 4 * part, :] + second_ref[0 : 2 * part, :])
    place((1 - core) * 4 * part, mine_ref[4 * part :, :] + second_ref[2 * part :, :])
    total[used:, :] = jnp.zeros((total.shape[0] - used, total.shape[1]), jnp.float32)
    left = jnp.dot(onehot_ref[...], near[...], preferred_element_type=jnp.float32).astype(jnp.bfloat16)

    def rim(ref, at):
        return ref[pl.ds(pl.multiple_of(at, 16), side), :]

    for q in range(4):
        column = (2 + q // 2) * side if q < 3 else (2 + core) * side
        right = jnp.concatenate(
            [value for ref in (rim_ref, mate_ref) for value in (rim(ref, core * side), rim(ref, column))],
            axis=0,
        )
        value = lax.dot_general(
            left[q * 4 * side : (q + 1) * 4 * side],
            right,
            (((0,), (0,)), ((), ())),
            preferred_element_type=jnp.float32,
        )
        if q < 3:
            start = q * part + core * (part // 2 + part)
        else:
            start = 3 * part - core * (3 * part - part // 2)
        here = pl.ds(pl.multiple_of(start, 16), part)
        total[here, :] = total[here, :] + value * scale
    size = outs[0].shape[0]
    for index in range(count // 2):
        to = slot_of_mask(2 * index, count) * chunk
        block = pl.multiple_of(((own // 2) ^ index) * chunk, 16)
        out = outs[to // size]
        out[to % size : to % size + chunk, :] = total[pl.ds(block, chunk), :].astype(out.dtype)


def sum_kernel(n_got, n_out, *refs):
    held_ref, got_refs, outs = refs[0], refs[1 : 1 + n_got], refs[1 + n_got :]
    size = held_ref.shape[0] // n_out
    for index in range(n_out):
        here = slice(index * size, (index + 1) * size)
        value = held_ref[here, :]
        for ref in got_refs:
            value = value + ref[here, :].astype(jnp.float32)
        outs[index][...] = value.astype(outs[index].dtype)


def join_kernel(*refs):
    row = 0
    for ref in refs[:-1]:
        refs[-1][row : row + ref.shape[0], :] = ref[...]
        row += ref.shape[0]


def unfold_kernel(used, chunk, bits, masks, n_dep, *refs):
    refs = refs[n_dep:]
    n = len(masks)
    in_refs, out_ref, wide, sems = refs[:n], refs[n], refs[n + 1], refs[n + 2]
    own = lax.axis_index("tile")
    full, rest = used // chunk, used % chunk
    copies = []
    for i, (ref, inner, bit) in enumerate(zip(in_refs, masks, bits)):
        origin = (lax.rem(own, 2) ^ bit) * used
        for k, mask in enumerate(inner):
            at = i * len(inner) + k
            wide[at] = ref[k * chunk : (k + 1) * chunk, :].astype(jnp.float32)
            block = (own ^ mask) // 2
            start = pl.multiple_of(origin + block * chunk, 16)
            copies.append(
                (
                    block < full,
                    pltpu.make_async_copy(wide.at[at], out_ref.at[pl.ds(start, chunk), :], sems.at[at]),
                )
            )
            if rest:
                start = pl.multiple_of(origin + full * chunk, 16)
                copies.append(
                    (
                        block == full,
                        pltpu.make_async_copy(
                            wide.at[at, 0:rest], out_ref.at[pl.ds(start, rest), :], sems.at[at]
                        ),
                    )
                )
    for going, copy in copies:
        pl.when(going)(copy.start)
    for going, copy in copies:
        pl.when(going)(copy.wait)


def unfold(whole, chunk, bits, masks, blocks, before):
    n_dep = 0 if before is None else 1
    anywhere = pl.BlockSpec(memory_space=pl.ANY)
    n_copies = len(masks) * len(masks[0])
    return pl.pallas_call(
        functools.partial(unfold_kernel, whole.shape[0] // 2, chunk, bits, masks, n_dep),
        out_shape=whole,
        in_specs=[anywhere] * n_dep + [pl.BlockSpec(memory_space=pltpu.VMEM)] * len(blocks),
        out_specs=anywhere,
        scratch_shapes=[
            pltpu.VMEM((n_copies, chunk, whole.shape[1]), jnp.float32),
            pltpu.SemaphoreType.DMA((n_copies,)),
        ],
        input_output_aliases={0: 0} if n_dep else {},
        compiler_params=pltpu.CompilerParams(vmem_limit_bytes=40 * 1024 * 1024),
    )(*([before] if n_dep else []), *blocks)


def back_kernel(side, part, tall, weight_ref, inner_ref, pieces_ref):
    rows = side * side
    flat = rows + 2 * side
    start = pl.multiple_of(lax.axis_index("ch") * part, 16)
    backs = []
    for b in range(3):
        back = jnp.zeros((flat, part), jnp.float32)
        for a in range(3):
            back = back + lax.dot_general(
                tall[(2 - a) * side : (2 - a) * side + flat, :],
                weight_ref[3 * a + b, pl.ds(start, part), :],
                (((1,), (1,)), ((), ())),
                preferred_element_type=jnp.float32,
            )
        backs.append(back)
    column = lax.broadcasted_iota(jnp.int32, (flat, part), 0) % side
    inner = (
        jnp.where(column == side - 1, 0.0, pltpu.roll(backs[0], flat - 1, 0))
        + backs[1]
        + jnp.where(column == 0, 0.0, pltpu.roll(backs[2], 1, 0))
    )
    inner_ref[...] = inner[side : side + rows]
    west = backs[0].reshape(side + 2, side, part)[:, 0, :]
    east = backs[2].reshape(side + 2, side, part)[:, side - 1, :]
    pieces = jnp.concatenate(
        [
            inner[0:side],
            east[1 : side + 1],
            inner[side + rows :],
            west[1 : side + 1],
            west[0:1],
            east[0:1],
            east[side + 1 :],
            west[side + 1 :],
            jnp.zeros((EXTRA - 4, part), jnp.float32),
        ],
        axis=0,
    )
    pack(pieces.astype(jnp.bfloat16), pieces_ref)


def add_halo_kernel(side, part, place_ref, inner_ref, *refs):
    got_refs, out_ref, got = refs[:-2], refs[-2], refs[-1]
    block = 4 * side + EXTRA
    size = packed_shape(block, part)[0]
    for i, ref in enumerate(got_refs):
        for k in range(3):
            unpack(ref, got, k * size, (3 * i + k) * block, block, part)
    sums = jnp.dot(place_ref[...], got[...], preferred_element_type=jnp.float32)
    rows = side * side
    spread = lambda col: jnp.broadcast_to(col[:, None, :], (side, side, part)).reshape(rows, part)
    column = lax.broadcasted_iota(jnp.int32, (rows, part), 0) % side
    inner = inner_ref[...]
    inner = inner + jnp.where(column == side - 1, spread(sums[side : 2 * side]), 0.0)
    inner = inner + jnp.where(column == 0, spread(sums[3 * side :]), 0.0)
    ends = jnp.concatenate(
        [
            inner[0:side] + sums[0:side],
            inner[side : rows - side],
            inner[rows - side :] + sums[2 * side : 3 * side],
        ],
        axis=0,
    )
    out_ref[...] = ends.astype(jnp.bfloat16)


def halo_kernel(side, part, n_near, *refs):
    near_refs, tables_in, field_ref = refs[:n_near], refs[n_near], refs[n_near + 1]
    halos_ref, packet_ref, near, tables, sem = refs[n_near + 2 :]
    copy = pltpu.make_async_copy(tables_in, tables, sem)
    copy.start()
    rows = side * side
    unpack_near(near_refs, near, side, part)
    pack(field_ref[...].reshape(rows, part), packet_ref)
    copy.wait()
    index = Neighbours(side, tables)
    step = lax.broadcasted_iota(jnp.int32, (side, 1), 0)
    wanted = []
    for e in range(4):
        block, at = index.edge(index.own, e)
        wanted.append(block * (4 * side) + at(step))
    spots = lax.broadcasted_iota(jnp.int32, (EXTRA, 1), 0)
    ends = jnp.full((EXTRA, 1), -1, jnp.int32)
    for c in range(4):
        block, spot = index.corner(index.own, c)
        ends = jnp.where(spots == c, block * (4 * side) + spot, ends)
    pick = onehot(jnp.concatenate(wanted + [ends], axis=0), near.shape[0])
    halos = jnp.dot(pick, near[...], preferred_element_type=jnp.float32).astype(jnp.bfloat16)
    halos_ref[...] = halos
    pack(halos, packet_ref, packed_shape(rows, part)[0])


def output_kernel(side, part, field_ref, halos_ref, other_ref, weight_ref, out_ref, cols, other_cols, other):
    rows = side * side
    ch = lax.axis_index("ch")
    wide = -(-part // 128) * 128
    lanes = pl.multiple_of(ch * (weight_ref.shape[2] - wide), 128)
    unpack(other_ref, other, 0, 0, rows, part)
    unpack(other_ref, other, packed_shape(rows, part)[0], rows, 4 * side + EXTRA, part)
    shifted_columns(side, part, field_ref[...].reshape(rows, part), halos_ref[...], cols)
    shifted_columns(side, part, other[0:rows, :], other[rows:, :], other_cols)
    starts = (pl.multiple_of(ch * part, 16), pl.multiple_of((1 - ch) * part, 16))
    total = jnp.zeros((rows, wide), jnp.float32)
    for a in range(3):
        for b in range(3):
            for ref, first in zip((cols, other_cols), starts):
                total = total + jnp.dot(
                    ref[b, a * side : a * side + rows, :],
                    weight_ref[3 * a + b, pl.ds(first, part), pl.ds(lanes, wide)],
                    preferred_element_type=jnp.float32,
                )
    result = jnp.where(ch == 0, total[:, :part], total[:, wide - part :])
    out_ref[...] = result.astype(jnp.bfloat16)


def body(features, weight, cotangent, edge_tiles, edge_turns, corner_tiles, corner_turns):
    count = lax.axis_size("tile")
    field = features[0]
    side, part = field.shape[0], field.shape[2]
    chans = weight.shape[3]
    rows = side * side
    flat = rows + 2 * side
    block = 4 * side + EXTRA
    taps = weight.reshape(9, chans, chans)
    others = [(0, 1), (1, 0)]
    flops = 2 * rows * 9 * part * chans
    half_bytes = jnp.bfloat16
    chunk = -(-9 * part // (16 * count)) * 16
    half = count * chunk // 2
    scale = 1.0 / math.sqrt(count * rows)

    cot_own = cotangent[0].reshape(rows, part)
    cot_other = lax.ppermute(cot_own, "ch", others)
    sides, field = call(
        functools.partial(sides_kernel, side),
        [vmem(packed_shape(4 * side, part), half_bytes), vmem(field.shape, half_bytes)],
        [field],
    )
    swaps = [by_swap(sides, odd, count) for odd in (0, 1)]
    across = by_mask(sides, 2, count)
    tables = jnp.concatenate([edge_tiles.T, edge_turns.T, corner_tiles.T, corner_turns.T], axis=0)
    table_scratch = [pltpu.SMEM(tables.shape, jnp.int32), pltpu.SemaphoreType.DMA]
    border_pick, cot_own = call(
        functools.partial(border_onehot_kernel, side),
        [vmem((16 * side, 48 * side), half_bytes), vmem((rows, part), half_bytes)],
        [tables, cot_own],
        scratch=table_scratch,
    )
    pair = packed_shape(8 * side, part)
    (beyond,) = call(join_kernel, [vmem(pair, half_bytes)], swaps)
    near = [sides, across, *swaps, by_mask(beyond, 2, count)]
    near, cot_other, border_pick = lax.optimization_barrier((near, cot_other, border_pick))
    (near,) = call(join_kernel, [vmem(packed_shape(24 * side, part), half_bytes)], near)
    mates = by_mask(near, 1, count)
    first, tall, rim, cols = call(
        functools.partial(send_kernel, side, part, scale),
        [
            vmem((2 * part, chans), jnp.float32),
            vmem((rows + 4 * side, chans), half_bytes),
            vmem((4 * side, chans), half_bytes),
            vmem((3, part, rows), half_bytes),
        ],
        [field, cot_own, cot_other],
        flops=flops // 4,
    )
    (second,) = call(
        functools.partial(half_kernel, side, part, scale, 1, (2, 3)),
        [vmem((5 * part // 2, chans), jnp.float32)],
        [cols, tall],
        scratch=[pltpu.VMEM((part, chans), jnp.float32)],
        flops=flops,
    )
    tall, second = lax.optimization_barrier((tall, second))
    (mine,) = call(
        functools.partial(half_kernel, side, part, scale, 0, (0, 1, 2, 3)),
        [vmem((9 * part // 2, chans), jnp.float32)],
        [cols, tall],
        scratch=[pltpu.VMEM((part, chans), jnp.float32)],
        costed=False,
    )
    mates, mine, rim_mate = lax.optimization_barrier((mates, mine, by_mask(rim, 1, count)))
    near = [near, mates]

    stages = mask_stages(count)
    masks = group_masks(stages[1])
    size = half // len(masks)
    held, *send = call(
        functools.partial(border_kernel, side, part, chunk, scale, len(near)),
        [vmem((size, chans), jnp.float32)] + [vmem((size, chans), half_bytes)] * (len(masks) - 1),
        [*near, border_pick, mine, rim, rim_mate, by_mask(first, 1, count), by_mask(second, 1, count)],
        scratch=[pltpu.VMEM((48 * side, part), half_bytes), pltpu.VMEM((half, chans), jnp.float32)],
    )
    send, tall, near = lax.optimization_barrier((send, tall, near))
    got = [by_mask(v, m, count) for v, m in zip(send, masks[1:])]
    inner, pieces = call(
        functools.partial(back_kernel, side, part),
        [vmem((rows, part), jnp.float32), vmem(packed_shape(block, part), half_bytes)],
        [tall, taps],
        flops=flops,
    )
    pieces, near = lax.optimization_barrier((pieces, near))
    here = [pieces, *[by_swap(pieces, odd, count) for odd in (0, 1)]]
    (place,) = call(
        functools.partial(place_kernel, side),
        [vmem((4 * side, 12 * block), half_bytes)],
        [tables],
        scratch=table_scratch,
    )
    halos, packet = call(
        functools.partial(halo_kernel, side, part, len(near)),
        [vmem((block, part), half_bytes), vmem(packed_shape(rows + block, part), half_bytes)],
        [*near, tables, field],
        scratch=[pltpu.VMEM((48 * side, part), half_bytes), *table_scratch],
    )
    got, here, inner, halos, packet, place = lax.optimization_barrier(
        (got, here, inner, halos, packet, place)
    )
    for index, bits in enumerate(stages[2:]):
        masks = group_masks(bits)
        size = held.shape[0] // len(masks)
        held, *send = call(
            functools.partial(sum_kernel, len(got), len(masks)),
            [vmem((size, chans), jnp.float32)] + [vmem((size, chans), half_bytes)] * (len(masks) - 1),
            [held, *got],
        )
        if index == 0:
            send, here = lax.optimization_barrier((send, here))
        got = [by_mask(v, m, count) for v, m in zip(send, masks[1:])]
        if index == 0:
            (here,) = call(join_kernel, [vmem((3 * pieces.shape[0], pieces.shape[1]), half_bytes)], here)
            beside = by_mask(here, 2, count)
            other_field = lax.ppermute(packet, "ch", others)
            got, here = lax.optimization_barrier((got, here))
    (held,) = call(functools.partial(sum_kernel, len(got), 1), [vmem(held.shape, half_bytes)], [held, *got])
    order = [0]
    for index, bits in enumerate(stages[:0:-1]):
        masks = group_masks(bits)
        got = [by_mask(held, m, count) for m in masks[1:]]
        if index == 0:
            held, got, beside = lax.optimization_barrier((held, got, beside))
        if index < len(stages) - 2:
            order = [m + v for m in masks for v in order]
            (held,) = call(
                join_kernel, [vmem((held.shape[0] * len(masks), chans), half_bytes)], [held, *got]
            )
            continue
        got_pieces = [here, beside, by_mask(here, 1, count), by_mask(beside, 1, count)]
        (grad_features,) = call(
            functools.partial(add_halo_kernel, side, part),
            [vmem((rows, part), half_bytes)],
            [place, inner, *got_pieces],
            scratch=[pltpu.VMEM((12 * block, part), half_bytes)],
        )
        (output,) = call(
            functools.partial(output_kernel, side, part),
            [vmem((rows, part), half_bytes)],
            [field, halos, other_field, taps],
            scratch=[
                pltpu.VMEM((3, flat, part), half_bytes),
                pltpu.VMEM((3, flat, part), half_bytes),
                pltpu.VMEM((rows + block, part), half_bytes),
            ],
            flops=2 * flops,
        )
        got, grad_features, output = lax.optimization_barrier((got, grad_features, output))
        got = [held, *got]
        order = [[m + v for v in order] for m in masks]
    mates = [by_mask(v, 1, count) for v in got]
    whole = vmem((9 * part, chans), jnp.float32)
    own = len(got)
    first = unfold(whole, chunk, [0] * own + [1], order + order[:1], got + mates[:1], None)
    grad_weight = unfold(whole, chunk, [1] * (own - 1), order[1:], mates[1:], first)
    shape = (1, side, side, part)
    return (
        output.reshape(shape),
        grad_features.reshape(shape),
        grad_weight.reshape(3, 3, part, chans),
    )


def solution(mesh):
    return jax.shard_map(
        body,
        mesh=mesh,
        in_specs=(
            P("tile", None, None, "ch"),
            P(),
            P("tile", None, None, "ch"),
            P(),
            P(),
            P(),
            P(),
        ),
        out_specs=(
            P("tile", None, None, "ch"),
            P("tile", None, None, "ch"),
            P(None, None, "ch", None),
        ),
        check_vma=False,
    )
```

```python
import functools
import math

import jax
import jax.numpy as jnp
import numpy as np
from jax import lax
from jax.experimental import pallas as pl
from jax.experimental.pallas import tpu as pltpu
from jax.sharding import PartitionSpec as P

SPAN = 4
EXTRA = 16


def turn_tables():
    labels = [[3 * row + col for col in range(3)] for row in range(3)]

    def turn_once(block):
        return [[block[col][2 - row] for col in range(3)] for row in range(3)]

    def sides_of(block):
        return [
            list(block[0]),
            [block[row][2] for row in range(3)],
            list(block[2]),
            [block[row][0] for row in range(3)],
        ]

    def corners_of(block):
        return [block[0][0], block[0][2], block[2][2], block[2][0]]

    base_sides = sides_of(labels)
    base_corners = corners_of(labels)
    edge_table = np.zeros((4, 4), np.int32)
    corner_table = np.zeros((4, 4), np.int32)
    for border in range(4):
        turned = labels
        for quarter in range(4):
            wanted = sides_of(turned)[(border + 2) % 4]
            for side_index in range(4):
                if base_sides[side_index] == wanted:
                    edge_table[border, quarter] = side_index
                if base_sides[side_index][::-1] == wanted:
                    edge_table[border, quarter] = side_index + 4
            corner_cell = corners_of(turned)[(border + 2) % 4]
            for corner_index in range(4):
                if base_corners[corner_index] == corner_cell:
                    corner_table[border, quarter] = corner_index
            turned = turn_once(turned)
    tables = np.concatenate([edge_table, corner_table], axis=0)
    return [sum(int(slot) << (3 * quarter) for quarter, slot in enumerate(row)) for row in tables]


def by_swap(value, odd, count):
    pairs = [
        (i, (i + (SPAN if (i // SPAN) % 2 == odd else -SPAN)) % count) for i in range(count)
    ]
    return lax.ppermute(value, "tile", pairs)


def by_mask(value, mask, count):
    return lax.ppermute(value, "tile", [(i, i ^ mask) for i in range(count)])


def mask_stages(count):
    bits = [1 << b for b in range(count.bit_length() - 1)]
    stages = [bits[:1]]
    rest = bits[1:]
    while rest:
        stages.append(rest[:2])
        rest = rest[2:]
    return stages


def group_masks(bits):
    masks = [0]
    for bit in bits:
        masks = masks + [m + bit for m in masks]
    return masks


def slot_of_mask(mask, count):
    place = 0
    for bits in mask_stages(count)[1:]:
        size = 1 << len(bits)
        place = place * size + (mask // bits[0]) % size
    return place


def slot_in(row, quarter):
    return (row >> (3 * quarter)) & 7


def corner_spot(slot, side):
    return jnp.where(
        slot == 0, 0, jnp.where(slot == 1, side - 1, jnp.where(slot == 2, 3 * side - 1, 2 * side))
    )


def vmem(shape, dtype):
    return jax.ShapeDtypeStruct(shape, dtype)


def call(kernel, outs, args, anywhere=(), scratch=(), flops=0, costed=True):
    in_specs = [
        pl.BlockSpec(memory_space=pltpu.HBM if i in anywhere else pltpu.VMEM) for i in range(len(args))
    ]
    size = costed * sum(math.prod(x.shape) * x.dtype.itemsize for x in list(args) + list(outs))
    return pl.pallas_call(
        kernel,
        out_shape=tuple(outs),
        in_specs=in_specs,
        out_specs=tuple(pl.BlockSpec(memory_space=pltpu.VMEM) for _ in outs),
        scratch_shapes=list(scratch),
        compiler_params=pltpu.CompilerParams(vmem_limit_bytes=40 * 1024 * 1024),
        cost_estimate=pl.CostEstimate(flops=flops, bytes_accessed=size, transcendentals=0),
    )(*args)


def packed_shape(rows, part):
    if part % 128 != 64:
        return (rows, part)
    return (rows * (part // 128) + rows // 2, 128)


def pack(value, out_ref, first=0):
    rows, part = value.shape
    if part % 128 != 64:
        out_ref[first : first + rows, :] = value
        return
    for i in range(part // 128):
        out_ref[first + i * rows : first + (i + 1) * rows, :] = value[:, i * 128 : (i + 1) * 128]
    rest = value[:, part - 64 :]
    at = first + rows * (part // 128)
    out_ref[at : at + rows // 2, :] = jnp.concatenate([rest[: rows // 2], rest[rows // 2 :]], axis=1)


def unpack(ref, out_ref, first, row, rows, part):
    if part % 128 != 64:
        out_ref[row : row + rows, :] = ref[first : first + rows, :]
        return
    for i in range(part // 128):
        out_ref[row : row + rows, i * 128 : (i + 1) * 128] = ref[first + i * rows : first + (i + 1) * rows, :]
    at = first + rows * (part // 128)
    rest = ref[at : at + rows // 2, :]
    out_ref[row : row + rows // 2, part - 64 :] = rest[:, :64]
    out_ref[row + rows // 2 : row + rows, part - 64 :] = rest[:, 64:]


def sides_kernel(side, field_ref, sides_ref, copy_ref):
    sides = jnp.concatenate(
        [field_ref[0], field_ref[:, side - 1, :], field_ref[side - 1], field_ref[:, 0, :]], axis=0
    )
    pack(sides, sides_ref)
    copy_ref[...] = field_ref[...]


def shifted_columns(side, part, field, halos, out_ref):
    rows = side * side
    flat = rows + 2 * side
    column = lax.broadcasted_iota(jnp.int32, (flat, part), 0) % side
    if halos is None:
        none = jnp.zeros((side, part), jnp.float32)
        tall = jnp.concatenate([none, field.astype(jnp.float32), none], axis=0)
        west = east = 0.0
    else:
        edge = halos.astype(jnp.float32)
        tall = jnp.concatenate([edge[0:side], field.astype(jnp.float32), edge[2 * side : 3 * side]], axis=0)
        corner = [edge[4 * side + c : 4 * side + c + 1] for c in range(4)]
        spread = lambda col: jnp.broadcast_to(col[:, None, :], (side + 2, side, part)).reshape(flat, part)
        east = spread(jnp.concatenate([corner[1], edge[side : 2 * side], corner[2]], axis=0))
        west = spread(jnp.concatenate([corner[0], edge[3 * side : 4 * side], corner[3]], axis=0))
    out_ref[0] = jnp.where(column == 0, west, pltpu.roll(tall, 1, 0)).astype(jnp.bfloat16)
    out_ref[1] = tall.astype(jnp.bfloat16)
    out_ref[2] = jnp.where(column == side - 1, east, pltpu.roll(tall, flat - 1, 0)).astype(jnp.bfloat16)


class Neighbours:
    def __init__(self, side, tables):
        self.side = side
        self.et, self.eu, self.ct, self.cu = [tables.at[4 * i : 4 * i + 4] for i in range(4)]
        self.digits = turn_tables()
        self.count = lax.axis_size("tile")
        self.own = lax.axis_index("tile")

    def block(self, source):
        groups = self.count // SPAN
        slab = lax.rem(source // SPAN - self.own // SPAN + groups, groups)
        cross = source ^ self.own
        turn = lax.rem(cross // 2, 2)
        even = lax.rem(self.own // SPAN, 2) == 0
        at = jnp.where(slab == 0, turn, jnp.where((slab == 1) == even, 2, 3) + 2 * turn)
        return 6 * lax.rem(cross, 2) + at

    def edge(self, tile, e):
        slot = slot_in(self.digits[e], self.eu[e, tile])
        start = lax.rem(slot, 4) * self.side
        end = start + self.side - 1
        return self.block(self.et[e, tile]), lambda at: jnp.where(slot >= 4, end - at, start + at)

    def corner(self, tile, c):
        slot = slot_in(self.digits[4 + c], self.cu[c, tile])
        return self.block(self.ct[c, tile]), corner_spot(slot, self.side)


def onehot(wanted, width):
    lane = lax.broadcasted_iota(jnp.int32, (wanted.shape[0], width), 1)
    return jnp.where(lane == wanted, 1.0, 0.0).astype(jnp.bfloat16)


def border_onehot_kernel(side, tables_in, cot_in, border_ref, cot_ref, tables, sem):
    copy = pltpu.make_async_copy(tables_in, tables, sem)
    copy.start()
    cot_ref[...] = cot_in[...]
    border_ref[...] = jnp.zeros_like(border_ref)
    copy.wait()
    near = Neighbours(side, tables)
    low = lax.rem(near.own, 2) == 0
    width = 4 * side
    step = lax.broadcasted_iota(jnp.int32, (side, 1), 0)

    def put(row, block, wanted, add=False):
        here = (slice(row, row + side), pl.ds(pl.multiple_of(block * width, 128), width))
        value = onehot(wanted, width)
        border_ref[here] = border_ref[here] + value if add else value

    for m, tile in enumerate((near.own, near.own ^ 1)):
        first = 2 * m * side
        flat = [near.edge(tile, e) for e in range(4)]
        corners = [near.corner(tile, c) for c in range(4)]
        pick = lambda a, b: (jnp.where(low, a[0], b[0]), lambda at: jnp.where(low, a[1](at), b[1](at)))
        block, at = pick(flat[0], flat[2])
        left, right = [
            (jnp.where(low, corners[a][0], corners[b][0]), jnp.where(low, corners[a][1], corners[b][1]))
            for a, b in ((0, 3), (1, 2))
        ]
        along = jnp.where(low, step - 1, step + 1)
        fits = (along >= 0) & (along < side)
        put(first, block, jnp.where(step == 0, -1, at(step - 1)))
        put(first, left[0], jnp.where(step == 0, left[1], -1), add=True)
        put(first + side, flat[3][0], jnp.where(fits, flat[3][1](along), -1))
        put(first + 4 * side, block, at(step))
        put(first + 8 * side, block, jnp.where(step == side - 1, -1, at(step + 1)))
        put(first + 8 * side, right[0], jnp.where(step == side - 1, right[1], -1), add=True)
        put(first + 9 * side, flat[1][0], jnp.where(fits, flat[1][1](along), -1))
        block, at = pick(flat[3], flat[1])
        put(first + 13 * side, block, at(step))


def place_kernel(side, tables_in, place_ref, tables, sem):
    copy = pltpu.make_async_copy(tables_in, tables, sem)
    copy.start()
    copy.wait()
    near = Neighbours(side, tables)
    block = 4 * side + EXTRA
    lane = lax.broadcasted_iota(jnp.int32, (1, block), 1)
    row = lax.broadcasted_iota(jnp.int32, (4 * side, block), 0)
    places = []
    swap = jnp.where(lax.rem(near.own // SPAN, 2) == 0, SPAN, -SPAN)
    for mask in (0, 2, 1, 3):
        for offset in (0, swap, -swap):
            source = lax.rem((near.own ^ mask) + offset + near.count, near.count)
            target = jnp.full((1, block), -1, jnp.int32)
            for e in range(4):
                slot = slot_in(near.digits[e], near.eu[e, source])
                along = lane - e * side
                along = jnp.where(slot >= 4, side - 1 - along, along)
                hit = (lane >= e * side) & (lane < (e + 1) * side) & (near.et[e, source] == near.own)
                target = jnp.where(hit, lax.rem(slot, 4) * side + along, target)
                spot = corner_spot(slot_in(near.digits[4 + e], near.cu[e, source]), side)
                hit = (lane == 4 * side + e) & (near.ct[e, source] == near.own)
                target = jnp.where(hit, spot, target)
            places.append(jnp.where(row == target, 1.0, 0.0))
    place_ref[...] = jnp.concatenate(places, axis=1).astype(jnp.bfloat16)


def tap_product(side, scale, tap, cols, tall):
    rows = side * side
    start = pl.multiple_of((3 - tap // 3) * side, 16)
    value = jnp.dot(
        cols[lax.rem(tap, 3)], tall[pl.ds(start, rows), :], preferred_element_type=jnp.float32
    )
    return value * scale


def send_kernel(
    side, part, scale, field_ref, own_ref, other_ref, send_ref, tall_ref, rim_ref, cols_ref
):
    rows = side * side
    first = lax.axis_index("ch") == 0
    here = slice(2 * side, 2 * side + rows)
    blank = jnp.zeros((2 * side, tall_ref.shape[1]), jnp.bfloat16)
    tall_ref[0 : 2 * side, :] = blank
    tall_ref[2 * side + rows :, :] = blank

    @pl.when(first)
    def _():
        tall_ref[here, 0:part] = own_ref[...]
        tall_ref[here, part:] = other_ref[...]

    @pl.when(jnp.logical_not(first))
    def _():
        tall_ref[here, 0:part] = other_ref[...]
        tall_ref[here, part:] = own_ref[...]

    cot = tall_ref[here, :]
    column = lax.broadcasted_iota(jnp.int32, (rows, part), 0) % side
    field = field_ref[...].reshape(rows, part).astype(jnp.float32)
    cols_ref[0] = jnp.where(column == 0, 0.0, pltpu.roll(field, 1, 0)).astype(jnp.bfloat16).T
    cols_ref[1] = field.astype(jnp.bfloat16).T
    cols_ref[2] = jnp.where(column == side - 1, 0.0, pltpu.roll(field, rows - 1, 0)).astype(jnp.bfloat16).T
    which = 1 - lax.rem(lax.axis_index("tile"), 2)
    for j in range(2):
        send_ref[j * part : (j + 1) * part, :] = tap_product(side, scale, j + 5 * which, cols_ref, tall_ref)
    rim = cot.reshape(side, side, cot.shape[1])
    rim_ref[...] = jnp.concatenate([cot[0:side], cot[rows - side :], rim[:, 0, :], rim[:, side - 1, :]], axis=0)


def half_kernel(side, part, scale, mate, taps, cols, tall, out_ref, middle):
    which = lax.rem(lax.axis_index("tile") + mate, 2)
    for at, j in enumerate(taps):
        out_ref[at * part : (at + 1) * part, :] = tap_product(side, scale, j + 5 * which, cols, tall)
    middle[...] = tap_product(side, scale, 4, cols, tall)
    start = pl.multiple_of(which * (part // 2), 16)
    out_ref[len(taps) * part :, :] = middle[pl.ds(start, part // 2), :]


def unpack_near(near_refs, near, side, part):
    size = packed_shape(4 * side, part)[0]
    row = 0
    for ref in near_refs:
        for k in range(ref.shape[0] // size):
            unpack(ref, near, k * size, row, 4 * side, part)
            row += 4 * side


def border_kernel(side, part, chunk, scale, n_near, *refs):
    near_refs = refs[:n_near]
    onehot_ref, mine_ref, rim_ref, mate_ref, first_ref, second_ref = refs[n_near : n_near + 6]
    outs, near, total = refs[n_near + 6 : -2], refs[-2], refs[-1]
    count = lax.axis_size("tile")
    own = lax.axis_index("tile")
    core = lax.rem(own, 2)
    unpack_near(near_refs, near, side, part)
    half = part // 2
    used = 9 * half

    def place(start, value):
        total[pl.ds(pl.multiple_of(start, 16), value.shape[0]), :] = value

    place(core * half, mine_ref[0 : 2 * part, :] + first_ref[...])
    place(core * half + 2 * part, mine_ref[2 * part : 4 * part, :] + second_ref[0 : 2 * part, :])
    place((1 - core) * 4 * part, mine_ref[4 * part :, :] + second_ref[2 * part :, :])
    total[used:, :] = jnp.zeros((total.shape[0] - used, total.shape[1]), jnp.float32)
    left = jnp.dot(onehot_ref[...], near[...], preferred_element_type=jnp.float32).astype(jnp.bfloat16)

    def rim(ref, at):
        return ref[pl.ds(pl.multiple_of(at, 16), side), :]

    for q in range(4):
        column = (2 + q // 2) * side if q < 3 else (2 + core) * side
        right = jnp.concatenate(
            [value for ref in (rim_ref, mate_ref) for value in (rim(ref, core * side), rim(ref, column))],
            axis=0,
        )
        value = lax.dot_general(
            left[q * 4 * side : (q + 1) * 4 * side],
            right,
            (((0,), (0,)), ((), ())),
            preferred_element_type=jnp.float32,
        )
        if q < 3:
            start = q * part + core * (part // 2 + part)
        else:
            start = 3 * part - core * (3 * part - part // 2)
        here = pl.ds(pl.multiple_of(start, 16), part)
        total[here, :] = total[here, :] + value * scale
    size = outs[0].shape[0]
    for index in range(count // 2):
        to = slot_of_mask(2 * index, count) * chunk
        block = pl.multiple_of(((own // 2) ^ index) * chunk, 16)
        out = outs[to // size]
        out[to % size : to % size + chunk, :] = total[pl.ds(block, chunk), :].astype(out.dtype)


def sum_kernel(n_got, n_out, *refs):
    held_ref, got_refs, outs = refs[0], refs[1 : 1 + n_got], refs[1 + n_got :]
    size = held_ref.shape[0] // n_out
    for index in range(n_out):
        here = slice(index * size, (index + 1) * size)
        value = held_ref[here, :]
        for ref in got_refs:
            value = value + ref[here, :].astype(jnp.float32)
        outs[index][...] = value.astype(outs[index].dtype)


def exchange_kernel(held_ref, got_ref, out_ref):
    half = held_ref.shape[0] // 2
    for a, b in ((0, half), (half, 0)):
        value = held_ref[a : a + half, :].astype(jnp.float32) + got_ref[b : b + half, :].astype(jnp.float32)
        out_ref[a : a + half, :] = value.astype(out_ref.dtype)


def join_kernel(*refs):
    row = 0
    for ref in refs[:-1]:
        refs[-1][row : row + ref.shape[0], :] = ref[...]
        row += ref.shape[0]


def unfold_kernel(used, chunk, bits, masks, n_dep, *refs):
    refs = refs[n_dep:]
    n = len(masks)
    in_refs, out_ref, wide, sems = refs[:n], refs[n], refs[n + 1], refs[n + 2]
    own = lax.axis_index("tile")
    full, rest = used // chunk, used % chunk
    copies = []
    for i, (ref, inner, bit) in enumerate(zip(in_refs, masks, bits)):
        origin = (lax.rem(own, 2) ^ bit) * used
        for k, mask in enumerate(inner):
            at = i * len(inner) + k
            wide[at] = ref[k * chunk : (k + 1) * chunk, :].astype(jnp.float32)
            block = (own ^ mask) // 2
            start = pl.multiple_of(origin + block * chunk, 16)
            copies.append(
                (
                    block < full,
                    pltpu.make_async_copy(wide.at[at], out_ref.at[pl.ds(start, chunk), :], sems.at[at]),
                )
            )
            if rest:
                start = pl.multiple_of(origin + full * chunk, 16)
                copies.append(
                    (
                        block == full,
                        pltpu.make_async_copy(
                            wide.at[at, 0:rest], out_ref.at[pl.ds(start, rest), :], sems.at[at]
                        ),
                    )
                )
    for going, copy in copies:
        pl.when(going)(copy.start)
    for going, copy in copies:
        pl.when(going)(copy.wait)


def unfold(whole, chunk, bits, masks, blocks, before):
    n_dep = 0 if before is None else 1
    anywhere = pl.BlockSpec(memory_space=pl.ANY)
    n_copies = len(masks) * len(masks[0])
    return pl.pallas_call(
        functools.partial(unfold_kernel, whole.shape[0] // 2, chunk, bits, masks, n_dep),
        out_shape=whole,
        in_specs=[anywhere] * n_dep + [pl.BlockSpec(memory_space=pltpu.VMEM)] * len(blocks),
        out_specs=anywhere,
        scratch_shapes=[
            pltpu.VMEM((n_copies, chunk, whole.shape[1]), jnp.float32),
            pltpu.SemaphoreType.DMA((n_copies,)),
        ],
        input_output_aliases={0: 0} if n_dep else {},
        compiler_params=pltpu.CompilerParams(vmem_limit_bytes=40 * 1024 * 1024),
    )(*([before] if n_dep else []), *blocks)


def back_kernel(side, part, tall, weight_ref, inner_ref, pieces_ref):
    rows = side * side
    flat = rows + 2 * side
    start = pl.multiple_of(lax.axis_index("ch") * part, 16)
    backs = []
    for b in range(3):
        back = jnp.zeros((flat, part), jnp.float32)
        for a in range(3):
            back = back + lax.dot_general(
                tall[(2 - a) * side : (2 - a) * side + flat, :],
                weight_ref[3 * a + b, pl.ds(start, part), :],
                (((1,), (1,)), ((), ())),
                preferred_element_type=jnp.float32,
            )
        backs.append(back)
    column = lax.broadcasted_iota(jnp.int32, (flat, part), 0) % side
    inner = (
        jnp.where(column == side - 1, 0.0, pltpu.roll(backs[0], flat - 1, 0))
        + backs[1]
        + jnp.where(column == 0, 0.0, pltpu.roll(backs[2], 1, 0))
    )
    inner_ref[...] = inner[side : side + rows]
    west = backs[0].reshape(side + 2, side, part)[:, 0, :]
    east = backs[2].reshape(side + 2, side, part)[:, side - 1, :]
    pieces = jnp.concatenate(
        [
            inner[0:side],
            east[1 : side + 1],
            inner[side + rows :],
            west[1 : side + 1],
            west[0:1],
            east[0:1],
            east[side + 1 :],
            west[side + 1 :],
            jnp.zeros((EXTRA - 4, part), jnp.float32),
        ],
        axis=0,
    )
    pack(pieces.astype(jnp.bfloat16), pieces_ref)


def add_halo_kernel(side, part, place_ref, inner_ref, *refs):
    got_refs, out_ref, got = refs[:-2], refs[-2], refs[-1]
    block = 4 * side + EXTRA
    size = packed_shape(block, part)[0]
    for i, ref in enumerate(got_refs):
        for k in range(3):
            unpack(ref, got, k * size, (3 * i + k) * block, block, part)
    sums = jnp.dot(place_ref[...], got[...], preferred_element_type=jnp.float32)
    rows = side * side
    spread = lambda col: jnp.broadcast_to(col[:, None, :], (side, side, part)).reshape(rows, part)
    column = lax.broadcasted_iota(jnp.int32, (rows, part), 0) % side
    inner = inner_ref[...]
    inner = inner + jnp.where(column == side - 1, spread(sums[side : 2 * side]), 0.0)
    inner = inner + jnp.where(column == 0, spread(sums[3 * side :]), 0.0)
    ends = jnp.concatenate(
        [
            inner[0:side] + sums[0:side],
            inner[side : rows - side],
            inner[rows - side :] + sums[2 * side : 3 * side],
        ],
        axis=0,
    )
    out_ref[...] = ends.astype(jnp.bfloat16)


def halo_kernel(side, part, n_near, *refs):
    near_refs, tables_in, field_ref = refs[:n_near], refs[n_near], refs[n_near + 1]
    halos_ref, packet_ref, near, tables, sem = refs[n_near + 2 :]
    copy = pltpu.make_async_copy(tables_in, tables, sem)
    copy.start()
    rows = side * side
    unpack_near(near_refs, near, side, part)
    pack(field_ref[...].reshape(rows, part), packet_ref)
    copy.wait()
    index = Neighbours(side, tables)
    step = lax.broadcasted_iota(jnp.int32, (side, 1), 0)
    wanted = []
    for e in range(4):
        block, at = index.edge(index.own, e)
        wanted.append(block * (4 * side) + at(step))
    spots = lax.broadcasted_iota(jnp.int32, (EXTRA, 1), 0)
    ends = jnp.full((EXTRA, 1), -1, jnp.int32)
    for c in range(4):
        block, spot = index.corner(index.own, c)
        ends = jnp.where(spots == c, block * (4 * side) + spot, ends)
    pick = onehot(jnp.concatenate(wanted + [ends], axis=0), near.shape[0])
    halos = jnp.dot(pick, near[...], preferred_element_type=jnp.float32).astype(jnp.bfloat16)
    halos_ref[...] = halos
    pack(halos, packet_ref, packed_shape(rows, part)[0])


def output_kernel(side, part, field_ref, halos_ref, other_ref, weight_ref, out_ref, cols, other_cols, other):
    rows = side * side
    ch = lax.axis_index("ch")
    wide = -(-part // 128) * 128
    lanes = pl.multiple_of(ch * (weight_ref.shape[2] - wide), 128)
    unpack(other_ref, other, 0, 0, rows, part)
    unpack(other_ref, other, packed_shape(rows, part)[0], rows, 4 * side + EXTRA, part)
    shifted_columns(side, part, field_ref[...].reshape(rows, part), halos_ref[...], cols)
    shifted_columns(side, part, other[0:rows, :], other[rows:, :], other_cols)
    starts = (pl.multiple_of(ch * part, 16), pl.multiple_of((1 - ch) * part, 16))
    total = jnp.zeros((rows, wide), jnp.float32)
    for a in range(3):
        for b in range(3):
            for ref, first in zip((cols, other_cols), starts):
                total = total + jnp.dot(
                    ref[b, a * side : a * side + rows, :],
                    weight_ref[3 * a + b, pl.ds(first, part), pl.ds(lanes, wide)],
                    preferred_element_type=jnp.float32,
                )
    result = jnp.where(ch == 0, total[:, :part], total[:, wide - part :])
    out_ref[...] = result.astype(jnp.bfloat16)


def body(features, weight, cotangent, edge_tiles, edge_turns, corner_tiles, corner_turns):
    count = lax.axis_size("tile")
    field = features[0]
    side, part = field.shape[0], field.shape[2]
    chans = weight.shape[3]
    rows = side * side
    flat = rows + 2 * side
    block = 4 * side + EXTRA
    taps = weight.reshape(9, chans, chans)
    others = [(0, 1), (1, 0)]
    flops = 2 * rows * 9 * part * chans
    half_bytes = jnp.bfloat16
    chunk = -(-9 * part // (16 * count)) * 16
    half = count * chunk // 2
    scale = 1.0 / math.sqrt(count * rows)

    cot_own = cotangent[0].reshape(rows, part)
    cot_other = lax.ppermute(cot_own, "ch", others)
    sides, field = call(
        functools.partial(sides_kernel, side),
        [vmem(packed_shape(4 * side, part), half_bytes), vmem(field.shape, half_bytes)],
        [field],
    )
    swaps = [by_swap(sides, odd, count) for odd in (0, 1)]
    across = by_mask(sides, 2, count)
    tables = jnp.concatenate([edge_tiles.T, edge_turns.T, corner_tiles.T, corner_turns.T], axis=0)
    table_scratch = [pltpu.SMEM(tables.shape, jnp.int32), pltpu.SemaphoreType.DMA]
    border_pick, cot_own = call(
        functools.partial(border_onehot_kernel, side),
        [vmem((16 * side, 48 * side), half_bytes), vmem((rows, part), half_bytes)],
        [tables, cot_own],
        scratch=table_scratch,
    )
    pair = packed_shape(8 * side, part)
    (beyond,) = call(join_kernel, [vmem(pair, half_bytes)], swaps)
    near = [sides, across, *swaps, by_mask(beyond, 2, count)]
    near, cot_other, border_pick = lax.optimization_barrier((near, cot_other, border_pick))
    (near,) = call(join_kernel, [vmem(packed_shape(24 * side, part), half_bytes)], near)
    mates = by_mask(near, 1, count)
    first, tall, rim, cols = call(
        functools.partial(send_kernel, side, part, scale),
        [
            vmem((2 * part, chans), jnp.float32),
            vmem((rows + 4 * side, chans), half_bytes),
            vmem((4 * side, chans), half_bytes),
            vmem((3, part, rows), half_bytes),
        ],
        [field, cot_own, cot_other],
        flops=flops // 4,
    )
    (second,) = call(
        functools.partial(half_kernel, side, part, scale, 1, (2, 3)),
        [vmem((5 * part // 2, chans), jnp.float32)],
        [cols, tall],
        scratch=[pltpu.VMEM((part, chans), jnp.float32)],
        flops=flops,
    )
    tall, second = lax.optimization_barrier((tall, second))
    (mine,) = call(
        functools.partial(half_kernel, side, part, scale, 0, (0, 1, 2, 3)),
        [vmem((9 * part // 2, chans), jnp.float32)],
        [cols, tall],
        scratch=[pltpu.VMEM((part, chans), jnp.float32)],
        costed=False,
    )
    mates, mine, rim_mate = lax.optimization_barrier((mates, mine, by_mask(rim, 1, count)))
    near = [near, mates]

    stages = mask_stages(count)
    masks = group_masks(stages[1])
    size = half // len(masks)
    held, *send = call(
        functools.partial(border_kernel, side, part, chunk, scale, len(near)),
        [vmem((size, chans), jnp.float32)] + [vmem((size, chans), half_bytes)] * (len(masks) - 1),
        [*near, border_pick, mine, rim, rim_mate, by_mask(first, 1, count), by_mask(second, 1, count)],
        scratch=[pltpu.VMEM((48 * side, part), half_bytes), pltpu.VMEM((half, chans), jnp.float32)],
    )
    send, tall, near = lax.optimization_barrier((send, tall, near))
    got = [by_mask(v, m, count) for v, m in zip(send, masks[1:])]
    inner, pieces = call(
        functools.partial(back_kernel, side, part),
        [vmem((rows, part), jnp.float32), vmem(packed_shape(block, part), half_bytes)],
        [tall, taps],
        flops=flops,
    )
    pieces, near = lax.optimization_barrier((pieces, near))
    here = [pieces, *[by_swap(pieces, odd, count) for odd in (0, 1)]]
    (place,) = call(
        functools.partial(place_kernel, side),
        [vmem((4 * side, 12 * block), half_bytes)],
        [tables],
        scratch=table_scratch,
    )
    halos, packet = call(
        functools.partial(halo_kernel, side, part, len(near)),
        [vmem((block, part), half_bytes), vmem(packed_shape(rows + block, part), half_bytes)],
        [*near, tables, field],
        scratch=[pltpu.VMEM((48 * side, part), half_bytes), *table_scratch],
    )
    got, here, inner, halos, packet, place = lax.optimization_barrier(
        (got, here, inner, halos, packet, place)
    )
    swap = len(stages[-1]) == 1 and len(stages) > 2
    rs_stages = stages[2:-1] if swap else stages[2:]
    aside = [here, packet]

    def start_aside(send, aside):
        send, here, packet = lax.optimization_barrier((send, *aside))
        (here,) = call(join_kernel, [vmem((3 * pieces.shape[0], pieces.shape[1]), half_bytes)], here)
        return send, here, by_mask(here, 2, count), lax.ppermute(packet, "ch", others)

    for index, bits in enumerate(rs_stages):
        masks = group_masks(bits)
        size = held.shape[0] // len(masks)
        held, *send = call(
            functools.partial(sum_kernel, len(got), len(masks)),
            [vmem((size, chans), jnp.float32)] + [vmem((size, chans), half_bytes)] * (len(masks) - 1),
            [held, *got],
        )
        if index == 0:
            send, here, beside, other_field = start_aside(send, aside)
        got = [by_mask(v, m, count) for v, m in zip(send, masks[1:])]
    (held,) = call(functools.partial(sum_kernel, len(got), 1), [vmem(held.shape, half_bytes)], [held, *got])
    def add_halos(here, beside):
        got_pieces = [here, beside, by_mask(here, 1, count), by_mask(beside, 1, count)]
        return call(
            functools.partial(add_halo_kernel, side, part),
            [vmem((rows, part), half_bytes)],
            [place, inner, *got_pieces],
            scratch=[pltpu.VMEM((12 * block, part), half_bytes)],
        )[0]

    if swap:
        if not rs_stages:
            held, here, beside, other_field = start_aside(held, aside)
        got = by_mask(held, stages[-1][0], count)
        got, grad_features = lax.optimization_barrier((got, add_halos(here, beside)))
        (held,) = call(exchange_kernel, [vmem(held.shape, half_bytes)], [held, got])
    else:
        grad_features = add_halos(here, beside)
    order = [0] if not swap else [0, stages[-1][0]]
    ag_stages = stages[-2:0:-1] if swap else stages[:0:-1]
    for index, bits in enumerate(ag_stages):
        masks = group_masks(bits)
        got = [by_mask(held, m, count) for m in masks[1:]]
        if index < len(ag_stages) - 1:
            order = [m + v for m in masks for v in order]
            (held,) = call(
                join_kernel, [vmem((held.shape[0] * len(masks), chans), half_bytes)], [held, *got]
            )
    order = [[m + v for v in order] for m in masks]
    (output,) = call(
        functools.partial(output_kernel, side, part),
        [vmem((rows, part), half_bytes)],
        [field, halos, other_field, taps],
        scratch=[
            pltpu.VMEM((3, flat, part), half_bytes),
            pltpu.VMEM((3, flat, part), half_bytes),
            pltpu.VMEM((rows + block, part), half_bytes),
        ],
        flops=2 * flops,
    )
    got, grad_features, output = lax.optimization_barrier((got, grad_features, output))
    got = [held, *got]
    mates = [by_mask(v, 1, count) for v in got]
    whole = vmem((9 * part, chans), jnp.float32)
    own = len(got)
    first = unfold(whole, chunk, [0] * own + [1], order + order[:1], got + mates[:1], None)
    grad_weight = unfold(whole, chunk, [1] * (own - 1), order[1:], mates[1:], first)
    shape = (1, side, side, part)
    return (
        output.reshape(shape),
        grad_features.reshape(shape),
        grad_weight.reshape(3, 3, part, chans),
    )


def solution(mesh):
    return jax.shard_map(
        body,
        mesh=mesh,
        in_specs=(
            P("tile", None, None, "ch"),
            P(),
            P("tile", None, None, "ch"),
            P(),
            P(),
            P(),
            P(),
        ),
        out_specs=(
            P("tile", None, None, "ch"),
            P("tile", None, None, "ch"),
            P(None, None, "ch", None),
        ),
        check_vma=False,
    )
```

```python
import functools
import math

import jax
import jax.numpy as jnp
import numpy as np
from jax import lax
from jax.experimental import pallas as pl
from jax.experimental.pallas import tpu as pltpu
from jax.sharding import PartitionSpec as P

SPAN = 4
EXTRA = 16
PARTS = 3


def turn_tables():
    labels = [[3 * row + col for col in range(3)] for row in range(3)]

    def turn_once(block):
        return [[block[col][2 - row] for col in range(3)] for row in range(3)]

    def sides_of(block):
        return [
            list(block[0]),
            [block[row][2] for row in range(3)],
            list(block[2]),
            [block[row][0] for row in range(3)],
        ]

    def corners_of(block):
        return [block[0][0], block[0][2], block[2][2], block[2][0]]

    base_sides = sides_of(labels)
    base_corners = corners_of(labels)
    edge_table = np.zeros((4, 4), np.int32)
    corner_table = np.zeros((4, 4), np.int32)
    for border in range(4):
        turned = labels
        for quarter in range(4):
            wanted = sides_of(turned)[(border + 2) % 4]
            for side_index in range(4):
                if base_sides[side_index] == wanted:
                    edge_table[border, quarter] = side_index
                if base_sides[side_index][::-1] == wanted:
                    edge_table[border, quarter] = side_index + 4
            corner_cell = corners_of(turned)[(border + 2) % 4]
            for corner_index in range(4):
                if base_corners[corner_index] == corner_cell:
                    corner_table[border, quarter] = corner_index
            turned = turn_once(turned)
    tables = np.concatenate([edge_table, corner_table], axis=0)
    return [sum(int(slot) << (3 * quarter) for quarter, slot in enumerate(row)) for row in tables]


def by_swap(value, odd, count):
    pairs = [
        (i, (i + (SPAN if (i // SPAN) % 2 == odd else -SPAN)) % count) for i in range(count)
    ]
    return lax.ppermute(value, "tile", pairs)


def by_mask(value, mask, count):
    return lax.ppermute(value, "tile", [(i, i ^ mask) for i in range(count)])


def mask_stages(count):
    bits = [1 << b for b in range(count.bit_length() - 1)]
    stages = [bits[:1]]
    rest = bits[1:]
    while rest:
        stages.append(rest[:2])
        rest = rest[2:]
    return stages


def group_masks(bits):
    masks = [0]
    for bit in bits:
        masks = masks + [m + bit for m in masks]
    return masks


def slot_of_mask(mask, count):
    place = 0
    for bits in mask_stages(count)[1:]:
        size = 1 << len(bits)
        place = place * size + (mask // bits[0]) % size
    return place


def slot_in(row, quarter):
    return (row >> (3 * quarter)) & 7


def corner_spot(slot, side):
    return jnp.where(
        slot == 0, 0, jnp.where(slot == 1, side - 1, jnp.where(slot == 2, 3 * side - 1, 2 * side))
    )


def vmem(shape, dtype):
    return jax.ShapeDtypeStruct(shape, dtype)


def call(kernel, outs, args, anywhere=(), scratch=(), flops=0, costed=True):
    in_specs = [
        pl.BlockSpec(memory_space=pltpu.HBM if i in anywhere else pltpu.VMEM) for i in range(len(args))
    ]
    size = costed * sum(math.prod(x.shape) * x.dtype.itemsize for x in list(args) + list(outs))
    return pl.pallas_call(
        kernel,
        out_shape=tuple(outs),
        in_specs=in_specs,
        out_specs=tuple(pl.BlockSpec(memory_space=pltpu.VMEM) for _ in outs),
        scratch_shapes=list(scratch),
        compiler_params=pltpu.CompilerParams(vmem_limit_bytes=40 * 1024 * 1024),
        cost_estimate=pl.CostEstimate(flops=flops, bytes_accessed=size, transcendentals=0),
    )(*args)


def packed_shape(rows, part):
    if part % 128 != 64:
        return (rows, part)
    return (rows * (part // 128) + rows // 2, 128)


def pack(value, out_ref, first=0):
    rows, part = value.shape
    if part % 128 != 64:
        out_ref[first : first + rows, :] = value
        return
    for i in range(part // 128):
        out_ref[first + i * rows : first + (i + 1) * rows, :] = value[:, i * 128 : (i + 1) * 128]
    rest = value[:, part - 64 :]
    at = first + rows * (part // 128)
    out_ref[at : at + rows // 2, :] = jnp.concatenate([rest[: rows // 2], rest[rows // 2 :]], axis=1)


def unpack(ref, out_ref, first, row, rows, part):
    if part % 128 != 64:
        out_ref[row : row + rows, :] = ref[first : first + rows, :]
        return
    for i in range(part // 128):
        out_ref[row : row + rows, i * 128 : (i + 1) * 128] = ref[first + i * rows : first + (i + 1) * rows, :]
    at = first + rows * (part // 128)
    rest = ref[at : at + rows // 2, :]
    out_ref[row : row + rows // 2, part - 64 :] = rest[:, :64]
    out_ref[row + rows // 2 : row + rows, part - 64 :] = rest[:, 64:]


def sides_kernel(side, field_ref, sides_ref, copy_ref):
    sides = jnp.concatenate(
        [field_ref[0], field_ref[:, side - 1, :], field_ref[side - 1], field_ref[:, 0, :]], axis=0
    )
    pack(sides, sides_ref)
    copy_ref[...] = field_ref[...]


def shifted_columns(side, part, field, halos, out_ref):
    rows = side * side
    flat = rows + 2 * side
    column = lax.broadcasted_iota(jnp.int32, (flat, part), 0) % side
    if halos is None:
        none = jnp.zeros((side, part), jnp.float32)
        tall = jnp.concatenate([none, field.astype(jnp.float32), none], axis=0)
        west = east = 0.0
    else:
        edge = halos.astype(jnp.float32)
        tall = jnp.concatenate([edge[0:side], field.astype(jnp.float32), edge[2 * side : 3 * side]], axis=0)
        corner = [edge[4 * side + c : 4 * side + c + 1] for c in range(4)]
        spread = lambda col: jnp.broadcast_to(col[:, None, :], (side + 2, side, part)).reshape(flat, part)
        east = spread(jnp.concatenate([corner[1], edge[side : 2 * side], corner[2]], axis=0))
        west = spread(jnp.concatenate([corner[0], edge[3 * side : 4 * side], corner[3]], axis=0))
    out_ref[0] = jnp.where(column == 0, west, pltpu.roll(tall, 1, 0)).astype(jnp.bfloat16)
    out_ref[1] = tall.astype(jnp.bfloat16)
    out_ref[2] = jnp.where(column == side - 1, east, pltpu.roll(tall, flat - 1, 0)).astype(jnp.bfloat16)


class Neighbours:
    def __init__(self, side, tables):
        self.side = side
        self.et, self.eu, self.ct, self.cu = [tables.at[4 * i : 4 * i + 4] for i in range(4)]
        self.digits = turn_tables()
        self.count = lax.axis_size("tile")
        self.own = lax.axis_index("tile")

    def block(self, source):
        groups = self.count // SPAN
        slab = lax.rem(source // SPAN - self.own // SPAN + groups, groups)
        cross = source ^ self.own
        turn = lax.rem(cross // 2, 2)
        even = lax.rem(self.own // SPAN, 2) == 0
        at = jnp.where(slab == 0, turn, jnp.where((slab == 1) == even, 2, 3) + 2 * turn)
        return 6 * lax.rem(cross, 2) + at

    def edge(self, tile, e):
        slot = slot_in(self.digits[e], self.eu[e, tile])
        start = lax.rem(slot, 4) * self.side
        end = start + self.side - 1
        return self.block(self.et[e, tile]), lambda at: jnp.where(slot >= 4, end - at, start + at)

    def corner(self, tile, c):
        slot = slot_in(self.digits[4 + c], self.cu[c, tile])
        return self.block(self.ct[c, tile]), corner_spot(slot, self.side)


def onehot(wanted, width):
    lane = lax.broadcasted_iota(jnp.int32, (wanted.shape[0], width), 1)
    return jnp.where(lane == wanted, 1.0, 0.0).astype(jnp.bfloat16)


def border_onehot_kernel(side, tables_in, cot_in, border_ref, cot_ref, tables, sem):
    copy = pltpu.make_async_copy(tables_in, tables, sem)
    copy.start()
    cot_ref[...] = cot_in[...]
    border_ref[...] = jnp.zeros_like(border_ref)
    copy.wait()
    near = Neighbours(side, tables)
    low = lax.rem(near.own, 2) == 0
    width = 4 * side
    step = lax.broadcasted_iota(jnp.int32, (side, 1), 0)

    def put(row, block, wanted, add=False):
        here = (slice(row, row + side), pl.ds(pl.multiple_of(block * width, 128), width))
        value = onehot(wanted, width)
        border_ref[here] = border_ref[here] + value if add else value

    for m, tile in enumerate((near.own, near.own ^ 1)):
        first = 2 * m * side
        flat = [near.edge(tile, e) for e in range(4)]
        corners = [near.corner(tile, c) for c in range(4)]
        pick = lambda a, b: (jnp.where(low, a[0], b[0]), lambda at: jnp.where(low, a[1](at), b[1](at)))
        block, at = pick(flat[0], flat[2])
        left, right = [
            (jnp.where(low, corners[a][0], corners[b][0]), jnp.where(low, corners[a][1], corners[b][1]))
            for a, b in ((0, 3), (1, 2))
        ]
        along = jnp.where(low, step - 1, step + 1)
        fits = (along >= 0) & (along < side)
        put(first, block, jnp.where(step == 0, -1, at(step - 1)))
        put(first, left[0], jnp.where(step == 0, left[1], -1), add=True)
        put(first + side, flat[3][0], jnp.where(fits, flat[3][1](along), -1))
        put(first + 4 * side, block, at(step))
        put(first + 8 * side, block, jnp.where(step == side - 1, -1, at(step + 1)))
        put(first + 8 * side, right[0], jnp.where(step == side - 1, right[1], -1), add=True)
        put(first + 9 * side, flat[1][0], jnp.where(fits, flat[1][1](along), -1))
        block, at = pick(flat[3], flat[1])
        put(first + 13 * side, block, at(step))


def place_kernel(side, tables_in, place_ref, tables, sem):
    copy = pltpu.make_async_copy(tables_in, tables, sem)
    copy.start()
    copy.wait()
    near = Neighbours(side, tables)
    block = 4 * side + EXTRA
    lane = lax.broadcasted_iota(jnp.int32, (1, block), 1)
    row = lax.broadcasted_iota(jnp.int32, (4 * side, block), 0)
    places = []
    swap = jnp.where(lax.rem(near.own // SPAN, 2) == 0, SPAN, -SPAN)
    for mask in (0, 2, 1, 3):
        for offset in (0, swap, -swap):
            source = lax.rem((near.own ^ mask) + offset + near.count, near.count)
            target = jnp.full((1, block), -1, jnp.int32)
            for e in range(4):
                slot = slot_in(near.digits[e], near.eu[e, source])
                along = lane - e * side
                along = jnp.where(slot >= 4, side - 1 - along, along)
                hit = (lane >= e * side) & (lane < (e + 1) * side) & (near.et[e, source] == near.own)
                target = jnp.where(hit, lax.rem(slot, 4) * side + along, target)
                spot = corner_spot(slot_in(near.digits[4 + e], near.cu[e, source]), side)
                hit = (lane == 4 * side + e) & (near.ct[e, source] == near.own)
                target = jnp.where(hit, spot, target)
            places.append(jnp.where(row == target, 1.0, 0.0))
    place_ref[...] = jnp.concatenate(places, axis=1).astype(jnp.bfloat16)


def tap_product(side, scale, tap, cols, tall):
    rows = side * side
    start = pl.multiple_of((3 - tap // 3) * side, 16)
    value = jnp.dot(
        cols[lax.rem(tap, 3)], tall[pl.ds(start, rows), :], preferred_element_type=jnp.float32
    )
    return value * scale


def send_kernel(
    side, part, scale, field_ref, own_ref, other_ref, send_ref, tall_ref, rim_ref, cols_ref
):
    rows = side * side
    first = lax.axis_index("ch") == 0
    here = slice(2 * side, 2 * side + rows)
    blank = jnp.zeros((2 * side, tall_ref.shape[1]), jnp.bfloat16)
    tall_ref[0 : 2 * side, :] = blank
    tall_ref[2 * side + rows :, :] = blank

    @pl.when(first)
    def _():
        tall_ref[here, 0:part] = own_ref[...]
        tall_ref[here, part:] = other_ref[...]

    @pl.when(jnp.logical_not(first))
    def _():
        tall_ref[here, 0:part] = other_ref[...]
        tall_ref[here, part:] = own_ref[...]

    cot = tall_ref[here, :]
    column = lax.broadcasted_iota(jnp.int32, (rows, part), 0) % side
    field = field_ref[...].reshape(rows, part).astype(jnp.float32)
    cols_ref[0] = jnp.where(column == 0, 0.0, pltpu.roll(field, 1, 0)).astype(jnp.bfloat16).T
    cols_ref[1] = field.astype(jnp.bfloat16).T
    cols_ref[2] = jnp.where(column == side - 1, 0.0, pltpu.roll(field, rows - 1, 0)).astype(jnp.bfloat16).T
    which = 1 - lax.rem(lax.axis_index("tile"), 2)
    for j in range(2):
        send_ref[j * part : (j + 1) * part, :] = tap_product(side, scale, j + 5 * which, cols_ref, tall_ref)
    rim = cot.reshape(side, side, cot.shape[1])
    rim_ref[...] = jnp.concatenate([cot[0:side], cot[rows - side :], rim[:, 0, :], rim[:, side - 1, :]], axis=0)


def half_kernel(side, part, scale, mate, taps, cols, tall, out_ref, middle):
    which = lax.rem(lax.axis_index("tile") + mate, 2)
    for at, j in enumerate(taps):
        out_ref[at * part : (at + 1) * part, :] = tap_product(side, scale, j + 5 * which, cols, tall)
    middle[...] = tap_product(side, scale, 4, cols, tall)
    start = pl.multiple_of(which * (part // 2), 16)
    out_ref[len(taps) * part :, :] = middle[pl.ds(start, part // 2), :]


def unpack_near(near_refs, near, side, part):
    size = packed_shape(4 * side, part)[0]
    row = 0
    for ref in near_refs:
        for k in range(ref.shape[0] // size):
            unpack(ref, near, k * size, row, 4 * side, part)
            row += 4 * side


def border_kernel(side, part, chunk, scale, n_near, *refs):
    near_refs = refs[:n_near]
    onehot_ref, mine_ref, rim_ref, mate_ref, first_ref, second_ref = refs[n_near : n_near + 6]
    outs, near, total = refs[n_near + 6 : -2], refs[-2], refs[-1]
    count = lax.axis_size("tile")
    own = lax.axis_index("tile")
    core = lax.rem(own, 2)
    unpack_near(near_refs, near, side, part)
    half = part // 2
    used = 9 * half

    def place(start, value):
        total[pl.ds(pl.multiple_of(start, 16), value.shape[0]), :] = value

    place(core * half, mine_ref[0 : 2 * part, :] + first_ref[...])
    place(core * half + 2 * part, mine_ref[2 * part : 4 * part, :] + second_ref[0 : 2 * part, :])
    place((1 - core) * 4 * part, mine_ref[4 * part :, :] + second_ref[2 * part :, :])
    total[used:, :] = jnp.zeros((total.shape[0] - used, total.shape[1]), jnp.float32)
    left = jnp.dot(onehot_ref[...], near[...], preferred_element_type=jnp.float32).astype(jnp.bfloat16)

    def rim(ref, at):
        return ref[pl.ds(pl.multiple_of(at, 16), side), :]

    for q in range(4):
        column = (2 + q // 2) * side if q < 3 else (2 + core) * side
        right = jnp.concatenate(
            [value for ref in (rim_ref, mate_ref) for value in (rim(ref, core * side), rim(ref, column))],
            axis=0,
        )
        value = lax.dot_general(
            left[q * 4 * side : (q + 1) * 4 * side],
            right,
            (((0,), (0,)), ((), ())),
            preferred_element_type=jnp.float32,
        )
        if q < 3:
            start = q * part + core * (part // 2 + part)
        else:
            start = 3 * part - core * (3 * part - part // 2)
        here = pl.ds(pl.multiple_of(start, 16), part)
        total[here, :] = total[here, :] + value * scale
    size = outs[0].shape[0]
    for index in range(count // 2):
        to = slot_of_mask(2 * index, count) * chunk
        block = pl.multiple_of(((own // 2) ^ index) * chunk, 16)
        out = outs[to // size]
        out[to % size : to % size + chunk, :] = total[pl.ds(block, chunk), :].astype(out.dtype)


def sum_kernel(n_got, n_out, *refs):
    held_ref, got_refs, outs = refs[0], refs[1 : 1 + n_got], refs[1 + n_got :]
    size = held_ref.shape[0] // n_out
    for index in range(n_out):
        here = slice(index * size, (index + 1) * size)
        value = held_ref[here, :]
        for ref in got_refs:
            value = value + ref[here, :].astype(jnp.float32)
        outs[index][...] = value.astype(outs[index].dtype)


def exchange_kernel(held_ref, got_ref, out_ref):
    half = held_ref.shape[0] // 2
    for a, b in ((0, half), (half, 0)):
        value = held_ref[a : a + half, :].astype(jnp.float32) + got_ref[b : b + half, :].astype(jnp.float32)
        out_ref[a : a + half, :] = value.astype(out_ref.dtype)


def join_kernel(*refs):
    row = 0
    for ref in refs[:-1]:
        refs[-1][row : row + ref.shape[0], :] = ref[...]
        row += ref.shape[0]


def unfold_kernel(used, chunk, bits, masks, n_dep, *refs):
    refs = refs[n_dep:]
    n = len(masks)
    in_refs, out_ref, wide, sems = refs[:n], refs[n], refs[n + 1], refs[n + 2]
    own = lax.axis_index("tile")
    full, rest = used // chunk, used % chunk
    copies = []
    for i, (ref, inner, bit) in enumerate(zip(in_refs, masks, bits)):
        origin = (lax.rem(own, 2) ^ bit) * used
        for k, mask in enumerate(inner):
            at = i * len(inner) + k
            wide[at] = ref[k * chunk : (k + 1) * chunk, :].astype(jnp.float32)
            block = (own ^ mask) // 2
            start = pl.multiple_of(origin + block * chunk, 16)
            copies.append(
                (
                    block < full,
                    pltpu.make_async_copy(wide.at[at], out_ref.at[pl.ds(start, chunk), :], sems.at[at]),
                )
            )
            if rest:
                start = pl.multiple_of(origin + full * chunk, 16)
                copies.append(
                    (
                        block == full,
                        pltpu.make_async_copy(
                            wide.at[at, 0:rest], out_ref.at[pl.ds(start, rest), :], sems.at[at]
                        ),
                    )
                )
    for going, copy in copies:
        pl.when(going)(copy.start)
    for going, copy in copies:
        pl.when(going)(copy.wait)


def unfold(whole, chunk, bits, masks, blocks, before):
    n_dep = 0 if before is None else 1
    anywhere = pl.BlockSpec(memory_space=pl.ANY)
    n_copies = len(masks) * len(masks[0])
    return pl.pallas_call(
        functools.partial(unfold_kernel, whole.shape[0] // 2, chunk, bits, masks, n_dep),
        out_shape=whole,
        in_specs=[anywhere] * n_dep + [pl.BlockSpec(memory_space=pltpu.VMEM)] * len(blocks),
        out_specs=anywhere,
        scratch_shapes=[
            pltpu.VMEM((n_copies, chunk, whole.shape[1]), jnp.float32),
            pltpu.SemaphoreType.DMA((n_copies,)),
        ],
        input_output_aliases={0: 0} if n_dep else {},
        compiler_params=pltpu.CompilerParams(vmem_limit_bytes=40 * 1024 * 1024),
    )(*([before] if n_dep else []), *blocks)


def back_kernel(side, part, tall, weight_ref, inner_ref, pieces_ref):
    rows = side * side
    flat = rows + 2 * side
    start = pl.multiple_of(lax.axis_index("ch") * part, 16)
    backs = []
    for b in range(3):
        back = jnp.zeros((flat, part), jnp.float32)
        for a in range(3):
            back = back + lax.dot_general(
                tall[(2 - a) * side : (2 - a) * side + flat, :],
                weight_ref[3 * a + b, pl.ds(start, part), :],
                (((1,), (1,)), ((), ())),
                preferred_element_type=jnp.float32,
            )
        backs.append(back)
    column = lax.broadcasted_iota(jnp.int32, (flat, part), 0) % side
    inner = (
        jnp.where(column == side - 1, 0.0, pltpu.roll(backs[0], flat - 1, 0))
        + backs[1]
        + jnp.where(column == 0, 0.0, pltpu.roll(backs[2], 1, 0))
    )
    inner_ref[...] = inner[side : side + rows]
    west = backs[0].reshape(side + 2, side, part)[:, 0, :]
    east = backs[2].reshape(side + 2, side, part)[:, side - 1, :]
    pieces = jnp.concatenate(
        [
            inner[0:side],
            east[1 : side + 1],
            inner[side + rows :],
            west[1 : side + 1],
            west[0:1],
            east[0:1],
            east[side + 1 :],
            west[side + 1 :],
            jnp.zeros((EXTRA - 4, part), jnp.float32),
        ],
        axis=0,
    )
    pack(pieces.astype(jnp.bfloat16), pieces_ref)


def add_halo_kernel(side, part, place_ref, inner_ref, *refs):
    got_refs, out_ref, got = refs[:-2], refs[-2], refs[-1]
    block = 4 * side + EXTRA
    size = packed_shape(block, part)[0]
    for i, ref in enumerate(got_refs):
        for k in range(3):
            unpack(ref, got, k * size, (3 * i + k) * block, block, part)
    sums = jnp.dot(place_ref[...], got[...], preferred_element_type=jnp.float32)
    rows = side * side
    spread = lambda col: jnp.broadcast_to(col[:, None, :], (side, side, part)).reshape(rows, part)
    column = lax.broadcasted_iota(jnp.int32, (rows, part), 0) % side
    inner = inner_ref[...]
    inner = inner + jnp.where(column == side - 1, spread(sums[side : 2 * side]), 0.0)
    inner = inner + jnp.where(column == 0, spread(sums[3 * side :]), 0.0)
    ends = jnp.concatenate(
        [
            inner[0:side] + sums[0:side],
            inner[side : rows - side],
            inner[rows - side :] + sums[2 * side : 3 * side],
        ],
        axis=0,
    )
    out_ref[...] = ends.astype(jnp.bfloat16)


def parts_of(rows):
    size = -(-rows // (32 * PARTS)) * 32
    return [min(size, rows - first) for first in range(0, rows, size)]


def halo_kernel(side, part, n_near, *refs):
    near_refs, tables_in, field_ref = refs[:n_near], refs[n_near], refs[n_near + 1]
    halos_ref, *packet_refs = refs[n_near + 2 : -3]
    near, tables, sem = refs[-3:]
    copy = pltpu.make_async_copy(tables_in, tables, sem)
    copy.start()
    rows = side * side
    unpack_near(near_refs, near, side, part)
    field = field_ref[...].reshape(rows, part)
    sizes = parts_of(rows)
    for k, ref in enumerate(packet_refs):
        pack(field[sum(sizes[:k]) : sum(sizes[: k + 1])], ref)
    copy.wait()
    index = Neighbours(side, tables)
    step = lax.broadcasted_iota(jnp.int32, (side, 1), 0)
    wanted = []
    for e in range(4):
        block, at = index.edge(index.own, e)
        wanted.append(block * (4 * side) + at(step))
    spots = lax.broadcasted_iota(jnp.int32, (EXTRA, 1), 0)
    ends = jnp.full((EXTRA, 1), -1, jnp.int32)
    for c in range(4):
        block, spot = index.corner(index.own, c)
        ends = jnp.where(spots == c, block * (4 * side) + spot, ends)
    pick = onehot(jnp.concatenate(wanted + [ends], axis=0), near.shape[0])
    halos = jnp.dot(pick, near[...], preferred_element_type=jnp.float32).astype(jnp.bfloat16)
    halos_ref[...] = halos
    pack(halos, packet_refs[-1], packed_shape(sizes[-1], part)[0])


def output_kernel(side, part, field_ref, halos_ref, weight_ref, *refs):
    rows = side * side
    ch = lax.axis_index("ch")
    other_refs, (out_ref, cols, other_cols, other) = refs[:PARTS], refs[PARTS:]
    wide = -(-part // 128) * 128
    lanes = pl.multiple_of(ch * (weight_ref.shape[2] - wide), 128)
    sizes = parts_of(rows)
    for k, ref in enumerate(other_refs):
        unpack(ref, other, 0, sum(sizes[:k]), sizes[k], part)
    unpack(other_refs[-1], other, packed_shape(sizes[-1], part)[0], rows, 4 * side + EXTRA, part)
    shifted_columns(side, part, field_ref[...].reshape(rows, part), halos_ref[...], cols)
    shifted_columns(side, part, other[0:rows, :], other[rows:, :], other_cols)
    starts = (pl.multiple_of(ch * part, 16), pl.multiple_of((1 - ch) * part, 16))
    total = jnp.zeros((rows, wide), jnp.float32)
    for a in range(3):
        for b in range(3):
            for ref, first in zip((cols, other_cols), starts):
                total = total + jnp.dot(
                    ref[b, a * side : a * side + rows, :],
                    weight_ref[3 * a + b, pl.ds(first, part), pl.ds(lanes, wide)],
                    preferred_element_type=jnp.float32,
                )
    result = jnp.where(ch == 0, total[:, :part], total[:, wide - part :])
    out_ref[...] = result.astype(jnp.bfloat16)


def body(features, weight, cotangent, edge_tiles, edge_turns, corner_tiles, corner_turns):
    count = lax.axis_size("tile")
    field = features[0]
    side, part = field.shape[0], field.shape[2]
    chans = weight.shape[3]
    rows = side * side
    flat = rows + 2 * side
    block = 4 * side + EXTRA
    taps = weight.reshape(9, chans, chans)
    others = [(0, 1), (1, 0)]
    flops = 2 * rows * 9 * part * chans
    half_bytes = jnp.bfloat16
    chunk = -(-9 * part // (16 * count)) * 16
    half = count * chunk // 2
    scale = 1.0 / math.sqrt(count * rows)

    cot_own = cotangent[0].reshape(rows, part)
    cot_other = lax.ppermute(cot_own, "ch", others)
    sides, field = call(
        functools.partial(sides_kernel, side),
        [vmem(packed_shape(4 * side, part), half_bytes), vmem(field.shape, half_bytes)],
        [field],
    )
    swaps = [by_swap(sides, odd, count) for odd in (0, 1)]
    across = by_mask(sides, 2, count)
    tables = jnp.concatenate([edge_tiles.T, edge_turns.T, corner_tiles.T, corner_turns.T], axis=0)
    table_scratch = [pltpu.SMEM(tables.shape, jnp.int32), pltpu.SemaphoreType.DMA]
    border_pick, cot_own = call(
        functools.partial(border_onehot_kernel, side),
        [vmem((16 * side, 48 * side), half_bytes), vmem((rows, part), half_bytes)],
        [tables, cot_own],
        scratch=table_scratch,
    )
    pair = packed_shape(8 * side, part)
    (beyond,) = call(join_kernel, [vmem(pair, half_bytes)], swaps)
    near = [sides, across, *swaps, by_mask(beyond, 2, count)]
    near, cot_other, border_pick = lax.optimization_barrier((near, cot_other, border_pick))
    (near,) = call(join_kernel, [vmem(packed_shape(24 * side, part), half_bytes)], near)
    mates = by_mask(near, 1, count)
    first, tall, rim, cols = call(
        functools.partial(send_kernel, side, part, scale),
        [
            vmem((2 * part, chans), jnp.float32),
            vmem((rows + 4 * side, chans), half_bytes),
            vmem((4 * side, chans), half_bytes),
            vmem((3, part, rows), half_bytes),
        ],
        [field, cot_own, cot_other],
        flops=flops // 4,
    )
    (second,) = call(
        functools.partial(half_kernel, side, part, scale, 1, (2, 3)),
        [vmem((5 * part // 2, chans), jnp.float32)],
        [cols, tall],
        scratch=[pltpu.VMEM((part, chans), jnp.float32)],
        flops=flops,
    )
    tall, second = lax.optimization_barrier((tall, second))
    (mine,) = call(
        functools.partial(half_kernel, side, part, scale, 0, (0, 1, 2, 3)),
        [vmem((9 * part // 2, chans), jnp.float32)],
        [cols, tall],
        scratch=[pltpu.VMEM((part, chans), jnp.float32)],
        costed=False,
    )
    mates, mine, rim_mate = lax.optimization_barrier((mates, mine, by_mask(rim, 1, count)))
    near = [near, mates]

    stages = mask_stages(count)
    masks = group_masks(stages[1])
    size = half // len(masks)
    held, *send = call(
        functools.partial(border_kernel, side, part, chunk, scale, len(near)),
        [vmem((size, chans), jnp.float32)] + [vmem((size, chans), half_bytes)] * (len(masks) - 1),
        [*near, border_pick, mine, rim, rim_mate, by_mask(first, 1, count), by_mask(second, 1, count)],
        scratch=[pltpu.VMEM((48 * side, part), half_bytes), pltpu.VMEM((half, chans), jnp.float32)],
    )
    send, tall, near = lax.optimization_barrier((send, tall, near))
    got = [by_mask(v, m, count) for v, m in zip(send, masks[1:])]
    inner, pieces = call(
        functools.partial(back_kernel, side, part),
        [vmem((rows, part), jnp.float32), vmem(packed_shape(block, part), half_bytes)],
        [tall, taps],
        flops=flops,
    )
    pieces, near = lax.optimization_barrier((pieces, near))
    here = [pieces, *[by_swap(pieces, odd, count) for odd in (0, 1)]]
    (place,) = call(
        functools.partial(place_kernel, side),
        [vmem((4 * side, 12 * block), half_bytes)],
        [tables],
        scratch=table_scratch,
    )
    halos, *packet = call(
        functools.partial(halo_kernel, side, part, len(near)),
        [vmem((block, part), half_bytes)]
        + [vmem(packed_shape(size, part), half_bytes) for size in parts_of(rows)[:-1]]
        + [vmem(packed_shape(parts_of(rows)[-1] + block, part), half_bytes)],
        [*near, tables, field],
        scratch=[pltpu.VMEM((48 * side, part), half_bytes), *table_scratch],
    )
    got, here, inner, halos, packet, place = lax.optimization_barrier(
        (got, here, inner, halos, packet, place)
    )
    swap = len(stages[-1]) == 1 and len(stages) > 2
    rs_stages = stages[2:-1] if swap else stages[2:]
    aside = [here, packet]

    def start_aside(send, aside):
        send, here, packet = lax.optimization_barrier((send, *aside))
        (here,) = call(join_kernel, [vmem((3 * pieces.shape[0], pieces.shape[1]), half_bytes)], here)
        return send, here, by_mask(here, 2, count), [lax.ppermute(v, "ch", others) for v in packet]

    for index, bits in enumerate(rs_stages):
        masks = group_masks(bits)
        size = held.shape[0] // len(masks)
        held, *send = call(
            functools.partial(sum_kernel, len(got), len(masks)),
            [vmem((size, chans), jnp.float32)] + [vmem((size, chans), half_bytes)] * (len(masks) - 1),
            [held, *got],
        )
        if index == 0:
            send, here, beside, other_field = start_aside(send, aside)
        got = [by_mask(v, m, count) for v, m in zip(send, masks[1:])]
    (held,) = call(functools.partial(sum_kernel, len(got), 1), [vmem(held.shape, half_bytes)], [held, *got])
    if swap:
        if not rs_stages:
            held, here, beside, other_field = start_aside(held, aside)
        got = by_mask(held, stages[-1][0], count)
        got, here, beside = lax.optimization_barrier((got, here, beside))
        (held,) = call(exchange_kernel, [vmem(held.shape, half_bytes)], [held, got])
    order = [0] if not swap else [0, stages[-1][0]]
    ag_stages = stages[-2:0:-1] if swap else stages[:0:-1]
    for index, bits in enumerate(ag_stages):
        masks = group_masks(bits)
        got = [by_mask(held, m, count) for m in masks[1:]]
        if index < len(ag_stages) - 1:
            order = [m + v for m in masks for v in order]
            (held,) = call(
                join_kernel, [vmem((held.shape[0] * len(masks), chans), half_bytes)], [held, *got]
            )
    order = [[m + v for v in order] for m in masks]
    got_pieces = [here, beside, by_mask(here, 1, count), by_mask(beside, 1, count)]
    (grad_features,) = call(
        functools.partial(add_halo_kernel, side, part),
        [vmem((rows, part), half_bytes)],
        [place, inner, *got_pieces],
        scratch=[pltpu.VMEM((12 * block, part), half_bytes)],
    )
    (output,) = call(
        functools.partial(output_kernel, side, part),
        [vmem((rows, part), half_bytes)],
        [field, halos, taps, *other_field],
        scratch=[
            pltpu.VMEM((3, flat, part), half_bytes),
            pltpu.VMEM((3, flat, part), half_bytes),
            pltpu.VMEM((rows + block, part), half_bytes),
        ],
        flops=2 * flops,
    )
    got, grad_features, output = lax.optimization_barrier((got, grad_features, output))
    got = [held, *got]
    mates = [by_mask(v, 1, count) for v in got]
    whole = vmem((9 * part, chans), jnp.float32)
    own = len(got)
    first = unfold(whole, chunk, [0] * own + [1], order + order[:1], got + mates[:1], None)
    grad_weight = unfold(whole, chunk, [1] * (own - 1), order[1:], mates[1:], first)
    shape = (1, side, side, part)
    return (
        output.reshape(shape),
        grad_features.reshape(shape),
        grad_weight.reshape(3, 3, part, chans),
    )


def solution(mesh):
    return jax.shard_map(
        body,
        mesh=mesh,
        in_specs=(
            P("tile", None, None, "ch"),
            P(),
            P("tile", None, None, "ch"),
            P(),
            P(),
            P(),
            P(),
        ),
        out_specs=(
            P("tile", None, None, "ch"),
            P("tile", None, None, "ch"),
            P(None, None, "ch", None),
        ),
        check_vma=False,
    )
```

```python
import functools
import math

import jax
import jax.numpy as jnp
import numpy as np
from jax import lax
from jax.experimental import pallas as pl
from jax.experimental.pallas import tpu as pltpu
from jax.sharding import PartitionSpec as P

SPAN = 4
EXTRA = 16
PARTS = 3


def turn_tables():
    labels = [[3 * row + col for col in range(3)] for row in range(3)]

    def turn_once(block):
        return [[block[col][2 - row] for col in range(3)] for row in range(3)]

    def sides_of(block):
        return [
            list(block[0]),
            [block[row][2] for row in range(3)],
            list(block[2]),
            [block[row][0] for row in range(3)],
        ]

    def corners_of(block):
        return [block[0][0], block[0][2], block[2][2], block[2][0]]

    base_sides = sides_of(labels)
    base_corners = corners_of(labels)
    edge_table = np.zeros((4, 4), np.int32)
    corner_table = np.zeros((4, 4), np.int32)
    for border in range(4):
        turned = labels
        for quarter in range(4):
            wanted = sides_of(turned)[(border + 2) % 4]
            for side_index in range(4):
                if base_sides[side_index] == wanted:
                    edge_table[border, quarter] = side_index
                if base_sides[side_index][::-1] == wanted:
                    edge_table[border, quarter] = side_index + 4
            corner_cell = corners_of(turned)[(border + 2) % 4]
            for corner_index in range(4):
                if base_corners[corner_index] == corner_cell:
                    corner_table[border, quarter] = corner_index
            turned = turn_once(turned)
    tables = np.concatenate([edge_table, corner_table], axis=0)
    return [sum(int(slot) << (3 * quarter) for quarter, slot in enumerate(row)) for row in tables]


def by_swap(value, odd, count):
    pairs = [
        (i, (i + (SPAN if (i // SPAN) % 2 == odd else -SPAN)) % count) for i in range(count)
    ]
    return lax.ppermute(value, "tile", pairs)


def by_mask(value, mask, count):
    return lax.ppermute(value, "tile", [(i, i ^ mask) for i in range(count)])


def mask_stages(count):
    bits = [1 << b for b in range(count.bit_length() - 1)]
    stages = [bits[:1]]
    rest = bits[1:]
    while rest:
        stages.append(rest[:2])
        rest = rest[2:]
    return stages


def group_masks(bits):
    masks = [0]
    for bit in bits:
        masks = masks + [m + bit for m in masks]
    return masks


def slot_of_mask(mask, count):
    place = 0
    for bits in mask_stages(count)[1:]:
        size = 1 << len(bits)
        place = place * size + (mask // bits[0]) % size
    return place


def slot_in(row, quarter):
    return (row >> (3 * quarter)) & 7


def corner_spot(slot, side):
    return jnp.where(
        slot == 0, 0, jnp.where(slot == 1, side - 1, jnp.where(slot == 2, 3 * side - 1, 2 * side))
    )


def vmem(shape, dtype):
    return jax.ShapeDtypeStruct(shape, dtype)


def call(kernel, outs, args, anywhere=(), scratch=(), flops=0, costed=True):
    in_specs = [
        pl.BlockSpec(memory_space=pltpu.HBM if i in anywhere else pltpu.VMEM) for i in range(len(args))
    ]
    size = costed * sum(math.prod(x.shape) * x.dtype.itemsize for x in list(args) + list(outs))
    return pl.pallas_call(
        kernel,
        out_shape=tuple(outs),
        in_specs=in_specs,
        out_specs=tuple(pl.BlockSpec(memory_space=pltpu.VMEM) for _ in outs),
        scratch_shapes=list(scratch),
        compiler_params=pltpu.CompilerParams(vmem_limit_bytes=40 * 1024 * 1024),
        cost_estimate=pl.CostEstimate(flops=flops, bytes_accessed=size, transcendentals=0),
    )(*args)


def packed_shape(rows, part):
    if part % 128 != 64:
        return (rows, part)
    return (rows * (part // 128) + rows // 2, 128)


def pack(value, out_ref, first=0):
    rows, part = value.shape
    if part % 128 != 64:
        out_ref[first : first + rows, :] = value
        return
    for i in range(part // 128):
        out_ref[first + i * rows : first + (i + 1) * rows, :] = value[:, i * 128 : (i + 1) * 128]
    rest = value[:, part - 64 :]
    at = first + rows * (part // 128)
    out_ref[at : at + rows // 2, :] = jnp.concatenate([rest[: rows // 2], rest[rows // 2 :]], axis=1)


def unpack(ref, out_ref, first, row, rows, part):
    if part % 128 != 64:
        out_ref[row : row + rows, :] = ref[first : first + rows, :]
        return
    for i in range(part // 128):
        out_ref[row : row + rows, i * 128 : (i + 1) * 128] = ref[first + i * rows : first + (i + 1) * rows, :]
    at = first + rows * (part // 128)
    rest = ref[at : at + rows // 2, :]
    out_ref[row : row + rows // 2, part - 64 :] = rest[:, :64]
    out_ref[row + rows // 2 : row + rows, part - 64 :] = rest[:, 64:]


def sides_kernel(side, field_ref, sides_ref, copy_ref):
    sides = jnp.concatenate(
        [field_ref[0], field_ref[:, side - 1, :], field_ref[side - 1], field_ref[:, 0, :]], axis=0
    )
    pack(sides, sides_ref)
    copy_ref[...] = field_ref[...]


def shifted_columns(side, part, field, halos, out_ref):
    rows = side * side
    flat = rows + 2 * side
    column = lax.broadcasted_iota(jnp.int32, (flat, part), 0) % side
    if halos is None:
        none = jnp.zeros((side, part), jnp.float32)
        tall = jnp.concatenate([none, field.astype(jnp.float32), none], axis=0)
        west = east = 0.0
    else:
        edge = halos.astype(jnp.float32)
        tall = jnp.concatenate([edge[0:side], field.astype(jnp.float32), edge[2 * side : 3 * side]], axis=0)
        corner = [edge[4 * side + c : 4 * side + c + 1] for c in range(4)]
        spread = lambda col: jnp.broadcast_to(col[:, None, :], (side + 2, side, part)).reshape(flat, part)
        east = spread(jnp.concatenate([corner[1], edge[side : 2 * side], corner[2]], axis=0))
        west = spread(jnp.concatenate([corner[0], edge[3 * side : 4 * side], corner[3]], axis=0))
    out_ref[0] = jnp.where(column == 0, west, pltpu.roll(tall, 1, 0)).astype(jnp.bfloat16)
    out_ref[1] = tall.astype(jnp.bfloat16)
    out_ref[2] = jnp.where(column == side - 1, east, pltpu.roll(tall, flat - 1, 0)).astype(jnp.bfloat16)


class Neighbours:
    def __init__(self, side, tables):
        self.side = side
        self.et, self.eu, self.ct, self.cu = [tables.at[4 * i : 4 * i + 4] for i in range(4)]
        self.digits = turn_tables()
        self.count = lax.axis_size("tile")
        self.own = lax.axis_index("tile")

    def block(self, source):
        groups = self.count // SPAN
        slab = lax.rem(source // SPAN - self.own // SPAN + groups, groups)
        cross = source ^ self.own
        turn = lax.rem(cross // 2, 2)
        even = lax.rem(self.own // SPAN, 2) == 0
        at = jnp.where(slab == 0, turn, jnp.where((slab == 1) == even, 2, 3) + 2 * turn)
        return 6 * lax.rem(cross, 2) + at

    def edge(self, tile, e):
        slot = slot_in(self.digits[e], self.eu[e, tile])
        start = lax.rem(slot, 4) * self.side
        end = start + self.side - 1
        return self.block(self.et[e, tile]), lambda at: jnp.where(slot >= 4, end - at, start + at)

    def corner(self, tile, c):
        slot = slot_in(self.digits[4 + c], self.cu[c, tile])
        return self.block(self.ct[c, tile]), corner_spot(slot, self.side)


def onehot(wanted, width):
    lane = lax.broadcasted_iota(jnp.int32, (wanted.shape[0], width), 1)
    return jnp.where(lane == wanted, 1.0, 0.0).astype(jnp.bfloat16)


def border_onehot_kernel(side, tables_in, cot_in, border_ref, cot_ref, tables, sem):
    copy = pltpu.make_async_copy(tables_in, tables, sem)
    copy.start()
    cot_ref[...] = cot_in[...]
    border_ref[...] = jnp.zeros_like(border_ref)
    copy.wait()
    near = Neighbours(side, tables)
    low = lax.rem(near.own, 2) == 0
    width = 4 * side
    step = lax.broadcasted_iota(jnp.int32, (side, 1), 0)

    def put(row, block, wanted, add=False):
        here = (slice(row, row + side), pl.ds(pl.multiple_of(block * width, 128), width))
        value = onehot(wanted, width)
        border_ref[here] = border_ref[here] + value if add else value

    for m, tile in enumerate((near.own, near.own ^ 1)):
        first = 2 * m * side
        flat = [near.edge(tile, e) for e in range(4)]
        corners = [near.corner(tile, c) for c in range(4)]
        pick = lambda a, b: (jnp.where(low, a[0], b[0]), lambda at: jnp.where(low, a[1](at), b[1](at)))
        block, at = pick(flat[0], flat[2])
        left, right = [
            (jnp.where(low, corners[a][0], corners[b][0]), jnp.where(low, corners[a][1], corners[b][1]))
            for a, b in ((0, 3), (1, 2))
        ]
        along = jnp.where(low, step - 1, step + 1)
        fits = (along >= 0) & (along < side)
        put(first, block, jnp.where(step == 0, -1, at(step - 1)))
        put(first, left[0], jnp.where(step == 0, left[1], -1), add=True)
        put(first + side, flat[3][0], jnp.where(fits, flat[3][1](along), -1))
        put(first + 4 * side, block, at(step))
        put(first + 8 * side, block, jnp.where(step == side - 1, -1, at(step + 1)))
        put(first + 8 * side, right[0], jnp.where(step == side - 1, right[1], -1), add=True)
        put(first + 9 * side, flat[1][0], jnp.where(fits, flat[1][1](along), -1))
        block, at = pick(flat[3], flat[1])
        put(first + 13 * side, block, at(step))


def place_kernel(side, tables_in, place_ref, tables, sem):
    copy = pltpu.make_async_copy(tables_in, tables, sem)
    copy.start()
    copy.wait()
    near = Neighbours(side, tables)
    block = 4 * side + EXTRA
    lane = lax.broadcasted_iota(jnp.int32, (1, block), 1)
    row = lax.broadcasted_iota(jnp.int32, (4 * side, block), 0)
    places = []
    swap = jnp.where(lax.rem(near.own // SPAN, 2) == 0, SPAN, -SPAN)
    for mask in (0, 2, 1, 3):
        for offset in (0, swap, -swap):
            source = lax.rem((near.own ^ mask) + offset + near.count, near.count)
            target = jnp.full((1, block), -1, jnp.int32)
            for e in range(4):
                slot = slot_in(near.digits[e], near.eu[e, source])
                along = lane - e * side
                along = jnp.where(slot >= 4, side - 1 - along, along)
                hit = (lane >= e * side) & (lane < (e + 1) * side) & (near.et[e, source] == near.own)
                target = jnp.where(hit, lax.rem(slot, 4) * side + along, target)
                spot = corner_spot(slot_in(near.digits[4 + e], near.cu[e, source]), side)
                hit = (lane == 4 * side + e) & (near.ct[e, source] == near.own)
                target = jnp.where(hit, spot, target)
            places.append(jnp.where(row == target, 1.0, 0.0))
    place_ref[...] = jnp.concatenate(places, axis=1).astype(jnp.bfloat16)


def tap_product(side, scale, tap, cols, tall):
    rows = side * side
    start = pl.multiple_of((3 - tap // 3) * side, 16)
    value = jnp.dot(
        cols[lax.rem(tap, 3)], tall[pl.ds(start, rows), :], preferred_element_type=jnp.float32
    )
    return value * scale


def send_kernel(
    side, part, scale, field_ref, own_ref, other_ref, send_ref, tall_ref, rim_ref, cols_ref
):
    rows = side * side
    first = lax.axis_index("ch") == 0
    here = slice(2 * side, 2 * side + rows)
    blank = jnp.zeros((2 * side, tall_ref.shape[1]), jnp.bfloat16)
    tall_ref[0 : 2 * side, :] = blank
    tall_ref[2 * side + rows :, :] = blank

    @pl.when(first)
    def _():
        tall_ref[here, 0:part] = own_ref[...]
        tall_ref[here, part:] = other_ref[...]

    @pl.when(jnp.logical_not(first))
    def _():
        tall_ref[here, 0:part] = other_ref[...]
        tall_ref[here, part:] = own_ref[...]

    cot = tall_ref[here, :]
    column = lax.broadcasted_iota(jnp.int32, (rows, part), 0) % side
    field = field_ref[...].reshape(rows, part).astype(jnp.float32)
    cols_ref[0] = jnp.where(column == 0, 0.0, pltpu.roll(field, 1, 0)).astype(jnp.bfloat16).T
    cols_ref[1] = field.astype(jnp.bfloat16).T
    cols_ref[2] = jnp.where(column == side - 1, 0.0, pltpu.roll(field, rows - 1, 0)).astype(jnp.bfloat16).T
    which = 1 - lax.rem(lax.axis_index("tile"), 2)
    for j in range(2):
        send_ref[j * part : (j + 1) * part, :] = tap_product(side, scale, j + 5 * which, cols_ref, tall_ref)
    rim = cot.reshape(side, side, cot.shape[1])
    rim_ref[...] = jnp.concatenate([cot[0:side], cot[rows - side :], rim[:, 0, :], rim[:, side - 1, :]], axis=0)


def half_kernel(side, part, scale, mate, taps, cols, tall, out_ref, middle):
    which = lax.rem(lax.axis_index("tile") + mate, 2)
    for at, j in enumerate(taps):
        out_ref[at * part : (at + 1) * part, :] = tap_product(side, scale, j + 5 * which, cols, tall)
    middle[...] = tap_product(side, scale, 4, cols, tall)
    start = pl.multiple_of(which * (part // 2), 16)
    out_ref[len(taps) * part :, :] = middle[pl.ds(start, part // 2), :]


def unpack_near(near_refs, near, side, part):
    size = packed_shape(4 * side, part)[0]
    row = 0
    for ref in near_refs:
        for k in range(ref.shape[0] // size):
            unpack(ref, near, k * size, row, 4 * side, part)
            row += 4 * side


def border_kernel(side, part, chunk, scale, n_near, *refs):
    near_refs = refs[:n_near]
    onehot_ref, mine_ref, rim_ref, mate_ref, first_ref, second_ref = refs[n_near : n_near + 6]
    outs, near, total = refs[n_near + 6 : -2], refs[-2], refs[-1]
    count = lax.axis_size("tile")
    own = lax.axis_index("tile")
    core = lax.rem(own, 2)
    unpack_near(near_refs, near, side, part)
    half = part // 2
    used = 9 * half

    def place(start, value):
        total[pl.ds(pl.multiple_of(start, 16), value.shape[0]), :] = value

    place(core * half, mine_ref[0 : 2 * part, :] + first_ref[...])
    place(core * half + 2 * part, mine_ref[2 * part : 4 * part, :] + second_ref[0 : 2 * part, :])
    place((1 - core) * 4 * part, mine_ref[4 * part :, :] + second_ref[2 * part :, :])
    total[used:, :] = jnp.zeros((total.shape[0] - used, total.shape[1]), jnp.float32)
    left = jnp.dot(onehot_ref[...], near[...], preferred_element_type=jnp.float32).astype(jnp.bfloat16)

    def rim(ref, at):
        return ref[pl.ds(pl.multiple_of(at, 16), side), :]

    for q in range(4):
        column = (2 + q // 2) * side if q < 3 else (2 + core) * side
        right = jnp.concatenate(
            [value for ref in (rim_ref, mate_ref) for value in (rim(ref, core * side), rim(ref, column))],
            axis=0,
        )
        value = lax.dot_general(
            left[q * 4 * side : (q + 1) * 4 * side],
            right,
            (((0,), (0,)), ((), ())),
            preferred_element_type=jnp.float32,
        )
        if q < 3:
            start = q * part + core * (part // 2 + part)
        else:
            start = 3 * part - core * (3 * part - part // 2)
        here = pl.ds(pl.multiple_of(start, 16), part)
        total[here, :] = total[here, :] + value * scale
    size = outs[0].shape[0]
    for index in range(count // 2):
        to = slot_of_mask(2 * index, count) * chunk
        block = pl.multiple_of(((own // 2) ^ index) * chunk, 16)
        out = outs[to // size]
        out[to % size : to % size + chunk, :] = total[pl.ds(block, chunk), :].astype(out.dtype)


def sum_kernel(n_got, n_out, *refs):
    held_ref, got_refs, outs = refs[0], refs[1 : 1 + n_got], refs[1 + n_got :]
    size = held_ref.shape[0] // n_out
    for index in range(n_out):
        here = slice(index * size, (index + 1) * size)
        value = held_ref[here, :]
        for ref in got_refs:
            value = value + ref[here, :].astype(jnp.float32)
        outs[index][...] = value.astype(outs[index].dtype)


def exchange_kernel(held_ref, got_ref, out_ref):
    half = held_ref.shape[0] // 2
    for a, b in ((0, half), (half, 0)):
        value = held_ref[a : a + half, :].astype(jnp.float32) + got_ref[b : b + half, :].astype(jnp.float32)
        out_ref[a : a + half, :] = value.astype(out_ref.dtype)


def join_kernel(*refs):
    row = 0
    for ref in refs[:-1]:
        refs[-1][row : row + ref.shape[0], :] = ref[...]
        row += ref.shape[0]


def unfold_kernel(used, chunk, bits, masks, n_dep, *refs):
    refs = refs[n_dep:]
    n = len(masks)
    in_refs, out_ref, wide, sems = refs[:n], refs[n], refs[n + 1], refs[n + 2]
    own = lax.axis_index("tile")
    full, rest = used // chunk, used % chunk
    copies = []
    for i, (ref, inner, bit) in enumerate(zip(in_refs, masks, bits)):
        origin = (lax.rem(own, 2) ^ bit) * used
        for k, mask in enumerate(inner):
            at = i * len(inner) + k
            wide[at] = ref[k * chunk : (k + 1) * chunk, :].astype(jnp.float32)
            block = (own ^ mask) // 2
            start = pl.multiple_of(origin + block * chunk, 16)
            copies.append(
                (
                    block < full,
                    pltpu.make_async_copy(wide.at[at], out_ref.at[pl.ds(start, chunk), :], sems.at[at]),
                )
            )
            if rest:
                start = pl.multiple_of(origin + full * chunk, 16)
                copies.append(
                    (
                        block == full,
                        pltpu.make_async_copy(
                            wide.at[at, 0:rest], out_ref.at[pl.ds(start, rest), :], sems.at[at]
                        ),
                    )
                )
    for going, copy in copies:
        pl.when(going)(copy.start)
    for going, copy in copies:
        pl.when(going)(copy.wait)


def unfold(whole, chunk, bits, masks, blocks, before):
    n_dep = 0 if before is None else 1
    anywhere = pl.BlockSpec(memory_space=pl.ANY)
    n_copies = len(masks) * len(masks[0])
    return pl.pallas_call(
        functools.partial(unfold_kernel, whole.shape[0] // 2, chunk, bits, masks, n_dep),
        out_shape=whole,
        in_specs=[anywhere] * n_dep + [pl.BlockSpec(memory_space=pltpu.VMEM)] * len(blocks),
        out_specs=anywhere,
        scratch_shapes=[
            pltpu.VMEM((n_copies, chunk, whole.shape[1]), jnp.float32),
            pltpu.SemaphoreType.DMA((n_copies,)),
        ],
        input_output_aliases={0: 0} if n_dep else {},
        compiler_params=pltpu.CompilerParams(vmem_limit_bytes=40 * 1024 * 1024),
    )(*([before] if n_dep else []), *blocks)


def back_kernel(side, part, tall, weight_ref, inner_ref, pieces_ref):
    rows = side * side
    flat = rows + 2 * side
    start = pl.multiple_of(lax.axis_index("ch") * part, 16)
    backs = []
    for b in range(3):
        back = jnp.zeros((flat, part), jnp.float32)
        for a in range(3):
            back = back + lax.dot_general(
                tall[(2 - a) * side : (2 - a) * side + flat, :],
                weight_ref[3 * a + b, pl.ds(start, part), :],
                (((1,), (1,)), ((), ())),
                preferred_element_type=jnp.float32,
            )
        backs.append(back)
    column = lax.broadcasted_iota(jnp.int32, (flat, part), 0) % side
    inner = (
        jnp.where(column == side - 1, 0.0, pltpu.roll(backs[0], flat - 1, 0))
        + backs[1]
        + jnp.where(column == 0, 0.0, pltpu.roll(backs[2], 1, 0))
    )
    inner_ref[...] = inner[side : side + rows]
    west = backs[0].reshape(side + 2, side, part)[:, 0, :]
    east = backs[2].reshape(side + 2, side, part)[:, side - 1, :]
    pieces = jnp.concatenate(
        [
            inner[0:side],
            east[1 : side + 1],
            inner[side + rows :],
            west[1 : side + 1],
            west[0:1],
            east[0:1],
            east[side + 1 :],
            west[side + 1 :],
            jnp.zeros((EXTRA - 4, part), jnp.float32),
        ],
        axis=0,
    )
    pack(pieces.astype(jnp.bfloat16), pieces_ref)


def add_halo_kernel(side, part, place_ref, inner_ref, *refs):
    got_refs, out_ref, got = refs[:-2], refs[-2], refs[-1]
    block = 4 * side + EXTRA
    size = packed_shape(block, part)[0]
    for i, ref in enumerate(got_refs):
        for k in range(3):
            unpack(ref, got, k * size, (3 * i + k) * block, block, part)
    sums = jnp.dot(place_ref[...], got[...], preferred_element_type=jnp.float32)
    rows = side * side
    spread = lambda col: jnp.broadcast_to(col[:, None, :], (side, side, part)).reshape(rows, part)
    column = lax.broadcasted_iota(jnp.int32, (rows, part), 0) % side
    inner = inner_ref[...]
    inner = inner + jnp.where(column == side - 1, spread(sums[side : 2 * side]), 0.0)
    inner = inner + jnp.where(column == 0, spread(sums[3 * side :]), 0.0)
    ends = jnp.concatenate(
        [
            inner[0:side] + sums[0:side],
            inner[side : rows - side],
            inner[rows - side :] + sums[2 * side : 3 * side],
        ],
        axis=0,
    )
    out_ref[...] = ends.astype(jnp.bfloat16)


def parts_of(rows, extra):
    size = (rows + extra) // (32 * PARTS) * 32
    return [size] * (PARTS - 1) + [rows - size * (PARTS - 1)]


def halo_kernel(side, part, n_near, *refs):
    near_refs, tables_in, field_ref = refs[:n_near], refs[n_near], refs[n_near + 1]
    halos_ref, *packet_refs = refs[n_near + 2 : -3]
    near, tables, sem = refs[-3:]
    copy = pltpu.make_async_copy(tables_in, tables, sem)
    copy.start()
    rows = side * side
    unpack_near(near_refs, near, side, part)
    field = field_ref[...].reshape(rows, part)
    sizes = parts_of(rows, 4 * side + EXTRA)
    for k, ref in enumerate(packet_refs):
        pack(field[sum(sizes[:k]) : sum(sizes[: k + 1])], ref)
    copy.wait()
    index = Neighbours(side, tables)
    step = lax.broadcasted_iota(jnp.int32, (side, 1), 0)
    wanted = []
    for e in range(4):
        block, at = index.edge(index.own, e)
        wanted.append(block * (4 * side) + at(step))
    spots = lax.broadcasted_iota(jnp.int32, (EXTRA, 1), 0)
    ends = jnp.full((EXTRA, 1), -1, jnp.int32)
    for c in range(4):
        block, spot = index.corner(index.own, c)
        ends = jnp.where(spots == c, block * (4 * side) + spot, ends)
    pick = onehot(jnp.concatenate(wanted + [ends], axis=0), near.shape[0])
    halos = jnp.dot(pick, near[...], preferred_element_type=jnp.float32).astype(jnp.bfloat16)
    halos_ref[...] = halos
    pack(halos, packet_refs[-1], packed_shape(sizes[-1], part)[0])


def output_kernel(side, part, field_ref, halos_ref, weight_ref, *refs):
    rows = side * side
    ch = lax.axis_index("ch")
    other_refs, (out_ref, cols, other_cols, other) = refs[:PARTS], refs[PARTS:]
    wide = -(-part // 128) * 128
    lanes = pl.multiple_of(ch * (weight_ref.shape[2] - wide), 128)
    sizes = parts_of(rows, 4 * side + EXTRA)
    for k, ref in enumerate(other_refs):
        unpack(ref, other, 0, sum(sizes[:k]), sizes[k], part)
    unpack(other_refs[-1], other, packed_shape(sizes[-1], part)[0], rows, 4 * side + EXTRA, part)
    shifted_columns(side, part, field_ref[...].reshape(rows, part), halos_ref[...], cols)
    shifted_columns(side, part, other[0:rows, :], other[rows:, :], other_cols)
    starts = (pl.multiple_of(ch * part, 16), pl.multiple_of((1 - ch) * part, 16))
    total = jnp.zeros((rows, wide), jnp.float32)
    for a in range(3):
        for b in range(3):
            for ref, first in zip((cols, other_cols), starts):
                total = total + jnp.dot(
                    ref[b, a * side : a * side + rows, :],
                    weight_ref[3 * a + b, pl.ds(first, part), pl.ds(lanes, wide)],
                    preferred_element_type=jnp.float32,
                )
    result = jnp.where(ch == 0, total[:, :part], total[:, wide - part :])
    out_ref[...] = result.astype(jnp.bfloat16)


def body(features, weight, cotangent, edge_tiles, edge_turns, corner_tiles, corner_turns):
    count = lax.axis_size("tile")
    field = features[0]
    side, part = field.shape[0], field.shape[2]
    chans = weight.shape[3]
    rows = side * side
    flat = rows + 2 * side
    block = 4 * side + EXTRA
    taps = weight.reshape(9, chans, chans)
    others = [(0, 1), (1, 0)]
    flops = 2 * rows * 9 * part * chans
    half_bytes = jnp.bfloat16
    chunk = -(-9 * part // (16 * count)) * 16
    half = count * chunk // 2
    scale = 1.0 / math.sqrt(count * rows)

    cot_own = cotangent[0].reshape(rows, part)
    cot_other = lax.ppermute(cot_own, "ch", others)
    sides, field = call(
        functools.partial(sides_kernel, side),
        [vmem(packed_shape(4 * side, part), half_bytes), vmem(field.shape, half_bytes)],
        [field],
    )
    swaps = [by_swap(sides, odd, count) for odd in (0, 1)]
    across = by_mask(sides, 2, count)
    tables = jnp.concatenate([edge_tiles.T, edge_turns.T, corner_tiles.T, corner_turns.T], axis=0)
    table_scratch = [pltpu.SMEM(tables.shape, jnp.int32), pltpu.SemaphoreType.DMA]
    border_pick, cot_own = call(
        functools.partial(border_onehot_kernel, side),
        [vmem((16 * side, 48 * side), half_bytes), vmem((rows, part), half_bytes)],
        [tables, cot_own],
        scratch=table_scratch,
    )
    pair = packed_shape(8 * side, part)
    (beyond,) = call(join_kernel, [vmem(pair, half_bytes)], swaps)
    near = [sides, across, *swaps, by_mask(beyond, 2, count)]
    near, cot_other, border_pick = lax.optimization_barrier((near, cot_other, border_pick))
    (near,) = call(join_kernel, [vmem(packed_shape(24 * side, part), half_bytes)], near)
    mates = by_mask(near, 1, count)
    first, tall, rim, cols = call(
        functools.partial(send_kernel, side, part, scale),
        [
            vmem((2 * part, chans), jnp.float32),
            vmem((rows + 4 * side, chans), half_bytes),
            vmem((4 * side, chans), half_bytes),
            vmem((3, part, rows), half_bytes),
        ],
        [field, cot_own, cot_other],
        flops=flops // 4,
    )
    (second,) = call(
        functools.partial(half_kernel, side, part, scale, 1, (2, 3)),
        [vmem((5 * part // 2, chans), jnp.float32)],
        [cols, tall],
        scratch=[pltpu.VMEM((part, chans), jnp.float32)],
        flops=flops,
    )
    tall, second = lax.optimization_barrier((tall, second))
    (mine,) = call(
        functools.partial(half_kernel, side, part, scale, 0, (0, 1, 2, 3)),
        [vmem((9 * part // 2, chans), jnp.float32)],
        [cols, tall],
        scratch=[pltpu.VMEM((part, chans), jnp.float32)],
        costed=False,
    )
    mates, mine, rim_mate = lax.optimization_barrier((mates, mine, by_mask(rim, 1, count)))
    near = [near, mates]

    stages = mask_stages(count)
    masks = group_masks(stages[1])
    size = half // len(masks)
    held, *send = call(
        functools.partial(border_kernel, side, part, chunk, scale, len(near)),
        [vmem((size, chans), jnp.float32)] + [vmem((size, chans), half_bytes)] * (len(masks) - 1),
        [*near, border_pick, mine, rim, rim_mate, by_mask(first, 1, count), by_mask(second, 1, count)],
        scratch=[pltpu.VMEM((48 * side, part), half_bytes), pltpu.VMEM((half, chans), jnp.float32)],
    )
    send, tall, near = lax.optimization_barrier((send, tall, near))
    got = [by_mask(v, m, count) for v, m in zip(send, masks[1:])]
    inner, pieces = call(
        functools.partial(back_kernel, side, part),
        [vmem((rows, part), jnp.float32), vmem(packed_shape(block, part), half_bytes)],
        [tall, taps],
        flops=flops,
    )
    pieces, near = lax.optimization_barrier((pieces, near))
    here = [pieces, *[by_swap(pieces, odd, count) for odd in (0, 1)]]
    (place,) = call(
        functools.partial(place_kernel, side),
        [vmem((4 * side, 12 * block), half_bytes)],
        [tables],
        scratch=table_scratch,
    )
    halos, *packet = call(
        functools.partial(halo_kernel, side, part, len(near)),
        [vmem((block, part), half_bytes)]
        + [vmem(packed_shape(size, part), half_bytes) for size in parts_of(rows, block)[:-1]]
        + [vmem(packed_shape(parts_of(rows, block)[-1] + block, part), half_bytes)],
        [*near, tables, field],
        scratch=[pltpu.VMEM((48 * side, part), half_bytes), *table_scratch],
    )
    got, here, inner, halos, packet, place = lax.optimization_barrier(
        (got, here, inner, halos, packet, place)
    )
    swap = len(stages[-1]) == 1 and len(stages) > 2
    rs_stages = stages[2:-1] if swap else stages[2:]
    aside = [here, packet]

    def start_aside(send, aside):
        send, here, packet = lax.optimization_barrier((send, *aside))
        (here,) = call(join_kernel, [vmem((3 * pieces.shape[0], pieces.shape[1]), half_bytes)], here)
        return send, here, by_mask(here, 2, count), [lax.ppermute(v, "ch", others) for v in packet]

    for index, bits in enumerate(rs_stages):
        masks = group_masks(bits)
        size = held.shape[0] // len(masks)
        held, *send = call(
            functools.partial(sum_kernel, len(got), len(masks)),
            [vmem((size, chans), jnp.float32)] + [vmem((size, chans), half_bytes)] * (len(masks) - 1),
            [held, *got],
        )
        if index == 0:
            send, here, beside, other_field = start_aside(send, aside)
        got = [by_mask(v, m, count) for v, m in zip(send, masks[1:])]
    (held,) = call(functools.partial(sum_kernel, len(got), 1), [vmem(held.shape, half_bytes)], [held, *got])
    if swap:
        if not rs_stages:
            held, here, beside, other_field = start_aside(held, aside)
        got = by_mask(held, stages[-1][0], count)
        got, here, beside = lax.optimization_barrier((got, here, beside))
        (held,) = call(exchange_kernel, [vmem(held.shape, half_bytes)], [held, got])
    order = [0] if not swap else [0, stages[-1][0]]
    ag_stages = stages[-2:0:-1] if swap else stages[:0:-1]
    for index, bits in enumerate(ag_stages):
        masks = group_masks(bits)
        got = [by_mask(held, m, count) for m in masks[1:]]
        if index < len(ag_stages) - 1:
            order = [m + v for m in masks for v in order]
            (held,) = call(
                join_kernel, [vmem((held.shape[0] * len(masks), chans), half_bytes)], [held, *got]
            )
    order = [[m + v for v in order] for m in masks]
    got_pieces = [here, beside, by_mask(here, 1, count), by_mask(beside, 1, count)]
    (grad_features,) = call(
        functools.partial(add_halo_kernel, side, part),
        [vmem((rows, part), half_bytes)],
        [place, inner, *got_pieces],
        scratch=[pltpu.VMEM((12 * block, part), half_bytes)],
    )
    (output,) = call(
        functools.partial(output_kernel, side, part),
        [vmem((rows, part), half_bytes)],
        [field, halos, taps, *other_field],
        scratch=[
            pltpu.VMEM((3, flat, part), half_bytes),
            pltpu.VMEM((3, flat, part), half_bytes),
            pltpu.VMEM((rows + block, part), half_bytes),
        ],
        flops=2 * flops,
    )
    got, grad_features, output = lax.optimization_barrier((got, grad_features, output))
    got = [held, *got]
    mates = [by_mask(v, 1, count) for v in got]
    whole = vmem((9 * part, chans), jnp.float32)
    own = len(got)
    first = unfold(whole, chunk, [0] * own + [1], order + order[:1], got + mates[:1], None)
    grad_weight = unfold(whole, chunk, [1] * (own - 1), order[1:], mates[1:], first)
    shape = (1, side, side, part)
    return (
        output.reshape(shape),
        grad_features.reshape(shape),
        grad_weight.reshape(3, 3, part, chans),
    )


def solution(mesh):
    return jax.shard_map(
        body,
        mesh=mesh,
        in_specs=(
            P("tile", None, None, "ch"),
            P(),
            P("tile", None, None, "ch"),
            P(),
            P(),
            P(),
            P(),
        ),
        out_specs=(
            P("tile", None, None, "ch"),
            P("tile", None, None, "ch"),
            P(None, None, "ch", None),
        ),
        check_vma=False,
    )
```

```python
import functools
import math

import jax
import jax.numpy as jnp
import numpy as np
from jax import lax
from jax.experimental import pallas as pl
from jax.experimental.pallas import tpu as pltpu
from jax.sharding import PartitionSpec as P

SPAN = 4
EXTRA = 16
PARTS = 3


def turn_tables():
    labels = [[3 * row + col for col in range(3)] for row in range(3)]

    def turn_once(block):
        return [[block[col][2 - row] for col in range(3)] for row in range(3)]

    def sides_of(block):
        return [
            list(block[0]),
            [block[row][2] for row in range(3)],
            list(block[2]),
            [block[row][0] for row in range(3)],
        ]

    def corners_of(block):
        return [block[0][0], block[0][2], block[2][2], block[2][0]]

    base_sides = sides_of(labels)
    base_corners = corners_of(labels)
    edge_table = np.zeros((4, 4), np.int32)
    corner_table = np.zeros((4, 4), np.int32)
    for border in range(4):
        turned = labels
        for quarter in range(4):
            wanted = sides_of(turned)[(border + 2) % 4]
            for side_index in range(4):
                if base_sides[side_index] == wanted:
                    edge_table[border, quarter] = side_index
                if base_sides[side_index][::-1] == wanted:
                    edge_table[border, quarter] = side_index + 4
            corner_cell = corners_of(turned)[(border + 2) % 4]
            for corner_index in range(4):
                if base_corners[corner_index] == corner_cell:
                    corner_table[border, quarter] = corner_index
            turned = turn_once(turned)
    tables = np.concatenate([edge_table, corner_table], axis=0)
    return [sum(int(slot) << (3 * quarter) for quarter, slot in enumerate(row)) for row in tables]


def by_swap(value, odd, count):
    pairs = [
        (i, (i + (SPAN if (i // SPAN) % 2 == odd else -SPAN)) % count) for i in range(count)
    ]
    return lax.ppermute(value, "tile", pairs)


def by_mask(value, mask, count):
    return lax.ppermute(value, "tile", [(i, i ^ mask) for i in range(count)])


def mask_stages(count):
    bits = [1 << b for b in range(count.bit_length() - 1)]
    stages = [bits[:1]]
    rest = bits[1:]
    while rest:
        stages.append(rest[:2])
        rest = rest[2:]
    return stages


def group_masks(bits):
    masks = [0]
    for bit in bits:
        masks = masks + [m + bit for m in masks]
    return masks


def slot_of_mask(mask, count):
    place = 0
    for bits in mask_stages(count)[1:]:
        size = 1 << len(bits)
        place = place * size + (mask // bits[0]) % size
    return place


def slot_in(row, quarter):
    return (row >> (3 * quarter)) & 7


def corner_spot(slot, side):
    return jnp.where(
        slot == 0, 0, jnp.where(slot == 1, side - 1, jnp.where(slot == 2, 3 * side - 1, 2 * side))
    )


def vmem(shape, dtype):
    return jax.ShapeDtypeStruct(shape, dtype)


def call(kernel, outs, args, anywhere=(), scratch=(), flops=0, costed=True):
    in_specs = [
        pl.BlockSpec(memory_space=pltpu.HBM if i in anywhere else pltpu.VMEM) for i in range(len(args))
    ]
    size = costed * sum(math.prod(x.shape) * x.dtype.itemsize for x in list(args) + list(outs))
    return pl.pallas_call(
        kernel,
        out_shape=tuple(outs),
        in_specs=in_specs,
        out_specs=tuple(pl.BlockSpec(memory_space=pltpu.VMEM) for _ in outs),
        scratch_shapes=list(scratch),
        compiler_params=pltpu.CompilerParams(vmem_limit_bytes=40 * 1024 * 1024),
        cost_estimate=pl.CostEstimate(flops=flops, bytes_accessed=size, transcendentals=0),
    )(*args)


def packed_shape(rows, part):
    if part % 128 != 64:
        return (rows, part)
    return (rows * (part // 128) + rows // 2, 128)


def pack(value, out_ref, first=0):
    rows, part = value.shape
    if part % 128 != 64:
        out_ref[first : first + rows, :] = value
        return
    for i in range(part // 128):
        out_ref[first + i * rows : first + (i + 1) * rows, :] = value[:, i * 128 : (i + 1) * 128]
    rest = value[:, part - 64 :]
    at = first + rows * (part // 128)
    out_ref[at : at + rows // 2, :] = jnp.concatenate([rest[: rows // 2], rest[rows // 2 :]], axis=1)


def unpack(ref, out_ref, first, row, rows, part):
    if part % 128 != 64:
        out_ref[row : row + rows, :] = ref[first : first + rows, :]
        return
    for i in range(part // 128):
        out_ref[row : row + rows, i * 128 : (i + 1) * 128] = ref[first + i * rows : first + (i + 1) * rows, :]
    at = first + rows * (part // 128)
    rest = ref[at : at + rows // 2, :]
    out_ref[row : row + rows // 2, part - 64 :] = rest[:, :64]
    out_ref[row + rows // 2 : row + rows, part - 64 :] = rest[:, 64:]


def sides_kernel(side, field_ref, sides_ref, copy_ref):
    sides = jnp.concatenate(
        [field_ref[0], field_ref[:, side - 1, :], field_ref[side - 1], field_ref[:, 0, :]], axis=0
    )
    pack(sides, sides_ref)
    copy_ref[...] = field_ref[...]


def shifted_columns(side, part, field, halos, out_ref):
    rows = side * side
    flat = rows + 2 * side
    column = lax.broadcasted_iota(jnp.int32, (flat, part), 0) % side
    if halos is None:
        none = jnp.zeros((side, part), jnp.float32)
        tall = jnp.concatenate([none, field.astype(jnp.float32), none], axis=0)
        west = east = 0.0
    else:
        edge = halos.astype(jnp.float32)
        tall = jnp.concatenate([edge[0:side], field.astype(jnp.float32), edge[2 * side : 3 * side]], axis=0)
        corner = [edge[4 * side + c : 4 * side + c + 1] for c in range(4)]
        spread = lambda col: jnp.broadcast_to(col[:, None, :], (side + 2, side, part)).reshape(flat, part)
        east = spread(jnp.concatenate([corner[1], edge[side : 2 * side], corner[2]], axis=0))
        west = spread(jnp.concatenate([corner[0], edge[3 * side : 4 * side], corner[3]], axis=0))
    out_ref[0] = jnp.where(column == 0, west, pltpu.roll(tall, 1, 0)).astype(jnp.bfloat16)
    out_ref[1] = tall.astype(jnp.bfloat16)
    out_ref[2] = jnp.where(column == side - 1, east, pltpu.roll(tall, flat - 1, 0)).astype(jnp.bfloat16)


class Neighbours:
    def __init__(self, side, tables):
        self.side = side
        self.et, self.eu, self.ct, self.cu = [tables.at[4 * i : 4 * i + 4] for i in range(4)]
        self.digits = turn_tables()
        self.count = lax.axis_size("tile")
        self.own = lax.axis_index("tile")

    def block(self, source):
        groups = self.count // SPAN
        slab = lax.rem(source // SPAN - self.own // SPAN + groups, groups)
        cross = source ^ self.own
        turn = lax.rem(cross // 2, 2)
        even = lax.rem(self.own // SPAN, 2) == 0
        at = jnp.where(slab == 0, turn, jnp.where((slab == 1) == even, 2, 3) + 2 * turn)
        return 6 * lax.rem(cross, 2) + at

    def edge(self, tile, e):
        slot = slot_in(self.digits[e], self.eu[e, tile])
        start = lax.rem(slot, 4) * self.side
        end = start + self.side - 1
        return self.block(self.et[e, tile]), lambda at: jnp.where(slot >= 4, end - at, start + at)

    def corner(self, tile, c):
        slot = slot_in(self.digits[4 + c], self.cu[c, tile])
        return self.block(self.ct[c, tile]), corner_spot(slot, self.side)


def onehot(wanted, width):
    lane = lax.broadcasted_iota(jnp.int32, (wanted.shape[0], width), 1)
    return jnp.where(lane == wanted, 1.0, 0.0).astype(jnp.bfloat16)


def border_onehot_kernel(side, tables_in, cot_in, border_ref, cot_ref, tables, sem):
    copy = pltpu.make_async_copy(tables_in, tables, sem)
    copy.start()
    cot_ref[...] = cot_in[...]
    border_ref[...] = jnp.zeros_like(border_ref)
    copy.wait()
    near = Neighbours(side, tables)
    low = lax.rem(near.own, 2) == 0
    width = 4 * side
    step = lax.broadcasted_iota(jnp.int32, (side, 1), 0)

    def put(row, block, wanted, add=False):
        here = (slice(row, row + side), pl.ds(pl.multiple_of(block * width, 128), width))
        value = onehot(wanted, width)
        border_ref[here] = border_ref[here] + value if add else value

    for m, tile in enumerate((near.own, near.own ^ 1)):
        first = 2 * m * side
        flat = [near.edge(tile, e) for e in range(4)]
        corners = [near.corner(tile, c) for c in range(4)]
        pick = lambda a, b: (jnp.where(low, a[0], b[0]), lambda at: jnp.where(low, a[1](at), b[1](at)))
        block, at = pick(flat[0], flat[2])
        left, right = [
            (jnp.where(low, corners[a][0], corners[b][0]), jnp.where(low, corners[a][1], corners[b][1]))
            for a, b in ((0, 3), (1, 2))
        ]
        along = jnp.where(low, step - 1, step + 1)
        fits = (along >= 0) & (along < side)
        put(first, block, jnp.where(step == 0, -1, at(step - 1)))
        put(first, left[0], jnp.where(step == 0, left[1], -1), add=True)
        put(first + side, flat[3][0], jnp.where(fits, flat[3][1](along), -1))
        put(first + 4 * side, block, at(step))
        put(first + 8 * side, block, jnp.where(step == side - 1, -1, at(step + 1)))
        put(first + 8 * side, right[0], jnp.where(step == side - 1, right[1], -1), add=True)
        put(first + 9 * side, flat[1][0], jnp.where(fits, flat[1][1](along), -1))
        block, at = pick(flat[3], flat[1])
        put(first + 13 * side, block, at(step))


def place_kernel(side, tables_in, place_ref, tables, sem):
    copy = pltpu.make_async_copy(tables_in, tables, sem)
    copy.start()
    copy.wait()
    near = Neighbours(side, tables)
    block = 4 * side + EXTRA
    lane = lax.broadcasted_iota(jnp.int32, (1, block), 1)
    row = lax.broadcasted_iota(jnp.int32, (4 * side, block), 0)
    places = []
    swap = jnp.where(lax.rem(near.own // SPAN, 2) == 0, SPAN, -SPAN)
    for mask in (0, 2, 1, 3):
        for offset in (0, swap, -swap):
            source = lax.rem((near.own ^ mask) + offset + near.count, near.count)
            target = jnp.full((1, block), -1, jnp.int32)
            for e in range(4):
                slot = slot_in(near.digits[e], near.eu[e, source])
                along = lane - e * side
                along = jnp.where(slot >= 4, side - 1 - along, along)
                hit = (lane >= e * side) & (lane < (e + 1) * side) & (near.et[e, source] == near.own)
                target = jnp.where(hit, lax.rem(slot, 4) * side + along, target)
                spot = corner_spot(slot_in(near.digits[4 + e], near.cu[e, source]), side)
                hit = (lane == 4 * side + e) & (near.ct[e, source] == near.own)
                target = jnp.where(hit, spot, target)
            places.append(jnp.where(row == target, 1.0, 0.0))
    place_ref[...] = jnp.concatenate(places, axis=1).astype(jnp.bfloat16)


def tap_product(side, scale, tap, cols, tall):
    rows = side * side
    start = pl.multiple_of((3 - tap // 3) * side, 16)
    value = jnp.dot(
        cols[lax.rem(tap, 3)], tall[pl.ds(start, rows), :], preferred_element_type=jnp.float32
    )
    return value * scale


def send_kernel(
    side, part, scale, field_ref, own_ref, other_ref, send_ref, tall_ref, rim_ref, cols_ref
):
    rows = side * side
    first = lax.axis_index("ch") == 0
    here = slice(2 * side, 2 * side + rows)
    blank = jnp.zeros((2 * side, tall_ref.shape[1]), jnp.bfloat16)
    tall_ref[0 : 2 * side, :] = blank
    tall_ref[2 * side + rows :, :] = blank

    @pl.when(first)
    def _():
        tall_ref[here, 0:part] = own_ref[...]
        tall_ref[here, part:] = other_ref[...]

    @pl.when(jnp.logical_not(first))
    def _():
        tall_ref[here, 0:part] = other_ref[...]
        tall_ref[here, part:] = own_ref[...]

    cot = tall_ref[here, :]
    column = lax.broadcasted_iota(jnp.int32, (rows, part), 0) % side
    field = field_ref[...].reshape(rows, part).astype(jnp.float32)
    cols_ref[0] = jnp.where(column == 0, 0.0, pltpu.roll(field, 1, 0)).astype(jnp.bfloat16).T
    cols_ref[1] = field.astype(jnp.bfloat16).T
    cols_ref[2] = jnp.where(column == side - 1, 0.0, pltpu.roll(field, rows - 1, 0)).astype(jnp.bfloat16).T
    which = 1 - lax.rem(lax.axis_index("tile"), 2)
    for j in range(3):
        send_ref[j * part : (j + 1) * part, :] = tap_product(side, scale, j + 5 * which, cols_ref, tall_ref)
    rim = cot.reshape(side, side, cot.shape[1])
    rim_ref[...] = jnp.concatenate([cot[0:side], cot[rows - side :], rim[:, 0, :], rim[:, side - 1, :]], axis=0)


def half_kernel(side, part, scale, mate, taps, cols, tall, out_ref, middle):
    which = lax.rem(lax.axis_index("tile") + mate, 2)
    for at, j in enumerate(taps):
        out_ref[at * part : (at + 1) * part, :] = tap_product(side, scale, j + 5 * which, cols, tall)
    middle[...] = tap_product(side, scale, 4, cols, tall)
    start = pl.multiple_of(which * (part // 2), 16)
    out_ref[len(taps) * part :, :] = middle[pl.ds(start, part // 2), :]


def unpack_near(near_refs, near, side, part):
    size = packed_shape(4 * side, part)[0]
    row = 0
    for ref in near_refs:
        for k in range(ref.shape[0] // size):
            unpack(ref, near, k * size, row, 4 * side, part)
            row += 4 * side


def border_kernel(side, part, chunk, scale, n_near, *refs):
    near_refs = refs[:n_near]
    onehot_ref, mine_ref, rim_ref, mate_ref, first_ref, second_ref = refs[n_near : n_near + 6]
    outs, near, total = refs[n_near + 6 : -2], refs[-2], refs[-1]
    count = lax.axis_size("tile")
    own = lax.axis_index("tile")
    core = lax.rem(own, 2)
    unpack_near(near_refs, near, side, part)
    half = part // 2
    used = 9 * half

    def place(start, value):
        total[pl.ds(pl.multiple_of(start, 16), value.shape[0]), :] = value

    cut = first_ref.shape[0]
    place(core * half, mine_ref[0:cut, :] + first_ref[...])
    if cut < 4 * part:
        place(core * half + cut, mine_ref[cut : 4 * part, :] + second_ref[0 : 4 * part - cut, :])
    place((1 - core) * 4 * part, mine_ref[4 * part :, :] + second_ref[4 * part - cut :, :])
    total[used:, :] = jnp.zeros((total.shape[0] - used, total.shape[1]), jnp.float32)
    left = jnp.dot(onehot_ref[...], near[...], preferred_element_type=jnp.float32).astype(jnp.bfloat16)

    def rim(ref, at):
        return ref[pl.ds(pl.multiple_of(at, 16), side), :]

    for q in range(4):
        column = (2 + q // 2) * side if q < 3 else (2 + core) * side
        right = jnp.concatenate(
            [value for ref in (rim_ref, mate_ref) for value in (rim(ref, core * side), rim(ref, column))],
            axis=0,
        )
        value = lax.dot_general(
            left[q * 4 * side : (q + 1) * 4 * side],
            right,
            (((0,), (0,)), ((), ())),
            preferred_element_type=jnp.float32,
        )
        if q < 3:
            start = q * part + core * (part // 2 + part)
        else:
            start = 3 * part - core * (3 * part - part // 2)
        here = pl.ds(pl.multiple_of(start, 16), part)
        total[here, :] = total[here, :] + value * scale
    size = outs[0].shape[0]
    for index in range(count // 2):
        to = slot_of_mask(2 * index, count) * chunk
        block = pl.multiple_of(((own // 2) ^ index) * chunk, 16)
        out = outs[to // size]
        out[to % size : to % size + chunk, :] = total[pl.ds(block, chunk), :].astype(out.dtype)


def sum_kernel(n_got, n_out, *refs):
    held_ref, got_refs, outs = refs[0], refs[1 : 1 + n_got], refs[1 + n_got :]
    size = held_ref.shape[0] // n_out
    for index in range(n_out):
        here = slice(index * size, (index + 1) * size)
        value = held_ref[here, :]
        for ref in got_refs:
            value = value + ref[here, :].astype(jnp.float32)
        outs[index][...] = value.astype(outs[index].dtype)


def exchange_kernel(held_ref, got_ref, out_ref):
    half = held_ref.shape[0] // 2
    for a, b in ((0, half), (half, 0)):
        value = held_ref[a : a + half, :].astype(jnp.float32) + got_ref[b : b + half, :].astype(jnp.float32)
        out_ref[a : a + half, :] = value.astype(out_ref.dtype)


def join_kernel(*refs):
    row = 0
    for ref in refs[:-1]:
        refs[-1][row : row + ref.shape[0], :] = ref[...]
        row += ref.shape[0]


def unfold_kernel(used, chunk, bits, masks, n_dep, *refs):
    refs = refs[n_dep:]
    n = len(masks)
    in_refs, out_ref, wide, sems = refs[:n], refs[n], refs[n + 1], refs[n + 2]
    own = lax.axis_index("tile")
    full, rest = used // chunk, used % chunk
    copies = []
    for i, (ref, inner, bit) in enumerate(zip(in_refs, masks, bits)):
        origin = (lax.rem(own, 2) ^ bit) * used
        for k, mask in enumerate(inner):
            at = i * len(inner) + k
            wide[at] = ref[k * chunk : (k + 1) * chunk, :].astype(jnp.float32)
            block = (own ^ mask) // 2
            start = pl.multiple_of(origin + block * chunk, 16)
            copies.append(
                (
                    block < full,
                    pltpu.make_async_copy(wide.at[at], out_ref.at[pl.ds(start, chunk), :], sems.at[at]),
                )
            )
            if rest:
                start = pl.multiple_of(origin + full * chunk, 16)
                copies.append(
                    (
                        block == full,
                        pltpu.make_async_copy(
                            wide.at[at, 0:rest], out_ref.at[pl.ds(start, rest), :], sems.at[at]
                        ),
                    )
                )
    for going, copy in copies:
        pl.when(going)(copy.start)
    for going, copy in copies:
        pl.when(going)(copy.wait)


def unfold(whole, chunk, bits, masks, blocks, before):
    n_dep = 0 if before is None else 1
    anywhere = pl.BlockSpec(memory_space=pl.ANY)
    n_copies = len(masks) * len(masks[0])
    return pl.pallas_call(
        functools.partial(unfold_kernel, whole.shape[0] // 2, chunk, bits, masks, n_dep),
        out_shape=whole,
        in_specs=[anywhere] * n_dep + [pl.BlockSpec(memory_space=pltpu.VMEM)] * len(blocks),
        out_specs=anywhere,
        scratch_shapes=[
            pltpu.VMEM((n_copies, chunk, whole.shape[1]), jnp.float32),
            pltpu.SemaphoreType.DMA((n_copies,)),
        ],
        input_output_aliases={0: 0} if n_dep else {},
        compiler_params=pltpu.CompilerParams(vmem_limit_bytes=40 * 1024 * 1024),
    )(*([before] if n_dep else []), *blocks)


def back_kernel(side, part, tall, weight_ref, inner_ref, pieces_ref):
    rows = side * side
    flat = rows + 2 * side
    start = pl.multiple_of(lax.axis_index("ch") * part, 16)
    backs = []
    for b in range(3):
        back = jnp.zeros((flat, part), jnp.float32)
        for a in range(3):
            back = back + lax.dot_general(
                tall[(2 - a) * side : (2 - a) * side + flat, :],
                weight_ref[3 * a + b, pl.ds(start, part), :],
                (((1,), (1,)), ((), ())),
                preferred_element_type=jnp.float32,
            )
        backs.append(back)
    column = lax.broadcasted_iota(jnp.int32, (flat, part), 0) % side
    inner = (
        jnp.where(column == side - 1, 0.0, pltpu.roll(backs[0], flat - 1, 0))
        + backs[1]
        + jnp.where(column == 0, 0.0, pltpu.roll(backs[2], 1, 0))
    )
    inner_ref[...] = inner[side : side + rows]
    west = backs[0].reshape(side + 2, side, part)[:, 0, :]
    east = backs[2].reshape(side + 2, side, part)[:, side - 1, :]
    pieces = jnp.concatenate(
        [
            inner[0:side],
            east[1 : side + 1],
            inner[side + rows :],
            west[1 : side + 1],
            west[0:1],
            east[0:1],
            east[side + 1 :],
            west[side + 1 :],
            jnp.zeros((EXTRA - 4, part), jnp.float32),
        ],
        axis=0,
    )
    pack(pieces.astype(jnp.bfloat16), pieces_ref)


def add_halo_kernel(side, part, place_ref, inner_ref, *refs):
    got_refs, out_ref, got = refs[:-2], refs[-2], refs[-1]
    block = 4 * side + EXTRA
    size = packed_shape(block, part)[0]
    for i, ref in enumerate(got_refs):
        for k in range(3):
            unpack(ref, got, k * size, (3 * i + k) * block, block, part)
    sums = jnp.dot(place_ref[...], got[...], preferred_element_type=jnp.float32)
    rows = side * side
    spread = lambda col: jnp.broadcast_to(col[:, None, :], (side, side, part)).reshape(rows, part)
    column = lax.broadcasted_iota(jnp.int32, (rows, part), 0) % side
    inner = inner_ref[...]
    inner = inner + jnp.where(column == side - 1, spread(sums[side : 2 * side]), 0.0)
    inner = inner + jnp.where(column == 0, spread(sums[3 * side :]), 0.0)
    ends = jnp.concatenate(
        [
            inner[0:side] + sums[0:side],
            inner[side : rows - side],
            inner[rows - side :] + sums[2 * side : 3 * side],
        ],
        axis=0,
    )
    out_ref[...] = ends.astype(jnp.bfloat16)


def parts_of(rows, extra):
    size = (rows + extra) // (32 * PARTS) * 32
    return [size] * (PARTS - 1) + [rows - size * (PARTS - 1)]


def halo_kernel(side, part, n_near, *refs):
    near_refs, tables_in, field_ref = refs[:n_near], refs[n_near], refs[n_near + 1]
    halos_ref, *packet_refs = refs[n_near + 2 : -3]
    near, tables, sem = refs[-3:]
    copy = pltpu.make_async_copy(tables_in, tables, sem)
    copy.start()
    rows = side * side
    unpack_near(near_refs, near, side, part)
    field = field_ref[...].reshape(rows, part)
    sizes = parts_of(rows, 4 * side + EXTRA)
    for k, ref in enumerate(packet_refs):
        pack(field[sum(sizes[:k]) : sum(sizes[: k + 1])], ref)
    copy.wait()
    index = Neighbours(side, tables)
    step = lax.broadcasted_iota(jnp.int32, (side, 1), 0)
    wanted = []
    for e in range(4):
        block, at = index.edge(index.own, e)
        wanted.append(block * (4 * side) + at(step))
    spots = lax.broadcasted_iota(jnp.int32, (EXTRA, 1), 0)
    ends = jnp.full((EXTRA, 1), -1, jnp.int32)
    for c in range(4):
        block, spot = index.corner(index.own, c)
        ends = jnp.where(spots == c, block * (4 * side) + spot, ends)
    pick = onehot(jnp.concatenate(wanted + [ends], axis=0), near.shape[0])
    halos = jnp.dot(pick, near[...], preferred_element_type=jnp.float32).astype(jnp.bfloat16)
    halos_ref[...] = halos
    pack(halos, packet_refs[-1], packed_shape(sizes[-1], part)[0])


def output_kernel(side, part, field_ref, halos_ref, weight_ref, *refs):
    rows = side * side
    ch = lax.axis_index("ch")
    other_refs, (out_ref, cols, other_cols, other) = refs[:PARTS], refs[PARTS:]
    wide = -(-part // 128) * 128
    lanes = pl.multiple_of(ch * (weight_ref.shape[2] - wide), 128)
    sizes = parts_of(rows, 4 * side + EXTRA)
    for k, ref in enumerate(other_refs):
        unpack(ref, other, 0, sum(sizes[:k]), sizes[k], part)
    unpack(other_refs[-1], other, packed_shape(sizes[-1], part)[0], rows, 4 * side + EXTRA, part)
    shifted_columns(side, part, field_ref[...].reshape(rows, part), halos_ref[...], cols)
    shifted_columns(side, part, other[0:rows, :], other[rows:, :], other_cols)
    starts = (pl.multiple_of(ch * part, 16), pl.multiple_of((1 - ch) * part, 16))
    total = jnp.zeros((rows, wide), jnp.float32)
    for a in range(3):
        for b in range(3):
            for ref, first in zip((cols, other_cols), starts):
                total = total + jnp.dot(
                    ref[b, a * side : a * side + rows, :],
                    weight_ref[3 * a + b, pl.ds(first, part), pl.ds(lanes, wide)],
                    preferred_element_type=jnp.float32,
                )
    result = jnp.where(ch == 0, total[:, :part], total[:, wide - part :])
    out_ref[...] = result.astype(jnp.bfloat16)


def body(features, weight, cotangent, edge_tiles, edge_turns, corner_tiles, corner_turns):
    count = lax.axis_size("tile")
    field = features[0]
    side, part = field.shape[0], field.shape[2]
    chans = weight.shape[3]
    rows = side * side
    flat = rows + 2 * side
    block = 4 * side + EXTRA
    taps = weight.reshape(9, chans, chans)
    others = [(0, 1), (1, 0)]
    flops = 2 * rows * 9 * part * chans
    half_bytes = jnp.bfloat16
    chunk = -(-9 * part // (16 * count)) * 16
    half = count * chunk // 2
    scale = 1.0 / math.sqrt(count * rows)

    cot_own = cotangent[0].reshape(rows, part)
    cot_other = lax.ppermute(cot_own, "ch", others)
    sides, field = call(
        functools.partial(sides_kernel, side),
        [vmem(packed_shape(4 * side, part), half_bytes), vmem(field.shape, half_bytes)],
        [field],
    )
    swaps = [by_swap(sides, odd, count) for odd in (0, 1)]
    across = by_mask(sides, 2, count)
    tables = jnp.concatenate([edge_tiles.T, edge_turns.T, corner_tiles.T, corner_turns.T], axis=0)
    table_scratch = [pltpu.SMEM(tables.shape, jnp.int32), pltpu.SemaphoreType.DMA]
    border_pick, cot_own = call(
        functools.partial(border_onehot_kernel, side),
        [vmem((16 * side, 48 * side), half_bytes), vmem((rows, part), half_bytes)],
        [tables, cot_own],
        scratch=table_scratch,
    )
    pair = packed_shape(8 * side, part)
    (beyond,) = call(join_kernel, [vmem(pair, half_bytes)], swaps)
    near = [sides, across, *swaps, by_mask(beyond, 2, count)]
    near, cot_other, border_pick = lax.optimization_barrier((near, cot_other, border_pick))
    (near,) = call(join_kernel, [vmem(packed_shape(24 * side, part), half_bytes)], near)
    mates = by_mask(near, 1, count)
    first, tall, rim, cols = call(
        functools.partial(send_kernel, side, part, scale),
        [
            vmem((3 * part, chans), jnp.float32),
            vmem((rows + 4 * side, chans), half_bytes),
            vmem((4 * side, chans), half_bytes),
            vmem((3, part, rows), half_bytes),
        ],
        [field, cot_own, cot_other],
        flops=flops // 4,
    )
    (second,) = call(
        functools.partial(half_kernel, side, part, scale, 1, (3,)),
        [vmem((3 * part // 2, chans), jnp.float32)],
        [cols, tall],
        scratch=[pltpu.VMEM((part, chans), jnp.float32)],
        flops=flops,
    )
    tall, second = lax.optimization_barrier((tall, second))
    (mine,) = call(
        functools.partial(half_kernel, side, part, scale, 0, (0, 1, 2, 3)),
        [vmem((9 * part // 2, chans), jnp.float32)],
        [cols, tall],
        scratch=[pltpu.VMEM((part, chans), jnp.float32)],
        costed=False,
    )
    mates, mine, rim_mate = lax.optimization_barrier((mates, mine, by_mask(rim, 1, count)))
    near = [near, mates]

    stages = mask_stages(count)
    masks = group_masks(stages[1])
    size = half // len(masks)
    held, *send = call(
        functools.partial(border_kernel, side, part, chunk, scale, len(near)),
        [vmem((size, chans), jnp.float32)] + [vmem((size, chans), half_bytes)] * (len(masks) - 1),
        [*near, border_pick, mine, rim, rim_mate, by_mask(first, 1, count), by_mask(second, 1, count)],
        scratch=[pltpu.VMEM((48 * side, part), half_bytes), pltpu.VMEM((half, chans), jnp.float32)],
    )
    send, tall, near = lax.optimization_barrier((send, tall, near))
    got = [by_mask(v, m, count) for v, m in zip(send, masks[1:])]
    inner, pieces = call(
        functools.partial(back_kernel, side, part),
        [vmem((rows, part), jnp.float32), vmem(packed_shape(block, part), half_bytes)],
        [tall, taps],
        flops=flops,
    )
    pieces, near = lax.optimization_barrier((pieces, near))
    here = [pieces, *[by_swap(pieces, odd, count) for odd in (1, 0)][::-1]]
    (place,) = call(
        functools.partial(place_kernel, side),
        [vmem((4 * side, 12 * block), half_bytes)],
        [tables],
        scratch=table_scratch,
    )
    halos, *packet = call(
        functools.partial(halo_kernel, side, part, len(near)),
        [vmem((block, part), half_bytes)]
        + [vmem(packed_shape(size, part), half_bytes) for size in parts_of(rows, block)[:-1]]
        + [vmem(packed_shape(parts_of(rows, block)[-1] + block, part), half_bytes)],
        [*near, tables, field],
        scratch=[pltpu.VMEM((48 * side, part), half_bytes), *table_scratch],
    )
    got, here, inner, halos, packet, place = lax.optimization_barrier(
        (got, here, inner, halos, packet, place)
    )
    swap = len(stages[-1]) == 1 and len(stages) > 2
    rs_stages = stages[2:-1] if swap else stages[2:]
    aside = [here, packet]

    def start_aside(send, aside):
        send, here, packet = lax.optimization_barrier((send, *aside))
        (here,) = call(join_kernel, [vmem((3 * pieces.shape[0], pieces.shape[1]), half_bytes)], here)
        return send, here, by_mask(here, 2, count), [lax.ppermute(v, "ch", others) for v in packet]

    for index, bits in enumerate(rs_stages):
        masks = group_masks(bits)
        size = held.shape[0] // len(masks)
        held, *send = call(
            functools.partial(sum_kernel, len(got), len(masks)),
            [vmem((size, chans), jnp.float32)] + [vmem((size, chans), half_bytes)] * (len(masks) - 1),
            [held, *got],
        )
        if index == 0:
            send, here, beside, other_field = start_aside(send, aside)
        got = [by_mask(v, m, count) for v, m in zip(send, masks[1:])]
    (held,) = call(functools.partial(sum_kernel, len(got), 1), [vmem(held.shape, half_bytes)], [held, *got])
    if swap:
        if not rs_stages:
            held, here, beside, other_field = start_aside(held, aside)
        got = by_mask(held, stages[-1][0], count)
        got, here, beside = lax.optimization_barrier((got, here, beside))
        (held,) = call(exchange_kernel, [vmem(held.shape, half_bytes)], [held, got])
    order = [0] if not swap else [0, stages[-1][0]]
    ag_stages = stages[-2:0:-1] if swap else stages[:0:-1]
    for index, bits in enumerate(ag_stages):
        masks = group_masks(bits)
        got = [by_mask(held, m, count) for m in masks[1:]]
        if index < len(ag_stages) - 1:
            order = [m + v for m in masks for v in order]
            (held,) = call(
                join_kernel, [vmem((held.shape[0] * len(masks), chans), half_bytes)], [held, *got]
            )
    order = [[m + v for v in order] for m in masks]
    got_pieces = [here, beside, by_mask(here, 1, count), by_mask(beside, 1, count)]
    (grad_features,) = call(
        functools.partial(add_halo_kernel, side, part),
        [vmem((rows, part), half_bytes)],
        [place, inner, *got_pieces],
        scratch=[pltpu.VMEM((12 * block, part), half_bytes)],
    )
    (output,) = call(
        functools.partial(output_kernel, side, part),
        [vmem((rows, part), half_bytes)],
        [field, halos, taps, *other_field],
        scratch=[
            pltpu.VMEM((3, flat, part), half_bytes),
            pltpu.VMEM((3, flat, part), half_bytes),
            pltpu.VMEM((rows + block, part), half_bytes),
        ],
        flops=2 * flops,
    )
    got, grad_features, output = lax.optimization_barrier((got, grad_features, output))
    got = [held, *got]
    mates = [by_mask(v, 1, count) for v in got]
    whole = vmem((9 * part, chans), jnp.float32)
    own = len(got)
    first = unfold(whole, chunk, [0] * own + [1], order + order[:1], got + mates[:1], None)
    grad_weight = unfold(whole, chunk, [1] * (own - 1), order[1:], mates[1:], first)
    shape = (1, side, side, part)
    return (
        output.reshape(shape),
        grad_features.reshape(shape),
        grad_weight.reshape(3, 3, part, chans),
    )


def solution(mesh):
    return jax.shard_map(
        body,
        mesh=mesh,
        in_specs=(
            P("tile", None, None, "ch"),
            P(),
            P("tile", None, None, "ch"),
            P(),
            P(),
            P(),
            P(),
        ),
        out_specs=(
            P("tile", None, None, "ch"),
            P("tile", None, None, "ch"),
            P(None, None, "ch", None),
        ),
        check_vma=False,
    )
```

```python
import functools
import math

import jax
import jax.numpy as jnp
import numpy as np
from jax import lax
from jax.experimental import pallas as pl
from jax.experimental.pallas import tpu as pltpu
from jax.sharding import PartitionSpec as P

SPAN = 4
EXTRA = 16
PARTS = 3


def turn_tables():
    labels = [[3 * row + col for col in range(3)] for row in range(3)]

    def turn_once(block):
        return [[block[col][2 - row] for col in range(3)] for row in range(3)]

    def sides_of(block):
        return [
            list(block[0]),
            [block[row][2] for row in range(3)],
            list(block[2]),
            [block[row][0] for row in range(3)],
        ]

    def corners_of(block):
        return [block[0][0], block[0][2], block[2][2], block[2][0]]

    base_sides = sides_of(labels)
    base_corners = corners_of(labels)
    edge_table = np.zeros((4, 4), np.int32)
    corner_table = np.zeros((4, 4), np.int32)
    for border in range(4):
        turned = labels
        for quarter in range(4):
            wanted = sides_of(turned)[(border + 2) % 4]
            for side_index in range(4):
                if base_sides[side_index] == wanted:
                    edge_table[border, quarter] = side_index
                if base_sides[side_index][::-1] == wanted:
                    edge_table[border, quarter] = side_index + 4
            corner_cell = corners_of(turned)[(border + 2) % 4]
            for corner_index in range(4):
                if base_corners[corner_index] == corner_cell:
                    corner_table[border, quarter] = corner_index
            turned = turn_once(turned)
    tables = np.concatenate([edge_table, corner_table], axis=0)
    return [sum(int(slot) << (3 * quarter) for quarter, slot in enumerate(row)) for row in tables]


def by_swap(value, odd, count):
    pairs = [
        (i, (i + (SPAN if (i // SPAN) % 2 == odd else -SPAN)) % count) for i in range(count)
    ]
    return lax.ppermute(value, "tile", pairs)


def by_mask(value, mask, count):
    return lax.ppermute(value, "tile", [(i, i ^ mask) for i in range(count)])


def mask_stages(count):
    bits = [1 << b for b in range(count.bit_length() - 1)]
    stages = [bits[:1]]
    rest = bits[1:]
    while rest:
        stages.append(rest[:2])
        rest = rest[2:]
    return stages


def group_masks(bits):
    masks = [0]
    for bit in bits:
        masks = masks + [m + bit for m in masks]
    return masks


def slot_of_mask(mask, count):
    place = 0
    for bits in mask_stages(count)[1:]:
        size = 1 << len(bits)
        place = place * size + (mask // bits[0]) % size
    return place


def slot_in(row, quarter):
    return (row >> (3 * quarter)) & 7


def corner_spot(slot, side):
    return jnp.where(
        slot == 0, 0, jnp.where(slot == 1, side - 1, jnp.where(slot == 2, 3 * side - 1, 2 * side))
    )


def vmem(shape, dtype):
    return jax.ShapeDtypeStruct(shape, dtype)


def call(kernel, outs, args, anywhere=(), scratch=(), flops=0, costed=True):
    in_specs = [
        pl.BlockSpec(memory_space=pltpu.HBM if i in anywhere else pltpu.VMEM) for i in range(len(args))
    ]
    size = costed * sum(math.prod(x.shape) * x.dtype.itemsize for x in list(args) + list(outs))
    return pl.pallas_call(
        kernel,
        out_shape=tuple(outs),
        in_specs=in_specs,
        out_specs=tuple(pl.BlockSpec(memory_space=pltpu.VMEM) for _ in outs),
        scratch_shapes=list(scratch),
        compiler_params=pltpu.CompilerParams(vmem_limit_bytes=40 * 1024 * 1024),
        cost_estimate=pl.CostEstimate(flops=flops, bytes_accessed=size, transcendentals=0),
    )(*args)


def packed_shape(rows, part):
    if part % 128 != 64:
        return (rows, part)
    return (rows * (part // 128) + rows // 2, 128)


def pack(value, out_ref, first=0):
    rows, part = value.shape
    if part % 128 != 64:
        out_ref[first : first + rows, :] = value
        return
    for i in range(part // 128):
        out_ref[first + i * rows : first + (i + 1) * rows, :] = value[:, i * 128 : (i + 1) * 128]
    rest = value[:, part - 64 :]
    at = first + rows * (part // 128)
    out_ref[at : at + rows // 2, :] = jnp.concatenate([rest[: rows // 2], rest[rows // 2 :]], axis=1)


def unpack(ref, out_ref, first, row, rows, part):
    if part % 128 != 64:
        out_ref[row : row + rows, :] = ref[first : first + rows, :]
        return
    for i in range(part // 128):
        out_ref[row : row + rows, i * 128 : (i + 1) * 128] = ref[first + i * rows : first + (i + 1) * rows, :]
    at = first + rows * (part // 128)
    rest = ref[at : at + rows // 2, :]
    out_ref[row : row + rows // 2, part - 64 :] = rest[:, :64]
    out_ref[row + rows // 2 : row + rows, part - 64 :] = rest[:, 64:]


def sides_kernel(side, field_ref, sides_ref, copy_ref):
    sides = jnp.concatenate(
        [field_ref[0], field_ref[:, side - 1, :], field_ref[side - 1], field_ref[:, 0, :]], axis=0
    )
    pack(sides, sides_ref)
    copy_ref[...] = field_ref[...]


def shifted_columns(side, part, field, halos, out_ref):
    rows = side * side
    flat = rows + 2 * side
    column = lax.broadcasted_iota(jnp.int32, (flat, part), 0) % side
    if halos is None:
        none = jnp.zeros((side, part), jnp.float32)
        tall = jnp.concatenate([none, field.astype(jnp.float32), none], axis=0)
        west = east = 0.0
    else:
        edge = halos.astype(jnp.float32)
        tall = jnp.concatenate([edge[0:side], field.astype(jnp.float32), edge[2 * side : 3 * side]], axis=0)
        corner = [edge[4 * side + c : 4 * side + c + 1] for c in range(4)]
        spread = lambda col: jnp.broadcast_to(col[:, None, :], (side + 2, side, part)).reshape(flat, part)
        east = spread(jnp.concatenate([corner[1], edge[side : 2 * side], corner[2]], axis=0))
        west = spread(jnp.concatenate([corner[0], edge[3 * side : 4 * side], corner[3]], axis=0))
    out_ref[0] = jnp.where(column == 0, west, pltpu.roll(tall, 1, 0)).astype(jnp.bfloat16)
    out_ref[1] = tall.astype(jnp.bfloat16)
    out_ref[2] = jnp.where(column == side - 1, east, pltpu.roll(tall, flat - 1, 0)).astype(jnp.bfloat16)


class Neighbours:
    def __init__(self, side, tables):
        self.side = side
        self.et, self.eu, self.ct, self.cu = [tables.at[4 * i : 4 * i + 4] for i in range(4)]
        self.digits = turn_tables()
        self.count = lax.axis_size("tile")
        self.own = lax.axis_index("tile")

    def block(self, source):
        groups = self.count // SPAN
        slab = lax.rem(source // SPAN - self.own // SPAN + groups, groups)
        cross = source ^ self.own
        turn = lax.rem(cross // 2, 2)
        even = lax.rem(self.own // SPAN, 2) == 0
        at = jnp.where(slab == 0, turn, jnp.where((slab == 1) == even, 2, 3) + 2 * turn)
        return 6 * lax.rem(cross, 2) + at

    def edge(self, tile, e):
        slot = slot_in(self.digits[e], self.eu[e, tile])
        start = lax.rem(slot, 4) * self.side
        end = start + self.side - 1
        return self.block(self.et[e, tile]), lambda at: jnp.where(slot >= 4, end - at, start + at)

    def corner(self, tile, c):
        slot = slot_in(self.digits[4 + c], self.cu[c, tile])
        return self.block(self.ct[c, tile]), corner_spot(slot, self.side)


def onehot(wanted, width):
    lane = lax.broadcasted_iota(jnp.int32, (wanted.shape[0], width), 1)
    return jnp.where(lane == wanted, 1.0, 0.0).astype(jnp.bfloat16)


def border_onehot_kernel(side, tables_in, cot_in, border_ref, cot_ref, tables, sem):
    copy = pltpu.make_async_copy(tables_in, tables, sem)
    copy.start()
    cot_ref[...] = cot_in[...]
    border_ref[...] = jnp.zeros_like(border_ref)
    copy.wait()
    near = Neighbours(side, tables)
    low = lax.rem(near.own, 2) == 0
    width = 4 * side
    step = lax.broadcasted_iota(jnp.int32, (side, 1), 0)

    def put(row, block, wanted, add=False):
        here = (slice(row, row + side), pl.ds(pl.multiple_of(block * width, 128), width))
        value = onehot(wanted, width)
        border_ref[here] = border_ref[here] + value if add else value

    for m, tile in enumerate((near.own, near.own ^ 1)):
        first = 2 * m * side
        flat = [near.edge(tile, e) for e in range(4)]
        corners = [near.corner(tile, c) for c in range(4)]
        pick = lambda a, b: (jnp.where(low, a[0], b[0]), lambda at: jnp.where(low, a[1](at), b[1](at)))
        block, at = pick(flat[0], flat[2])
        left, right = [
            (jnp.where(low, corners[a][0], corners[b][0]), jnp.where(low, corners[a][1], corners[b][1]))
            for a, b in ((0, 3), (1, 2))
        ]
        along = jnp.where(low, step - 1, step + 1)
        fits = (along >= 0) & (along < side)
        put(first, block, jnp.where(step == 0, -1, at(step - 1)))
        put(first, left[0], jnp.where(step == 0, left[1], -1), add=True)
        put(first + side, flat[3][0], jnp.where(fits, flat[3][1](along), -1))
        put(first + 4 * side, block, at(step))
        put(first + 8 * side, block, jnp.where(step == side - 1, -1, at(step + 1)))
        put(first + 8 * side, right[0], jnp.where(step == side - 1, right[1], -1), add=True)
        put(first + 9 * side, flat[1][0], jnp.where(fits, flat[1][1](along), -1))
        block, at = pick(flat[3], flat[1])
        put(first + 13 * side, block, at(step))


def place_kernel(side, tables_in, place_ref, tables, sem):
    copy = pltpu.make_async_copy(tables_in, tables, sem)
    copy.start()
    copy.wait()
    near = Neighbours(side, tables)
    block = 4 * side + EXTRA
    lane = lax.broadcasted_iota(jnp.int32, (1, block), 1)
    row = lax.broadcasted_iota(jnp.int32, (4 * side, block), 0)
    places = []
    swap = jnp.where(lax.rem(near.own // SPAN, 2) == 0, SPAN, -SPAN)
    for mask in (0, 2, 1, 3):
        for offset in (0, swap, -swap):
            source = lax.rem((near.own ^ mask) + offset + near.count, near.count)
            target = jnp.full((1, block), -1, jnp.int32)
            for e in range(4):
                slot = slot_in(near.digits[e], near.eu[e, source])
                along = lane - e * side
                along = jnp.where(slot >= 4, side - 1 - along, along)
                hit = (lane >= e * side) & (lane < (e + 1) * side) & (near.et[e, source] == near.own)
                target = jnp.where(hit, lax.rem(slot, 4) * side + along, target)
                spot = corner_spot(slot_in(near.digits[4 + e], near.cu[e, source]), side)
                hit = (lane == 4 * side + e) & (near.ct[e, source] == near.own)
                target = jnp.where(hit, spot, target)
            places.append(jnp.where(row == target, 1.0, 0.0))
    place_ref[...] = jnp.concatenate(places, axis=1).astype(jnp.bfloat16)


def tap_product(side, scale, tap, cols, tall):
    rows = side * side
    start = pl.multiple_of((3 - tap // 3) * side, 16)
    value = jnp.dot(
        cols[lax.rem(tap, 3)], tall[pl.ds(start, rows), :], preferred_element_type=jnp.float32
    )
    return value * scale


def send_kernel(
    side, part, scale, field_ref, own_ref, other_ref, send_ref, tall_ref, rim_ref, cols_ref
):
    rows = side * side
    first = lax.axis_index("ch") == 0
    here = slice(2 * side, 2 * side + rows)
    blank = jnp.zeros((2 * side, tall_ref.shape[1]), jnp.bfloat16)
    tall_ref[0 : 2 * side, :] = blank
    tall_ref[2 * side + rows :, :] = blank

    @pl.when(first)
    def _():
        tall_ref[here, 0:part] = own_ref[...]
        tall_ref[here, part:] = other_ref[...]

    @pl.when(jnp.logical_not(first))
    def _():
        tall_ref[here, 0:part] = other_ref[...]
        tall_ref[here, part:] = own_ref[...]

    cot = tall_ref[here, :]
    column = lax.broadcasted_iota(jnp.int32, (rows, part), 0) % side
    field = field_ref[...].reshape(rows, part).astype(jnp.float32)
    cols_ref[0] = jnp.where(column == 0, 0.0, pltpu.roll(field, 1, 0)).astype(jnp.bfloat16).T
    cols_ref[1] = field.astype(jnp.bfloat16).T
    cols_ref[2] = jnp.where(column == side - 1, 0.0, pltpu.roll(field, rows - 1, 0)).astype(jnp.bfloat16).T
    which = 1 - lax.rem(lax.axis_index("tile"), 2)
    for j in range(3):
        send_ref[j * part : (j + 1) * part, :] = tap_product(side, scale, j + 5 * which, cols_ref, tall_ref)
    rim = cot.reshape(side, side, cot.shape[1])
    rim_ref[...] = jnp.concatenate([cot[0:side], cot[rows - side :], rim[:, 0, :], rim[:, side - 1, :]], axis=0)


def half_kernel(side, part, scale, mate, taps, cols, tall, out_ref, middle):
    which = lax.rem(lax.axis_index("tile") + mate, 2)
    for at, j in enumerate(taps):
        out_ref[at * part : (at + 1) * part, :] = tap_product(side, scale, j + 5 * which, cols, tall)
    middle[...] = tap_product(side, scale, 4, cols, tall)
    start = pl.multiple_of(which * (part // 2), 16)
    out_ref[len(taps) * part :, :] = middle[pl.ds(start, part // 2), :]


def unpack_near(near_refs, near, side, part):
    size = packed_shape(4 * side, part)[0]
    row = 0
    for ref in near_refs:
        for k in range(ref.shape[0] // size):
            unpack(ref, near, k * size, row, 4 * side, part)
            row += 4 * side


def border_kernel(side, part, chunk, scale, n_near, *refs):
    near_refs = refs[:n_near]
    onehot_ref, mine_ref, rim_ref, mate_ref, first_ref, second_ref = refs[n_near : n_near + 6]
    outs, near, total = refs[n_near + 6 : -2], refs[-2], refs[-1]
    count = lax.axis_size("tile")
    own = lax.axis_index("tile")
    core = lax.rem(own, 2)
    unpack_near(near_refs, near, side, part)
    half = part // 2
    used = 9 * half

    def place(start, value):
        total[pl.ds(pl.multiple_of(start, 16), value.shape[0]), :] = value

    cut = first_ref.shape[0]
    place(core * half, mine_ref[0:cut, :] + first_ref[...])
    if cut < 4 * part:
        place(core * half + cut, mine_ref[cut : 4 * part, :] + second_ref[0 : 4 * part - cut, :])
    place((1 - core) * 4 * part, mine_ref[4 * part :, :] + second_ref[4 * part - cut :, :])
    total[used:, :] = jnp.zeros((total.shape[0] - used, total.shape[1]), jnp.float32)
    left = jnp.dot(onehot_ref[...], near[...], preferred_element_type=jnp.float32).astype(jnp.bfloat16)

    def rim(ref, at):
        return ref[pl.ds(pl.multiple_of(at, 16), side), :]

    for q in range(4):
        column = (2 + q // 2) * side if q < 3 else (2 + core) * side
        right = jnp.concatenate(
            [value for ref in (rim_ref, mate_ref) for value in (rim(ref, core * side), rim(ref, column))],
            axis=0,
        )
        value = lax.dot_general(
            left[q * 4 * side : (q + 1) * 4 * side],
            right,
            (((0,), (0,)), ((), ())),
            preferred_element_type=jnp.float32,
        )
        if q < 3:
            start = q * part + core * (part // 2 + part)
        else:
            start = 3 * part - core * (3 * part - part // 2)
        here = pl.ds(pl.multiple_of(start, 16), part)
        total[here, :] = total[here, :] + value * scale
    size = outs[0].shape[0]
    for index in range(count // 2):
        to = slot_of_mask(2 * index, count) * chunk
        block = pl.multiple_of(((own // 2) ^ index) * chunk, 16)
        out = outs[to // size]
        out[to % size : to % size + chunk, :] = total[pl.ds(block, chunk), :].astype(out.dtype)


def sum_kernel(n_got, n_out, *refs):
    held_ref, got_refs, outs = refs[0], refs[1 : 1 + n_got], refs[1 + n_got :]
    size = held_ref.shape[0] // n_out
    for index in range(n_out):
        here = slice(index * size, (index + 1) * size)
        value = held_ref[here, :]
        for ref in got_refs:
            value = value + ref[here, :].astype(jnp.float32)
        outs[index][...] = value.astype(outs[index].dtype)


def exchange_kernel(held_ref, got_ref, out_ref):
    half = held_ref.shape[0] // 2
    for a, b in ((0, half), (half, 0)):
        value = held_ref[a : a + half, :].astype(jnp.float32) + got_ref[b : b + half, :].astype(jnp.float32)
        out_ref[a : a + half, :] = value.astype(out_ref.dtype)


def join_kernel(*refs):
    row = 0
    for ref in refs[:-1]:
        refs[-1][row : row + ref.shape[0], :] = ref[...]
        row += ref.shape[0]


def unfold_kernel(used, chunk, bits, masks, n_dep, *refs):
    refs = refs[n_dep:]
    n = len(masks)
    in_refs, out_ref, wide, sems = refs[:n], refs[n], refs[n + 1], refs[n + 2]
    own = lax.axis_index("tile")
    full, rest = used // chunk, used % chunk
    copies = []
    for i, (ref, inner, bit) in enumerate(zip(in_refs, masks, bits)):
        origin = (lax.rem(own, 2) ^ bit) * used
        for k, mask in enumerate(inner):
            at = i * len(inner) + k
            wide[at] = ref[k * chunk : (k + 1) * chunk, :].astype(jnp.float32)
            block = (own ^ mask) // 2
            start = pl.multiple_of(origin + block * chunk, 16)
            copies.append(
                (
                    block < full,
                    pltpu.make_async_copy(wide.at[at], out_ref.at[pl.ds(start, chunk), :], sems.at[at]),
                )
            )
            if rest:
                start = pl.multiple_of(origin + full * chunk, 16)
                copies.append(
                    (
                        block == full,
                        pltpu.make_async_copy(
                            wide.at[at, 0:rest], out_ref.at[pl.ds(start, rest), :], sems.at[at]
                        ),
                    )
                )
    for going, copy in copies:
        pl.when(going)(copy.start)
    for going, copy in copies:
        pl.when(going)(copy.wait)


def unfold(whole, chunk, bits, masks, blocks, before):
    n_dep = 0 if before is None else 1
    anywhere = pl.BlockSpec(memory_space=pl.ANY)
    n_copies = len(masks) * len(masks[0])
    return pl.pallas_call(
        functools.partial(unfold_kernel, whole.shape[0] // 2, chunk, bits, masks, n_dep),
        out_shape=whole,
        in_specs=[anywhere] * n_dep + [pl.BlockSpec(memory_space=pltpu.VMEM)] * len(blocks),
        out_specs=anywhere,
        scratch_shapes=[
            pltpu.VMEM((n_copies, chunk, whole.shape[1]), jnp.float32),
            pltpu.SemaphoreType.DMA((n_copies,)),
        ],
        input_output_aliases={0: 0} if n_dep else {},
        compiler_params=pltpu.CompilerParams(vmem_limit_bytes=40 * 1024 * 1024),
    )(*([before] if n_dep else []), *blocks)


def back_kernel(side, part, tall, weight_ref, inner_ref, pieces_ref):
    rows = side * side
    flat = rows + 2 * side
    start = pl.multiple_of(lax.axis_index("ch") * part, 16)
    backs = []
    for b in range(3):
        back = jnp.zeros((flat, part), jnp.float32)
        for a in range(3):
            back = back + lax.dot_general(
                tall[(2 - a) * side : (2 - a) * side + flat, :],
                weight_ref[3 * a + b, pl.ds(start, part), :],
                (((1,), (1,)), ((), ())),
                preferred_element_type=jnp.float32,
            )
        backs.append(back)
    column = lax.broadcasted_iota(jnp.int32, (flat, part), 0) % side
    inner = (
        jnp.where(column == side - 1, 0.0, pltpu.roll(backs[0], flat - 1, 0))
        + backs[1]
        + jnp.where(column == 0, 0.0, pltpu.roll(backs[2], 1, 0))
    )
    inner_ref[...] = inner[side : side + rows]
    west = backs[0].reshape(side + 2, side, part)[:, 0, :]
    east = backs[2].reshape(side + 2, side, part)[:, side - 1, :]
    pieces = jnp.concatenate(
        [
            inner[0:side],
            east[1 : side + 1],
            inner[side + rows :],
            west[1 : side + 1],
            west[0:1],
            east[0:1],
            east[side + 1 :],
            west[side + 1 :],
            jnp.zeros((EXTRA - 4, part), jnp.float32),
        ],
        axis=0,
    )
    pack(pieces.astype(jnp.bfloat16), pieces_ref)


def add_halo_kernel(side, part, place_ref, inner_ref, *refs):
    got_refs, out_ref, got = refs[:-2], refs[-2], refs[-1]
    block = 4 * side + EXTRA
    size = packed_shape(block, part)[0]
    for i, ref in enumerate(got_refs):
        for k in range(3):
            unpack(ref, got, k * size, (3 * i + k) * block, block, part)
    sums = jnp.dot(place_ref[...], got[...], preferred_element_type=jnp.float32)
    rows = side * side
    spread = lambda col: jnp.broadcast_to(col[:, None, :], (side, side, part)).reshape(rows, part)
    column = lax.broadcasted_iota(jnp.int32, (rows, part), 0) % side
    inner = inner_ref[...]
    inner = inner + jnp.where(column == side - 1, spread(sums[side : 2 * side]), 0.0)
    inner = inner + jnp.where(column == 0, spread(sums[3 * side :]), 0.0)
    ends = jnp.concatenate(
        [
            inner[0:side] + sums[0:side],
            inner[side : rows - side],
            inner[rows - side :] + sums[2 * side : 3 * side],
        ],
        axis=0,
    )
    out_ref[...] = ends.astype(jnp.bfloat16)


def parts_of(rows, extra):
    size = (rows + extra) // (32 * PARTS) * 32
    return [size] * (PARTS - 1) + [rows - size * (PARTS - 1)]


def halo_kernel(side, part, n_near, *refs):
    near_refs, tables_in, field_ref = refs[:n_near], refs[n_near], refs[n_near + 1]
    halos_ref, *packet_refs = refs[n_near + 2 : -3]
    near, tables, sem = refs[-3:]
    copy = pltpu.make_async_copy(tables_in, tables, sem)
    copy.start()
    rows = side * side
    unpack_near(near_refs, near, side, part)
    field = field_ref[...].reshape(rows, part)
    sizes = parts_of(rows, 4 * side + EXTRA)
    for k, ref in enumerate(packet_refs):
        pack(field[sum(sizes[:k]) : sum(sizes[: k + 1])], ref)
    copy.wait()
    index = Neighbours(side, tables)
    step = lax.broadcasted_iota(jnp.int32, (side, 1), 0)
    wanted = []
    for e in range(4):
        block, at = index.edge(index.own, e)
        wanted.append(block * (4 * side) + at(step))
    spots = lax.broadcasted_iota(jnp.int32, (EXTRA, 1), 0)
    ends = jnp.full((EXTRA, 1), -1, jnp.int32)
    for c in range(4):
        block, spot = index.corner(index.own, c)
        ends = jnp.where(spots == c, block * (4 * side) + spot, ends)
    pick = onehot(jnp.concatenate(wanted + [ends], axis=0), near.shape[0])
    halos = jnp.dot(pick, near[...], preferred_element_type=jnp.float32).astype(jnp.bfloat16)
    halos_ref[...] = halos
    pack(halos, packet_refs[-1], packed_shape(sizes[-1], part)[0])


def output_kernel(side, part, field_ref, halos_ref, weight_ref, *refs):
    rows = side * side
    ch = lax.axis_index("ch")
    other_refs, (out_ref, cols, other_cols, other) = refs[:PARTS], refs[PARTS:]
    wide = -(-part // 128) * 128
    lanes = pl.multiple_of(ch * (weight_ref.shape[2] - wide), 128)
    sizes = parts_of(rows, 4 * side + EXTRA)
    for k, ref in enumerate(other_refs):
        unpack(ref, other, 0, sum(sizes[:k]), sizes[k], part)
    unpack(other_refs[-1], other, packed_shape(sizes[-1], part)[0], rows, 4 * side + EXTRA, part)
    shifted_columns(side, part, field_ref[...].reshape(rows, part), halos_ref[...], cols)
    shifted_columns(side, part, other[0:rows, :], other[rows:, :], other_cols)
    starts = (pl.multiple_of(ch * part, 16), pl.multiple_of((1 - ch) * part, 16))
    total = jnp.zeros((rows, wide), jnp.float32)
    for a in range(3):
        for b in range(3):
            for ref, first in zip((cols, other_cols), starts):
                total = total + jnp.dot(
                    ref[b, a * side : a * side + rows, :],
                    weight_ref[3 * a + b, pl.ds(first, part), pl.ds(lanes, wide)],
                    preferred_element_type=jnp.float32,
                )
    result = jnp.where(ch == 0, total[:, :part], total[:, wide - part :])
    out_ref[...] = result.astype(jnp.bfloat16)


def body(features, weight, cotangent, edge_tiles, edge_turns, corner_tiles, corner_turns):
    count = lax.axis_size("tile")
    field = features[0]
    side, part = field.shape[0], field.shape[2]
    chans = weight.shape[3]
    rows = side * side
    flat = rows + 2 * side
    block = 4 * side + EXTRA
    taps = weight.reshape(9, chans, chans)
    others = [(0, 1), (1, 0)]
    flops = 2 * rows * 9 * part * chans
    half_bytes = jnp.bfloat16
    chunk = -(-9 * part // (16 * count)) * 16
    half = count * chunk // 2
    scale = 1.0 / math.sqrt(count * rows)

    cot_own = cotangent[0].reshape(rows, part)
    cot_other = lax.ppermute(cot_own, "ch", others)
    sides, field = call(
        functools.partial(sides_kernel, side),
        [vmem(packed_shape(4 * side, part), half_bytes), vmem(field.shape, half_bytes)],
        [field],
    )
    swaps = [by_swap(sides, odd, count) for odd in (0, 1)]
    across = by_mask(sides, 2, count)
    tables = jnp.concatenate([edge_tiles.T, edge_turns.T, corner_tiles.T, corner_turns.T], axis=0)
    table_scratch = [pltpu.SMEM(tables.shape, jnp.int32), pltpu.SemaphoreType.DMA]
    border_pick, cot_own = call(
        functools.partial(border_onehot_kernel, side),
        [vmem((16 * side, 48 * side), half_bytes), vmem((rows, part), half_bytes)],
        [tables, cot_own],
        scratch=table_scratch,
    )
    pair = packed_shape(8 * side, part)
    (beyond,) = call(join_kernel, [vmem(pair, half_bytes)], swaps)
    near = [sides, across, *swaps, by_mask(beyond, 2, count)]
    near, cot_other, border_pick = lax.optimization_barrier((near, cot_other, border_pick))
    (near,) = call(join_kernel, [vmem(packed_shape(24 * side, part), half_bytes)], near)
    mates = by_mask(near, 1, count)
    first, tall, rim, cols = call(
        functools.partial(send_kernel, side, part, scale),
        [
            vmem((3 * part, chans), jnp.float32),
            vmem((rows + 4 * side, chans), half_bytes),
            vmem((4 * side, chans), half_bytes),
            vmem((3, part, rows), half_bytes),
        ],
        [field, cot_own, cot_other],
        flops=flops // 4,
    )
    (second,) = call(
        functools.partial(half_kernel, side, part, scale, 1, (3,)),
        [vmem((3 * part // 2, chans), jnp.float32)],
        [cols, tall],
        scratch=[pltpu.VMEM((part, chans), jnp.float32)],
        flops=flops,
    )
    tall, second = lax.optimization_barrier((tall, second))
    (mine,) = call(
        functools.partial(half_kernel, side, part, scale, 0, (0, 1, 2, 3)),
        [vmem((9 * part // 2, chans), jnp.float32)],
        [cols, tall],
        scratch=[pltpu.VMEM((part, chans), jnp.float32)],
        costed=False,
    )
    mates, mine, rim_mate = lax.optimization_barrier((mates, mine, by_mask(rim, 1, count)))
    near = [near, mates]

    stages = mask_stages(count)
    masks = group_masks(stages[1])
    size = half // len(masks)
    held, *send = call(
        functools.partial(border_kernel, side, part, chunk, scale, len(near)),
        [vmem((size, chans), jnp.float32)] + [vmem((size, chans), half_bytes)] * (len(masks) - 1),
        [*near, border_pick, mine, rim, rim_mate, by_mask(first, 1, count), by_mask(second, 1, count)],
        scratch=[pltpu.VMEM((48 * side, part), half_bytes), pltpu.VMEM((half, chans), jnp.float32)],
    )
    send, tall, near = lax.optimization_barrier((send, tall, near))
    got = [by_mask(v, m, count) for v, m in zip(send, masks[1:])]
    inner, pieces = call(
        functools.partial(back_kernel, side, part),
        [vmem((rows, part), jnp.float32), vmem(packed_shape(block, part), half_bytes)],
        [tall, taps],
        flops=flops,
    )
    pieces, near = lax.optimization_barrier((pieces, near))
    here = [pieces, *[by_swap(pieces, odd, count) for odd in (1, 0)][::-1]]
    (place,) = call(
        functools.partial(place_kernel, side),
        [vmem((4 * side, 12 * block), half_bytes)],
        [tables],
        scratch=table_scratch,
    )
    halos, *packet = call(
        functools.partial(halo_kernel, side, part, len(near)),
        [vmem((block, part), half_bytes)]
        + [vmem(packed_shape(size, part), half_bytes) for size in parts_of(rows, block)[:-1]]
        + [vmem(packed_shape(parts_of(rows, block)[-1] + block, part), half_bytes)],
        [*near, tables, field],
        scratch=[pltpu.VMEM((48 * side, part), half_bytes), *table_scratch],
    )
    got, here[:2], inner, halos, packet, place = lax.optimization_barrier(
        (got, here[:2], inner, halos, packet, place)
    )
    swap = len(stages[-1]) == 1 and len(stages) > 2
    rs_stages = stages[2:-1] if swap else stages[2:]
    aside = [here, packet]

    def start_aside(send, aside):
        here = aside[0]
        send, here[0], packet = lax.optimization_barrier((send, here[0], aside[1]))
        (here,) = call(join_kernel, [vmem((3 * pieces.shape[0], pieces.shape[1]), half_bytes)], here)
        return send, here, by_mask(here, 2, count), [lax.ppermute(v, "ch", others) for v in packet]

    for index, bits in enumerate(rs_stages):
        masks = group_masks(bits)
        size = held.shape[0] // len(masks)
        held, *send = call(
            functools.partial(sum_kernel, len(got), len(masks)),
            [vmem((size, chans), jnp.float32)] + [vmem((size, chans), half_bytes)] * (len(masks) - 1),
            [held, *got],
        )
        if index == 0:
            send, here, beside, other_field = start_aside(send, aside)
        got = [by_mask(v, m, count) for v, m in zip(send, masks[1:])]
    (held,) = call(functools.partial(sum_kernel, len(got), 1), [vmem(held.shape, half_bytes)], [held, *got])
    if swap:
        if not rs_stages:
            held, here, beside, other_field = start_aside(held, aside)
        got = by_mask(held, stages[-1][0], count)
        got, here, beside = lax.optimization_barrier((got, here, beside))
        (held,) = call(exchange_kernel, [vmem(held.shape, half_bytes)], [held, got])
    order = [0] if not swap else [0, stages[-1][0]]
    ag_stages = stages[-2:0:-1] if swap else stages[:0:-1]
    for index, bits in enumerate(ag_stages):
        masks = group_masks(bits)
        got = [by_mask(held, m, count) for m in masks[1:]]
        if index < len(ag_stages) - 1:
            order = [m + v for m in masks for v in order]
            (held,) = call(
                join_kernel, [vmem((held.shape[0] * len(masks), chans), half_bytes)], [held, *got]
            )
    order = [[m + v for v in order] for m in masks]
    got_pieces = [here, beside, by_mask(here, 1, count), by_mask(beside, 1, count)]
    (grad_features,) = call(
        functools.partial(add_halo_kernel, side, part),
        [vmem((rows, part), half_bytes)],
        [place, inner, *got_pieces],
        scratch=[pltpu.VMEM((12 * block, part), half_bytes)],
    )
    (output,) = call(
        functools.partial(output_kernel, side, part),
        [vmem((rows, part), half_bytes)],
        [field, halos, taps, *other_field],
        scratch=[
            pltpu.VMEM((3, flat, part), half_bytes),
            pltpu.VMEM((3, flat, part), half_bytes),
            pltpu.VMEM((rows + block, part), half_bytes),
        ],
        flops=2 * flops,
    )
    got, grad_features, output = lax.optimization_barrier((got, grad_features, output))
    got = [held, *got]
    mates = [by_mask(v, 1, count) for v in got]
    whole = vmem((9 * part, chans), jnp.float32)
    own = len(got)
    first = unfold(whole, chunk, [0] * own + [1], order + order[:1], got + mates[:1], None)
    grad_weight = unfold(whole, chunk, [1] * (own - 1), order[1:], mates[1:], first)
    shape = (1, side, side, part)
    return (
        output.reshape(shape),
        grad_features.reshape(shape),
        grad_weight.reshape(3, 3, part, chans),
    )


def solution(mesh):
    return jax.shard_map(
        body,
        mesh=mesh,
        in_specs=(
            P("tile", None, None, "ch"),
            P(),
            P("tile", None, None, "ch"),
            P(),
            P(),
            P(),
            P(),
        ),
        out_specs=(
            P("tile", None, None, "ch"),
            P("tile", None, None, "ch"),
            P(None, None, "ch", None),
        ),
        check_vma=False,
    )
```

```python
import functools
import math

import jax
import jax.numpy as jnp
import numpy as np
from jax import lax
from jax.experimental import pallas as pl
from jax.experimental.pallas import tpu as pltpu
from jax.sharding import PartitionSpec as P

SPAN = 4
EXTRA = 32
PARTS = 3


def turn_tables():
    labels = [[3 * row + col for col in range(3)] for row in range(3)]

    def turn_once(block):
        return [[block[col][2 - row] for col in range(3)] for row in range(3)]

    def sides_of(block):
        return [
            list(block[0]),
            [block[row][2] for row in range(3)],
            list(block[2]),
            [block[row][0] for row in range(3)],
        ]

    def corners_of(block):
        return [block[0][0], block[0][2], block[2][2], block[2][0]]

    base_sides = sides_of(labels)
    base_corners = corners_of(labels)
    edge_table = np.zeros((4, 4), np.int32)
    corner_table = np.zeros((4, 4), np.int32)
    for border in range(4):
        turned = labels
        for quarter in range(4):
            wanted = sides_of(turned)[(border + 2) % 4]
            for side_index in range(4):
                if base_sides[side_index] == wanted:
                    edge_table[border, quarter] = side_index
                if base_sides[side_index][::-1] == wanted:
                    edge_table[border, quarter] = side_index + 4
            corner_cell = corners_of(turned)[(border + 2) % 4]
            for corner_index in range(4):
                if base_corners[corner_index] == corner_cell:
                    corner_table[border, quarter] = corner_index
            turned = turn_once(turned)
    tables = np.concatenate([edge_table, corner_table], axis=0)
    return [sum(int(slot) << (3 * quarter) for quarter, slot in enumerate(row)) for row in tables]


def by_swap(value, odd, count):
    pairs = [
        (i, (i + (SPAN if (i // SPAN) % 2 == odd else -SPAN)) % count) for i in range(count)
    ]
    return lax.ppermute(value, "tile", pairs)


def by_mask(value, mask, count):
    return lax.ppermute(value, "tile", [(i, i ^ mask) for i in range(count)])


def mask_stages(count):
    bits = [1 << b for b in range(count.bit_length() - 1)]
    stages = [bits[:1]]
    rest = bits[1:]
    while rest:
        stages.append(rest[:2])
        rest = rest[2:]
    return stages


def group_masks(bits):
    masks = [0]
    for bit in bits:
        masks = masks + [m + bit for m in masks]
    return masks


def slot_of_mask(mask, count):
    place = 0
    for bits in mask_stages(count)[1:]:
        size = 1 << len(bits)
        place = place * size + (mask // bits[0]) % size
    return place


def slot_in(row, quarter):
    return (row >> (3 * quarter)) & 7


def corner_spot(slot, side):
    return jnp.where(
        slot == 0, 0, jnp.where(slot == 1, side - 1, jnp.where(slot == 2, 3 * side - 1, 2 * side))
    )


def vmem(shape, dtype):
    return jax.ShapeDtypeStruct(shape, dtype)


def call(kernel, outs, args, anywhere=(), scratch=(), flops=0, costed=True):
    in_specs = [
        pl.BlockSpec(memory_space=pltpu.HBM if i in anywhere else pltpu.VMEM) for i in range(len(args))
    ]
    size = costed * sum(math.prod(x.shape) * x.dtype.itemsize for x in list(args) + list(outs))
    return pl.pallas_call(
        kernel,
        out_shape=tuple(outs),
        in_specs=in_specs,
        out_specs=tuple(pl.BlockSpec(memory_space=pltpu.VMEM) for _ in outs),
        scratch_shapes=list(scratch),
        compiler_params=pltpu.CompilerParams(vmem_limit_bytes=40 * 1024 * 1024),
        cost_estimate=pl.CostEstimate(flops=flops, bytes_accessed=size, transcendentals=0),
    )(*args)


def packed_shape(rows, part):
    if part % 128 != 64:
        return (rows, part)
    return (rows * (part // 128) + rows // 2, 128)


def pack(value, out_ref, first=0):
    rows, part = value.shape
    if part % 128 != 64:
        out_ref[first : first + rows, :] = value
        return
    for i in range(part // 128):
        out_ref[first + i * rows : first + (i + 1) * rows, :] = value[:, i * 128 : (i + 1) * 128]
    rest = value[:, part - 64 :]
    at = first + rows * (part // 128)
    out_ref[at : at + rows // 2, :] = jnp.concatenate([rest[: rows // 2], rest[rows // 2 :]], axis=1)


def unpack(ref, out_ref, first, row, rows, part):
    if part % 128 != 64:
        out_ref[row : row + rows, :] = ref[first : first + rows, :]
        return
    for i in range(part // 128):
        out_ref[row : row + rows, i * 128 : (i + 1) * 128] = ref[first + i * rows : first + (i + 1) * rows, :]
    at = first + rows * (part // 128)
    rest = ref[at : at + rows // 2, :]
    out_ref[row : row + rows // 2, part - 64 :] = rest[:, :64]
    out_ref[row + rows // 2 : row + rows, part - 64 :] = rest[:, 64:]


def sides_kernel(side, field_ref, sides_ref, copy_ref):
    sides = jnp.concatenate(
        [field_ref[0], field_ref[:, side - 1, :], field_ref[side - 1], field_ref[:, 0, :]], axis=0
    )
    pack(sides, sides_ref)
    copy_ref[...] = field_ref[...]


def shifted_columns(side, part, field, halos, out_ref):
    rows = side * side
    flat = rows + 2 * side
    column = lax.broadcasted_iota(jnp.int32, (flat, part), 0) % side
    if halos is None:
        none = jnp.zeros((side, part), jnp.float32)
        tall = jnp.concatenate([none, field.astype(jnp.float32), none], axis=0)
        west = east = 0.0
    else:
        edge = halos.astype(jnp.float32)
        tall = jnp.concatenate([edge[0:side], field.astype(jnp.float32), edge[2 * side : 3 * side]], axis=0)
        corner = [edge[4 * side + c : 4 * side + c + 1] for c in range(4)]
        spread = lambda col: jnp.broadcast_to(col[:, None, :], (side + 2, side, part)).reshape(flat, part)
        east = spread(jnp.concatenate([corner[1], edge[side : 2 * side], corner[2]], axis=0))
        west = spread(jnp.concatenate([corner[0], edge[3 * side : 4 * side], corner[3]], axis=0))
    out_ref[0] = jnp.where(column == 0, west, pltpu.roll(tall, 1, 0)).astype(jnp.bfloat16)
    out_ref[1] = tall.astype(jnp.bfloat16)
    out_ref[2] = jnp.where(column == side - 1, east, pltpu.roll(tall, flat - 1, 0)).astype(jnp.bfloat16)


class Neighbours:
    def __init__(self, side, tables):
        self.side = side
        self.et, self.eu, self.ct, self.cu = [tables.at[4 * i : 4 * i + 4] for i in range(4)]
        self.digits = turn_tables()
        self.count = lax.axis_size("tile")
        self.own = lax.axis_index("tile")

    def block(self, source):
        groups = self.count // SPAN
        slab = lax.rem(source // SPAN - self.own // SPAN + groups, groups)
        cross = source ^ self.own
        turn = lax.rem(cross // 2, 2)
        even = lax.rem(self.own // SPAN, 2) == 0
        at = jnp.where(slab == 0, turn, jnp.where((slab == 1) == even, 2, 3) + 2 * turn)
        return 6 * lax.rem(cross, 2) + at

    def edge(self, tile, e):
        slot = slot_in(self.digits[e], self.eu[e, tile])
        start = lax.rem(slot, 4) * self.side
        end = start + self.side - 1
        return self.block(self.et[e, tile]), lambda at: jnp.where(slot >= 4, end - at, start + at)

    def corner(self, tile, c):
        slot = slot_in(self.digits[4 + c], self.cu[c, tile])
        return self.block(self.ct[c, tile]), corner_spot(slot, self.side)


def onehot(wanted, width):
    lane = lax.broadcasted_iota(jnp.int32, (wanted.shape[0], width), 1)
    return jnp.where(lane == wanted, 1.0, 0.0).astype(jnp.bfloat16)


def border_onehot_kernel(side, tables_in, cot_in, border_ref, cot_ref, tables, sem):
    copy = pltpu.make_async_copy(tables_in, tables, sem)
    copy.start()
    cot_ref[...] = cot_in[...]
    border_ref[...] = jnp.zeros_like(border_ref)
    copy.wait()
    near = Neighbours(side, tables)
    low = lax.rem(near.own, 2) == 0
    width = 4 * side
    step = lax.broadcasted_iota(jnp.int32, (side, 1), 0)

    def put(row, block, wanted, add=False):
        here = (slice(row, row + side), pl.ds(pl.multiple_of(block * width, 128), width))
        value = onehot(wanted, width)
        border_ref[here] = border_ref[here] + value if add else value

    for m, tile in enumerate((near.own, near.own ^ 1)):
        first = 2 * m * side
        flat = [near.edge(tile, e) for e in range(4)]
        corners = [near.corner(tile, c) for c in range(4)]
        pick = lambda a, b: (jnp.where(low, a[0], b[0]), lambda at: jnp.where(low, a[1](at), b[1](at)))
        block, at = pick(flat[0], flat[2])
        left, right = [
            (jnp.where(low, corners[a][0], corners[b][0]), jnp.where(low, corners[a][1], corners[b][1]))
            for a, b in ((0, 3), (1, 2))
        ]
        along = jnp.where(low, step - 1, step + 1)
        fits = (along >= 0) & (along < side)
        put(first, block, jnp.where(step == 0, -1, at(step - 1)))
        put(first, left[0], jnp.where(step == 0, left[1], -1), add=True)
        put(first + side, flat[3][0], jnp.where(fits, flat[3][1](along), -1))
        put(first + 4 * side, block, at(step))
        put(first + 8 * side, block, jnp.where(step == side - 1, -1, at(step + 1)))
        put(first + 8 * side, right[0], jnp.where(step == side - 1, right[1], -1), add=True)
        put(first + 9 * side, flat[1][0], jnp.where(fits, flat[1][1](along), -1))
        block, at = pick(flat[3], flat[1])
        put(first + 13 * side, block, at(step))


def place_kernel(side, tables_in, place_ref, tables, sem):
    copy = pltpu.make_async_copy(tables_in, tables, sem)
    copy.start()
    copy.wait()
    near = Neighbours(side, tables)
    block = 4 * side + EXTRA
    lane = lax.broadcasted_iota(jnp.int32, (1, block), 1)
    row = lax.broadcasted_iota(jnp.int32, (4 * side, block), 0)
    places = []
    swap = jnp.where(lax.rem(near.own // SPAN, 2) == 0, SPAN, -SPAN)
    for mask in (0, 2, 1, 3):
        for offset in (0, swap, -swap):
            source = lax.rem((near.own ^ mask) + offset + near.count, near.count)
            target = jnp.full((1, block), -1, jnp.int32)
            for e in range(4):
                slot = slot_in(near.digits[e], near.eu[e, source])
                along = lane - e * side
                along = jnp.where(slot >= 4, side - 1 - along, along)
                hit = (lane >= e * side) & (lane < (e + 1) * side) & (near.et[e, source] == near.own)
                target = jnp.where(hit, lax.rem(slot, 4) * side + along, target)
                spot = corner_spot(slot_in(near.digits[4 + e], near.cu[e, source]), side)
                hit = (lane == 4 * side + e) & (near.ct[e, source] == near.own)
                target = jnp.where(hit, spot, target)
            places.append(jnp.where(row == target, 1.0, 0.0))
    place_ref[...] = jnp.concatenate(places, axis=1).astype(jnp.bfloat16)


def tap_product(side, scale, tap, cols, tall):
    rows = side * side
    start = pl.multiple_of((3 - tap // 3) * side, 16)
    value = jnp.dot(
        cols[lax.rem(tap, 3)], tall[pl.ds(start, rows), :], preferred_element_type=jnp.float32
    )
    return value * scale


def send_kernel(
    side, part, scale, field_ref, own_ref, other_ref, send_ref, tall_ref, rim_ref, cols_ref
):
    rows = side * side
    first = lax.axis_index("ch") == 0
    here = slice(2 * side, 2 * side + rows)
    blank = jnp.zeros((2 * side, tall_ref.shape[1]), jnp.bfloat16)
    tall_ref[0 : 2 * side, :] = blank
    tall_ref[2 * side + rows :, :] = blank

    @pl.when(first)
    def _():
        tall_ref[here, 0:part] = own_ref[...]
        tall_ref[here, part:] = other_ref[...]

    @pl.when(jnp.logical_not(first))
    def _():
        tall_ref[here, 0:part] = other_ref[...]
        tall_ref[here, part:] = own_ref[...]

    cot = tall_ref[here, :]
    column = lax.broadcasted_iota(jnp.int32, (rows, part), 0) % side
    field = field_ref[...].reshape(rows, part).astype(jnp.float32)
    cols_ref[0] = jnp.where(column == 0, 0.0, pltpu.roll(field, 1, 0)).astype(jnp.bfloat16).T
    cols_ref[1] = field.astype(jnp.bfloat16).T
    cols_ref[2] = jnp.where(column == side - 1, 0.0, pltpu.roll(field, rows - 1, 0)).astype(jnp.bfloat16).T
    which = 1 - lax.rem(lax.axis_index("tile"), 2)
    for j in range(3):
        send_ref[j * part : (j + 1) * part, :] = tap_product(side, scale, j + 5 * which, cols_ref, tall_ref)
    rim = cot.reshape(side, side, cot.shape[1])
    rim_ref[...] = jnp.concatenate([cot[0:side], cot[rows - side :], rim[:, 0, :], rim[:, side - 1, :]], axis=0)


def half_kernel(side, part, scale, mate, taps, cols, tall, out_ref, middle):
    which = lax.rem(lax.axis_index("tile") + mate, 2)
    for at, j in enumerate(taps):
        out_ref[at * part : (at + 1) * part, :] = tap_product(side, scale, j + 5 * which, cols, tall)
    middle[...] = tap_product(side, scale, 4, cols, tall)
    start = pl.multiple_of(which * (part // 2), 16)
    out_ref[len(taps) * part :, :] = middle[pl.ds(start, part // 2), :]


def unpack_near(near_refs, near, side, part):
    size = packed_shape(4 * side, part)[0]
    row = 0
    for ref in near_refs:
        for k in range(ref.shape[0] // size):
            unpack(ref, near, k * size, row, 4 * side, part)
            row += 4 * side


def border_kernel(side, part, chunk, scale, n_near, *refs):
    near_refs = refs[:n_near]
    onehot_ref, mine_ref, rim_ref, mate_ref, first_ref, second_ref = refs[n_near : n_near + 6]
    outs, near, total = refs[n_near + 6 : -2], refs[-2], refs[-1]
    count = lax.axis_size("tile")
    own = lax.axis_index("tile")
    core = lax.rem(own, 2)
    unpack_near(near_refs, near, side, part)
    half = part // 2
    used = 9 * half

    def place(start, value):
        total[pl.ds(pl.multiple_of(start, 16), value.shape[0]), :] = value

    cut = first_ref.shape[0]
    place(core * half, mine_ref[0:cut, :] + first_ref[...])
    if cut < 4 * part:
        place(core * half + cut, mine_ref[cut : 4 * part, :] + second_ref[0 : 4 * part - cut, :])
    place((1 - core) * 4 * part, mine_ref[4 * part :, :] + second_ref[4 * part - cut :, :])
    total[used:, :] = jnp.zeros((total.shape[0] - used, total.shape[1]), jnp.float32)
    left = jnp.dot(onehot_ref[...], near[...], preferred_element_type=jnp.float32).astype(jnp.bfloat16)

    def rim(ref, at):
        return ref[pl.ds(pl.multiple_of(at, 16), side), :]

    for q in range(4):
        column = (2 + q // 2) * side if q < 3 else (2 + core) * side
        right = jnp.concatenate(
            [value for ref in (rim_ref, mate_ref) for value in (rim(ref, core * side), rim(ref, column))],
            axis=0,
        )
        value = lax.dot_general(
            left[q * 4 * side : (q + 1) * 4 * side],
            right,
            (((0,), (0,)), ((), ())),
            preferred_element_type=jnp.float32,
        )
        if q < 3:
            start = q * part + core * (part // 2 + part)
        else:
            start = 3 * part - core * (3 * part - part // 2)
        here = pl.ds(pl.multiple_of(start, 16), part)
        total[here, :] = total[here, :] + value * scale
    size = outs[0].shape[0]
    for index in range(count // 2):
        to = slot_of_mask(2 * index, count) * chunk
        block = pl.multiple_of(((own // 2) ^ index) * chunk, 16)
        out = outs[to // size]
        out[to % size : to % size + chunk, :] = total[pl.ds(block, chunk), :].astype(out.dtype)


def sum_kernel(n_got, n_out, *refs):
    held_ref, got_refs, outs = refs[0], refs[1 : 1 + n_got], refs[1 + n_got :]
    size = held_ref.shape[0] // n_out
    for index in range(n_out):
        here = slice(index * size, (index + 1) * size)
        value = held_ref[here, :]
        for ref in got_refs:
            value = value + ref[here, :].astype(jnp.float32)
        outs[index][...] = value.astype(outs[index].dtype)


def exchange_kernel(held_ref, got_ref, out_ref):
    half = held_ref.shape[0] // 2
    for a, b in ((0, half), (half, 0)):
        value = held_ref[a : a + half, :].astype(jnp.float32) + got_ref[b : b + half, :].astype(jnp.float32)
        out_ref[a : a + half, :] = value.astype(out_ref.dtype)


def join_kernel(*refs):
    row = 0
    for ref in refs[:-1]:
        refs[-1][row : row + ref.shape[0], :] = ref[...]
        row += ref.shape[0]


def unfold_kernel(used, chunk, bits, masks, n_dep, *refs):
    refs = refs[n_dep:]
    n = len(masks)
    in_refs, out_ref, wide, sems = refs[:n], refs[n], refs[n + 1], refs[n + 2]
    own = lax.axis_index("tile")
    full, rest = used // chunk, used % chunk
    copies = []
    for i, (ref, inner, bit) in enumerate(zip(in_refs, masks, bits)):
        origin = (lax.rem(own, 2) ^ bit) * used
        for k, mask in enumerate(inner):
            at = i * len(inner) + k
            wide[at] = ref[k * chunk : (k + 1) * chunk, :].astype(jnp.float32)
            block = (own ^ mask) // 2
            start = pl.multiple_of(origin + block * chunk, 16)
            copies.append(
                (
                    block < full,
                    pltpu.make_async_copy(wide.at[at], out_ref.at[pl.ds(start, chunk), :], sems.at[at]),
                )
            )
            if rest:
                start = pl.multiple_of(origin + full * chunk, 16)
                copies.append(
                    (
                        block == full,
                        pltpu.make_async_copy(
                            wide.at[at, 0:rest], out_ref.at[pl.ds(start, rest), :], sems.at[at]
                        ),
                    )
                )
    for going, copy in copies:
        pl.when(going)(copy.start)
    for going, copy in copies:
        pl.when(going)(copy.wait)


def unfold(whole, chunk, bits, masks, blocks, before):
    n_dep = 0 if before is None else 1
    anywhere = pl.BlockSpec(memory_space=pl.ANY)
    n_copies = len(masks) * len(masks[0])
    return pl.pallas_call(
        functools.partial(unfold_kernel, whole.shape[0] // 2, chunk, bits, masks, n_dep),
        out_shape=whole,
        in_specs=[anywhere] * n_dep + [pl.BlockSpec(memory_space=pltpu.VMEM)] * len(blocks),
        out_specs=anywhere,
        scratch_shapes=[
            pltpu.VMEM((n_copies, chunk, whole.shape[1]), jnp.float32),
            pltpu.SemaphoreType.DMA((n_copies,)),
        ],
        input_output_aliases={0: 0} if n_dep else {},
        compiler_params=pltpu.CompilerParams(vmem_limit_bytes=40 * 1024 * 1024),
    )(*([before] if n_dep else []), *blocks)


def back_kernel(side, part, tall, weight_ref, inner_ref, pieces_ref):
    rows = side * side
    flat = rows + 2 * side
    start = pl.multiple_of(lax.axis_index("ch") * part, 16)
    backs = []
    for b in range(3):
        back = jnp.zeros((flat, part), jnp.float32)
        for a in range(3):
            back = back + lax.dot_general(
                tall[(2 - a) * side : (2 - a) * side + flat, :],
                weight_ref[3 * a + b, pl.ds(start, part), :],
                (((1,), (1,)), ((), ())),
                preferred_element_type=jnp.float32,
            )
        backs.append(back)
    column = lax.broadcasted_iota(jnp.int32, (flat, part), 0) % side
    inner = (
        jnp.where(column == side - 1, 0.0, pltpu.roll(backs[0], flat - 1, 0))
        + backs[1]
        + jnp.where(column == 0, 0.0, pltpu.roll(backs[2], 1, 0))
    )
    inner_ref[...] = inner[side : side + rows]
    west = backs[0].reshape(side + 2, side, part)[:, 0, :]
    east = backs[2].reshape(side + 2, side, part)[:, side - 1, :]
    pieces = jnp.concatenate(
        [
            inner[0:side],
            east[1 : side + 1],
            inner[side + rows :],
            west[1 : side + 1],
            west[0:1],
            east[0:1],
            east[side + 1 :],
            west[side + 1 :],
            jnp.zeros((EXTRA - 4, part), jnp.float32),
        ],
        axis=0,
    )
    pack(pieces.astype(jnp.bfloat16), pieces_ref)


def add_halo_kernel(side, part, place_ref, inner_ref, *refs):
    got_refs, out_ref, got = refs[:-2], refs[-2], refs[-1]
    block = 4 * side + EXTRA
    size = packed_shape(block, part)[0]
    for i, ref in enumerate(got_refs):
        for k in range(3):
            unpack(ref, got, k * size, (3 * i + k) * block, block, part)
    sums = jnp.dot(place_ref[...], got[...], preferred_element_type=jnp.float32)
    rows = side * side
    spread = lambda col: jnp.broadcast_to(col[:, None, :], (side, side, part)).reshape(rows, part)
    column = lax.broadcasted_iota(jnp.int32, (rows, part), 0) % side
    inner = inner_ref[...]
    inner = inner + jnp.where(column == side - 1, spread(sums[side : 2 * side]), 0.0)
    inner = inner + jnp.where(column == 0, spread(sums[3 * side :]), 0.0)
    ends = jnp.concatenate(
        [
            inner[0:side] + sums[0:side],
            inner[side : rows - side],
            inner[rows - side :] + sums[2 * side : 3 * side],
        ],
        axis=0,
    )
    out_ref[...] = ends.astype(jnp.bfloat16)


def parts_of(rows, extra):
    size = (rows + extra) // (32 * PARTS) * 32
    return [size] * (PARTS - 1) + [rows - size * (PARTS - 1)]


def halo_kernel(side, part, n_near, *refs):
    near_refs, tables_in, field_ref = refs[:n_near], refs[n_near], refs[n_near + 1]
    halos_ref, *packet_refs = refs[n_near + 2 : -3]
    near, tables, sem = refs[-3:]
    copy = pltpu.make_async_copy(tables_in, tables, sem)
    copy.start()
    rows = side * side
    unpack_near(near_refs, near, side, part)
    field = field_ref[...].reshape(rows, part)
    sizes = parts_of(rows, 4 * side + EXTRA)
    for k, ref in enumerate(packet_refs):
        pack(field[sum(sizes[:k]) : sum(sizes[: k + 1])], ref)
    copy.wait()
    index = Neighbours(side, tables)
    step = lax.broadcasted_iota(jnp.int32, (side, 1), 0)
    wanted = []
    for e in range(4):
        block, at = index.edge(index.own, e)
        wanted.append(block * (4 * side) + at(step))
    spots = lax.broadcasted_iota(jnp.int32, (EXTRA, 1), 0)
    ends = jnp.full((EXTRA, 1), -1, jnp.int32)
    for c in range(4):
        block, spot = index.corner(index.own, c)
        ends = jnp.where(spots == c, block * (4 * side) + spot, ends)
    pick = onehot(jnp.concatenate(wanted + [ends], axis=0), near.shape[0])
    halos = jnp.dot(pick, near[...], preferred_element_type=jnp.float32).astype(jnp.bfloat16)
    halos_ref[...] = halos
    pack(halos, packet_refs[-1], packed_shape(sizes[-1], part)[0])


def output_kernel(side, part, field_ref, halos_ref, weight_ref, *refs):
    rows = side * side
    ch = lax.axis_index("ch")
    other_refs, (out_ref, cols, other_cols, other) = refs[:PARTS], refs[PARTS:]
    wide = -(-part // 128) * 128
    lanes = pl.multiple_of(ch * (weight_ref.shape[2] - wide), 128)
    sizes = parts_of(rows, 4 * side + EXTRA)
    for k, ref in enumerate(other_refs):
        unpack(ref, other, 0, sum(sizes[:k]), sizes[k], part)
    unpack(other_refs[-1], other, packed_shape(sizes[-1], part)[0], rows, 4 * side + EXTRA, part)
    shifted_columns(side, part, field_ref[...].reshape(rows, part), halos_ref[...], cols)
    shifted_columns(side, part, other[0:rows, :], other[rows:, :], other_cols)
    starts = (pl.multiple_of(ch * part, 16), pl.multiple_of((1 - ch) * part, 16))
    total = jnp.zeros((rows, wide), jnp.float32)
    for a in range(3):
        for b in range(3):
            for ref, first in zip((cols, other_cols), starts):
                total = total + jnp.dot(
                    ref[b, a * side : a * side + rows, :],
                    weight_ref[3 * a + b, pl.ds(first, part), pl.ds(lanes, wide)],
                    preferred_element_type=jnp.float32,
                )
    result = jnp.where(ch == 0, total[:, :part], total[:, wide - part :])
    out_ref[...] = result.astype(jnp.bfloat16)


def body(features, weight, cotangent, edge_tiles, edge_turns, corner_tiles, corner_turns):
    count = lax.axis_size("tile")
    field = features[0]
    side, part = field.shape[0], field.shape[2]
    chans = weight.shape[3]
    rows = side * side
    flat = rows + 2 * side
    block = 4 * side + EXTRA
    taps = weight.reshape(9, chans, chans)
    others = [(0, 1), (1, 0)]
    flops = 2 * rows * 9 * part * chans
    half_bytes = jnp.bfloat16
    chunk = -(-9 * part // (16 * count)) * 16
    half = count * chunk // 2
    scale = 1.0 / math.sqrt(count * rows)

    cot_own = cotangent[0].reshape(rows, part)
    cot_other = lax.ppermute(cot_own, "ch", others)
    sides, field = call(
        functools.partial(sides_kernel, side),
        [vmem(packed_shape(4 * side, part), half_bytes), vmem(field.shape, half_bytes)],
        [field],
    )
    swaps = [by_swap(sides, odd, count) for odd in (0, 1)]
    across = by_mask(sides, 2, count)
    tables = jnp.concatenate([edge_tiles.T, edge_turns.T, corner_tiles.T, corner_turns.T], axis=0)
    table_scratch = [pltpu.SMEM(tables.shape, jnp.int32), pltpu.SemaphoreType.DMA]
    border_pick, cot_own = call(
        functools.partial(border_onehot_kernel, side),
        [vmem((16 * side, 48 * side), half_bytes), vmem((rows, part), half_bytes)],
        [tables, cot_own],
        scratch=table_scratch,
    )
    pair = packed_shape(8 * side, part)
    (beyond,) = call(join_kernel, [vmem(pair, half_bytes)], swaps)
    near = [sides, across, *swaps, by_mask(beyond, 2, count)]
    near, cot_other, border_pick = lax.optimization_barrier((near, cot_other, border_pick))
    (near,) = call(join_kernel, [vmem(packed_shape(24 * side, part), half_bytes)], near)
    mates = by_mask(near, 1, count)
    first, tall, rim, cols = call(
        functools.partial(send_kernel, side, part, scale),
        [
            vmem((3 * part, chans), jnp.float32),
            vmem((rows + 4 * side, chans), half_bytes),
            vmem((4 * side, chans), half_bytes),
            vmem((3, part, rows), half_bytes),
        ],
        [field, cot_own, cot_other],
        flops=flops // 4,
    )
    (second,) = call(
        functools.partial(half_kernel, side, part, scale, 1, (3,)),
        [vmem((3 * part // 2, chans), jnp.float32)],
        [cols, tall],
        scratch=[pltpu.VMEM((part, chans), jnp.float32)],
        flops=flops,
    )
    tall, second = lax.optimization_barrier((tall, second))
    (mine,) = call(
        functools.partial(half_kernel, side, part, scale, 0, (0, 1, 2, 3)),
        [vmem((9 * part // 2, chans), jnp.float32)],
        [cols, tall],
        scratch=[pltpu.VMEM((part, chans), jnp.float32)],
        costed=False,
    )
    mates, mine, rim_mate = lax.optimization_barrier((mates, mine, by_mask(rim, 1, count)))
    near = [near, mates]

    stages = mask_stages(count)
    masks = group_masks(stages[1])
    size = half // len(masks)
    held, *send = call(
        functools.partial(border_kernel, side, part, chunk, scale, len(near)),
        [vmem((size, chans), jnp.float32)] + [vmem((size, chans), half_bytes)] * (len(masks) - 1),
        [*near, border_pick, mine, rim, rim_mate, by_mask(first, 1, count), by_mask(second, 1, count)],
        scratch=[pltpu.VMEM((48 * side, part), half_bytes), pltpu.VMEM((half, chans), jnp.float32)],
    )
    send, tall, near = lax.optimization_barrier((send, tall, near))
    got = [by_mask(v, m, count) for v, m in zip(send, masks[1:])]
    inner, pieces = call(
        functools.partial(back_kernel, side, part),
        [vmem((rows, part), jnp.float32), vmem(packed_shape(block, part), half_bytes)],
        [tall, taps],
        flops=flops,
    )
    pieces, near = lax.optimization_barrier((pieces, near))
    here = [pieces, *[by_swap(pieces, odd, count) for odd in (1, 0)][::-1]]
    (place,) = call(
        functools.partial(place_kernel, side),
        [vmem((4 * side, 12 * block), half_bytes)],
        [tables],
        scratch=table_scratch,
    )
    halos, *packet = call(
        functools.partial(halo_kernel, side, part, len(near)),
        [vmem((block, part), half_bytes)]
        + [vmem(packed_shape(size, part), half_bytes) for size in parts_of(rows, block)[:-1]]
        + [vmem(packed_shape(parts_of(rows, block)[-1] + block, part), half_bytes)],
        [*near, tables, field],
        scratch=[pltpu.VMEM((48 * side, part), half_bytes), *table_scratch],
    )
    got, here[:2], inner, halos, packet, place = lax.optimization_barrier(
        (got, here[:2], inner, halos, packet, place)
    )
    swap = len(stages[-1]) == 1 and len(stages) > 2
    rs_stages = stages[2:-1] if swap else stages[2:]
    aside = [here, packet]

    def start_aside(send, aside):
        here = aside[0]
        send, here[0], packet = lax.optimization_barrier((send, here[0], aside[1]))
        (here,) = call(join_kernel, [vmem((3 * pieces.shape[0], pieces.shape[1]), half_bytes)], here)
        return send, here, by_mask(here, 2, count), [lax.ppermute(v, "ch", others) for v in packet]

    for index, bits in enumerate(rs_stages):
        masks = group_masks(bits)
        size = held.shape[0] // len(masks)
        held, *send = call(
            functools.partial(sum_kernel, len(got), len(masks)),
            [vmem((size, chans), jnp.float32)] + [vmem((size, chans), half_bytes)] * (len(masks) - 1),
            [held, *got],
        )
        if index == 0:
            send, here, beside, other_field = start_aside(send, aside)
        got = [by_mask(v, m, count) for v, m in zip(send, masks[1:])]
    (held,) = call(functools.partial(sum_kernel, len(got), 1), [vmem(held.shape, half_bytes)], [held, *got])
    if swap:
        if not rs_stages:
            held, here, beside, other_field = start_aside(held, aside)
        got = by_mask(held, stages[-1][0], count)
        got, here, beside = lax.optimization_barrier((got, here, beside))
        (held,) = call(exchange_kernel, [vmem(held.shape, half_bytes)], [held, got])
    order = [0] if not swap else [0, stages[-1][0]]
    ag_stages = stages[-2:0:-1] if swap else stages[:0:-1]
    for index, bits in enumerate(ag_stages):
        masks = group_masks(bits)
        got = [by_mask(held, m, count) for m in masks[1:]]
        if index < len(ag_stages) - 1:
            order = [m + v for m in masks for v in order]
            (held,) = call(
                join_kernel, [vmem((held.shape[0] * len(masks), chans), half_bytes)], [held, *got]
            )
    order = [[m + v for v in order] for m in masks]
    got_pieces = [here, beside, by_mask(here, 1, count), by_mask(beside, 1, count)]
    (grad_features,) = call(
        functools.partial(add_halo_kernel, side, part),
        [vmem((rows, part), half_bytes)],
        [place, inner, *got_pieces],
        scratch=[pltpu.VMEM((12 * block, part), half_bytes)],
    )
    (output,) = call(
        functools.partial(output_kernel, side, part),
        [vmem((rows, part), half_bytes)],
        [field, halos, taps, *other_field],
        scratch=[
            pltpu.VMEM((3, flat, part), half_bytes),
            pltpu.VMEM((3, flat, part), half_bytes),
            pltpu.VMEM((rows + block, part), half_bytes),
        ],
        flops=2 * flops,
    )
    got, grad_features, output = lax.optimization_barrier((got, grad_features, output))
    got = [held, *got]
    mates = [by_mask(v, 1, count) for v in got]
    whole = vmem((9 * part, chans), jnp.float32)
    own = len(got)
    first = unfold(whole, chunk, [0] * own + [1], order + order[:1], got + mates[:1], None)
    grad_weight = unfold(whole, chunk, [1] * (own - 1), order[1:], mates[1:], first)
    shape = (1, side, side, part)
    return (
        output.reshape(shape),
        grad_features.reshape(shape),
        grad_weight.reshape(3, 3, part, chans),
    )


def solution(mesh):
    return jax.shard_map(
        body,
        mesh=mesh,
        in_specs=(
            P("tile", None, None, "ch"),
            P(),
            P("tile", None, None, "ch"),
            P(),
            P(),
            P(),
            P(),
        ),
        out_specs=(
            P("tile", None, None, "ch"),
            P("tile", None, None, "ch"),
            P(None, None, "ch", None),
        ),
        check_vma=False,
    )
```

```python
import functools
import math

import jax
import jax.numpy as jnp
import numpy as np
from jax import lax
from jax.experimental import pallas as pl
from jax.experimental.pallas import tpu as pltpu
from jax.sharding import PartitionSpec as P

SPAN = 4
EXTRA = 16
PARTS = 3


def turn_tables():
    labels = [[3 * row + col for col in range(3)] for row in range(3)]

    def turn_once(block):
        return [[block[col][2 - row] for col in range(3)] for row in range(3)]

    def sides_of(block):
        return [
            list(block[0]),
            [block[row][2] for row in range(3)],
            list(block[2]),
            [block[row][0] for row in range(3)],
        ]

    def corners_of(block):
        return [block[0][0], block[0][2], block[2][2], block[2][0]]

    base_sides = sides_of(labels)
    base_corners = corners_of(labels)
    edge_table = np.zeros((4, 4), np.int32)
    corner_table = np.zeros((4, 4), np.int32)
    for border in range(4):
        turned = labels
        for quarter in range(4):
            wanted = sides_of(turned)[(border + 2) % 4]
            for side_index in range(4):
                if base_sides[side_index] == wanted:
                    edge_table[border, quarter] = side_index
                if base_sides[side_index][::-1] == wanted:
                    edge_table[border, quarter] = side_index + 4
            corner_cell = corners_of(turned)[(border + 2) % 4]
            for corner_index in range(4):
                if base_corners[corner_index] == corner_cell:
                    corner_table[border, quarter] = corner_index
            turned = turn_once(turned)
    tables = np.concatenate([edge_table, corner_table], axis=0)
    return [sum(int(slot) << (3 * quarter) for quarter, slot in enumerate(row)) for row in tables]


def by_swap(value, odd, count):
    pairs = [
        (i, (i + (SPAN if (i // SPAN) % 2 == odd else -SPAN)) % count) for i in range(count)
    ]
    return lax.ppermute(value, "tile", pairs)


def by_mask(value, mask, count):
    return lax.ppermute(value, "tile", [(i, i ^ mask) for i in range(count)])


def mask_stages(count):
    bits = [1 << b for b in range(count.bit_length() - 1)]
    stages = [bits[:1]]
    rest = bits[1:]
    while rest:
        stages.append(rest[:2])
        rest = rest[2:]
    return stages


def group_masks(bits):
    masks = [0]
    for bit in bits:
        masks = masks + [m + bit for m in masks]
    return masks


def slot_of_mask(mask, count):
    place = 0
    for bits in mask_stages(count)[1:]:
        size = 1 << len(bits)
        place = place * size + (mask // bits[0]) % size
    return place


def slot_in(row, quarter):
    return (row >> (3 * quarter)) & 7


def corner_spot(slot, side):
    return jnp.where(
        slot == 0, 0, jnp.where(slot == 1, side - 1, jnp.where(slot == 2, 3 * side - 1, 2 * side))
    )


def vmem(shape, dtype):
    return jax.ShapeDtypeStruct(shape, dtype)


def call(kernel, outs, args, anywhere=(), scratch=(), flops=0, costed=True):
    in_specs = [
        pl.BlockSpec(memory_space=pltpu.HBM if i in anywhere else pltpu.VMEM) for i in range(len(args))
    ]
    size = costed * sum(math.prod(x.shape) * x.dtype.itemsize for x in list(args) + list(outs))
    return pl.pallas_call(
        kernel,
        out_shape=tuple(outs),
        in_specs=in_specs,
        out_specs=tuple(pl.BlockSpec(memory_space=pltpu.VMEM) for _ in outs),
        scratch_shapes=list(scratch),
        compiler_params=pltpu.CompilerParams(vmem_limit_bytes=40 * 1024 * 1024),
        cost_estimate=pl.CostEstimate(flops=flops, bytes_accessed=size, transcendentals=0),
    )(*args)


def packed_shape(rows, part):
    if part % 128 != 64:
        return (rows, part)
    return (rows * (part // 128) + upper_half(rows), 128)


def upper_half(rows):
    return -(-rows // 32) * 16


def pack(value, out_ref, first=0):
    rows, part = value.shape
    if part % 128 != 64:
        out_ref[first : first + rows, :] = value
        return
    for i in range(part // 128):
        out_ref[first + i * rows : first + (i + 1) * rows, :] = value[:, i * 128 : (i + 1) * 128]
    rest = value[:, part - 64 :]
    at = first + rows * (part // 128)
    cut = upper_half(rows)
    out_ref[at : at + cut, 0:64] = rest[:cut]
    out_ref[at : at + rows - cut, 64:128] = rest[cut:]
    if rows < 2 * cut:
        out_ref[at + rows - cut : at + cut, 64:128] = jnp.zeros((2 * cut - rows, 64), out_ref.dtype)


def unpack(ref, out_ref, first, row, rows, part):
    if part % 128 != 64:
        out_ref[row : row + rows, :] = ref[first : first + rows, :]
        return
    for i in range(part // 128):
        out_ref[row : row + rows, i * 128 : (i + 1) * 128] = ref[first + i * rows : first + (i + 1) * rows, :]
    at = first + rows * (part // 128)
    cut = upper_half(rows)
    out_ref[row : row + cut, part - 64 :] = ref[at : at + cut, :][:, :64]
    out_ref[row + cut : row + rows, part - 64 :] = ref[at : at + rows - cut, :][:, 64:]


def sides_kernel(side, field_ref, sides_ref, copy_ref):
    sides = jnp.concatenate(
        [field_ref[0], field_ref[:, side - 1, :], field_ref[side - 1], field_ref[:, 0, :]], axis=0
    )
    pack(sides, sides_ref)
    copy_ref[...] = field_ref[...]


def shifted_columns(side, part, field, halos, out_ref):
    rows = side * side
    flat = rows + 2 * side
    column = lax.broadcasted_iota(jnp.int32, (flat, part), 0) % side
    if halos is None:
        none = jnp.zeros((side, part), jnp.float32)
        tall = jnp.concatenate([none, field.astype(jnp.float32), none], axis=0)
        west = east = 0.0
    else:
        edge = halos.astype(jnp.float32)
        tall = jnp.concatenate([edge[0:side], field.astype(jnp.float32), edge[2 * side : 3 * side]], axis=0)
        corner = [edge[4 * side + c : 4 * side + c + 1] for c in range(4)]
        spread = lambda col: jnp.broadcast_to(col[:, None, :], (side + 2, side, part)).reshape(flat, part)
        east = spread(jnp.concatenate([corner[1], edge[side : 2 * side], corner[2]], axis=0))
        west = spread(jnp.concatenate([corner[0], edge[3 * side : 4 * side], corner[3]], axis=0))
    out_ref[0] = jnp.where(column == 0, west, pltpu.roll(tall, 1, 0)).astype(jnp.bfloat16)
    out_ref[1] = tall.astype(jnp.bfloat16)
    out_ref[2] = jnp.where(column == side - 1, east, pltpu.roll(tall, flat - 1, 0)).astype(jnp.bfloat16)


class Neighbours:
    def __init__(self, side, tables):
        self.side = side
        self.et, self.eu, self.ct, self.cu = [tables.at[4 * i : 4 * i + 4] for i in range(4)]
        self.digits = turn_tables()
        self.count = lax.axis_size("tile")
        self.own = lax.axis_index("tile")

    def block(self, source):
        groups = self.count // SPAN
        slab = lax.rem(source // SPAN - self.own // SPAN + groups, groups)
        cross = source ^ self.own
        turn = lax.rem(cross // 2, 2)
        even = lax.rem(self.own // SPAN, 2) == 0
        at = jnp.where(slab == 0, turn, jnp.where((slab == 1) == even, 2, 3) + 2 * turn)
        return 6 * lax.rem(cross, 2) + at

    def edge(self, tile, e):
        slot = slot_in(self.digits[e], self.eu[e, tile])
        start = lax.rem(slot, 4) * self.side
        end = start + self.side - 1
        return self.block(self.et[e, tile]), lambda at: jnp.where(slot >= 4, end - at, start + at)

    def corner(self, tile, c):
        slot = slot_in(self.digits[4 + c], self.cu[c, tile])
        return self.block(self.ct[c, tile]), corner_spot(slot, self.side)


def onehot(wanted, width):
    lane = lax.broadcasted_iota(jnp.int32, (wanted.shape[0], width), 1)
    return jnp.where(lane == wanted, 1.0, 0.0).astype(jnp.bfloat16)


def border_onehot_kernel(side, tables_in, cot_in, border_ref, cot_ref, tables, sem):
    copy = pltpu.make_async_copy(tables_in, tables, sem)
    copy.start()
    cot_ref[...] = cot_in[...]
    border_ref[...] = jnp.zeros_like(border_ref)
    copy.wait()
    near = Neighbours(side, tables)
    low = lax.rem(near.own, 2) == 0
    width = 4 * side
    step = lax.broadcasted_iota(jnp.int32, (side, 1), 0)

    def put(row, block, wanted, add=False):
        here = (slice(row, row + side), pl.ds(pl.multiple_of(block * width, 128), width))
        value = onehot(wanted, width)
        border_ref[here] = border_ref[here] + value if add else value

    for m, tile in enumerate((near.own, near.own ^ 1)):
        first = 2 * m * side
        flat = [near.edge(tile, e) for e in range(4)]
        corners = [near.corner(tile, c) for c in range(4)]
        pick = lambda a, b: (jnp.where(low, a[0], b[0]), lambda at: jnp.where(low, a[1](at), b[1](at)))
        block, at = pick(flat[0], flat[2])
        left, right = [
            (jnp.where(low, corners[a][0], corners[b][0]), jnp.where(low, corners[a][1], corners[b][1]))
            for a, b in ((0, 3), (1, 2))
        ]
        along = jnp.where(low, step - 1, step + 1)
        fits = (along >= 0) & (along < side)
        put(first, block, jnp.where(step == 0, -1, at(step - 1)))
        put(first, left[0], jnp.where(step == 0, left[1], -1), add=True)
        put(first + side, flat[3][0], jnp.where(fits, flat[3][1](along), -1))
        put(first + 4 * side, block, at(step))
        put(first + 8 * side, block, jnp.where(step == side - 1, -1, at(step + 1)))
        put(first + 8 * side, right[0], jnp.where(step == side - 1, right[1], -1), add=True)
        put(first + 9 * side, flat[1][0], jnp.where(fits, flat[1][1](along), -1))
        block, at = pick(flat[3], flat[1])
        put(first + 13 * side, block, at(step))


def place_kernel(side, tables_in, place_ref, tables, sem):
    copy = pltpu.make_async_copy(tables_in, tables, sem)
    copy.start()
    copy.wait()
    near = Neighbours(side, tables)
    block = 4 * side + EXTRA
    lane = lax.broadcasted_iota(jnp.int32, (1, block), 1)
    row = lax.broadcasted_iota(jnp.int32, (4 * side, block), 0)
    places = []
    swap = jnp.where(lax.rem(near.own // SPAN, 2) == 0, SPAN, -SPAN)
    for mask in (0, 2, 1, 3):
        for offset in (0, swap, -swap):
            source = lax.rem((near.own ^ mask) + offset + near.count, near.count)
            target = jnp.full((1, block), -1, jnp.int32)
            for e in range(4):
                slot = slot_in(near.digits[e], near.eu[e, source])
                along = lane - e * side
                along = jnp.where(slot >= 4, side - 1 - along, along)
                hit = (lane >= e * side) & (lane < (e + 1) * side) & (near.et[e, source] == near.own)
                target = jnp.where(hit, lax.rem(slot, 4) * side + along, target)
                spot = corner_spot(slot_in(near.digits[4 + e], near.cu[e, source]), side)
                hit = (lane == 4 * side + e) & (near.ct[e, source] == near.own)
                target = jnp.where(hit, spot, target)
            places.append(jnp.where(row == target, 1.0, 0.0))
    place_ref[...] = jnp.concatenate(places, axis=1).astype(jnp.bfloat16)


def tap_product(side, scale, tap, cols, tall):
    rows = side * side
    start = pl.multiple_of((3 - tap // 3) * side, 16)
    value = jnp.dot(
        cols[lax.rem(tap, 3)], tall[pl.ds(start, rows), :], preferred_element_type=jnp.float32
    )
    return value * scale


def send_kernel(
    side, part, scale, field_ref, own_ref, other_ref, send_ref, tall_ref, rim_ref, cols_ref
):
    rows = side * side
    first = lax.axis_index("ch") == 0
    here = slice(2 * side, 2 * side + rows)
    blank = jnp.zeros((2 * side, tall_ref.shape[1]), jnp.bfloat16)
    tall_ref[0 : 2 * side, :] = blank
    tall_ref[2 * side + rows :, :] = blank

    @pl.when(first)
    def _():
        tall_ref[here, 0:part] = own_ref[...]
        tall_ref[here, part:] = other_ref[...]

    @pl.when(jnp.logical_not(first))
    def _():
        tall_ref[here, 0:part] = other_ref[...]
        tall_ref[here, part:] = own_ref[...]

    cot = tall_ref[here, :]
    column = lax.broadcasted_iota(jnp.int32, (rows, part), 0) % side
    field = field_ref[...].reshape(rows, part).astype(jnp.float32)
    cols_ref[0] = jnp.where(column == 0, 0.0, pltpu.roll(field, 1, 0)).astype(jnp.bfloat16).T
    cols_ref[1] = field.astype(jnp.bfloat16).T
    cols_ref[2] = jnp.where(column == side - 1, 0.0, pltpu.roll(field, rows - 1, 0)).astype(jnp.bfloat16).T
    which = 1 - lax.rem(lax.axis_index("tile"), 2)
    for j in range(3):
        send_ref[j * part : (j + 1) * part, :] = tap_product(side, scale, j + 5 * which, cols_ref, tall_ref)
    rim = cot.reshape(side, side, cot.shape[1])
    rim_ref[...] = jnp.concatenate([cot[0:side], cot[rows - side :], rim[:, 0, :], rim[:, side - 1, :]], axis=0)


def half_kernel(side, part, scale, mate, taps, cols, tall, out_ref, middle):
    which = lax.rem(lax.axis_index("tile") + mate, 2)
    for at, j in enumerate(taps):
        out_ref[at * part : (at + 1) * part, :] = tap_product(side, scale, j + 5 * which, cols, tall)
    middle[...] = tap_product(side, scale, 4, cols, tall)
    start = pl.multiple_of(which * (part // 2), 16)
    out_ref[len(taps) * part :, :] = middle[pl.ds(start, part // 2), :]


def unpack_near(near_refs, near, side, part):
    size = packed_shape(4 * side, part)[0]
    row = 0
    for ref in near_refs:
        for k in range(ref.shape[0] // size):
            unpack(ref, near, k * size, row, 4 * side, part)
            row += 4 * side


def border_kernel(side, part, chunk, scale, n_near, *refs):
    near_refs = refs[:n_near]
    onehot_ref, mine_ref, rim_ref, mate_ref, first_ref, second_ref = refs[n_near : n_near + 6]
    outs, near, total = refs[n_near + 6 : -2], refs[-2], refs[-1]
    count = lax.axis_size("tile")
    own = lax.axis_index("tile")
    core = lax.rem(own, 2)
    unpack_near(near_refs, near, side, part)
    half = part // 2
    used = 9 * half

    def place(start, value):
        total[pl.ds(pl.multiple_of(start, 16), value.shape[0]), :] = value

    cut = first_ref.shape[0]
    place(core * half, mine_ref[0:cut, :] + first_ref[...])
    if cut < 4 * part:
        place(core * half + cut, mine_ref[cut : 4 * part, :] + second_ref[0 : 4 * part - cut, :])
    place((1 - core) * 4 * part, mine_ref[4 * part :, :] + second_ref[4 * part - cut :, :])
    total[used:, :] = jnp.zeros((total.shape[0] - used, total.shape[1]), jnp.float32)
    left = jnp.dot(onehot_ref[...], near[...], preferred_element_type=jnp.float32).astype(jnp.bfloat16)

    def rim(ref, at):
        return ref[pl.ds(pl.multiple_of(at, 16), side), :]

    for q in range(4):
        column = (2 + q // 2) * side if q < 3 else (2 + core) * side
        right = jnp.concatenate(
            [value for ref in (rim_ref, mate_ref) for value in (rim(ref, core * side), rim(ref, column))],
            axis=0,
        )
        value = lax.dot_general(
            left[q * 4 * side : (q + 1) * 4 * side],
            right,
            (((0,), (0,)), ((), ())),
            preferred_element_type=jnp.float32,
        )
        if q < 3:
            start = q * part + core * (part // 2 + part)
        else:
            start = 3 * part - core * (3 * part - part // 2)
        here = pl.ds(pl.multiple_of(start, 16), part)
        total[here, :] = total[here, :] + value * scale
    size = outs[0].shape[0]
    for index in range(count // 2):
        to = slot_of_mask(2 * index, count) * chunk
        block = pl.multiple_of(((own // 2) ^ index) * chunk, 16)
        out = outs[to // size]
        out[to % size : to % size + chunk, :] = total[pl.ds(block, chunk), :].astype(out.dtype)


def sum_kernel(n_got, n_out, *refs):
    held_ref, got_refs, outs = refs[0], refs[1 : 1 + n_got], refs[1 + n_got :]
    size = held_ref.shape[0] // n_out
    for index in range(n_out):
        here = slice(index * size, (index + 1) * size)
        value = held_ref[here, :]
        for ref in got_refs:
            value = value + ref[here, :].astype(jnp.float32)
        outs[index][...] = value.astype(outs[index].dtype)


def exchange_kernel(held_ref, got_ref, out_ref):
    half = held_ref.shape[0] // 2
    for a, b in ((0, half), (half, 0)):
        value = held_ref[a : a + half, :].astype(jnp.float32) + got_ref[b : b + half, :].astype(jnp.float32)
        out_ref[a : a + half, :] = value.astype(out_ref.dtype)


def join_kernel(*refs):
    row = 0
    for ref in refs[:-1]:
        refs[-1][row : row + ref.shape[0], :] = ref[...]
        row += ref.shape[0]


def unfold_kernel(used, chunk, bits, masks, n_dep, *refs):
    refs = refs[n_dep:]
    n = len(masks)
    in_refs, out_ref, wide, sems = refs[:n], refs[n], refs[n + 1], refs[n + 2]
    own = lax.axis_index("tile")
    full, rest = used // chunk, used % chunk
    copies = []
    for i, (ref, inner, bit) in enumerate(zip(in_refs, masks, bits)):
        origin = (lax.rem(own, 2) ^ bit) * used
        for k, mask in enumerate(inner):
            at = i * len(inner) + k
            wide[at] = ref[k * chunk : (k + 1) * chunk, :].astype(jnp.float32)
            block = (own ^ mask) // 2
            start = pl.multiple_of(origin + block * chunk, 16)
            copies.append(
                (
                    block < full,
                    pltpu.make_async_copy(wide.at[at], out_ref.at[pl.ds(start, chunk), :], sems.at[at]),
                )
            )
            if rest:
                start = pl.multiple_of(origin + full * chunk, 16)
                copies.append(
                    (
                        block == full,
                        pltpu.make_async_copy(
                            wide.at[at, 0:rest], out_ref.at[pl.ds(start, rest), :], sems.at[at]
                        ),
                    )
                )
    for going, copy in copies:
        pl.when(going)(copy.start)
    for going, copy in copies:
        pl.when(going)(copy.wait)


def unfold(whole, chunk, bits, masks, blocks, before):
    n_dep = 0 if before is None else 1
    anywhere = pl.BlockSpec(memory_space=pl.ANY)
    n_copies = len(masks) * len(masks[0])
    return pl.pallas_call(
        functools.partial(unfold_kernel, whole.shape[0] // 2, chunk, bits, masks, n_dep),
        out_shape=whole,
        in_specs=[anywhere] * n_dep + [pl.BlockSpec(memory_space=pltpu.VMEM)] * len(blocks),
        out_specs=anywhere,
        scratch_shapes=[
            pltpu.VMEM((n_copies, chunk, whole.shape[1]), jnp.float32),
            pltpu.SemaphoreType.DMA((n_copies,)),
        ],
        input_output_aliases={0: 0} if n_dep else {},
        compiler_params=pltpu.CompilerParams(vmem_limit_bytes=40 * 1024 * 1024),
    )(*([before] if n_dep else []), *blocks)


def back_kernel(side, part, tall, weight_ref, inner_ref, pieces_ref):
    rows = side * side
    flat = rows + 2 * side
    start = pl.multiple_of(lax.axis_index("ch") * part, 16)
    backs = []
    for b in range(3):
        back = jnp.zeros((flat, part), jnp.float32)
        for a in range(3):
            back = back + lax.dot_general(
                tall[(2 - a) * side : (2 - a) * side + flat, :],
                weight_ref[3 * a + b, pl.ds(start, part), :],
                (((1,), (1,)), ((), ())),
                preferred_element_type=jnp.float32,
            )
        backs.append(back)
    column = lax.broadcasted_iota(jnp.int32, (flat, part), 0) % side
    inner = (
        jnp.where(column == side - 1, 0.0, pltpu.roll(backs[0], flat - 1, 0))
        + backs[1]
        + jnp.where(column == 0, 0.0, pltpu.roll(backs[2], 1, 0))
    )
    inner_ref[...] = inner[side : side + rows]
    west = backs[0].reshape(side + 2, side, part)[:, 0, :]
    east = backs[2].reshape(side + 2, side, part)[:, side - 1, :]
    pieces = jnp.concatenate(
        [
            inner[0:side],
            east[1 : side + 1],
            inner[side + rows :],
            west[1 : side + 1],
            west[0:1],
            east[0:1],
            east[side + 1 :],
            west[side + 1 :],
            jnp.zeros((EXTRA - 4, part), jnp.float32),
        ],
        axis=0,
    )
    pack(pieces.astype(jnp.bfloat16), pieces_ref)


def add_halo_kernel(side, part, place_ref, inner_ref, *refs):
    got_refs, out_ref, got = refs[:-2], refs[-2], refs[-1]
    block = 4 * side + EXTRA
    size = packed_shape(block, part)[0]
    for i, ref in enumerate(got_refs):
        for k in range(3):
            unpack(ref, got, k * size, (3 * i + k) * block, block, part)
    sums = jnp.dot(place_ref[...], got[...], preferred_element_type=jnp.float32)
    rows = side * side
    spread = lambda col: jnp.broadcast_to(col[:, None, :], (side, side, part)).reshape(rows, part)
    column = lax.broadcasted_iota(jnp.int32, (rows, part), 0) % side
    inner = inner_ref[...]
    inner = inner + jnp.where(column == side - 1, spread(sums[side : 2 * side]), 0.0)
    inner = inner + jnp.where(column == 0, spread(sums[3 * side :]), 0.0)
    ends = jnp.concatenate(
        [
            inner[0:side] + sums[0:side],
            inner[side : rows - side],
            inner[rows - side :] + sums[2 * side : 3 * side],
        ],
        axis=0,
    )
    out_ref[...] = ends.astype(jnp.bfloat16)


def parts_of(rows, extra):
    size = (rows + extra) // (32 * PARTS) * 32
    return [size] * (PARTS - 1) + [rows - size * (PARTS - 1)]


def halo_kernel(side, part, n_near, *refs):
    near_refs, tables_in, field_ref = refs[:n_near], refs[n_near], refs[n_near + 1]
    halos_ref, *packet_refs = refs[n_near + 2 : -3]
    near, tables, sem = refs[-3:]
    copy = pltpu.make_async_copy(tables_in, tables, sem)
    copy.start()
    rows = side * side
    unpack_near(near_refs, near, side, part)
    field = field_ref[...].reshape(rows, part)
    sizes = parts_of(rows, 4 * side + EXTRA)
    for k, ref in enumerate(packet_refs):
        pack(field[sum(sizes[:k]) : sum(sizes[: k + 1])], ref)
    copy.wait()
    index = Neighbours(side, tables)
    step = lax.broadcasted_iota(jnp.int32, (side, 1), 0)
    wanted = []
    for e in range(4):
        block, at = index.edge(index.own, e)
        wanted.append(block * (4 * side) + at(step))
    spots = lax.broadcasted_iota(jnp.int32, (EXTRA, 1), 0)
    ends = jnp.full((EXTRA, 1), -1, jnp.int32)
    for c in range(4):
        block, spot = index.corner(index.own, c)
        ends = jnp.where(spots == c, block * (4 * side) + spot, ends)
    pick = onehot(jnp.concatenate(wanted + [ends], axis=0), near.shape[0])
    halos = jnp.dot(pick, near[...], preferred_element_type=jnp.float32).astype(jnp.bfloat16)
    halos_ref[...] = halos
    pack(halos, packet_refs[-1], packed_shape(sizes[-1], part)[0])


def output_kernel(side, part, field_ref, halos_ref, weight_ref, *refs):
    rows = side * side
    ch = lax.axis_index("ch")
    other_refs, (out_ref, cols, other_cols, other) = refs[:PARTS], refs[PARTS:]
    wide = -(-part // 128) * 128
    lanes = pl.multiple_of(ch * (weight_ref.shape[2] - wide), 128)
    sizes = parts_of(rows, 4 * side + EXTRA)
    for k, ref in enumerate(other_refs):
        unpack(ref, other, 0, sum(sizes[:k]), sizes[k], part)
    unpack(other_refs[-1], other, packed_shape(sizes[-1], part)[0], rows, 4 * side + EXTRA, part)
    shifted_columns(side, part, field_ref[...].reshape(rows, part), halos_ref[...], cols)
    shifted_columns(side, part, other[0:rows, :], other[rows:, :], other_cols)
    starts = (pl.multiple_of(ch * part, 16), pl.multiple_of((1 - ch) * part, 16))
    total = jnp.zeros((rows, wide), jnp.float32)
    for a in range(3):
        for b in range(3):
            for ref, first in zip((cols, other_cols), starts):
                total = total + jnp.dot(
                    ref[b, a * side : a * side + rows, :],
                    weight_ref[3 * a + b, pl.ds(first, part), pl.ds(lanes, wide)],
                    preferred_element_type=jnp.float32,
                )
    result = jnp.where(ch == 0, total[:, :part], total[:, wide - part :])
    out_ref[...] = result.astype(jnp.bfloat16)


def body(features, weight, cotangent, edge_tiles, edge_turns, corner_tiles, corner_turns):
    count = lax.axis_size("tile")
    field = features[0]
    side, part = field.shape[0], field.shape[2]
    chans = weight.shape[3]
    rows = side * side
    flat = rows + 2 * side
    block = 4 * side + EXTRA
    taps = weight.reshape(9, chans, chans)
    others = [(0, 1), (1, 0)]
    flops = 2 * rows * 9 * part * chans
    half_bytes = jnp.bfloat16
    chunk = -(-9 * part // (16 * count)) * 16
    half = count * chunk // 2
    scale = 1.0 / math.sqrt(count * rows)

    cot_own = cotangent[0].reshape(rows, part)
    cot_other = lax.ppermute(cot_own, "ch", others)
    sides, field = call(
        functools.partial(sides_kernel, side),
        [vmem(packed_shape(4 * side, part), half_bytes), vmem(field.shape, half_bytes)],
        [field],
    )
    swaps = [by_swap(sides, odd, count) for odd in (0, 1)]
    across = by_mask(sides, 2, count)
    tables = jnp.concatenate([edge_tiles.T, edge_turns.T, corner_tiles.T, corner_turns.T], axis=0)
    table_scratch = [pltpu.SMEM(tables.shape, jnp.int32), pltpu.SemaphoreType.DMA]
    border_pick, cot_own = call(
        functools.partial(border_onehot_kernel, side),
        [vmem((16 * side, 48 * side), half_bytes), vmem((rows, part), half_bytes)],
        [tables, cot_own],
        scratch=table_scratch,
    )
    pair = packed_shape(8 * side, part)
    (beyond,) = call(join_kernel, [vmem(pair, half_bytes)], swaps)
    near = [sides, across, *swaps, by_mask(beyond, 2, count)]
    near, cot_other, border_pick = lax.optimization_barrier((near, cot_other, border_pick))
    (near,) = call(join_kernel, [vmem(packed_shape(24 * side, part), half_bytes)], near)
    mates = by_mask(near, 1, count)
    first, tall, rim, cols = call(
        functools.partial(send_kernel, side, part, scale),
        [
            vmem((3 * part, chans), jnp.float32),
            vmem((rows + 4 * side, chans), half_bytes),
            vmem((4 * side, chans), half_bytes),
            vmem((3, part, rows), half_bytes),
        ],
        [field, cot_own, cot_other],
        flops=flops // 4,
    )
    (second,) = call(
        functools.partial(half_kernel, side, part, scale, 1, (3,)),
        [vmem((3 * part // 2, chans), jnp.float32)],
        [cols, tall],
        scratch=[pltpu.VMEM((part, chans), jnp.float32)],
        flops=flops,
    )
    tall, second = lax.optimization_barrier((tall, second))
    (mine,) = call(
        functools.partial(half_kernel, side, part, scale, 0, (0, 1, 2, 3)),
        [vmem((9 * part // 2, chans), jnp.float32)],
        [cols, tall],
        scratch=[pltpu.VMEM((part, chans), jnp.float32)],
        costed=False,
    )
    mates, mine, rim_mate = lax.optimization_barrier((mates, mine, by_mask(rim, 1, count)))
    near = [near, mates]

    stages = mask_stages(count)
    masks = group_masks(stages[1])
    size = half // len(masks)
    held, *send = call(
        functools.partial(border_kernel, side, part, chunk, scale, len(near)),
        [vmem((size, chans), jnp.float32)] + [vmem((size, chans), half_bytes)] * (len(masks) - 1),
        [*near, border_pick, mine, rim, rim_mate, by_mask(first, 1, count), by_mask(second, 1, count)],
        scratch=[pltpu.VMEM((48 * side, part), half_bytes), pltpu.VMEM((half, chans), jnp.float32)],
    )
    send, tall, near = lax.optimization_barrier((send, tall, near))
    got = [by_mask(v, m, count) for v, m in zip(send, masks[1:])]
    inner, pieces = call(
        functools.partial(back_kernel, side, part),
        [vmem((rows, part), jnp.float32), vmem(packed_shape(block, part), half_bytes)],
        [tall, taps],
        flops=flops,
    )
    pieces, near = lax.optimization_barrier((pieces, near))
    here = [pieces, *[by_swap(pieces, odd, count) for odd in (1, 0)][::-1]]
    (place,) = call(
        functools.partial(place_kernel, side),
        [vmem((4 * side, 12 * block), half_bytes)],
        [tables],
        scratch=table_scratch,
    )
    halos, *packet = call(
        functools.partial(halo_kernel, side, part, len(near)),
        [vmem((block, part), half_bytes)]
        + [vmem(packed_shape(size, part), half_bytes) for size in parts_of(rows, block)[:-1]]
        + [vmem(packed_shape(parts_of(rows, block)[-1] + block, part), half_bytes)],
        [*near, tables, field],
        scratch=[pltpu.VMEM((48 * side, part), half_bytes), *table_scratch],
    )
    got, here[:2], inner, halos, packet, place = lax.optimization_barrier(
        (got, here[:2], inner, halos, packet, place)
    )
    swap = len(stages[-1]) == 1 and len(stages) > 2
    rs_stages = stages[2:-1] if swap else stages[2:]
    aside = [here, packet]

    def start_aside(send, aside):
        here = aside[0]
        send, here[0], packet = lax.optimization_barrier((send, here[0], aside[1]))
        lines, lanes = pieces.shape
        (swapped,) = call(join_kernel, [vmem((2 * lines, lanes), half_bytes)], here[1:])
        parts = [by_mask(v, 2, count) for v in (here[0], swapped)]
        (here,) = call(join_kernel, [vmem((3 * lines, lanes), half_bytes)], [here[0], swapped])
        (beside,) = call(join_kernel, [vmem((3 * lines, lanes), half_bytes)], parts)
        return send, here, beside, [lax.ppermute(v, "ch", others) for v in packet]

    for index, bits in enumerate(rs_stages):
        masks = group_masks(bits)
        size = held.shape[0] // len(masks)
        held, *send = call(
            functools.partial(sum_kernel, len(got), len(masks)),
            [vmem((size, chans), jnp.float32)] + [vmem((size, chans), half_bytes)] * (len(masks) - 1),
            [held, *got],
        )
        if index == 0:
            send, here, beside, other_field = start_aside(send, aside)
        got = [by_mask(v, m, count) for v, m in zip(send, masks[1:])]
    (held,) = call(functools.partial(sum_kernel, len(got), 1), [vmem(held.shape, half_bytes)], [held, *got])
    if swap:
        if not rs_stages:
            held, here, beside, other_field = start_aside(held, aside)
        got = by_mask(held, stages[-1][0], count)
        got, here, beside = lax.optimization_barrier((got, here, beside))
        (held,) = call(exchange_kernel, [vmem(held.shape, half_bytes)], [held, got])
    order = [0] if not swap else [0, stages[-1][0]]
    ag_stages = stages[-2:0:-1] if swap else stages[:0:-1]
    for index, bits in enumerate(ag_stages):
        masks = group_masks(bits)
        got = [by_mask(held, m, count) for m in masks[1:]]
        if index < len(ag_stages) - 1:
            order = [m + v for m in masks for v in order]
            (held,) = call(
                join_kernel, [vmem((held.shape[0] * len(masks), chans), half_bytes)], [held, *got]
            )
    order = [[m + v for v in order] for m in masks]
    got_pieces = [here, beside, by_mask(here, 1, count), by_mask(beside, 1, count)]
    (grad_features,) = call(
        functools.partial(add_halo_kernel, side, part),
        [vmem((rows, part), half_bytes)],
        [place, inner, *got_pieces],
        scratch=[pltpu.VMEM((12 * block, part), half_bytes)],
    )
    (output,) = call(
        functools.partial(output_kernel, side, part),
        [vmem((rows, part), half_bytes)],
        [field, halos, taps, *other_field],
        scratch=[
            pltpu.VMEM((3, flat, part), half_bytes),
            pltpu.VMEM((3, flat, part), half_bytes),
            pltpu.VMEM((rows + block, part), half_bytes),
        ],
        flops=2 * flops,
    )
    got, grad_features, output = lax.optimization_barrier((got, grad_features, output))
    got = [held, *got]
    mates = [by_mask(v, 1, count) for v in got]
    whole = vmem((9 * part, chans), jnp.float32)
    own = len(got)
    first = unfold(whole, chunk, [0] * own + [1], order + order[:1], got + mates[:1], None)
    grad_weight = unfold(whole, chunk, [1] * (own - 1), order[1:], mates[1:], first)
    shape = (1, side, side, part)
    return (
        output.reshape(shape),
        grad_features.reshape(shape),
        grad_weight.reshape(3, 3, part, chans),
    )


def solution(mesh):
    return jax.shard_map(
        body,
        mesh=mesh,
        in_specs=(
            P("tile", None, None, "ch"),
            P(),
            P("tile", None, None, "ch"),
            P(),
            P(),
            P(),
            P(),
        ),
        out_specs=(
            P("tile", None, None, "ch"),
            P("tile", None, None, "ch"),
            P(None, None, "ch", None),
        ),
        check_vma=False,
    )
```
